32 devices in a mesh: batch: 2 (over y), orient: 8 (over z, core), cls: 2 (over x), rep: 1.
Axes of the slice: x: 2, y: 2, z: 4, core: 2. Of those that a mesh axis runs over, the one named last changes fastest.
Arguments:
- images: bfloat16 [4, 128, 2, 7296], P(('batch', 'cls'), 'orient', 'rep'), parts along dimension 0, may hold values from -9.5 to 9.5
- defocus: bfloat16 [4, 128], P(('batch', 'cls'), 'orient'), parts along dimension 0, may hold values from 0.5 to 2
- block_ids: int32 [4, 128, 4], P(('batch', 'cls'), 'orient'), parts along dimension 0, may hold values from 0 to 7, all different within a row; in each aligned block of 16 rows (0 to 15, 16 to 31, ..., all dimensions but the last counted through in order) at most 16 rows name the same one
- noise_weight: float32 [7296], replicated, may hold values from 0.02 to 0.2
- panels: bfloat16 [4, 8, 128, 2, 7296], P(('batch', 'cls'), 'orient', None, 'rep'), parts along dimension 0, may hold values from -4 to 4
Outputs:
- posteriors: float32 [4, 8, 128, 256], P(('batch', 'cls'), 'orient', None, 'rep'), parts along dimension 0
The draws below stay inside these ranges and needn't reach their ends.
There are 2 independent parts, one for each index of `batch`. The reference program is written for one: setup_inputs(seed, part) draws one part's arguments, and reference() takes and returns one part's arrays. A program takes and returns all parts, laid end to end along the dimension named above; an argument that names none is the same for every part. Nothing has to cross between parts.
Inputs may be any that keep to these rules, and one draw needn't show every extreme that they name: `block_ids`: each particle names 4 different blocks; among the 16 particles of one index of orient (aligned runs of 16 rows over the first two dimensions) no block is named more than 16 times, and 16 is reached.
All inputs are finite; a program needn't handle non-finite values.
Results may differ from the reference program's by a relative error of at most 0.0215.
Values may be sent and summed in bfloat16 or wider, within the bound.
No kernel may reach another device: no remote copies, remote signals or barrier semaphores. Data moves between devices by JAX's collectives and lax.ppermute only.
A program may use at most 64 MiB of HBM per device.

```python
import math
import jax
import jax.numpy as jnp
import numpy as np
from jax import lax

K = 7296
BLK = 128
PD = 16
C = 2
GROUPS = 2
NPG = 128
NB = 8
M = 4
Q = 16
CAP = 128
N_ORIENT = 8


def shared_defocus(key):
    return jax.random.uniform(jax.random.fold_in(key, 71), (GROUPS, NPG), jnp.float32, 0.5, 2.0)


def draw_defocus(key, part):
    return shared_defocus(key).astype(jnp.bfloat16)


def draw_images(key, part):
    key = jax.random.fold_in(key, 3)
    result = jnp.clip(jax.random.normal(key, (GROUPS, NPG, 2, K), jnp.float32), -4.0, 4.0)
    return result.astype(jnp.bfloat16)


def draw_panels(key, part):
    key = jax.random.fold_in(key, 4)
    result = jnp.clip(jax.random.normal(key, (C, NB, BLK, 2, K), jnp.float32), -4.0, 4.0)
    return result.astype(jnp.bfloat16)


def assign_block(rng, own, number, rows, amount, top, bound, lean):
    order = jax.random.permutation(rng, amount)
    heavy_load, ordinary = shares(amount, rows * top, bound, lean, True), shares(amount, rows * top, bound, lean, False)
    places = jnp.arange(amount)

    def named(tallies, rotation):
        used = int((tallies > 0).sum())
        fixed = max(1, used // 4)
        shifted = fixed + (places - fixed + rotation * (used - fixed)) % max(1, amount - fixed)
        return jnp.zeros((amount,), jnp.int32).at[order[jnp.where(places < fixed, places, shifted)]].set(jnp.asarray(tallies, jnp.int32))

    tallies = jnp.where(number % 4 == 0, named(heavy_load, number // 4), named(ordinary, number - number // 4 - 1))
    mixed = jax.random.permutation(jax.random.fold_in(own, 3), amount)
    donor, sink = mixed[0:amount // 2 * 2:2], mixed[1:amount // 2 * 2:2]
    room = jnp.minimum(tallies[donor] - 1, bound - tallies[sink]) // 2
    room = jnp.where((donor == order[0]) | (sink == order[0]) | (tallies[sink] == 0), 0, jnp.maximum(room, 0))
    shifted = jax.random.randint(jax.random.fold_in(own, 4), (amount // 2,), 0, 1 << 20) % (room + 1)
    tallies = tallies.at[donor].add(-shifted).at[sink].add(shifted)
    labels = jnp.searchsorted(jnp.cumsum(tallies), jnp.arange(rows * top), side="right").astype(jnp.int32)
    table = labels.reshape(top, rows).T
    table = table[jax.random.permutation(jax.random.fold_in(own, 1), rows)]
    rotation = jax.random.randint(jax.random.fold_in(own, 2), (rows, 1), 0, top)
    return jnp.take_along_axis(table, (jnp.arange(top)[None, :] + rotation) % top, axis=1)


def shares(amount, total, most, lean, full):
    weights = [(1 << 20) // math.isqrt(rank ** lean) + 1 for rank in range(1, amount + 1)]
    largest = most if full else min(most, max(-(-total // amount), total * weights[0] // sum(weights)))
    least = 1 if total - largest >= amount - 1 else 0
    counts, spare = [largest] + [least] * (amount - 1), total - largest - least * (amount - 1)
    while spare > 0:
        free = [i for i in range(1, amount) if counts[i] < largest] or [i for i in range(1, amount) if counts[i] < most]
        whole, budget = sum([weights[i] for i in free]), spare
        for i in free:
            more = min(most - counts[i], max(1, budget * weights[i] // whole), spare)
            counts[i] = counts[i] + more
            spare = spare - more
    return np.array(counts)


def setup_inputs(seed: int = 0, part: int = 0) -> dict:
    keys = jax.random.split(jax.random.key(seed), 6)
    own_keys = jax.random.split(jax.random.fold_in(keys[5], part), 6)
    images = draw_images(jax.random.fold_in(jax.random.fold_in(keys[5], part), 71), part)
    defocus = draw_defocus(jax.random.fold_in(jax.random.fold_in(keys[5], part), 71), part)
    block_ids_keys = jax.random.split(jax.random.fold_in(own_keys[2], 1), GROUPS * NPG // PD)
    block_ids_turns = jax.random.permutation(jax.random.fold_in(own_keys[2], 3), GROUPS * NPG // PD)
    block_ids = jax.vmap(lambda own, number: assign_block(jax.random.fold_in(own_keys[2], 2), own, number, PD, NB, M, Q, 2))(block_ids_keys, block_ids_turns).reshape((GROUPS, NPG, M))
    noise_weight = jnp.clip(jnp.exp(jax.random.uniform(keys[3], (K,), jnp.float32, math.log(0.02), math.log(0.2))), 0.02, 0.2)
    panels = draw_panels(jax.random.fold_in(jax.random.fold_in(keys[5], part), 71), part)
    return {"images": images, "defocus": defocus, "block_ids": block_ids, "noise_weight": noise_weight, "panels": panels}


CTF_PHASE = 40.0


def reference(images, defocus, block_ids, noise_weight, panels):
    frequency = (jnp.arange(K, dtype=jnp.float32) + 0.5) / K
    contrast = -jnp.sin(CTF_PHASE * defocus.astype(jnp.float32)[:, :, None] * frequency + 0.1)
    weighted = contrast * noise_weight
    scaled = (weighted[:, :, None, :] * images.astype(jnp.float32)).astype(jnp.bfloat16)
    energy = (contrast * weighted).astype(jnp.bfloat16)
    widened = panels.astype(jnp.float32)
    squared = (widened * widened).astype(jnp.bfloat16)
    block_hits = jnp.any(block_ids[:, :, :, None] == jnp.arange(NB, dtype=jnp.int32), axis=2).astype(jnp.int32)
    spanned = block_hits.reshape(GROUPS, N_ORIENT, PD, NB)
    slot_rank = (jnp.cumsum(spanned, axis=2) - spanned).astype(jnp.int32)
    places = (jnp.arange(N_ORIENT, dtype=jnp.int32)[None, :, None, None] * Q + slot_rank).reshape(GROUPS, NPG, NB).astype(jnp.int32)
    chosen = (places[:, :, :, None] == jnp.arange(CAP, dtype=jnp.int32)) & (block_hits[:, :, :, None] == 1)
    slot_owner = jnp.sum(jnp.where(chosen, jnp.arange(NPG, dtype=jnp.int32)[None, :, None, None], 0), axis=1).astype(jnp.int32)

    def one_block(index):
        owners = lax.dynamic_index_in_dim(slot_owner, index, 1, keepdims=False)
        picked = jnp.take_along_axis(scaled, owners[:, :, None, None], axis=1).astype(jnp.float32)
        picked_energy = jnp.take_along_axis(energy, owners[:, :, None], axis=1).astype(jnp.float32)
        block_panel = lax.dynamic_index_in_dim(panels, index, 1, keepdims=False).astype(jnp.float32)
        block_square = lax.dynamic_index_in_dim(squared, index, 1, keepdims=False).astype(jnp.float32)
        correlate = jnp.einsum("gsrk,cjrk->gscj", picked, block_panel)
        energy_term = jnp.einsum("gsk,cjrk->gscj", picked_energy, block_square)
        return (correlate - 0.5 * energy_term).reshape(GROUPS, CAP, C * BLK)

    every = lax.map(one_block, jnp.arange(NB, dtype=jnp.int32))
    every = jnp.transpose(every, (1, 0, 2, 3)).reshape(GROUPS, NB * CAP, C * BLK)
    taken_slot = jnp.take_along_axis(places, block_ids, axis=2)
    flat_index = (block_ids * CAP + taken_slot).astype(jnp.int32).reshape(GROUPS, NPG * M)
    gathered = jnp.take_along_axis(every, flat_index[:, :, None], axis=1).reshape(GROUPS, NPG, M * C * BLK)
    peak = jnp.max(gathered, axis=2, keepdims=True)
    expo = jnp.exp(gathered - peak)
    posterior = expo / jnp.sum(expo, axis=2, keepdims=True)
    result = jnp.zeros((GROUPS, NB * CAP, C * BLK), jnp.float32)
    result = result.at[jnp.arange(GROUPS, dtype=jnp.int32)[:, None], flat_index].set(posterior.reshape(GROUPS, NPG * M, C * BLK))
    return result.reshape(GROUPS, NB, CAP, C * BLK)
```

```python
import functools

import jax
import jax.numpy as jnp
from jax import lax
from jax.experimental import pallas as pl
from jax.experimental.pallas import tpu as pltpu
from jax.sharding import PartitionSpec as P

CTF_PHASE = 40.0
FLOOR = -1e30
LANES = 128


def score_kernel(chunks, tiles, columns, *refs):
    rows = refs[:chunks]
    meta = refs[chunks : 2 * chunks]
    noise, own_panel, mate_panel, own_out, mate_out, sin_a, cos_a, sin_b, cos_b = refs[2 * chunks :]
    step = pl.program_id(0)
    count = sin_a.shape[0]

    @pl.when(step == 0)
    def _():
        focus = jnp.concatenate([m[:, 0:1] for m in meta], axis=0).astype(jnp.float32)
        rate = CTF_PHASE * focus
        lane = lax.broadcasted_iota(jnp.int32, (count, LANES), 1).astype(jnp.float32)
        coarse = rate * (lane * (LANES / columns)) + 0.1
        fine = rate * ((lane + 0.5) / columns)
        sin_a[...] = jnp.sin(coarse)
        cos_a[...] = jnp.cos(coarse)
        sin_b[...] = jnp.sin(fine)
        cos_b[...] = jnp.cos(fine)
        own_out[...] = jnp.zeros_like(own_out)
        mate_out[...] = jnp.zeros_like(mate_out)

    shift = lax.rem(LANES - step * tiles, LANES)
    sa = pltpu.roll(sin_a[...], shift, 1)
    ca = pltpu.roll(cos_a[...], shift, 1)
    sb = sin_b[...]
    cb = cos_b[...]
    scaled_parts, energy_parts = [], []
    for t in range(tiles):
        window = slice(t * LANES, (t + 1) * LANES)
        contrast = -(sa[:, t : t + 1] * cb + ca[:, t : t + 1] * sb)
        weighted = contrast * noise[:, window]
        image = jnp.concatenate([r[:, window] for r in rows], axis=0).astype(jnp.float32)
        scaled_parts.append((weighted * image).astype(jnp.bfloat16))
        energy_parts.append((-0.5 * (contrast * weighted)).astype(jnp.bfloat16))
    scaled = jnp.concatenate(scaled_parts, axis=1)
    energy = jnp.concatenate(energy_parts, axis=1)
    for panel, out in ((own_panel, own_out), (mate_panel, mate_out)):
        values = panel[...]
        wide = values.astype(jnp.float32)
        squared = (wide * wide).astype(jnp.bfloat16)
        contract = (((1,), (1,)), ((), ()))
        out[...] += lax.dot_general(
            scaled, values, contract, preferred_element_type=jnp.float32
        ) + lax.dot_general(energy, squared, contract, preferred_element_type=jnp.float32)


def partial_scores(chunks, noise, own_panel, mate_panel):
    each = chunks[0].shape[0]
    columns = own_panel.shape[1]
    orientations = own_panel.shape[0]
    whole = columns // LANES
    steps = next(s for s in (3, 2, 4, 5, 6, 7, 1) if whole % s == 0)
    tiles = whole // steps
    width = tiles * LANES
    count = each * len(chunks)
    n = len(chunks)
    row_spec = pl.BlockSpec((each, width), lambda s: (0, s))
    meta_spec = pl.BlockSpec((each, LANES), lambda s: (0, whole))
    panel_spec = pl.BlockSpec((orientations, width), lambda s: (0, s))
    out_spec = pl.BlockSpec((count, orientations), lambda s: (0, 0))
    return pl.pallas_call(
        functools.partial(score_kernel, n, tiles, columns),
        grid=(steps,),
        in_specs=[row_spec] * n
        + [meta_spec] * n
        + [pl.BlockSpec((1, width), lambda s: (0, s)), panel_spec, panel_spec],
        out_specs=[out_spec, out_spec],
        out_shape=[jax.ShapeDtypeStruct((count, orientations), jnp.float32)] * 2,
        scratch_shapes=[pltpu.VMEM((count, LANES), jnp.float32)] * 4,
        compiler_params=pltpu.CompilerParams(vmem_limit_bytes=32 * 1024 * 1024),
        cost_estimate=pl.CostEstimate(
            flops=8 * count * orientations * columns,
            bytes_accessed=4 * orientations * columns + 2 * count * columns,
            transcendentals=4 * count * LANES,
        ),
    )(*chunks, *chunks, noise, own_panel, mate_panel)


def swap_halves(values, per_device):
    shape = values.shape
    split = values.reshape((-1, 2, per_device) + shape[1:])
    return jnp.flip(split, axis=1).reshape(shape)


def chip_shards(images, defocus, block_ids, noise_weight, panels):
    per_device, halves, columns = images.shape[1:]
    devices = lax.axis_size("orient")
    chips = devices // 2
    groups = lax.axis_size("cls")
    local_search = block_ids.shape[2]
    orientations = panels.shape[2]
    slots_each = min(per_device, max(2, 2 * per_device * local_search // devices))
    capacity = slots_each * devices
    place = lax.axis_index("orient")
    chip, core = place // 2, place % 2
    first = core == 0

    mate_pairs = [(d, d ^ 1) for d in range(devices)]
    x_pairs = [(0, 1), (1, 0)]

    def turn(step, cross=False):
        return [(d, (d + 2 * step) % devices ^ int(cross)) for d in range(devices)]

    facts = jnp.concatenate(
        [defocus[0][:, None], block_ids[0].astype(jnp.bfloat16)], axis=1
    )
    facts = jnp.pad(facts, ((0, 0), (0, LANES - facts.shape[1])))
    part = [jnp.concatenate([images[0, :, r, :], facts], axis=1) for r in range(2)]
    kept = jnp.where(first, part[0], part[1])
    given = jnp.where(first, part[1], part[0])
    own_chunk = jnp.concatenate([kept, lax.ppermute(given, "orient", mate_pairs)], axis=0)

    chunks = [own_chunk]
    for step in range(1, chips):
        chunks.append(lax.ppermute(own_chunk, "orient", turn(step)))
    other_chunks = [lax.ppermute(c, "cls", x_pairs) for c in chunks]

    sides = [panels[0, 0, :, r, :] for r in range(2)]
    own_panel = jnp.where(first, sides[0], sides[1])
    given_panel = jnp.where(first, sides[1], sides[0])
    mate_panel = lax.ppermute(given_panel, "orient", mate_pairs)

    noise = noise_weight[None, :]
    here_own, here_mate = partial_scores(chunks, noise, own_panel, mate_panel)
    there_own, there_mate = partial_scores(other_chunks, noise, own_panel, mate_panel)

    from_mate = lax.ppermute(here_mate, "orient", mate_pairs)
    from_x = lax.ppermute(there_own, "cls", x_pairs)
    from_both = lax.ppermute(
        there_mate,
        ("orient", "cls"),
        [(d * 2 + g, (d ^ 1) * 2 + 1 - g) for d in range(devices) for g in range(2)],
    )
    mine = here_own + swap_halves(from_mate, per_device)
    theirs = from_x + swap_halves(from_both, per_device)
    zero_class = lax.axis_index("cls") == 0
    scores = jnp.concatenate(
        [jnp.where(zero_class, mine, theirs), jnp.where(zero_class, theirs, mine)], axis=1
    )

    everyone = per_device * devices
    lists = jnp.concatenate([c[:, columns + 1 : columns + 1 + local_search] for c in chunks], axis=0)
    named = jnp.any(lists.astype(jnp.int32) == place, axis=1)
    hits = named.astype(jnp.int32).reshape(devices, per_device)
    rank = jnp.cumsum(hits, axis=1) - hits
    run = jnp.arange(devices, dtype=jnp.int32)
    owner = ((chip - run // 2 + chips) % chips) * 2 + (core ^ (run % 2))
    places = jnp.where(
        named, (owner[:, None] * slots_each + rank).reshape(everyone), -1
    )
    chosen = places[None, :] == jnp.arange(capacity, dtype=jnp.int32)[:, None]

    top = jnp.where(named, jnp.max(scores, axis=1), FLOOR)
    expo = jnp.where(named[:, None], jnp.exp(scores - top[:, None]), 0.0)
    total = jnp.sum(expo, axis=1)
    stats = jnp.stack([top, total])
    gathered = [stats]
    for step in range(chips):
        for cross in (False, True):
            if step == 0 and not cross:
                continue
            got = lax.ppermute(stats, "orient", turn(step, cross))
            got = got.reshape(2, chips, 2, per_device)
            got = jnp.roll(got, step, axis=1)
            if cross:
                got = jnp.flip(got, axis=2)
            gathered.append(got.reshape(2, everyone))
    slots = jnp.dot(
        chosen.astype(jnp.float32),
        expo,
        precision=lax.Precision.HIGHEST,
        preferred_element_type=jnp.float32,
    )
    peak = functools.reduce(jnp.maximum, [s[0] for s in gathered])
    denominator = functools.reduce(jnp.add, [s[1] * jnp.exp(s[0] - peak) for s in gathered])
    factor = jnp.exp(top - peak) / denominator
    slot_factor = jnp.sum(jnp.where(chosen, factor[None, :], 0.0), axis=1)
    posterior = slots * slot_factor[:, None]
    return posterior.reshape(1, 1, capacity, -1)


def spread_max(member, is_live, values):
    picked = jnp.max(jnp.where(member, values[None, :], FLOOR), axis=1)
    return jnp.where(is_live, picked, 0.0)


def collect_sums(member, expo):
    return jnp.sum(jnp.where(member, jnp.sum(expo, axis=1)[:, None], 0.0), axis=0)


def shards(images, defocus, block_ids, noise_weight, panels):
    per_device = images.shape[1]
    columns = images.shape[3]
    devices = lax.axis_size("orient")
    local_search = block_ids.shape[2]
    slots_each = min(per_device, max(2, 2 * per_device * local_search // devices))
    capacity = slots_each * devices
    everyone = per_device * devices
    all_lists = lax.all_gather(block_ids[0], "orient", axis=0, tiled=True)
    all_rows, all_focus = (
        lax.all_gather(images[0], "orient", axis=0, tiled=True),
        lax.all_gather(defocus[0], "orient", axis=0, tiled=True),
    )
    own_block = lax.axis_index("orient")
    block_hits = (
        jnp.any(all_lists == own_block, axis=1).astype(jnp.int32).reshape(devices, per_device)
    )
    slot_rank = jnp.cumsum(block_hits, axis=1) - block_hits
    places = (jnp.arange(devices, dtype=jnp.int32)[:, None] * slots_each + slot_rank).reshape(
        everyone
    )
    chosen = (places[None, :] == jnp.arange(capacity, dtype=jnp.int32)[:, None]) & (
        block_hits.reshape(everyone)[None, :] == 1
    )
    is_live = jnp.any(chosen, axis=1)
    slot_owner = jnp.sum(
        jnp.where(chosen, jnp.arange(everyone, dtype=jnp.int32)[None, :], 0), axis=1
    )
    slot_rows = jnp.take(all_rows, slot_owner, axis=0)
    slot_focus = jnp.take(all_focus, slot_owner, axis=0).astype(jnp.float32)
    frequency = (jnp.arange(columns, dtype=jnp.float32) + 0.5) / columns
    contrast = -jnp.sin(CTF_PHASE * slot_focus[:, None] * frequency[None, :] + 0.1)
    weighted = contrast * noise_weight[None, :]
    scaled_rows = (weighted[:, None, :] * slot_rows.astype(jnp.float32)).astype(jnp.bfloat16)
    energy = (contrast * weighted).astype(jnp.bfloat16)
    piece = lax.all_gather(panels[:, 0], "cls", axis=0, tiled=True)
    widened = piece.astype(jnp.float32)
    squared = (widened * widened).astype(jnp.bfloat16)
    correlate = jnp.einsum("srk,cjrk->scj", scaled_rows, piece, preferred_element_type=jnp.float32)
    energy_term = jnp.einsum("sk,cjrk->scj", energy, squared, preferred_element_type=jnp.float32)
    terms = correlate - 0.5 * energy_term
    combined = terms.reshape(capacity, -1)
    scores = lax.psum_scatter(combined, "rep", scatter_dimension=1, tiled=True)
    member = (slot_owner[:, None] == jnp.arange(everyone, dtype=jnp.int32)[None, :]) & is_live[
        :, None
    ]
    slot_top = jnp.max(scores, axis=1)
    local_peak = jnp.max(jnp.where(member, slot_top[:, None], FLOOR), axis=0)
    peak = lax.pmax(local_peak, ("orient", "rep"))
    slot_peak = spread_max(member, is_live, peak)
    expo = jnp.where(is_live[:, None], jnp.exp(scores - slot_peak[:, None]), 0.0)
    total = lax.psum(collect_sums(member, expo), ("orient", "rep"))
    slot_total = jnp.where(is_live, jnp.sum(jnp.where(member, total[None, :], 0.0), axis=1), 1.0)
    posterior = expo / slot_total[:, None]
    return posterior.reshape(1, 1, capacity, -1)


def solution(mesh):
    in_specs = (
        P(("batch", "cls"), "orient", "rep", None),
        P(("batch", "cls"), "orient"),
        P(("batch", "cls"), "orient", None),
        P(),
        P(("batch", "cls"), "orient", None, "rep", None),
    )
    out_specs = P(("batch", "cls"), "orient", None, "rep")
    sizes = mesh.shape
    paired = sizes["rep"] == 1 and sizes["cls"] == 2 and sizes["orient"] % 2 == 0
    return jax.shard_map(
        chip_shards if paired else shards,
        mesh=mesh,
        in_specs=in_specs,
        out_specs=out_specs,
        check_vma=False,
    )
```

```python
import functools

import jax
import jax.numpy as jnp
from jax import lax
from jax.experimental import pallas as pl
from jax.experimental.pallas import tpu as pltpu
from jax.sharding import PartitionSpec as P

CTF_PHASE = 40.0
FLOOR = -1e30
LANES = 128
VMEM_LIMIT = 32 * 1024 * 1024


def sin_cos(angle):
    turns = jnp.floor(angle * 0.6366197723675814 + 0.5)
    rest = angle - turns * 1.5703125
    rest = rest - turns * 4.837512969970703e-4
    rest = rest - turns * 7.549789948768648e-8
    square = rest * rest
    sine = rest + rest * square * (
        -1.6666654611e-1 + square * (8.3321608736e-3 - square * 1.9515295891e-4)
    )
    cosine = (
        1.0
        - 0.5 * square
        + square
        * square
        * (4.166664568298827e-2 + square * (-1.388731625493765e-3 + square * 2.443315711809948e-5))
    )
    quarter = turns.astype(jnp.int32)
    odd = (quarter & 1) == 1
    low = jnp.where(odd, cosine, sine)
    high = jnp.where(odd, sine, cosine)
    return (
        jnp.where((quarter & 2) == 2, -low, low),
        jnp.where(((quarter + 1) & 2) == 2, -high, high),
    )


def add_scores(rows, meta, noise, panels, outs, tables, tiles, columns):
    step = pl.program_id(0)
    sin_a, cos_a, sin_b, cos_b = tables
    count = sin_a.shape[0]

    @pl.when(step == 0)
    def _():
        focus = jnp.concatenate([m[:, 0:1] for m in meta], axis=0).astype(jnp.float32)
        rate = CTF_PHASE * focus
        lane = lax.broadcasted_iota(jnp.int32, (count, LANES), 1).astype(jnp.float32)
        coarse_sin, coarse_cos = sin_cos(rate * (lane * (LANES / columns)) + 0.1)
        sin_a[...] = -coarse_sin
        cos_a[...] = -coarse_cos
        fine_sin, fine_cos = sin_cos(rate * ((lane + 0.5) / columns))
        sin_b[...] = fine_sin
        cos_b[...] = fine_cos
        for out in outs:
            out[...] = jnp.zeros_like(out)

    shift = lax.rem(LANES - step * tiles, LANES)
    sa = pltpu.roll(sin_a[...], shift, 1)
    ca = pltpu.roll(cos_a[...], shift, 1)
    sb = sin_b[...]
    cb = cos_b[...]
    scaled_parts, energy_parts = [], []
    for t in range(tiles):
        window = slice(t * LANES, (t + 1) * LANES)
        contrast = sa[:, t : t + 1] * cb + ca[:, t : t + 1] * sb
        weighted = contrast * noise[:, window]
        image = jnp.concatenate([r[:, window] for r in rows], axis=0).astype(jnp.float32)
        scaled_parts.append((weighted * image).astype(jnp.bfloat16))
        energy_parts.append((contrast * weighted).astype(jnp.bfloat16))
    scaled = jnp.concatenate(scaled_parts, axis=1)
    energy = jnp.concatenate(energy_parts, axis=1)
    contract = (((1,), (1,)), ((), ()))
    for panel, out in zip(panels, outs):
        values = panel[...]
        squared = values * values
        correlate = lax.dot_general(scaled, values, contract, preferred_element_type=jnp.float32)
        power = lax.dot_general(energy, squared, contract, preferred_element_type=jnp.float32)
        out[...] += correlate - 0.5 * power


def batch_kernel(n, tiles, columns, spot, *refs):
    del spot
    rows, meta = refs[:n], refs[n : 2 * n]
    noise, own_panel, mate_panel, own_out, mate_out, fact_out = refs[2 * n : 2 * n + 6]
    tables = refs[2 * n + 6 :]
    add_scores(
        rows, meta, noise, (own_panel, mate_panel), (own_out, mate_out), tables, tiles, columns
    )
    fact_out[...] = jnp.concatenate([m[...] for m in meta], axis=0).astype(jnp.float32)


def last_kernel(n, tiles, columns, steps, orders, spot, *refs):
    rows, meta = refs[:n], refs[n : 2 * n]
    noise, own_panel, mate_panel = refs[2 * n : 2 * n + 3]
    earlier = refs[2 * n + 3 : 2 * n + 3 + 3 * (len(orders) - 1)]
    here_own, here_mate, there_own, there_mate, facts, own_sum, mate_sum, *rest = refs[
        2 * n + 3 + len(earlier) :
    ]
    tables, (own_all, mate_all, fact_all) = rest[:4], rest[4:]
    add_scores(
        rows, meta, noise, (own_panel, mate_panel), (own_sum, mate_sum), tables, tiles, columns
    )

    @pl.when(pl.program_id(0) == steps - 1)
    def _():
        group, position, core = spot[0], spot[1], spot[2]
        each = rows[0].shape[0]
        ring = own_all.shape[0] // (2 * each)
        half = ring // 2
        last_facts = jnp.concatenate([m[...] for m in meta], axis=0).astype(jnp.float32)
        for index, order in enumerate(orders):
            if index < len(orders) - 1:
                own, mate, fact = [r[...] for r in earlier[3 * index : 3 * index + 3]]
            else:
                own, mate, fact = own_sum[...], mate_sum[...], last_facts
            for k, (distance, crossed) in enumerate(order):
                place = lax.rem(position + distance + ring, ring)
                far = place >= half
                level = jnp.where(far, ring - 1 - place, place)
                device = 2 * level + (1 - core if crossed else core)
                side = jnp.where(far, 1, 0)
                other = jnp.where(side == group, 0, 1)
                start = pl.multiple_of((other * ring + device) * each, each)
                piece = slice(k * each, (k + 1) * each)
                own_all[pl.ds(start, each), :] = own[piece]
                mate_all[pl.ds(start, each), :] = mate[piece]
                fact_all[pl.ds(start, each), :] = fact[piece]
        everyone = ring * each
        here_own[...] = own_all[:everyone]
        here_mate[...] = mate_all[:everyone]
        there_own[...] = own_all[everyone:]
        there_mate[...] = mate_all[everyone:]
        facts[...] = fact_all[:everyone]


def score_call(chunks, orders, earlier, spot, noise, sides, mate_panel):
    each = chunks[0].shape[0]
    orientations, columns = mate_panel.shape
    whole = columns // LANES
    steps = next(s for s in (3, 2, 4, 5, 6, 7, 1) if whole % s == 0)
    tiles = whole // steps
    width = tiles * LANES
    n = len(chunks)
    count = each * n
    row_spec = pl.BlockSpec((each, width), lambda s, spot: (0, s))
    meta_spec = pl.BlockSpec((each, LANES), lambda s, spot: (0, whole))
    fixed = lambda shape: pl.BlockSpec(shape, lambda s, spot: (0, 0))
    in_specs = (
        [row_spec] * n
        + [meta_spec] * n
        + [
            pl.BlockSpec((1, width), lambda s, spot: (0, s)),
            pl.BlockSpec((None, orientations, width), lambda s, spot: (spot[2], 0, s)),
            pl.BlockSpec((orientations, width), lambda s, spot: (0, s)),
        ]
    )
    table = [pltpu.VMEM((count, LANES), jnp.float32)] * 4
    single = jax.ShapeDtypeStruct((count, orientations), jnp.float32)
    if orders is None:
        kernel = functools.partial(batch_kernel, n, tiles, columns)
        out_shape = [single, single, jax.ShapeDtypeStruct((count, LANES), jnp.float32)]
        scratch = table
        extra = []
    else:
        everyone = each * sum(len(o) for o in orders) // 2
        kernel = functools.partial(last_kernel, n, tiles, columns, steps, orders)
        block = jax.ShapeDtypeStruct((everyone, orientations), jnp.float32)
        out_shape = [block] * 4 + [jax.ShapeDtypeStruct((everyone, LANES), jnp.float32)]
        sums = pltpu.VMEM((count, orientations), jnp.float32)
        whole_sums = pltpu.VMEM((2 * everyone, orientations), jnp.float32)
        scratch = (
            [sums, sums]
            + table
            + [whole_sums, whole_sums, pltpu.VMEM((2 * everyone, LANES), jnp.float32)]
        )
        extra = [e for triple in earlier for e in triple]
        in_specs = in_specs + [fixed(e.shape) for e in extra]
    return pl.pallas_call(
        kernel,
        grid_spec=pltpu.PrefetchScalarGridSpec(
            num_scalar_prefetch=1,
            grid=(steps,),
            in_specs=in_specs,
            out_specs=[fixed(o.shape) for o in out_shape],
            scratch_shapes=scratch,
        ),
        out_shape=out_shape,
        compiler_params=pltpu.CompilerParams(vmem_limit_bytes=VMEM_LIMIT),
        cost_estimate=pl.CostEstimate(
            flops=8 * max(count, 128) * orientations * columns,
            bytes_accessed=4 * orientations * columns + 2 * count * columns,
            transcendentals=0,
        ),
    )(spot, *chunks, *chunks, noise, sides, mate_panel, *extra)


def stats_kernel(search, slots_each, each, spot, mine, mate, across, both, facts, slots, chosen, stats):
    group, block = spot[0], spot[3]
    count = mine.shape[0]
    same = mine[...] + mate[...]
    other = across[...] + both[...]
    first = group == 0
    scores = jnp.concatenate(
        [jnp.where(first, same, other), jnp.where(first, other, same)], axis=1
    )
    lane = lax.broadcasted_iota(jnp.int32, (count, LANES), 1)
    row = lax.broadcasted_iota(jnp.int32, (count, LANES), 0)
    match = (lane >= 1) & (lane <= search) & (facts[...] == block.astype(jnp.float32))
    hit = jnp.max(jnp.where(match, 1.0, 0.0), axis=1, keepdims=True)
    named = hit > 0.0
    line = lax.broadcasted_iota(jnp.int32, (count, count), 0)
    column = lax.broadcasted_iota(jnp.int32, (count, count), 1)
    before = (column < line) & (column // each == line // each)
    rank = jnp.dot(
        jnp.where(before, 1.0, 0.0).astype(jnp.bfloat16),
        jnp.broadcast_to(hit, (count, LANES)).astype(jnp.bfloat16),
        preferred_element_type=jnp.float32,
    )
    slot = (row // each) * slots_each + rank.astype(jnp.int32)
    capacity = chosen.shape[0]
    if capacity != LANES:
        slot = jnp.broadcast_to(slot[:, :1], (count, capacity))
    target = lax.broadcasted_iota(jnp.int32, (count, capacity), 1)
    taken = jnp.where((slot == target) & named, 1.0, 0.0)
    top = jnp.where(named, jnp.max(scores, axis=1, keepdims=True), FLOOR)
    terms = jnp.where(named, jnp.exp(scores - top), 0.0)
    total = jnp.sum(terms, axis=1, keepdims=True)
    slots[...] = lax.dot_general(
        taken,
        terms,
        (((0,), (0,)), ((), ())),
        precision=lax.Precision.HIGHEST,
        preferred_element_type=jnp.float32,
    )
    chosen[...] = taken.T
    pair = jnp.where(lane == 0, top, jnp.where(lane == 1, total, 0.0))
    stats[...] = pair.T[: stats.shape[0]]


def final_kernel(n, *refs):
    own, parts, slots, chosen, out = refs[0], refs[1 : 1 + n], refs[1 + n], refs[2 + n], refs[3 + n]
    tops = [p[0:1, :] for p in parts]
    peak = functools.reduce(jnp.maximum, tops)
    total = functools.reduce(jnp.add, [p[1:2, :] * jnp.exp(p[0:1, :] - peak) for p in parts])
    factor = jnp.exp(own[0:1, :] - peak) / total
    scale = jnp.sum(chosen[...] * factor, axis=1, keepdims=True)
    out[...] = slots[...] * scale


def chip_shards(images, defocus, block_ids, noise_weight, panels):
    per_device, halves, columns = images.shape[1:]
    devices = lax.axis_size("orient")
    chips = devices // 2
    ring = 2 * chips
    everyone = per_device * devices
    local_search = block_ids.shape[2]
    orientations = panels.shape[2]
    slots_each = min(per_device, max(2, 2 * per_device * local_search // devices))
    capacity = slots_each * devices
    place = lax.axis_index("orient")
    group = lax.axis_index("cls")
    chip, core = place // 2, place % 2
    position = jnp.where(group == 0, chip, ring - 1 - chip)
    spot = jnp.stack([group, position, core, place]).astype(jnp.int32)
    first = core == 0

    mate_pairs = [(d, d ^ 1) for d in range(devices)]
    x_pairs = [(0, 1), (1, 0)]

    def joint(place, core):
        place = place % ring
        far = place >= chips
        level = ring - 1 - place if far else place
        return (2 * level + core) * 2 + int(far)

    def forward(values, step):
        pairs = [(joint(p, c), joint(p + step, c)) for p in range(ring) for c in range(2)]
        return lax.ppermute(values, ("orient", "cls"), pairs)

    facts = jnp.concatenate([defocus[0][:, None], block_ids[0].astype(jnp.bfloat16)], axis=1)
    facts = jnp.pad(facts, ((0, 0), (0, LANES - facts.shape[1])))
    planes = lax.optimization_barrier(jnp.transpose(images[0], (1, 0, 2)))
    kept = jnp.concatenate([jnp.where(first, planes[0], planes[1]), facts], axis=1)
    given = jnp.concatenate([jnp.where(first, planes[1], planes[0]), facts], axis=1)
    got = lax.ppermute(given, "orient", mate_pairs)

    got, panels = lax.optimization_barrier((got, panels))
    sides = lax.optimization_barrier(jnp.transpose(panels[0, 0], (1, 0, 2)))
    mate_panel = lax.ppermute(
        lax.dynamic_index_in_dim(sides, 1 - core, 0, keepdims=False), "orient", mate_pairs
    )

    batches = [[((0, False), kept), ((0, True), got)]]
    ahead = {False: kept, True: got}
    behind = {False: kept, True: got}
    for step in range(1, chips + 1):
        arrived = []
        for crossed in (False, True):
            if step < chips or not crossed:
                ahead[crossed] = forward(ahead[crossed], 1)
                arrived.append(((-step, crossed), ahead[crossed]))
            if step < chips or crossed:
                behind[crossed] = forward(behind[crossed], -1)
                arrived.append(((step, crossed), behind[crossed]))
        batches.append(arrived)
    batches = [batches[0] + batches[1]] + batches[2:]

    noise = noise_weight[None, :]
    orders = [[key for key, _ in batch] for batch in batches]
    earlier = [
        score_call([c for _, c in batch], None, None, spot, noise, sides, mate_panel)
        for batch in batches[:-1]
    ]
    here_own, here_mate, there_own, there_mate, own_facts = score_call(
        [c for _, c in batches[-1]], orders, earlier, spot, noise, sides, mate_panel
    )

    from_mate = lax.ppermute(here_mate, "orient", mate_pairs)
    from_x = lax.ppermute(there_own, "cls", x_pairs)
    from_both = lax.ppermute(
        there_mate,
        ("orient", "cls"),
        [(d * 2 + g, (d ^ 1) * 2 + 1 - g) for d in range(devices) for g in range(2)],
    )
    vmem = pl.BlockSpec(memory_space=pltpu.VMEM)
    slots, chosen, stats = pl.pallas_call(
        functools.partial(stats_kernel, local_search, slots_each, per_device),
        in_specs=[pl.BlockSpec(memory_space=pltpu.SMEM)] + [vmem] * 5,
        out_specs=[vmem] * 3,
        out_shape=[
            jax.ShapeDtypeStruct((capacity, 2 * orientations), jnp.float32),
            jax.ShapeDtypeStruct((capacity, everyone), jnp.float32),
            jax.ShapeDtypeStruct((8, everyone), jnp.float32),
        ],
        compiler_params=pltpu.CompilerParams(vmem_limit_bytes=VMEM_LIMIT),
    )(spot, here_own, from_mate, from_x, from_both, own_facts)

    mate_stats = lax.ppermute(stats, "orient", mate_pairs)
    peak = jnp.maximum(stats[0], mate_stats[0])
    total = stats[1] * jnp.exp(stats[0] - peak) + mate_stats[1] * jnp.exp(mate_stats[0] - peak)
    pair = jnp.zeros_like(stats).at[0].set(peak).at[1].set(total)
    pairs = [pair] + [
        lax.ppermute(pair, "orient", [(d, (d + 2 * s) % devices) for d in range(devices)])
        for s in range(1, chips)
    ]
    posterior = pl.pallas_call(
        functools.partial(final_kernel, chips),
        in_specs=[vmem] * (chips + 3),
        out_specs=vmem,
        out_shape=jax.ShapeDtypeStruct((capacity, 2 * orientations), jnp.float32),
        compiler_params=pltpu.CompilerParams(vmem_limit_bytes=VMEM_LIMIT),
    )(stats, *pairs, slots, chosen)
    return posterior.reshape(1, 1, capacity, -1)


def spread_max(member, is_live, values):
    picked = jnp.max(jnp.where(member, values[None, :], FLOOR), axis=1)
    return jnp.where(is_live, picked, 0.0)


def collect_sums(member, expo):
    return jnp.sum(jnp.where(member, jnp.sum(expo, axis=1)[:, None], 0.0), axis=0)


def shards(images, defocus, block_ids, noise_weight, panels):
    per_device = images.shape[1]
    columns = images.shape[3]
    devices = lax.axis_size("orient")
    local_search = block_ids.shape[2]
    slots_each = min(per_device, max(2, 2 * per_device * local_search // devices))
    capacity = slots_each * devices
    everyone = per_device * devices
    all_lists = lax.all_gather(block_ids[0], "orient", axis=0, tiled=True)
    all_rows, all_focus = (
        lax.all_gather(images[0], "orient", axis=0, tiled=True),
        lax.all_gather(defocus[0], "orient", axis=0, tiled=True),
    )
    own_block = lax.axis_index("orient")
    block_hits = (
        jnp.any(all_lists == own_block, axis=1).astype(jnp.int32).reshape(devices, per_device)
    )
    slot_rank = jnp.cumsum(block_hits, axis=1) - block_hits
    places = (jnp.arange(devices, dtype=jnp.int32)[:, None] * slots_each + slot_rank).reshape(
        everyone
    )
    chosen = (places[None, :] == jnp.arange(capacity, dtype=jnp.int32)[:, None]) & (
        block_hits.reshape(everyone)[None, :] == 1
    )
    is_live = jnp.any(chosen, axis=1)
    slot_owner = jnp.sum(
        jnp.where(chosen, jnp.arange(everyone, dtype=jnp.int32)[None, :], 0), axis=1
    )
    slot_rows = jnp.take(all_rows, slot_owner, axis=0)
    slot_focus = jnp.take(all_focus, slot_owner, axis=0).astype(jnp.float32)
    frequency = (jnp.arange(columns, dtype=jnp.float32) + 0.5) / columns
    contrast = -jnp.sin(CTF_PHASE * slot_focus[:, None] * frequency[None, :] + 0.1)
    weighted = contrast * noise_weight[None, :]
    scaled_rows = (weighted[:, None, :] * slot_rows.astype(jnp.float32)).astype(jnp.bfloat16)
    energy = (contrast * weighted).astype(jnp.bfloat16)
    piece = lax.all_gather(panels[:, 0], "cls", axis=0, tiled=True)
    widened = piece.astype(jnp.float32)
    squared = (widened * widened).astype(jnp.bfloat16)
    correlate = jnp.einsum("srk,cjrk->scj", scaled_rows, piece, preferred_element_type=jnp.float32)
    energy_term = jnp.einsum("sk,cjrk->scj", energy, squared, preferred_element_type=jnp.float32)
    terms = correlate - 0.5 * energy_term
    combined = terms.reshape(capacity, -1)
    scores = lax.psum_scatter(combined, "rep", scatter_dimension=1, tiled=True)
    member = (slot_owner[:, None] == jnp.arange(everyone, dtype=jnp.int32)[None, :]) & is_live[
        :, None
    ]
    slot_top = jnp.max(scores, axis=1)
    local_peak = jnp.max(jnp.where(member, slot_top[:, None], FLOOR), axis=0)
    peak = lax.pmax(local_peak, ("orient", "rep"))
    slot_peak = spread_max(member, is_live, peak)
    expo = jnp.where(is_live[:, None], jnp.exp(scores - slot_peak[:, None]), 0.0)
    total = lax.psum(collect_sums(member, expo), ("orient", "rep"))
    slot_total = jnp.where(is_live, jnp.sum(jnp.where(member, total[None, :], 0.0), axis=1), 1.0)
    posterior = expo / slot_total[:, None]
    return posterior.reshape(1, 1, capacity, -1)


def solution(mesh):
    in_specs = (
        P(("batch", "cls"), "orient", "rep", None),
        P(("batch", "cls"), "orient"),
        P(("batch", "cls"), "orient", None),
        P(),
        P(("batch", "cls"), "orient", None, "rep", None),
    )
    out_specs = P(("batch", "cls"), "orient", None, "rep")
    sizes = mesh.shape
    paired = sizes["rep"] == 1 and sizes["cls"] == 2 and sizes["orient"] % 2 == 0
    return jax.shard_map(
        chip_shards if paired else shards,
        mesh=mesh,
        in_specs=in_specs,
        out_specs=out_specs,
        check_vma=False,
    )
```

```python
import functools

import jax
import jax.numpy as jnp
from jax import lax
from jax.experimental import pallas as pl
from jax.experimental.pallas import tpu as pltpu
from jax.sharding import PartitionSpec as P

CTF_PHASE = 40.0
FLOOR = -1e30
LANES = 128
VMEM_LIMIT = 32 * 1024 * 1024


def sin_cos(angle):
    turns = jnp.floor(angle * 0.6366197723675814 + 0.5)
    rest = angle - turns * 1.5703125
    rest = rest - turns * 4.837512969970703e-4
    rest = rest - turns * 7.549789948768648e-8
    square = rest * rest
    sine = rest + rest * square * (
        -1.6666654611e-1 + square * (8.3321608736e-3 - square * 1.9515295891e-4)
    )
    cosine = (
        1.0
        - 0.5 * square
        + square
        * square
        * (4.166664568298827e-2 + square * (-1.388731625493765e-3 + square * 2.443315711809948e-5))
    )
    quarter = turns.astype(jnp.int32)
    odd = (quarter & 1) == 1
    low = jnp.where(odd, cosine, sine)
    high = jnp.where(odd, sine, cosine)
    return (
        jnp.where((quarter & 2) == 2, -low, low),
        jnp.where(((quarter + 1) & 2) == 2, -high, high),
    )


def particle_facts(meta):
    return jnp.concatenate([m[...].astype(jnp.float32).T[: m.shape[0]] for m in meta], axis=0)


def add_scores(rows, spot, noise, sides, mate_panel, tables, sums, segments):
    columns = noise.shape[1]
    width = columns // segments
    tiles = width // LANES
    sin_a, cos_a, sin_b, cos_b = tables
    count = sin_a.shape[0]
    facts = particle_facts([r.at[:, pl.ds(columns, LANES)] for r in rows])
    rate = CTF_PHASE * facts[:, 0:1]
    lane = lax.broadcasted_iota(jnp.int32, (count, LANES), 1).astype(jnp.float32)
    coarse_sin, coarse_cos = sin_cos(rate * (lane * (LANES / columns)) + 0.1)
    sin_a[...] = -coarse_sin
    cos_a[...] = -coarse_cos
    fine_sin, fine_cos = sin_cos(rate * ((lane + 0.5) / columns))
    sin_b[...] = fine_sin
    cos_b[...] = fine_cos
    for total in sums:
        total[...] = jnp.zeros_like(total)
    core = spot[2]

    def segment(index, carry):
        start = pl.multiple_of(index * width, LANES)
        shift = lax.rem(LANES - index * tiles, LANES)
        sa = pltpu.roll(sin_a[...], shift, 1)
        ca = pltpu.roll(cos_a[...], shift, 1)
        sb = sin_b[...]
        cb = cos_b[...]
        scaled_parts, energy_parts = [], []
        for t in range(tiles):
            window = pl.ds(start + t * LANES, LANES)
            contrast = sa[:, t : t + 1] * cb + ca[:, t : t + 1] * sb
            weighted = contrast * noise[:, window]
            image = jnp.concatenate([r[:, window] for r in rows], axis=0).astype(jnp.float32)
            scaled_parts.append((weighted * image).astype(jnp.bfloat16))
            energy_parts.append((contrast * weighted).astype(jnp.bfloat16))
        scaled = jnp.concatenate(scaled_parts, axis=1)
        energy = jnp.concatenate(energy_parts, axis=1)
        contract = (((1,), (1,)), ((), ()))
        whole = pl.ds(start, width)
        for values, total in ((sides[core, :, whole], sums[0]), (mate_panel[:, whole], sums[1])):
            squared = values * values
            correlate = lax.dot_general(
                values, scaled, contract, preferred_element_type=jnp.float32
            )
            power = lax.dot_general(squared, energy, contract, preferred_element_type=jnp.float32)
            total[...] += correlate - 0.5 * power
        return carry

    lax.fori_loop(0, segments, segment, 0)
    return facts


def batch_kernel(n, segments, spot, *refs):
    rows = refs[:n]
    noise, sides, mate_panel, own_out, mate_out, fact_out = refs[n : n + 6]
    tables, sums = refs[n + 6 : n + 10], refs[n + 10 :]
    facts = add_scores(rows, spot, noise, sides, mate_panel, tables, sums, segments)
    own_out[...] = sums[0][...].T
    mate_out[...] = sums[1][...].T
    fact_out[...] = jnp.pad(facts, ((0, 0), (0, LANES - facts.shape[1])))


def last_kernel(n, segments, orders, spot, *refs):
    rows = refs[:n]
    noise, sides, mate_panel = refs[n : n + 3]
    earlier = refs[n + 3 : n + 3 + 3 * (len(orders) - 1)]
    outs = refs[n + 3 + len(earlier) :]
    here_own, here_mate, there_own, there_mate, facts = outs[:5]
    tables, sums, (own_all, mate_all, fact_all) = outs[5:9], outs[9:11], outs[11:]
    last_facts = add_scores(rows, spot, noise, sides, mate_panel, tables, sums, segments)
    last_facts = jnp.pad(last_facts, ((0, 0), (0, LANES - last_facts.shape[1])))
    group, position, core = spot[0], spot[1], spot[2]
    each = rows[0].shape[0]
    ring = own_all.shape[0] // (2 * each)
    half = ring // 2
    for index, order in enumerate(orders):
        if index < len(orders) - 1:
            own, mate, fact = [r[...] for r in earlier[3 * index : 3 * index + 3]]
        else:
            own, mate, fact = sums[0][...].T, sums[1][...].T, last_facts
        for k, (distance, crossed) in enumerate(order):
            place = lax.rem(position + distance + ring, ring)
            far = place >= half
            level = jnp.where(far, ring - 1 - place, place)
            device = 2 * level + (1 - core if crossed else core)
            side = jnp.where(far, 1, 0)
            other = jnp.where(side == group, 0, 1)
            start = pl.multiple_of((other * ring + device) * each, each)
            piece = slice(k * each, (k + 1) * each)
            own_all[pl.ds(start, each), :] = own[piece]
            mate_all[pl.ds(start, each), :] = mate[piece]
            fact_all[pl.ds(start, each), :] = fact[piece]
    everyone = ring * each
    here_own[...] = own_all[:everyone]
    here_mate[...] = mate_all[:everyone]
    there_own[...] = own_all[everyone:]
    there_mate[...] = mate_all[everyone:]
    facts[...] = fact_all[:everyone]


def score_call(chunks, orders, earlier, spot, noise, sides, mate_panel):
    each = chunks[0].shape[0]
    orientations, columns = mate_panel.shape
    whole = columns // LANES
    segments = next(s for s in (3, 2, 4, 5, 6, 7, 1) if whole % s == 0)
    n = len(chunks)
    count = each * n
    scratch = [pltpu.VMEM((count, LANES), jnp.float32)] * 4
    scratch += [pltpu.VMEM((orientations, count), jnp.float32)] * 2
    single = jax.ShapeDtypeStruct((count, orientations), jnp.float32)
    if orders is None:
        kernel = functools.partial(batch_kernel, n, segments)
        out_shape = [single, single, jax.ShapeDtypeStruct((count, LANES), jnp.float32)]
        extra = []
    else:
        everyone = each * sum(len(o) for o in orders) // 2
        kernel = functools.partial(last_kernel, n, segments, orders)
        block = jax.ShapeDtypeStruct((everyone, orientations), jnp.float32)
        out_shape = [block] * 4 + [jax.ShapeDtypeStruct((everyone, LANES), jnp.float32)]
        whole_sums = pltpu.VMEM((2 * everyone, orientations), jnp.float32)
        scratch += [whole_sums, whole_sums, pltpu.VMEM((2 * everyone, LANES), jnp.float32)]
        extra = [e for triple in earlier for e in triple]
    vmem = pl.BlockSpec(memory_space=pltpu.VMEM)
    return pl.pallas_call(
        kernel,
        in_specs=[pl.BlockSpec(memory_space=pltpu.SMEM)] + [vmem] * (n + 3 + len(extra)),
        out_specs=[vmem] * len(out_shape),
        out_shape=out_shape,
        scratch_shapes=scratch,
        compiler_params=pltpu.CompilerParams(vmem_limit_bytes=VMEM_LIMIT),
        cost_estimate=pl.CostEstimate(
            flops=8 * max(count, 128) * orientations * columns,
            bytes_accessed=4 * orientations * columns + 2 * count * columns,
            transcendentals=0,
        ),
    )(spot, *chunks, noise, sides, mate_panel, *extra)


def stats_kernel(search, slots_each, each, spot, mine, mate, across, both, facts, slots, chosen, stats):
    group, block = spot[0], spot[3]
    count = mine.shape[0]
    same = mine[...] + mate[...]
    other = across[...] + both[...]
    first = group == 0
    scores = jnp.concatenate(
        [jnp.where(first, same, other), jnp.where(first, other, same)], axis=1
    )
    lane = lax.broadcasted_iota(jnp.int32, (count, LANES), 1)
    row = lax.broadcasted_iota(jnp.int32, (count, LANES), 0)
    match = (lane >= 1) & (lane <= search) & (facts[...] == block.astype(jnp.float32))
    hit = jnp.max(jnp.where(match, 1.0, 0.0), axis=1, keepdims=True)
    named = hit > 0.0
    line = lax.broadcasted_iota(jnp.int32, (count, count), 0)
    column = lax.broadcasted_iota(jnp.int32, (count, count), 1)
    before = (column < line) & (column // each == line // each)
    rank = jnp.dot(
        jnp.where(before, 1.0, 0.0).astype(jnp.bfloat16),
        jnp.broadcast_to(hit, (count, LANES)).astype(jnp.bfloat16),
        preferred_element_type=jnp.float32,
    )
    slot = (row // each) * slots_each + rank.astype(jnp.int32)
    capacity = chosen.shape[0]
    if capacity != LANES:
        slot = jnp.broadcast_to(slot[:, :1], (count, capacity))
    target = lax.broadcasted_iota(jnp.int32, (count, capacity), 1)
    taken = jnp.where((slot == target) & named, 1.0, 0.0)
    top = jnp.where(named, jnp.max(scores, axis=1, keepdims=True), FLOOR)
    terms = jnp.where(named, jnp.exp(scores - top), 0.0)
    total = jnp.sum(terms, axis=1, keepdims=True)
    slots[...] = lax.dot_general(
        taken,
        terms,
        (((0,), (0,)), ((), ())),
        precision=lax.Precision.HIGHEST,
        preferred_element_type=jnp.float32,
    )
    chosen[...] = taken.T
    pair = jnp.where(lane == 0, top, jnp.where(lane == 1, total, 0.0))
    stats[...] = pair.T[: stats.shape[0]]


def final_kernel(n, *refs):
    own, parts, slots, chosen, out = refs[0], refs[1 : 1 + n], refs[1 + n], refs[2 + n], refs[3 + n]
    tops = [p[0:1, :] for p in parts]
    peak = functools.reduce(jnp.maximum, tops)
    total = functools.reduce(jnp.add, [p[1:2, :] * jnp.exp(p[0:1, :] - peak) for p in parts])
    factor = jnp.exp(own[0:1, :] - peak) / total
    scale = jnp.sum(chosen[...] * factor, axis=1, keepdims=True)
    out[...] = slots[...] * scale


def chip_shards(images, defocus, block_ids, noise_weight, panels):
    per_device, halves, columns = images.shape[1:]
    devices = lax.axis_size("orient")
    chips = devices // 2
    ring = 2 * chips
    everyone = per_device * devices
    local_search = block_ids.shape[2]
    orientations = panels.shape[2]
    slots_each = min(per_device, max(2, 2 * per_device * local_search // devices))
    capacity = slots_each * devices
    place = lax.axis_index("orient")
    group = lax.axis_index("cls")
    chip, core = place // 2, place % 2
    position = jnp.where(group == 0, chip, ring - 1 - chip)
    spot = jnp.stack([group, position, core, place]).astype(jnp.int32)
    first = core == 0

    mate_pairs = [(d, d ^ 1) for d in range(devices)]
    x_pairs = [(0, 1), (1, 0)]

    def joint(place, core):
        place = place % ring
        far = place >= chips
        level = ring - 1 - place if far else place
        return (2 * level + core) * 2 + int(far)

    def forward(values, step):
        pairs = [(joint(p, c), joint(p + step, c)) for p in range(ring) for c in range(2)]
        return lax.ppermute(values, ("orient", "cls"), pairs)

    facts = jnp.concatenate([defocus, block_ids[0].T.astype(jnp.bfloat16)], axis=0)
    facts = jnp.pad(facts, ((0, per_device - facts.shape[0]), (0, LANES - per_device)))
    planes = lax.optimization_barrier(jnp.transpose(images[0], (1, 0, 2)))
    kept = jnp.concatenate([jnp.where(first, planes[0], planes[1]), facts], axis=1)
    given = jnp.concatenate([jnp.where(first, planes[1], planes[0]), facts], axis=1)
    got = lax.ppermute(given, "orient", mate_pairs)

    noise = noise_weight[None, :]
    waiting = [((0, False), kept), ((0, True), got)]
    ahead = {False: kept, True: got}
    behind = {False: kept, True: got}
    orders, earlier = [], []
    for step in range(1, chips + 1):
        if earlier:
            tie = earlier[-1][2]
            ahead = {c: lax.optimization_barrier((v, tie))[0] for c, v in ahead.items()}
            behind = {c: lax.optimization_barrier((v, tie))[0] for c, v in behind.items()}
        arrived = []
        for crossed in (False, True):
            if step < chips or not crossed:
                ahead[crossed] = forward(ahead[crossed], 1)
                arrived.append(((-step, crossed), ahead[crossed]))
            if step < chips or crossed:
                behind[crossed] = forward(behind[crossed], -1)
                arrived.append(((step, crossed), behind[crossed]))
        if step == 1:
            _, panels = lax.optimization_barrier((ahead[False], panels))
            sides = lax.optimization_barrier(jnp.transpose(panels[0, 0], (1, 0, 2)))
            mate_panel = lax.ppermute(
                lax.dynamic_index_in_dim(sides, 1 - core, 0, keepdims=False), "orient", mate_pairs
            )
        if step > 1:
            orders.append([key for key, _ in waiting])
            earlier.append(
                score_call([c for _, c in waiting], None, None, spot, noise, sides, mate_panel)
            )
            waiting = []
        waiting = waiting + arrived
    orders.append([key for key, _ in waiting])
    here_own, here_mate, there_own, there_mate, own_facts = score_call(
        [c for _, c in waiting], orders, earlier, spot, noise, sides, mate_panel
    )

    from_mate = lax.ppermute(here_mate, "orient", mate_pairs)
    from_x = lax.ppermute(there_own, "cls", x_pairs)
    from_both = lax.ppermute(
        there_mate,
        ("orient", "cls"),
        [(d * 2 + g, (d ^ 1) * 2 + 1 - g) for d in range(devices) for g in range(2)],
    )
    vmem = pl.BlockSpec(memory_space=pltpu.VMEM)
    slots, chosen, stats = pl.pallas_call(
        functools.partial(stats_kernel, local_search, slots_each, per_device),
        in_specs=[pl.BlockSpec(memory_space=pltpu.SMEM)] + [vmem] * 5,
        out_specs=[vmem] * 3,
        out_shape=[
            jax.ShapeDtypeStruct((capacity, 2 * orientations), jnp.float32),
            jax.ShapeDtypeStruct((capacity, everyone), jnp.float32),
            jax.ShapeDtypeStruct((8, everyone), jnp.float32),
        ],
        compiler_params=pltpu.CompilerParams(vmem_limit_bytes=VMEM_LIMIT),
    )(spot, here_own, from_mate, from_x, from_both, own_facts)

    mate_stats = lax.ppermute(stats, "orient", mate_pairs)
    peak = jnp.maximum(stats[0], mate_stats[0])
    total = stats[1] * jnp.exp(stats[0] - peak) + mate_stats[1] * jnp.exp(mate_stats[0] - peak)
    pair = jnp.zeros_like(stats).at[0].set(peak).at[1].set(total)
    pairs = [pair] + [
        lax.ppermute(pair, "orient", [(d, (d + 2 * s) % devices) for d in range(devices)])
        for s in range(1, chips)
    ]
    posterior = pl.pallas_call(
        functools.partial(final_kernel, chips),
        in_specs=[vmem] * (chips + 3),
        out_specs=vmem,
        out_shape=jax.ShapeDtypeStruct((capacity, 2 * orientations), jnp.float32),
        compiler_params=pltpu.CompilerParams(vmem_limit_bytes=VMEM_LIMIT),
    )(stats, *pairs, slots, chosen)
    return posterior.reshape(1, 1, capacity, -1)


def spread_max(member, is_live, values):
    picked = jnp.max(jnp.where(member, values[None, :], FLOOR), axis=1)
    return jnp.where(is_live, picked, 0.0)


def collect_sums(member, expo):
    return jnp.sum(jnp.where(member, jnp.sum(expo, axis=1)[:, None], 0.0), axis=0)


def shards(images, defocus, block_ids, noise_weight, panels):
    per_device = images.shape[1]
    columns = images.shape[3]
    devices = lax.axis_size("orient")
    local_search = block_ids.shape[2]
    slots_each = min(per_device, max(2, 2 * per_device * local_search // devices))
    capacity = slots_each * devices
    everyone = per_device * devices
    all_lists = lax.all_gather(block_ids[0], "orient", axis=0, tiled=True)
    all_rows, all_focus = (
        lax.all_gather(images[0], "orient", axis=0, tiled=True),
        lax.all_gather(defocus[0], "orient", axis=0, tiled=True),
    )
    own_block = lax.axis_index("orient")
    block_hits = (
        jnp.any(all_lists == own_block, axis=1).astype(jnp.int32).reshape(devices, per_device)
    )
    slot_rank = jnp.cumsum(block_hits, axis=1) - block_hits
    places = (jnp.arange(devices, dtype=jnp.int32)[:, None] * slots_each + slot_rank).reshape(
        everyone
    )
    chosen = (places[None, :] == jnp.arange(capacity, dtype=jnp.int32)[:, None]) & (
        block_hits.reshape(everyone)[None, :] == 1
    )
    is_live = jnp.any(chosen, axis=1)
    slot_owner = jnp.sum(
        jnp.where(chosen, jnp.arange(everyone, dtype=jnp.int32)[None, :], 0), axis=1
    )
    slot_rows = jnp.take(all_rows, slot_owner, axis=0)
    slot_focus = jnp.take(all_focus, slot_owner, axis=0).astype(jnp.float32)
    frequency = (jnp.arange(columns, dtype=jnp.float32) + 0.5) / columns
    contrast = -jnp.sin(CTF_PHASE * slot_focus[:, None] * frequency[None, :] + 0.1)
    weighted = contrast * noise_weight[None, :]
    scaled_rows = (weighted[:, None, :] * slot_rows.astype(jnp.float32)).astype(jnp.bfloat16)
    energy = (contrast * weighted).astype(jnp.bfloat16)
    piece = lax.all_gather(panels[:, 0], "cls", axis=0, tiled=True)
    widened = piece.astype(jnp.float32)
    squared = (widened * widened).astype(jnp.bfloat16)
    correlate = jnp.einsum("srk,cjrk->scj", scaled_rows, piece, preferred_element_type=jnp.float32)
    energy_term = jnp.einsum("sk,cjrk->scj", energy, squared, preferred_element_type=jnp.float32)
    terms = correlate - 0.5 * energy_term
    combined = terms.reshape(capacity, -1)
    scores = lax.psum_scatter(combined, "rep", scatter_dimension=1, tiled=True)
    member = (slot_owner[:, None] == jnp.arange(everyone, dtype=jnp.int32)[None, :]) & is_live[
        :, None
    ]
    slot_top = jnp.max(scores, axis=1)
    local_peak = jnp.max(jnp.where(member, slot_top[:, None], FLOOR), axis=0)
    peak = lax.pmax(local_peak, ("orient", "rep"))
    slot_peak = spread_max(member, is_live, peak)
    expo = jnp.where(is_live[:, None], jnp.exp(scores - slot_peak[:, None]), 0.0)
    total = lax.psum(collect_sums(member, expo), ("orient", "rep"))
    slot_total = jnp.where(is_live, jnp.sum(jnp.where(member, total[None, :], 0.0), axis=1), 1.0)
    posterior = expo / slot_total[:, None]
    return posterior.reshape(1, 1, capacity, -1)


def solution(mesh):
    in_specs = (
        P(("batch", "cls"), "orient", "rep", None),
        P(("batch", "cls"), "orient"),
        P(("batch", "cls"), "orient", None),
        P(),
        P(("batch", "cls"), "orient", None, "rep", None),
    )
    out_specs = P(("batch", "cls"), "orient", None, "rep")
    sizes = mesh.shape
    paired = sizes["rep"] == 1 and sizes["cls"] == 2 and sizes["orient"] % 2 == 0
    return jax.shard_map(
        chip_shards if paired else shards,
        mesh=mesh,
        in_specs=in_specs,
        out_specs=out_specs,
        check_vma=False,
    )
```

```python
import functools

import jax
import jax.numpy as jnp
from jax import lax
from jax.experimental import pallas as pl
from jax.experimental.pallas import tpu as pltpu
from jax.sharding import PartitionSpec as P

CTF_PHASE = 40.0
FLOOR = -1e30
LANES = 128
VMEM_LIMIT = 32 * 1024 * 1024


def sin_cos(angle):
    turns = jnp.floor(angle * 0.6366197723675814 + 0.5)
    rest = angle - turns * 1.5703125
    rest = rest - turns * 4.837512969970703e-4
    rest = rest - turns * 7.549789948768648e-8
    square = rest * rest
    sine = rest + rest * square * (
        -1.6666654611e-1 + square * (8.3321608736e-3 - square * 1.9515295891e-4)
    )
    cosine = (
        1.0
        - 0.5 * square
        + square
        * square
        * (4.166664568298827e-2 + square * (-1.388731625493765e-3 + square * 2.443315711809948e-5))
    )
    quarter = turns.astype(jnp.int32)
    odd = (quarter & 1) == 1
    low = jnp.where(odd, cosine, sine)
    high = jnp.where(odd, sine, cosine)
    return (
        jnp.where((quarter & 2) == 2, -low, low),
        jnp.where(((quarter + 1) & 2) == 2, -high, high),
    )


def particle_facts(meta):
    return jnp.concatenate([m[...].astype(jnp.float32).T[: m.shape[0]] for m in meta], axis=0)


def add_scores(rows, spot, noise, sides, mate_panel, turn_sin, turn_cos, sums, segments):
    columns = noise.shape[1]
    width = columns // segments
    tiles = width // LANES
    count = turn_sin.shape[0]
    facts = particle_facts([r.at[:, pl.ds(columns, LANES)] for r in rows])
    rate = jnp.broadcast_to(CTF_PHASE * facts[:, 0:1], (count, LANES))
    lane = lax.broadcasted_iota(jnp.int32, (count, LANES), 1).astype(jnp.float32)
    first_sin, first_cos = sin_cos(rate * ((lane + 0.5) / columns) + 0.1)
    step_sin, step_cos = sin_cos(rate * (LANES / columns))
    turn_sin[...] = step_sin
    turn_cos[...] = step_cos
    for total in sums:
        total[...] = jnp.zeros_like(total)
    core = spot[2]

    def segment(index, carry):
        sine, cosine = carry
        start = pl.multiple_of(index * width, LANES)
        scaled_parts, energy_parts = [], []
        for t in range(tiles):
            window = pl.ds(start + t * LANES, LANES)
            weighted = sine * noise[:, window]
            image = jnp.concatenate([r[:, window] for r in rows], axis=0).astype(jnp.float32)
            scaled_parts.append((weighted * image).astype(jnp.bfloat16))
            energy_parts.append((sine * weighted).astype(jnp.bfloat16))
            ds, dc = turn_sin[...], turn_cos[...]
            sine, cosine = sine * dc + cosine * ds, cosine * dc - sine * ds
        scaled = jnp.concatenate(scaled_parts, axis=1)
        energy = jnp.concatenate(energy_parts, axis=1)
        contract = (((1,), (1,)), ((), ()))
        whole = pl.ds(start, width)
        for values, total in ((sides[core, :, whole], sums[0]), (mate_panel[:, whole], sums[1])):
            squared = values * values
            correlate = lax.dot_general(
                values, scaled, contract, preferred_element_type=jnp.float32
            )
            power = lax.dot_general(squared, energy, contract, preferred_element_type=jnp.float32)
            total[...] += correlate - 0.5 * power
        return sine, cosine

    lax.fori_loop(0, segments, segment, (-first_sin, -first_cos))
    return jnp.pad(facts, ((0, 0), (0, LANES - facts.shape[1])))


def batch_kernel(n, segments, spot, *refs):
    rows = refs[:n]
    noise, sides, mate_panel, own_out, mate_out, fact_out = refs[n : n + 6]
    turn_sin, turn_cos, *sums = refs[n + 6 :]
    fact_out[...] = add_scores(
        rows, spot, noise, sides, mate_panel, turn_sin, turn_cos, sums, segments
    )
    own_out[...] = sums[0][...].T
    mate_out[...] = sums[1][...].T


def last_kernel(n, segments, orders, spot, *refs):
    rows = refs[:n]
    noise, sides, mate_panel = refs[n : n + 3]
    earlier = refs[n + 3 : n + 3 + 3 * (len(orders) - 1)]
    partial, facts, turn_sin, turn_cos, *sums = refs[n + 3 + len(earlier) :]
    last_facts = add_scores(
        rows, spot, noise, sides, mate_panel, turn_sin, turn_cos, sums, segments
    )
    position, core = spot[1], spot[2]
    each = rows[0].shape[0]
    ring = facts.shape[0] // (2 * each)
    half = ring // 2
    for index, order in enumerate(orders):
        if index < len(orders) - 1:
            own, mate, fact = [r[...] for r in earlier[3 * index : 3 * index + 3]]
        else:
            own, mate, fact = sums[0][...].T, sums[1][...].T, last_facts
        for k, (distance, crossed) in enumerate(order):
            place = lax.rem(position + distance + ring, ring)
            far = place >= half
            level = jnp.where(far, ring - 1 - place, place)
            device = 2 * level + (1 - core if crossed else core)
            start = pl.multiple_of((jnp.where(far, ring, 0) + device) * each, each)
            piece = slice(k * each, (k + 1) * each)
            partial[core, pl.ds(start, each), :] = own[piece]
            partial[1 - core, pl.ds(start, each), :] = mate[piece]
            facts[pl.ds(start, each), :] = fact[piece]


def score_call(chunks, orders, earlier, spot, noise, sides, mate_panel):
    each = chunks[0].shape[0]
    orientations, columns = mate_panel.shape
    whole = columns // LANES
    segments = next(s for s in (3, 2, 4, 5, 6, 7, 1) if whole % s == 0)
    n = len(chunks)
    count = each * n
    scratch = [pltpu.VMEM((count, LANES), jnp.float32)] * 2
    scratch += [pltpu.VMEM((orientations, count), jnp.float32)] * 2
    single = jax.ShapeDtypeStruct((count, orientations), jnp.float32)
    if orders is None:
        kernel = functools.partial(batch_kernel, n, segments)
        out_shape = [single, single, jax.ShapeDtypeStruct((count, LANES), jnp.float32)]
        extra = []
    else:
        everyone = each * sum(len(o) for o in orders)
        kernel = functools.partial(last_kernel, n, segments, orders)
        out_shape = [
            jax.ShapeDtypeStruct((2, everyone, orientations), jnp.float32),
            jax.ShapeDtypeStruct((everyone, LANES), jnp.float32),
        ]
        extra = [e for triple in earlier for e in triple]
    vmem = pl.BlockSpec(memory_space=pltpu.VMEM)
    return pl.pallas_call(
        kernel,
        in_specs=[pl.BlockSpec(memory_space=pltpu.SMEM)] + [vmem] * (n + 3 + len(extra)),
        out_specs=[vmem] * len(out_shape),
        out_shape=out_shape,
        scratch_shapes=scratch,
        compiler_params=pltpu.CompilerParams(vmem_limit_bytes=VMEM_LIMIT),
        cost_estimate=pl.CostEstimate(
            flops=8 * max(count, 128) * orientations * columns,
            bytes_accessed=4 * orientations * columns + 2 * count * columns,
            transcendentals=0,
        ),
    )(spot, *chunks, noise, sides, mate_panel, *extra)


def names_block(facts, search, block):
    lane = lax.broadcasted_iota(jnp.int32, facts.shape, 1)
    match = (lane >= 1) & (lane <= search) & (facts == block.astype(jnp.float32))
    return jnp.max(jnp.where(match, 1.0, 0.0), axis=1, keepdims=True) > 0.0


def chip_kernel(search, spot, partial, mate, facts, mine, own_stats, across):
    group, core, place = spot[0], spot[2], spot[3]
    count = mine.shape[0]
    lane = lax.broadcasted_iota(jnp.int32, (count, LANES), 1)
    for relative in range(2):
        side = group if relative == 0 else 1 - group
        window = pl.ds(pl.multiple_of(side * count, count), count)
        listed = facts[window, :]
        masked = []
        for crossed in range(2):
            block = core if crossed == 0 else 1 - core
            scores = partial[block, window, :] + mate[block, window, :]
            if crossed == 0:
                if relative == 0:
                    mine[...] = scores
                else:
                    across[:count] = scores
            named = names_block(listed, search, place - core + block)
            masked.append(jnp.where(named, scores, FLOOR))
        top = jnp.max(jnp.maximum(*masked), axis=1, keepdims=True)
        terms = [jnp.where(m > FLOOR, jnp.exp(m - top), 0.0) for m in masked]
        total = jnp.sum(terms[0] + terms[1], axis=1, keepdims=True)
        pair = jnp.where(lane == 0, top, jnp.where(lane == 1, total, 0.0)).T
        if relative == 0:
            own_stats[...] = pair[: own_stats.shape[0]]
        else:
            across[count:] = pair[: across.shape[0] - count]


def slot_kernel(search, slots_each, each, spot, mine, across, pair, facts, slots, chosen):
    group, place = spot[0], spot[3]
    count = mine.shape[0]
    same, other = mine[...], across[:count]
    first = group == 0
    scores = jnp.concatenate(
        [jnp.where(first, same, other), jnp.where(first, other, same)], axis=1
    )
    listed = facts[pl.ds(pl.multiple_of(group * count, count), count), :]
    named = names_block(listed, search, place)
    hit = jnp.where(named, 1.0, 0.0)
    row = lax.broadcasted_iota(jnp.int32, (count, LANES), 0)
    line = lax.broadcasted_iota(jnp.int32, (count, count), 0)
    column = lax.broadcasted_iota(jnp.int32, (count, count), 1)
    before = (column < line) & (column // each == line // each)
    rank = jnp.dot(
        jnp.where(before, 1.0, 0.0).astype(jnp.bfloat16),
        jnp.broadcast_to(hit, (count, LANES)).astype(jnp.bfloat16),
        preferred_element_type=jnp.float32,
    )
    slot = (row // each) * slots_each + rank.astype(jnp.int32)
    capacity = chosen.shape[0]
    if capacity != LANES:
        slot = jnp.broadcast_to(slot[:, :1], (count, capacity))
    target = lax.broadcasted_iota(jnp.int32, (count, capacity), 1)
    taken = jnp.where((slot == target) & named, 1.0, 0.0)
    top = jnp.broadcast_to(pair[0:1, :], (count, count)).T[:, 0:1]
    terms = jnp.where(named, jnp.exp(scores - top), 0.0)
    slots[...] = lax.dot_general(
        taken,
        terms,
        (((0,), (0,)), ((), ())),
        precision=lax.Precision.HIGHEST,
        preferred_element_type=jnp.float32,
    )
    chosen[...] = taken.T


def final_kernel(n, *refs):
    parts, slots, chosen, out = refs[:n], refs[n], refs[n + 1], refs[n + 2]
    peak = functools.reduce(jnp.maximum, [p[0:1, :] for p in parts])
    shares = [p[1:2, :] * jnp.exp(p[0:1, :] - peak) for p in parts]
    total = functools.reduce(jnp.add, shares)
    factor = jnp.exp(parts[0][0:1, :] - peak) / total
    scale = jnp.sum(chosen[...] * factor, axis=1, keepdims=True)
    out[...] = slots[...] * scale


def chip_shards(images, defocus, block_ids, noise_weight, panels):
    per_device, halves, columns = images.shape[1:]
    devices = lax.axis_size("orient")
    chips = devices // 2
    ring = 2 * chips
    everyone = per_device * devices
    local_search = block_ids.shape[2]
    orientations = panels.shape[2]
    slots_each = min(per_device, max(2, 2 * per_device * local_search // devices))
    capacity = slots_each * devices
    place = lax.axis_index("orient")
    group = lax.axis_index("cls")
    chip, core = place // 2, place % 2
    position = jnp.where(group == 0, chip, ring - 1 - chip)
    spot = jnp.stack([group, position, core, place]).astype(jnp.int32)
    first = core == 0

    mate_pairs = [(d, d ^ 1) for d in range(devices)]
    x_pairs = [(0, 1), (1, 0)]

    def joint(place, core):
        place = place % ring
        far = place >= chips
        level = ring - 1 - place if far else place
        return (2 * level + core) * 2 + int(far)

    def forward(values, step):
        pairs = [(joint(p, c), joint(p + step, c)) for p in range(ring) for c in range(2)]
        return lax.ppermute(values, ("orient", "cls"), pairs)

    facts = jnp.concatenate([defocus, block_ids[0].T.astype(jnp.bfloat16)], axis=0)
    facts = jnp.pad(facts, ((0, per_device - facts.shape[0]), (0, LANES - per_device)))
    planes = lax.optimization_barrier(jnp.transpose(images[0], (1, 0, 2)))
    kept = jnp.concatenate([jnp.where(first, planes[0], planes[1]), facts], axis=1)
    given = jnp.concatenate([jnp.where(first, planes[1], planes[0]), facts], axis=1)
    got = lax.ppermute(given, "orient", mate_pairs)

    _, panels = lax.optimization_barrier((got, panels))
    sides = lax.optimization_barrier(jnp.transpose(panels[0, 0], (1, 0, 2)))
    given_panel = lax.dynamic_index_in_dim(sides, 1 - core, 0, keepdims=False)
    mate_panel = lax.ppermute(given_panel, "orient", mate_pairs)

    noise = noise_weight[None, :]
    waiting = [((0, False), kept), ((0, True), got)]
    ahead = {False: kept, True: got}
    behind = {False: kept, True: got}
    orders, earlier = [], []
    for step in range(1, chips + 1):
        if step > 1:
            tie = earlier[-1][2] if earlier else given_panel
            ahead = {c: lax.optimization_barrier((v, tie))[0] for c, v in ahead.items()}
            behind = {c: lax.optimization_barrier((v, tie))[0] for c, v in behind.items()}
        arrived = []
        for crossed in (False, True):
            if step < chips or not crossed:
                ahead[crossed] = forward(ahead[crossed], 1)
                arrived.append(((-step, crossed), ahead[crossed]))
            if step < chips or crossed:
                behind[crossed] = forward(behind[crossed], -1)
                arrived.append(((step, crossed), behind[crossed]))
        if step > 1:
            orders.append([key for key, _ in waiting])
            earlier.append(
                score_call([c for _, c in waiting], None, None, spot, noise, sides, mate_panel)
            )
            waiting = []
        waiting = waiting + arrived
    orders.append([key for key, _ in waiting])
    partial, all_facts = score_call(
        [c for _, c in waiting], orders, earlier, spot, noise, sides, mate_panel
    )

    mate_partial = lax.ppermute(partial, "orient", mate_pairs)
    vmem = pl.BlockSpec(memory_space=pltpu.VMEM)
    smem = pl.BlockSpec(memory_space=pltpu.SMEM)
    params = pltpu.CompilerParams(vmem_limit_bytes=VMEM_LIMIT)
    mine, own_stats, across = pl.pallas_call(
        functools.partial(chip_kernel, local_search),
        in_specs=[smem] + [vmem] * 3,
        out_specs=[vmem] * 3,
        out_shape=[
            jax.ShapeDtypeStruct((everyone, orientations), jnp.float32),
            jax.ShapeDtypeStruct((8, everyone), jnp.float32),
            jax.ShapeDtypeStruct((everyone + 8, orientations), jnp.float32),
        ],
        compiler_params=params,
    )(spot, partial, mate_partial, all_facts)
    from_x = lax.ppermute(across, "cls", x_pairs)

    tops = own_stats[0], from_x[everyone]
    peak = jnp.maximum(*tops)
    total = own_stats[1] * jnp.exp(tops[0] - peak) + from_x[everyone + 1] * jnp.exp(tops[1] - peak)
    pair = jnp.pad(jnp.stack([peak, total]), ((0, 6), (0, 0)))
    pairs = [pair] + [
        lax.ppermute(pair, "orient", [(d, (d + 2 * s) % devices) for d in range(devices)])
        for s in range(1, chips)
    ]
    slots, chosen = pl.pallas_call(
        functools.partial(slot_kernel, local_search, slots_each, per_device),
        in_specs=[smem] + [vmem] * 4,
        out_specs=[vmem] * 2,
        out_shape=[
            jax.ShapeDtypeStruct((capacity, 2 * orientations), jnp.float32),
            jax.ShapeDtypeStruct((capacity, everyone), jnp.float32),
        ],
        compiler_params=params,
    )(spot, mine, from_x, pair, all_facts)
    posterior = pl.pallas_call(
        functools.partial(final_kernel, chips),
        in_specs=[vmem] * (chips + 2),
        out_specs=vmem,
        out_shape=jax.ShapeDtypeStruct((capacity, 2 * orientations), jnp.float32),
        compiler_params=params,
    )(*pairs, slots, chosen)
    return posterior.reshape(1, 1, capacity, -1)


def spread_max(member, is_live, values):
    picked = jnp.max(jnp.where(member, values[None, :], FLOOR), axis=1)
    return jnp.where(is_live, picked, 0.0)


def collect_sums(member, expo):
    return jnp.sum(jnp.where(member, jnp.sum(expo, axis=1)[:, None], 0.0), axis=0)


def shards(images, defocus, block_ids, noise_weight, panels):
    per_device = images.shape[1]
    columns = images.shape[3]
    devices = lax.axis_size("orient")
    local_search = block_ids.shape[2]
    slots_each = min(per_device, max(2, 2 * per_device * local_search // devices))
    capacity = slots_each * devices
    everyone = per_device * devices
    all_lists = lax.all_gather(block_ids[0], "orient", axis=0, tiled=True)
    all_rows, all_focus = (
        lax.all_gather(images[0], "orient", axis=0, tiled=True),
        lax.all_gather(defocus[0], "orient", axis=0, tiled=True),
    )
    own_block = lax.axis_index("orient")
    block_hits = (
        jnp.any(all_lists == own_block, axis=1).astype(jnp.int32).reshape(devices, per_device)
    )
    slot_rank = jnp.cumsum(block_hits, axis=1) - block_hits
    places = (jnp.arange(devices, dtype=jnp.int32)[:, None] * slots_each + slot_rank).reshape(
        everyone
    )
    chosen = (places[None, :] == jnp.arange(capacity, dtype=jnp.int32)[:, None]) & (
        block_hits.reshape(everyone)[None, :] == 1
    )
    is_live = jnp.any(chosen, axis=1)
    slot_owner = jnp.sum(
        jnp.where(chosen, jnp.arange(everyone, dtype=jnp.int32)[None, :], 0), axis=1
    )
    slot_rows = jnp.take(all_rows, slot_owner, axis=0)
    slot_focus = jnp.take(all_focus, slot_owner, axis=0).astype(jnp.float32)
    frequency = (jnp.arange(columns, dtype=jnp.float32) + 0.5) / columns
    contrast = -jnp.sin(CTF_PHASE * slot_focus[:, None] * frequency[None, :] + 0.1)
    weighted = contrast * noise_weight[None, :]
    scaled_rows = (weighted[:, None, :] * slot_rows.astype(jnp.float32)).astype(jnp.bfloat16)
    energy = (contrast * weighted).astype(jnp.bfloat16)
    piece = lax.all_gather(panels[:, 0], "cls", axis=0, tiled=True)
    widened = piece.astype(jnp.float32)
    squared = (widened * widened).astype(jnp.bfloat16)
    correlate = jnp.einsum("srk,cjrk->scj", scaled_rows, piece, preferred_element_type=jnp.float32)
    energy_term = jnp.einsum("sk,cjrk->scj", energy, squared, preferred_element_type=jnp.float32)
    terms = correlate - 0.5 * energy_term
    combined = terms.reshape(capacity, -1)
    scores = lax.psum_scatter(combined, "rep", scatter_dimension=1, tiled=True)
    member = (slot_owner[:, None] == jnp.arange(everyone, dtype=jnp.int32)[None, :]) & is_live[
        :, None
    ]
    slot_top = jnp.max(scores, axis=1)
    local_peak = jnp.max(jnp.where(member, slot_top[:, None], FLOOR), axis=0)
    peak = lax.pmax(local_peak, ("orient", "rep"))
    slot_peak = spread_max(member, is_live, peak)
    expo = jnp.where(is_live[:, None], jnp.exp(scores - slot_peak[:, None]), 0.0)
    total = lax.psum(collect_sums(member, expo), ("orient", "rep"))
    slot_total = jnp.where(is_live, jnp.sum(jnp.where(member, total[None, :], 0.0), axis=1), 1.0)
    posterior = expo / slot_total[:, None]
    return posterior.reshape(1, 1, capacity, -1)


def solution(mesh):
    in_specs = (
        P(("batch", "cls"), "orient", "rep", None),
        P(("batch", "cls"), "orient"),
        P(("batch", "cls"), "orient", None),
        P(),
        P(("batch", "cls"), "orient", None, "rep", None),
    )
    out_specs = P(("batch", "cls"), "orient", None, "rep")
    sizes = mesh.shape
    paired = sizes["rep"] == 1 and sizes["cls"] == 2 and sizes["orient"] % 2 == 0
    return jax.shard_map(
        chip_shards if paired else shards,
        mesh=mesh,
        in_specs=in_specs,
        out_specs=out_specs,
        check_vma=False,
    )
```

```python
import functools

import jax
import jax.numpy as jnp
from jax import lax
from jax.experimental import pallas as pl
from jax.experimental.pallas import tpu as pltpu
from jax.sharding import PartitionSpec as P

CTF_PHASE = 40.0
FLOOR = -1e30
LANES = 128
VMEM_LIMIT = 8 * 1024 * 1024


def sin_cos(angle):
    turns = jnp.floor(angle * 0.6366197723675814 + 0.5)
    rest = angle - turns * 1.5703125
    rest = rest - turns * 4.837512969970703e-4
    rest = rest - turns * 7.549789948768648e-8
    square = rest * rest
    sine = rest + rest * square * (
        -1.6666654611e-1 + square * (8.3321608736e-3 - square * 1.9515295891e-4)
    )
    cosine = (
        1.0
        - 0.5 * square
        + square
        * square
        * (4.166664568298827e-2 + square * (-1.388731625493765e-3 + square * 2.443315711809948e-5))
    )
    quarter = turns.astype(jnp.int32)
    odd = (quarter & 1) == 1
    low = jnp.where(odd, cosine, sine)
    high = jnp.where(odd, sine, cosine)
    return (
        jnp.where((quarter & 2) == 2, -low, low),
        jnp.where(((quarter + 1) & 2) == 2, -high, high),
    )


def row_kernel(spot, planes, defocus, lists, kept, given, facts):
    core = spot[2]
    columns = planes.shape[2]
    count = defocus.shape[1]
    facts[...] = jnp.zeros_like(facts)
    facts[0:1, :count] = defocus[...].astype(jnp.float32)
    facts[1 : 1 + lists.shape[0], :count] = lists[...].astype(jnp.float32)
    for half, out in ((core, kept), (1 - core, given)):
        out[:, :columns] = planes[half]
        out[:, columns:] = facts[...].astype(out.dtype)


def particle_facts(meta):
    return jnp.concatenate([m[...].astype(jnp.float32).T[: m.shape[0]] for m in meta], axis=0)


def add_scores(rows, spot, noise, sides, mate_panel, turn_sin, turn_cos, sums, segments):
    columns = noise.shape[1]
    width = columns // segments
    tiles = width // LANES
    count = turn_sin.shape[0]
    facts = particle_facts([r.at[:, pl.ds(columns, LANES)] for r in rows])
    rate = jnp.broadcast_to(CTF_PHASE * facts[:, 0:1], (count, LANES))
    lane = lax.broadcasted_iota(jnp.int32, (count, LANES), 1).astype(jnp.float32)
    first_sin, first_cos = sin_cos(rate * ((lane + 0.5) / columns) + 0.1)
    step_sin, step_cos = sin_cos(rate * (LANES / columns))
    turn_sin[...] = step_sin
    turn_cos[...] = step_cos
    for total in sums:
        total[...] = jnp.zeros_like(total)
    core = spot[2]

    def segment(index, carry):
        sine, cosine = carry
        start = pl.multiple_of(index * width, LANES)
        scaled_parts, energy_parts = [], []
        for t in range(tiles):
            window = pl.ds(start + t * LANES, LANES)
            weighted = sine * noise[:, window]
            image = jnp.concatenate([r[:, window] for r in rows], axis=0).astype(jnp.float32)
            scaled_parts.append((weighted * image).astype(jnp.bfloat16))
            energy_parts.append((sine * weighted).astype(jnp.bfloat16))
            ds, dc = turn_sin[...], turn_cos[...]
            sine, cosine = sine * dc + cosine * ds, cosine * dc - sine * ds
        scaled = jnp.concatenate(scaled_parts, axis=1)
        energy = jnp.concatenate(energy_parts, axis=1)
        contract = (((1,), (1,)), ((), ()))
        whole = pl.ds(start, width)
        for values, total in ((sides[core, :, whole], sums[0]), (mate_panel[:, whole], sums[1])):
            squared = values * values
            correlate = lax.dot_general(
                values, scaled, contract, preferred_element_type=jnp.float32
            )
            power = lax.dot_general(squared, energy, contract, preferred_element_type=jnp.float32)
            total[...] += correlate - 0.5 * power
        return sine, cosine

    lax.fori_loop(0, segments, segment, (-first_sin, -first_cos))
    return jnp.pad(facts, ((0, 0), (0, LANES - facts.shape[1])))


def batch_kernel(n, segments, spot, *refs):
    rows = refs[:n]
    noise, sides, mate_panel, own_out, mate_out, fact_out = refs[n : n + 6]
    turn_sin, turn_cos, *sums = refs[n + 6 :]
    fact_out[...] = add_scores(
        rows, spot, noise, sides, mate_panel, turn_sin, turn_cos, sums, segments
    )
    own_out[...] = sums[0][...].T
    mate_out[...] = sums[1][...].T


def last_kernel(n, segments, orders, spot, *refs):
    rows = refs[:n]
    noise, sides, mate_panel = refs[n : n + 3]
    earlier = refs[n + 3 : n + 3 + 3 * (len(orders) - 1)]
    partial, facts, turn_sin, turn_cos, *sums = refs[n + 3 + len(earlier) :]
    last_facts = add_scores(
        rows, spot, noise, sides, mate_panel, turn_sin, turn_cos, sums, segments
    )
    position, core = spot[1], spot[2]
    each = rows[0].shape[0]
    ring = facts.shape[0] // (2 * each)
    half = ring // 2
    for index, order in enumerate(orders):
        if index < len(orders) - 1:
            own, mate, fact = [r[...] for r in earlier[3 * index : 3 * index + 3]]
        else:
            own, mate, fact = sums[0][...].T, sums[1][...].T, last_facts
        for k, (distance, crossed) in enumerate(order):
            place = lax.rem(position + distance + ring, ring)
            far = place >= half
            level = jnp.where(far, ring - 1 - place, place)
            device = 2 * level + (1 - core if crossed else core)
            start = pl.multiple_of((jnp.where(far, ring, 0) + device) * each, each)
            piece = slice(k * each, (k + 1) * each)
            partial[core, pl.ds(start, each), :] = own[piece]
            partial[1 - core, pl.ds(start, each), :] = mate[piece]
            facts[pl.ds(start, each), :] = fact[piece]


def score_call(chunks, orders, earlier, spot, noise, sides, mate_panel):
    each = chunks[0].shape[0]
    orientations, columns = mate_panel.shape
    whole = columns // LANES
    segments = next(s for s in (3, 2, 4, 5, 6, 7, 1) if whole % s == 0)
    n = len(chunks)
    count = each * n
    scratch = [pltpu.VMEM((count, LANES), jnp.float32)] * 2
    scratch += [pltpu.VMEM((orientations, count), jnp.float32)] * 2
    single = jax.ShapeDtypeStruct((count, orientations), jnp.float32)
    if orders is None:
        kernel = functools.partial(batch_kernel, n, segments)
        out_shape = [single, single, jax.ShapeDtypeStruct((count, LANES), jnp.float32)]
        extra = []
    else:
        everyone = each * sum(len(o) for o in orders)
        kernel = functools.partial(last_kernel, n, segments, orders)
        out_shape = [
            jax.ShapeDtypeStruct((2, everyone, orientations), jnp.float32),
            jax.ShapeDtypeStruct((everyone, LANES), jnp.float32),
        ]
        extra = [e for triple in earlier for e in triple]
    vmem = pl.BlockSpec(memory_space=pltpu.VMEM)
    return pl.pallas_call(
        kernel,
        in_specs=[pl.BlockSpec(memory_space=pltpu.SMEM)] + [vmem] * (n + 3 + len(extra)),
        out_specs=[vmem] * len(out_shape),
        out_shape=out_shape,
        scratch_shapes=scratch,
        compiler_params=pltpu.CompilerParams(vmem_limit_bytes=VMEM_LIMIT),
        cost_estimate=pl.CostEstimate(
            flops=8 * max(count, 128) * orientations * columns,
            bytes_accessed=4 * orientations * columns + 2 * count * columns,
            transcendentals=0,
        ),
    )(spot, *chunks, noise, sides, mate_panel, *extra)


def names_block(facts, search, block):
    lane = lax.broadcasted_iota(jnp.int32, facts.shape, 1)
    match = (lane >= 1) & (lane <= search) & (facts == block.astype(jnp.float32))
    return jnp.max(jnp.where(match, 1.0, 0.0), axis=1, keepdims=True) > 0.0


def chip_kernel(search, spot, partial, mate, facts, mine, own_stats, across):
    group, core, place = spot[0], spot[2], spot[3]
    count = mine.shape[0]
    lane = lax.broadcasted_iota(jnp.int32, (count, LANES), 1)
    for relative in range(2):
        side = group if relative == 0 else 1 - group
        window = pl.ds(pl.multiple_of(side * count, count), count)
        listed = facts[window, :]
        masked = []
        for crossed in range(2):
            block = core if crossed == 0 else 1 - core
            scores = partial[block, window, :] + mate[block, window, :]
            if crossed == 0:
                if relative == 0:
                    mine[...] = scores
                else:
                    across[:count] = scores
            named = names_block(listed, search, place - core + block)
            masked.append(jnp.where(named, scores, FLOOR))
        top = jnp.max(jnp.maximum(*masked), axis=1, keepdims=True)
        terms = [jnp.where(m > FLOOR, jnp.exp(m - top), 0.0) for m in masked]
        total = jnp.sum(terms[0] + terms[1], axis=1, keepdims=True)
        pair = jnp.where(lane == 0, top, jnp.where(lane == 1, total, 0.0)).T
        if relative == 0:
            own_stats[...] = pair[: own_stats.shape[0]]
        else:
            across[count:] = pair[: across.shape[0] - count]


def slot_kernel(search, slots_each, each, spot, mine, across, pair, facts, slots, chosen):
    group, place = spot[0], spot[3]
    count = mine.shape[0]
    same, other = mine[...], across[:count]
    first = group == 0
    scores = jnp.concatenate(
        [jnp.where(first, same, other), jnp.where(first, other, same)], axis=1
    )
    listed = facts[pl.ds(pl.multiple_of(group * count, count), count), :]
    named = names_block(listed, search, place)
    hit = jnp.where(named, 1.0, 0.0)
    row = lax.broadcasted_iota(jnp.int32, (count, LANES), 0)
    line = lax.broadcasted_iota(jnp.int32, (count, count), 0)
    column = lax.broadcasted_iota(jnp.int32, (count, count), 1)
    before = (column < line) & (column // each == line // each)
    rank = jnp.dot(
        jnp.where(before, 1.0, 0.0).astype(jnp.bfloat16),
        jnp.broadcast_to(hit, (count, LANES)).astype(jnp.bfloat16),
        preferred_element_type=jnp.float32,
    )
    slot = (row // each) * slots_each + rank.astype(jnp.int32)
    capacity = chosen.shape[0]
    if capacity != LANES:
        slot = jnp.broadcast_to(slot[:, :1], (count, capacity))
    target = lax.broadcasted_iota(jnp.int32, (count, capacity), 1)
    taken = jnp.where((slot == target) & named, 1.0, 0.0)
    top = jnp.broadcast_to(pair[0:1, :], (count, count)).T[:, 0:1]
    terms = jnp.where(named, jnp.exp(scores - top), 0.0)
    slots[...] = lax.dot_general(
        taken,
        terms,
        (((0,), (0,)), ((), ())),
        precision=lax.Precision.HIGHEST,
        preferred_element_type=jnp.float32,
    )
    chosen[...] = taken.T


def final_kernel(n, *refs):
    parts, slots, chosen, out = refs[:n], refs[n], refs[n + 1], refs[n + 2]
    peak = functools.reduce(jnp.maximum, [p[0:1, :] for p in parts])
    shares = [p[1:2, :] * jnp.exp(p[0:1, :] - peak) for p in parts]
    total = functools.reduce(jnp.add, shares)
    factor = jnp.exp(parts[0][0:1, :] - peak) / total
    scale = jnp.sum(chosen[...] * factor, axis=1, keepdims=True)
    out[...] = slots[...] * scale


def chip_shards(images, defocus, block_ids, noise_weight, panels):
    per_device, halves, columns = images.shape[1:]
    devices = lax.axis_size("orient")
    chips = devices // 2
    ring = 2 * chips
    everyone = per_device * devices
    local_search = block_ids.shape[2]
    orientations = panels.shape[2]
    slots_each = min(per_device, max(2, 2 * per_device * local_search // devices))
    capacity = slots_each * devices
    place = lax.axis_index("orient")
    group = lax.axis_index("cls")
    chip, core = place // 2, place % 2
    position = jnp.where(group == 0, chip, ring - 1 - chip)
    spot = jnp.stack([group, position, core, place]).astype(jnp.int32)
    first = core == 0

    mate_pairs = [(d, d ^ 1) for d in range(devices)]
    x_pairs = [(0, 1), (1, 0)]

    def joint(place, core):
        place = place % ring
        far = place >= chips
        level = ring - 1 - place if far else place
        return (2 * level + core) * 2 + int(far)

    def forward(values, step):
        pairs = [(joint(p, c), joint(p + step, c)) for p in range(ring) for c in range(2)]
        return lax.ppermute(values, ("orient", "cls"), pairs)

    vmem = pl.BlockSpec(memory_space=pltpu.VMEM)
    smem = pl.BlockSpec(memory_space=pltpu.SMEM)
    params = pltpu.CompilerParams(vmem_limit_bytes=VMEM_LIMIT)
    planes = lax.optimization_barrier(jnp.transpose(images[0], (1, 0, 2)))
    row_shape = jax.ShapeDtypeStruct((per_device, columns + LANES), jnp.bfloat16)
    kept, given = pl.pallas_call(
        row_kernel,
        in_specs=[smem] + [vmem] * 3,
        out_specs=[vmem] * 2,
        out_shape=[row_shape] * 2,
        scratch_shapes=[pltpu.VMEM((per_device, LANES), jnp.float32)],
        compiler_params=params,
    )(spot, planes, defocus, jnp.transpose(block_ids[0]))
    got = lax.ppermute(given, "orient", mate_pairs)

    _, panels = lax.optimization_barrier((got, panels))
    sides = lax.optimization_barrier(jnp.transpose(panels[0, 0], (1, 0, 2)))
    given_panel = lax.dynamic_index_in_dim(sides, 1 - core, 0, keepdims=False)

    noise = noise_weight[None, :]
    waiting = [((0, False), kept), ((0, True), got)]
    ahead = {False: kept, True: got}
    behind = {False: kept, True: got}
    orders, earlier = [], []
    for step in range(1, chips + 1):
        if step == 2 or (earlier and step == chips):
            tie = earlier[-1][2] if earlier else given_panel
            ahead = {c: lax.optimization_barrier((v, tie))[0] for c, v in ahead.items()}
            behind = {c: lax.optimization_barrier((v, tie))[0] for c, v in behind.items()}
        arrived = []
        for crossed in (False, True):
            if step < chips or not crossed:
                ahead[crossed] = forward(ahead[crossed], 1)
                arrived.append(((-step, crossed), ahead[crossed]))
            if step < chips or crossed:
                behind[crossed] = forward(behind[crossed], -1)
                arrived.append(((step, crossed), behind[crossed]))
        if step == 1:
            given_panel = lax.optimization_barrier((given_panel, *[v for _, v in arrived]))[0]
            mate_panel = lax.ppermute(given_panel, "orient", mate_pairs)
        if step in (2, chips):
            orders.append([key for key, _ in waiting])
            earlier.append(
                score_call([c for _, c in waiting], None, None, spot, noise, sides, mate_panel)
            )
            waiting = []
        waiting = waiting + arrived
    orders.append([key for key, _ in waiting])
    partial, all_facts = score_call(
        [c for _, c in waiting], orders, earlier, spot, noise, sides, mate_panel
    )

    mate_partial = lax.ppermute(partial, "orient", mate_pairs)
    mine, own_stats, across = pl.pallas_call(
        functools.partial(chip_kernel, local_search),
        in_specs=[smem] + [vmem] * 3,
        out_specs=[vmem] * 3,
        out_shape=[
            jax.ShapeDtypeStruct((everyone, orientations), jnp.float32),
            jax.ShapeDtypeStruct((8, everyone), jnp.float32),
            jax.ShapeDtypeStruct((everyone + 8, orientations), jnp.float32),
        ],
        compiler_params=params,
    )(spot, partial, mate_partial, all_facts)
    from_x = lax.ppermute(across, "cls", x_pairs)

    tops = own_stats[0], from_x[everyone]
    peak = jnp.maximum(*tops)
    total = own_stats[1] * jnp.exp(tops[0] - peak) + from_x[everyone + 1] * jnp.exp(tops[1] - peak)
    pair = jnp.pad(jnp.stack([peak, total]), ((0, 6), (0, 0)))
    pairs = [pair] + [
        lax.ppermute(pair, "orient", [(d, (d + 2 * s) % devices) for d in range(devices)])
        for s in range(1, chips)
    ]
    slots, chosen = pl.pallas_call(
        functools.partial(slot_kernel, local_search, slots_each, per_device),
        in_specs=[smem] + [vmem] * 4,
        out_specs=[vmem] * 2,
        out_shape=[
            jax.ShapeDtypeStruct((capacity, 2 * orientations), jnp.float32),
            jax.ShapeDtypeStruct((capacity, everyone), jnp.float32),
        ],
        compiler_params=params,
    )(spot, mine, from_x, pair, all_facts)
    posterior = pl.pallas_call(
        functools.partial(final_kernel, chips),
        in_specs=[vmem] * (chips + 2),
        out_specs=vmem,
        out_shape=jax.ShapeDtypeStruct((capacity, 2 * orientations), jnp.float32),
        compiler_params=params,
    )(*pairs, slots, chosen)
    return posterior.reshape(1, 1, capacity, -1)


def spread_max(member, is_live, values):
    picked = jnp.max(jnp.where(member, values[None, :], FLOOR), axis=1)
    return jnp.where(is_live, picked, 0.0)


def collect_sums(member, expo):
    return jnp.sum(jnp.where(member, jnp.sum(expo, axis=1)[:, None], 0.0), axis=0)


def shards(images, defocus, block_ids, noise_weight, panels):
    per_device = images.shape[1]
    columns = images.shape[3]
    devices = lax.axis_size("orient")
    local_search = block_ids.shape[2]
    slots_each = min(per_device, max(2, 2 * per_device * local_search // devices))
    capacity = slots_each * devices
    everyone = per_device * devices
    all_lists = lax.all_gather(block_ids[0], "orient", axis=0, tiled=True)
    all_rows, all_focus = (
        lax.all_gather(images[0], "orient", axis=0, tiled=True),
        lax.all_gather(defocus[0], "orient", axis=0, tiled=True),
    )
    own_block = lax.axis_index("orient")
    block_hits = (
        jnp.any(all_lists == own_block, axis=1).astype(jnp.int32).reshape(devices, per_device)
    )
    slot_rank = jnp.cumsum(block_hits, axis=1) - block_hits
    places = (jnp.arange(devices, dtype=jnp.int32)[:, None] * slots_each + slot_rank).reshape(
        everyone
    )
    chosen = (places[None, :] == jnp.arange(capacity, dtype=jnp.int32)[:, None]) & (
        block_hits.reshape(everyone)[None, :] == 1
    )
    is_live = jnp.any(chosen, axis=1)
    slot_owner = jnp.sum(
        jnp.where(chosen, jnp.arange(everyone, dtype=jnp.int32)[None, :], 0), axis=1
    )
    slot_rows = jnp.take(all_rows, slot_owner, axis=0)
    slot_focus = jnp.take(all_focus, slot_owner, axis=0).astype(jnp.float32)
    frequency = (jnp.arange(columns, dtype=jnp.float32) + 0.5) / columns
    contrast = -jnp.sin(CTF_PHASE * slot_focus[:, None] * frequency[None, :] + 0.1)
    weighted = contrast * noise_weight[None, :]
    scaled_rows = (weighted[:, None, :] * slot_rows.astype(jnp.float32)).astype(jnp.bfloat16)
    energy = (contrast * weighted).astype(jnp.bfloat16)
    piece = lax.all_gather(panels[:, 0], "cls", axis=0, tiled=True)
    widened = piece.astype(jnp.float32)
    squared = (widened * widened).astype(jnp.bfloat16)
    correlate = jnp.einsum("srk,cjrk->scj", scaled_rows, piece, preferred_element_type=jnp.float32)
    energy_term = jnp.einsum("sk,cjrk->scj", energy, squared, preferred_element_type=jnp.float32)
    terms = correlate - 0.5 * energy_term
    combined = terms.reshape(capacity, -1)
    scores = lax.psum_scatter(combined, "rep", scatter_dimension=1, tiled=True)
    member = (slot_owner[:, None] == jnp.arange(everyone, dtype=jnp.int32)[None, :]) & is_live[
        :, None
    ]
    slot_top = jnp.max(scores, axis=1)
    local_peak = jnp.max(jnp.where(member, slot_top[:, None], FLOOR), axis=0)
    peak = lax.pmax(local_peak, ("orient", "rep"))
    slot_peak = spread_max(member, is_live, peak)
    expo = jnp.where(is_live[:, None], jnp.exp(scores - slot_peak[:, None]), 0.0)
    total = lax.psum(collect_sums(member, expo), ("orient", "rep"))
    slot_total = jnp.where(is_live, jnp.sum(jnp.where(member, total[None, :], 0.0), axis=1), 1.0)
    posterior = expo / slot_total[:, None]
    return posterior.reshape(1, 1, capacity, -1)


def solution(mesh):
    in_specs = (
        P(("batch", "cls"), "orient", "rep", None),
        P(("batch", "cls"), "orient"),
        P(("batch", "cls"), "orient", None),
        P(),
        P(("batch", "cls"), "orient", None, "rep", None),
    )
    out_specs = P(("batch", "cls"), "orient", None, "rep")
    sizes = mesh.shape
    paired = sizes["rep"] == 1 and sizes["cls"] == 2 and sizes["orient"] % 2 == 0
    return jax.shard_map(
        chip_shards if paired else shards,
        mesh=mesh,
        in_specs=in_specs,
        out_specs=out_specs,
        check_vma=False,
    )
```

```python
import functools

import jax
import jax.numpy as jnp
from jax import lax
from jax.experimental import pallas as pl
from jax.experimental.pallas import tpu as pltpu
from jax.sharding import PartitionSpec as P

CTF_PHASE = 40.0
FLOOR = -1e30
LANES = 128
VMEM_LIMIT = 8 * 1024 * 1024


def sin_cos(angle):
    turns = jnp.floor(angle * 0.6366197723675814 + 0.5)
    rest = angle - turns * 1.5703125
    rest = rest - turns * 4.837512969970703e-4
    rest = rest - turns * 7.549789948768648e-8
    square = rest * rest
    sine = rest + rest * square * (
        -1.6666654611e-1 + square * (8.3321608736e-3 - square * 1.9515295891e-4)
    )
    cosine = (
        1.0
        - 0.5 * square
        + square
        * square
        * (4.166664568298827e-2 + square * (-1.388731625493765e-3 + square * 2.443315711809948e-5))
    )
    quarter = turns.astype(jnp.int32)
    odd = (quarter & 1) == 1
    low = jnp.where(odd, cosine, sine)
    high = jnp.where(odd, sine, cosine)
    return (
        jnp.where((quarter & 2) == 2, -low, low),
        jnp.where(((quarter + 1) & 2) == 2, -high, high),
    )


def row_kernel(spot, planes, defocus, lists, kept, given, facts):
    core = spot[2]
    columns = planes.shape[2]
    count = defocus.shape[1]
    facts[...] = jnp.zeros_like(facts)
    facts[0:1, :count] = defocus[...].astype(jnp.float32)
    facts[1 : 1 + lists.shape[0], :count] = lists[...].astype(jnp.float32)
    for half, out in ((core, kept), (1 - core, given)):
        out[:, :columns] = planes[half]
        out[:, columns:] = facts[...].astype(out.dtype)


def particle_facts(meta):
    return jnp.concatenate([m[...].astype(jnp.float32).T[: m.shape[0]] for m in meta], axis=0)


def add_scores(rows, spot, noise, sides, mate_panel, turn_sin, turn_cos, sums, segments):
    columns = noise.shape[1]
    width = columns // segments
    tiles = width // LANES
    count = turn_sin.shape[0]
    facts = particle_facts([r.at[:, pl.ds(columns, LANES)] for r in rows])
    rate = jnp.broadcast_to(CTF_PHASE * facts[:, 0:1], (count, LANES))
    lane = lax.broadcasted_iota(jnp.int32, (count, LANES), 1).astype(jnp.float32)
    first_sin, first_cos = sin_cos(rate * ((lane + 0.5) / columns) + 0.1)
    step_sin, step_cos = sin_cos(rate * (LANES / columns))
    turn_sin[...] = step_sin
    turn_cos[...] = step_cos
    for total in sums:
        total[...] = jnp.zeros_like(total)
    core = spot[2]

    def segment(index, carry):
        sine, cosine = carry
        start = pl.multiple_of(index * width, LANES)
        scaled_parts, energy_parts = [], []
        for t in range(tiles):
            window = pl.ds(start + t * LANES, LANES)
            weighted = sine * noise[:, window]
            image = jnp.concatenate([r[:, window] for r in rows], axis=0).astype(jnp.float32)
            scaled_parts.append((weighted * image).astype(jnp.bfloat16))
            energy_parts.append((sine * weighted).astype(jnp.bfloat16))
            ds, dc = turn_sin[...], turn_cos[...]
            sine, cosine = sine * dc + cosine * ds, cosine * dc - sine * ds
        scaled = jnp.concatenate(scaled_parts, axis=1)
        energy = jnp.concatenate(energy_parts, axis=1)
        contract = (((1,), (1,)), ((), ()))
        whole = pl.ds(start, width)
        for values, total in ((sides[core, :, whole], sums[0]), (mate_panel[:, whole], sums[1])):
            squared = values * values
            correlate = lax.dot_general(
                values, scaled, contract, preferred_element_type=jnp.float32
            )
            power = lax.dot_general(squared, energy, contract, preferred_element_type=jnp.float32)
            total[...] += correlate - 0.5 * power
        return sine, cosine

    lax.fori_loop(0, segments, segment, (-first_sin, -first_cos))
    return jnp.pad(facts, ((0, 0), (0, LANES - facts.shape[1])))


def batch_kernel(n, segments, spot, *refs):
    rows = refs[:n]
    noise, sides, mate_panel, own_out, mate_out, fact_out = refs[n : n + 6]
    turn_sin, turn_cos, *sums = refs[n + 6 :]
    fact_out[...] = add_scores(
        rows, spot, noise, sides, mate_panel, turn_sin, turn_cos, sums, segments
    )
    own_out[...] = sums[0][...].T
    mate_out[...] = sums[1][...].T


def last_kernel(n, segments, orders, spot, *refs):
    rows = refs[:n]
    noise, sides, mate_panel = refs[n : n + 3]
    earlier = refs[n + 3 : n + 3 + 3 * (len(orders) - 1)]
    partial, facts, turn_sin, turn_cos, *sums = refs[n + 3 + len(earlier) :]
    last_facts = add_scores(
        rows, spot, noise, sides, mate_panel, turn_sin, turn_cos, sums, segments
    )
    position, core = spot[1], spot[2]
    each = rows[0].shape[0]
    ring = facts.shape[0] // (2 * each)
    half = ring // 2
    for index, order in enumerate(orders):
        if index < len(orders) - 1:
            own, mate, fact = [r[...] for r in earlier[3 * index : 3 * index + 3]]
        else:
            own, mate, fact = sums[0][...].T, sums[1][...].T, last_facts
        for k, (distance, crossed) in enumerate(order):
            place = lax.rem(position + distance + ring, ring)
            far = place >= half
            level = jnp.where(far, ring - 1 - place, place)
            device = 2 * level + (1 - core if crossed else core)
            start = pl.multiple_of((jnp.where(far, ring, 0) + device) * each, each)
            piece = slice(k * each, (k + 1) * each)
            partial[core, pl.ds(start, each), :] = own[piece]
            partial[1 - core, pl.ds(start, each), :] = mate[piece]
            facts[pl.ds(start, each), :] = fact[piece]


def score_call(chunks, orders, earlier, spot, noise, sides, mate_panel):
    each = chunks[0].shape[0]
    orientations, columns = mate_panel.shape
    whole = columns // LANES
    segments = next(s for s in (3, 2, 4, 5, 6, 7, 1) if whole % s == 0)
    n = len(chunks)
    count = each * n
    scratch = [pltpu.VMEM((count, LANES), jnp.float32)] * 2
    scratch += [pltpu.VMEM((orientations, count), jnp.float32)] * 2
    single = jax.ShapeDtypeStruct((count, orientations), jnp.float32)
    if orders is None:
        kernel = functools.partial(batch_kernel, n, segments)
        out_shape = [single, single, jax.ShapeDtypeStruct((count, LANES), jnp.float32)]
        extra = []
    else:
        everyone = each * sum(len(o) for o in orders)
        kernel = functools.partial(last_kernel, n, segments, orders)
        out_shape = [
            jax.ShapeDtypeStruct((2, everyone, orientations), jnp.float32),
            jax.ShapeDtypeStruct((everyone, LANES), jnp.float32),
        ]
        extra = [e for triple in earlier for e in triple]
    vmem = pl.BlockSpec(memory_space=pltpu.VMEM)
    return pl.pallas_call(
        kernel,
        in_specs=[pl.BlockSpec(memory_space=pltpu.SMEM)] + [vmem] * (n + 3 + len(extra)),
        out_specs=[vmem] * len(out_shape),
        out_shape=out_shape,
        scratch_shapes=scratch,
        compiler_params=pltpu.CompilerParams(vmem_limit_bytes=VMEM_LIMIT),
        cost_estimate=pl.CostEstimate(
            flops=8 * max(count, 128) * orientations * columns,
            bytes_accessed=4 * orientations * columns + 2 * count * columns,
            transcendentals=0,
        ),
    )(spot, *chunks, noise, sides, mate_panel, *extra)


def names_block(facts, search, block):
    lane = lax.broadcasted_iota(jnp.int32, facts.shape, 1)
    match = (lane >= 1) & (lane <= search) & (facts == block.astype(jnp.float32))
    return jnp.max(jnp.where(match, 1.0, 0.0), axis=1, keepdims=True) > 0.0


def chip_kernel(search, spot, partial, mate, facts, mine, own_stats, across):
    group, core, place = spot[0], spot[2], spot[3]
    count = mine.shape[0]
    lane = lax.broadcasted_iota(jnp.int32, (count, LANES), 1)
    for relative in range(2):
        side = group if relative == 0 else 1 - group
        window = pl.ds(pl.multiple_of(side * count, count), count)
        listed = facts[window, :]
        masked = []
        for crossed in range(2):
            block = core if crossed == 0 else 1 - core
            scores = partial[block, window, :] + mate[block, window, :]
            if crossed == 0:
                if relative == 0:
                    mine[...] = scores
                else:
                    across[:count] = scores
            named = names_block(listed, search, place - core + block)
            masked.append(jnp.where(named, scores, FLOOR))
        top = jnp.max(jnp.maximum(*masked), axis=1, keepdims=True)
        terms = [jnp.where(m > FLOOR, jnp.exp(m - top), 0.0) for m in masked]
        total = jnp.sum(terms[0] + terms[1], axis=1, keepdims=True)
        pair = jnp.where(lane == 0, top, jnp.where(lane == 1, total, 0.0)).T
        if relative == 0:
            own_stats[...] = pair[: own_stats.shape[0]]
        else:
            across[count:] = pair[: across.shape[0] - count]


def slot_kernel(search, slots_each, each, spot, mine, across, pair, facts, slots, chosen):
    group, place = spot[0], spot[3]
    count = mine.shape[0]
    same, other = mine[...], across[:count]
    first = group == 0
    scores = jnp.concatenate(
        [jnp.where(first, same, other), jnp.where(first, other, same)], axis=1
    )
    listed = facts[pl.ds(pl.multiple_of(group * count, count), count), :]
    named = names_block(listed, search, place)
    hit = jnp.where(named, 1.0, 0.0)
    row = lax.broadcasted_iota(jnp.int32, (count, LANES), 0)
    line = lax.broadcasted_iota(jnp.int32, (count, count), 0)
    column = lax.broadcasted_iota(jnp.int32, (count, count), 1)
    before = (column < line) & (column // each == line // each)
    rank = jnp.dot(
        jnp.where(before, 1.0, 0.0).astype(jnp.bfloat16),
        jnp.broadcast_to(hit, (count, LANES)).astype(jnp.bfloat16),
        preferred_element_type=jnp.float32,
    )
    slot = (row // each) * slots_each + rank.astype(jnp.int32)
    capacity = chosen.shape[0]
    if capacity != LANES:
        slot = jnp.broadcast_to(slot[:, :1], (count, capacity))
    target = lax.broadcasted_iota(jnp.int32, (count, capacity), 1)
    taken = jnp.where((slot == target) & named, 1.0, 0.0)
    top = jnp.broadcast_to(pair[0:1, :], (count, count)).T[:, 0:1]
    terms = jnp.where(named, jnp.exp(scores - top), 0.0)
    slots[...] = lax.dot_general(
        taken,
        terms,
        (((0,), (0,)), ((), ())),
        precision=lax.Precision.HIGHEST,
        preferred_element_type=jnp.float32,
    )
    chosen[...] = taken.T


def final_kernel(n, *refs):
    parts, slots, chosen, out = refs[:n], refs[n], refs[n + 1], refs[n + 2]
    peak = functools.reduce(jnp.maximum, [p[0:1, :] for p in parts])
    shares = [p[1:2, :] * jnp.exp(p[0:1, :] - peak) for p in parts]
    total = functools.reduce(jnp.add, shares)
    factor = jnp.exp(parts[0][0:1, :] - peak) / total
    scale = jnp.sum(chosen[...] * factor, axis=1, keepdims=True)
    out[...] = slots[...] * scale


def chip_shards(images, defocus, block_ids, noise_weight, panels):
    per_device, halves, columns = images.shape[1:]
    devices = lax.axis_size("orient")
    chips = devices // 2
    ring = 2 * chips
    everyone = per_device * devices
    local_search = block_ids.shape[2]
    orientations = panels.shape[2]
    slots_each = min(per_device, max(2, 2 * per_device * local_search // devices))
    capacity = slots_each * devices
    place = lax.axis_index("orient")
    group = lax.axis_index("cls")
    chip, core = place // 2, place % 2
    position = jnp.where(group == 0, chip, ring - 1 - chip)
    spot = jnp.stack([group, position, core, place]).astype(jnp.int32)
    first = core == 0

    mate_pairs = [(d, d ^ 1) for d in range(devices)]
    x_pairs = [(0, 1), (1, 0)]

    def joint(place, core):
        place = place % ring
        far = place >= chips
        level = ring - 1 - place if far else place
        return (2 * level + core) * 2 + int(far)

    def forward(values, step):
        pairs = [(joint(p, c), joint(p + step, c)) for p in range(ring) for c in range(2)]
        return lax.ppermute(values, ("orient", "cls"), pairs)

    vmem = pl.BlockSpec(memory_space=pltpu.VMEM)
    smem = pl.BlockSpec(memory_space=pltpu.SMEM)
    params = pltpu.CompilerParams(vmem_limit_bytes=VMEM_LIMIT)
    planes = lax.optimization_barrier(jnp.transpose(images[0], (1, 0, 2)))
    row_shape = jax.ShapeDtypeStruct((per_device, columns + LANES), jnp.bfloat16)
    kept, given = pl.pallas_call(
        row_kernel,
        in_specs=[smem] + [vmem] * 3,
        out_specs=[vmem] * 2,
        out_shape=[row_shape] * 2,
        scratch_shapes=[pltpu.VMEM((per_device, LANES), jnp.float32)],
        compiler_params=params,
    )(spot, planes, defocus, jnp.transpose(block_ids[0]))
    with jax.named_scope("mate_rows"):
        got = lax.ppermute(given, "orient", mate_pairs)

    _, panels = lax.optimization_barrier((got, panels))
    sides = lax.optimization_barrier(jnp.transpose(panels[0, 0], (1, 0, 2)))
    given_panel = lax.dynamic_index_in_dim(sides, 1 - core, 0, keepdims=False)

    noise = noise_weight[None, :]
    waiting = [((0, False), kept), ((0, True), got)]
    ahead = {False: kept, True: got}
    behind = {False: kept, True: got}
    orders, earlier, late = [], [], []
    for step in range(1, chips + 1):
        if step == chips and step > 2:
            orders.append([key for key, _ in waiting])
            earlier.append(score([c for _, c in waiting]))
            waiting = []
            tie = earlier[-1][2]
            ahead = {c: lax.optimization_barrier((v, tie))[0] for c, v in ahead.items()}
            behind = {c: lax.optimization_barrier((v, tie))[0] for c, v in behind.items()}
        waiting = waiting + late
        late = []
        for crossed in (False, True):
            if step < chips or not crossed:
                with jax.named_scope(f"ahead_{'BA'[not crossed]}{step}"):
                    ahead[crossed] = forward(ahead[crossed], 1)
                late.append(((-step, crossed), ahead[crossed]))
            if step < chips or crossed:
                with jax.named_scope(f"behind_{'BA'[not crossed]}{step}"):
                    behind[crossed] = forward(behind[crossed], -1)
                late.append(((step, crossed), behind[crossed]))
        if step == 2:
            given_panel = lax.optimization_barrier((given_panel, *[v for _, v in late]))[0]
            with jax.named_scope("mate_panel"):
                mate_panel = lax.ppermute(given_panel, "orient", mate_pairs)
            score = lambda c: score_call(c, None, None, spot, noise, sides, mate_panel)
    orders.append([key for key, _ in waiting])
    earlier.append(score([c for _, c in waiting]))
    waiting = late
    orders.append([key for key, _ in waiting])
    partial, all_facts = score_call(
        [c for _, c in waiting], orders, earlier, spot, noise, sides, mate_panel
    )

    mate_partial = lax.ppermute(partial, "orient", mate_pairs)
    mine, own_stats, across = pl.pallas_call(
        functools.partial(chip_kernel, local_search),
        in_specs=[smem] + [vmem] * 3,
        out_specs=[vmem] * 3,
        out_shape=[
            jax.ShapeDtypeStruct((everyone, orientations), jnp.float32),
            jax.ShapeDtypeStruct((8, everyone), jnp.float32),
            jax.ShapeDtypeStruct((everyone + 8, orientations), jnp.float32),
        ],
        compiler_params=params,
    )(spot, partial, mate_partial, all_facts)
    from_x = lax.ppermute(across, "cls", x_pairs)

    tops = own_stats[0], from_x[everyone]
    peak = jnp.maximum(*tops)
    total = own_stats[1] * jnp.exp(tops[0] - peak) + from_x[everyone + 1] * jnp.exp(tops[1] - peak)
    pair = jnp.pad(jnp.stack([peak, total]), ((0, 6), (0, 0)))
    pairs = [pair] + [
        lax.ppermute(pair, "orient", [(d, (d + 2 * s) % devices) for d in range(devices)])
        for s in range(1, chips)
    ]
    slots, chosen = pl.pallas_call(
        functools.partial(slot_kernel, local_search, slots_each, per_device),
        in_specs=[smem] + [vmem] * 4,
        out_specs=[vmem] * 2,
        out_shape=[
            jax.ShapeDtypeStruct((capacity, 2 * orientations), jnp.float32),
            jax.ShapeDtypeStruct((capacity, everyone), jnp.float32),
        ],
        compiler_params=params,
    )(spot, mine, from_x, pair, all_facts)
    posterior = pl.pallas_call(
        functools.partial(final_kernel, chips),
        in_specs=[vmem] * (chips + 2),
        out_specs=vmem,
        out_shape=jax.ShapeDtypeStruct((capacity, 2 * orientations), jnp.float32),
        compiler_params=params,
    )(*pairs, slots, chosen)
    return posterior.reshape(1, 1, capacity, -1)


def spread_max(member, is_live, values):
    picked = jnp.max(jnp.where(member, values[None, :], FLOOR), axis=1)
    return jnp.where(is_live, picked, 0.0)


def collect_sums(member, expo):
    return jnp.sum(jnp.where(member, jnp.sum(expo, axis=1)[:, None], 0.0), axis=0)


def shards(images, defocus, block_ids, noise_weight, panels):
    per_device = images.shape[1]
    columns = images.shape[3]
    devices = lax.axis_size("orient")
    local_search = block_ids.shape[2]
    slots_each = min(per_device, max(2, 2 * per_device * local_search // devices))
    capacity = slots_each * devices
    everyone = per_device * devices
    all_lists = lax.all_gather(block_ids[0], "orient", axis=0, tiled=True)
    all_rows, all_focus = (
        lax.all_gather(images[0], "orient", axis=0, tiled=True),
        lax.all_gather(defocus[0], "orient", axis=0, tiled=True),
    )
    own_block = lax.axis_index("orient")
    block_hits = (
        jnp.any(all_lists == own_block, axis=1).astype(jnp.int32).reshape(devices, per_device)
    )
    slot_rank = jnp.cumsum(block_hits, axis=1) - block_hits
    places = (jnp.arange(devices, dtype=jnp.int32)[:, None] * slots_each + slot_rank).reshape(
        everyone
    )
    chosen = (places[None, :] == jnp.arange(capacity, dtype=jnp.int32)[:, None]) & (
        block_hits.reshape(everyone)[None, :] == 1
    )
    is_live = jnp.any(chosen, axis=1)
    slot_owner = jnp.sum(
        jnp.where(chosen, jnp.arange(everyone, dtype=jnp.int32)[None, :], 0), axis=1
    )
    slot_rows = jnp.take(all_rows, slot_owner, axis=0)
    slot_focus = jnp.take(all_focus, slot_owner, axis=0).astype(jnp.float32)
    frequency = (jnp.arange(columns, dtype=jnp.float32) + 0.5) / columns
    contrast = -jnp.sin(CTF_PHASE * slot_focus[:, None] * frequency[None, :] + 0.1)
    weighted = contrast * noise_weight[None, :]
    scaled_rows = (weighted[:, None, :] * slot_rows.astype(jnp.float32)).astype(jnp.bfloat16)
    energy = (contrast * weighted).astype(jnp.bfloat16)
    piece = lax.all_gather(panels[:, 0], "cls", axis=0, tiled=True)
    widened = piece.astype(jnp.float32)
    squared = (widened * widened).astype(jnp.bfloat16)
    correlate = jnp.einsum("srk,cjrk->scj", scaled_rows, piece, preferred_element_type=jnp.float32)
    energy_term = jnp.einsum("sk,cjrk->scj", energy, squared, preferred_element_type=jnp.float32)
    terms = correlate - 0.5 * energy_term
    combined = terms.reshape(capacity, -1)
    scores = lax.psum_scatter(combined, "rep", scatter_dimension=1, tiled=True)
    member = (slot_owner[:, None] == jnp.arange(everyone, dtype=jnp.int32)[None, :]) & is_live[
        :, None
    ]
    slot_top = jnp.max(scores, axis=1)
    local_peak = jnp.max(jnp.where(member, slot_top[:, None], FLOOR), axis=0)
    peak = lax.pmax(local_peak, ("orient", "rep"))
    slot_peak = spread_max(member, is_live, peak)
    expo = jnp.where(is_live[:, None], jnp.exp(scores - slot_peak[:, None]), 0.0)
    total = lax.psum(collect_sums(member, expo), ("orient", "rep"))
    slot_total = jnp.where(is_live, jnp.sum(jnp.where(member, total[None, :], 0.0), axis=1), 1.0)
    posterior = expo / slot_total[:, None]
    return posterior.reshape(1, 1, capacity, -1)


def solution(mesh):
    in_specs = (
        P(("batch", "cls"), "orient", "rep", None),
        P(("batch", "cls"), "orient"),
        P(("batch", "cls"), "orient", None),
        P(),
        P(("batch", "cls"), "orient", None, "rep", None),
    )
    out_specs = P(("batch", "cls"), "orient", None, "rep")
    sizes = mesh.shape
    paired = sizes["rep"] == 1 and sizes["cls"] == 2 and sizes["orient"] % 2 == 0
    return jax.shard_map(
        chip_shards if paired else shards,
        mesh=mesh,
        in_specs=in_specs,
        out_specs=out_specs,
        check_vma=False,
    )
```

```python
import functools

import jax
import jax.numpy as jnp
from jax import lax
from jax.experimental import pallas as pl
from jax.experimental.pallas import tpu as pltpu
from jax.sharding import PartitionSpec as P

CTF_PHASE = 40.0
FLOOR = -1e30
LANES = 128
VMEM_LIMIT = 8 * 1024 * 1024


def sin_cos(angle):
    turns = jnp.floor(angle * 0.6366197723675814 + 0.5)
    rest = angle - turns * 1.5703125
    rest = rest - turns * 4.837512969970703e-4
    rest = rest - turns * 7.549789948768648e-8
    square = rest * rest
    sine = rest + rest * square * (
        -1.6666654611e-1 + square * (8.3321608736e-3 - square * 1.9515295891e-4)
    )
    cosine = (
        1.0
        - 0.5 * square
        + square
        * square
        * (4.166664568298827e-2 + square * (-1.388731625493765e-3 + square * 2.443315711809948e-5))
    )
    quarter = turns.astype(jnp.int32)
    odd = (quarter & 1) == 1
    low = jnp.where(odd, cosine, sine)
    high = jnp.where(odd, sine, cosine)
    return (
        jnp.where((quarter & 2) == 2, -low, low),
        jnp.where(((quarter + 1) & 2) == 2, -high, high),
    )


def row_kernel(spot, planes, defocus, lists, kept, given, facts, focus, named, sems):
    core = spot[2]
    columns = planes.shape[2]
    count = defocus.shape[1]
    fetches = [
        pltpu.make_async_copy(defocus, focus, sems.at[0]),
        pltpu.make_async_copy(lists, named, sems.at[1]),
    ]
    for fetch in fetches:
        fetch.start()
    facts[...] = jnp.zeros_like(facts)
    for half, out in ((core, kept), (1 - core, given)):
        out[:, :columns] = planes[half]
    for fetch in fetches:
        fetch.wait()
    facts[0:1, :count] = focus[...].astype(jnp.float32)
    facts[1 : 1 + lists.shape[0], :count] = named[...].astype(jnp.float32)
    for out in (kept, given):
        out[:, columns:] = facts[...].astype(out.dtype)


def particle_facts(meta):
    return jnp.concatenate([m[...].astype(jnp.float32).T[: m.shape[0]] for m in meta], axis=0)


def add_scores(rows, spot, noise, sides, mate_panel, turn_sin, turn_cos, sums, segments):
    columns = noise.shape[1]
    width = columns // segments
    tiles = width // LANES
    count = turn_sin.shape[0]
    facts = particle_facts([r.at[:, pl.ds(columns, LANES)] for r in rows])
    rate = jnp.broadcast_to(CTF_PHASE * facts[:, 0:1], (count, LANES))
    lane = lax.broadcasted_iota(jnp.int32, (count, LANES), 1).astype(jnp.float32)
    first_sin, first_cos = sin_cos(rate * ((lane + 0.5) / columns) + 0.1)
    step_sin, step_cos = sin_cos(rate * (LANES / columns))
    turn_sin[...] = step_sin
    turn_cos[...] = step_cos
    for total in sums:
        total[...] = jnp.zeros_like(total)
    core = spot[2]

    def segment(index, carry):
        sine, cosine = carry
        start = pl.multiple_of(index * width, LANES)
        scaled_parts, energy_parts = [], []
        for t in range(tiles):
            window = pl.ds(start + t * LANES, LANES)
            weighted = sine * noise[:, window]
            image = jnp.concatenate([r[:, window] for r in rows], axis=0).astype(jnp.float32)
            scaled_parts.append((weighted * image).astype(jnp.bfloat16))
            energy_parts.append((sine * weighted).astype(jnp.bfloat16))
            ds, dc = turn_sin[...], turn_cos[...]
            sine, cosine = sine * dc + cosine * ds, cosine * dc - sine * ds
        scaled = jnp.concatenate(scaled_parts, axis=1)
        energy = jnp.concatenate(energy_parts, axis=1)
        contract = (((1,), (1,)), ((), ()))
        whole = pl.ds(start, width)
        for values, total in ((sides[core, :, whole], sums[0]), (mate_panel[:, whole], sums[1])):
            squared = values * values
            correlate = lax.dot_general(
                values, scaled, contract, preferred_element_type=jnp.float32
            )
            power = lax.dot_general(squared, energy, contract, preferred_element_type=jnp.float32)
            total[...] += correlate - 0.5 * power
        return sine, cosine

    lax.fori_loop(0, segments, segment, (-first_sin, -first_cos))
    return jnp.pad(facts, ((0, 0), (0, LANES - facts.shape[1])))


def batch_kernel(n, segments, spot, *refs):
    rows = refs[:n]
    noise, sides, mate_panel = refs[n : n + 3]
    own_out, mate_out, fact_out, turn_sin, turn_cos, *sums = refs[n + 3 :]
    fact_out[...] = add_scores(
        rows, spot, noise, sides, mate_panel, turn_sin, turn_cos, sums, segments
    )
    own_out[...] = sums[0][...].T
    mate_out[...] = sums[1][...].T


def last_kernel(n, segments, orders, spot, *refs):
    rows = refs[:n]
    noise, sides, mate_panel = refs[n : n + 3]
    rest = refs[n + 3 :]
    earlier, rest = rest[: 3 * (len(orders) - 1)], rest[3 * (len(orders) - 1) :]
    partial, facts, turn_sin, turn_cos, *sums = rest
    last_facts = add_scores(
        rows, spot, noise, sides, mate_panel, turn_sin, turn_cos, sums, segments
    )
    position, core = spot[1], spot[2]
    each = rows[0].shape[0]
    ring = facts.shape[0] // (2 * each)
    half = ring // 2
    for index, order in enumerate(orders):
        if index < len(orders) - 1:
            own, mate, fact = [r[...] for r in earlier[3 * index : 3 * index + 3]]
        else:
            own, mate, fact = sums[0][...].T, sums[1][...].T, last_facts
        for k, (distance, crossed) in enumerate(order):
            place = lax.rem(position + distance + ring, ring)
            far = place >= half
            level = jnp.where(far, ring - 1 - place, place)
            device = 2 * level + (1 - core if crossed else core)
            start = pl.multiple_of((jnp.where(far, ring, 0) + device) * each, each)
            piece = slice(k * each, (k + 1) * each)
            partial[core, pl.ds(start, each), :] = own[piece]
            partial[1 - core, pl.ds(start, each), :] = mate[piece]
            facts[pl.ds(start, each), :] = fact[piece]


def score_call(chunks, orders, earlier, spot, noise, sides, mate_panel):
    each = chunks[0].shape[0]
    orientations, columns = sides.shape[1:]
    whole = columns // LANES
    segments = next(s for s in (3, 2, 4, 5, 6, 7, 1) if whole % s == 0)
    n = len(chunks)
    count = each * n
    scratch = [pltpu.VMEM((count, LANES), jnp.float32)] * 2
    scratch += [pltpu.VMEM((orientations, count), jnp.float32)] * 2
    single = jax.ShapeDtypeStruct((count, orientations), jnp.float32)
    if orders is None:
        kernel = functools.partial(batch_kernel, n, segments)
        out_shape = [single, single, jax.ShapeDtypeStruct((count, LANES), jnp.float32)]
        extra = []
    else:
        everyone = each * sum(len(o) for o in orders)
        kernel = functools.partial(last_kernel, n, segments, orders)
        out_shape = [
            jax.ShapeDtypeStruct((2, everyone, orientations), jnp.float32),
            jax.ShapeDtypeStruct((everyone, LANES), jnp.float32),
        ]
        extra = [e for triple in earlier for e in triple]
    vmem = pl.BlockSpec(memory_space=pltpu.VMEM)
    return pl.pallas_call(
        kernel,
        in_specs=[pl.BlockSpec(memory_space=pltpu.SMEM)] + [vmem] * (n + 3 + len(extra)),
        out_specs=[vmem] * len(out_shape),
        out_shape=out_shape,
        scratch_shapes=scratch,
        compiler_params=pltpu.CompilerParams(vmem_limit_bytes=VMEM_LIMIT),
        cost_estimate=pl.CostEstimate(
            flops=8 * max(count, 128) * orientations * columns,
            bytes_accessed=4 * orientations * columns + 2 * count * columns,
            transcendentals=0,
        ),
    )(spot, *chunks, noise, sides, mate_panel, *extra)


def names_block(facts, search, block):
    lane = lax.broadcasted_iota(jnp.int32, facts.shape, 1)
    match = (lane >= 1) & (lane <= search) & (facts == block.astype(jnp.float32))
    return jnp.max(jnp.where(match, 1.0, 0.0), axis=1, keepdims=True) > 0.0


def chip_kernel(search, spot, partial, mate, facts, mine, own_stats, across):
    group, core, place = spot[0], spot[2], spot[3]
    count = mine.shape[0]
    lane = lax.broadcasted_iota(jnp.int32, (count, LANES), 1)
    for relative in range(2):
        side = group if relative == 0 else 1 - group
        window = pl.ds(pl.multiple_of(side * count, count), count)
        listed = facts[window, :]
        masked = []
        for crossed in range(2):
            block = core if crossed == 0 else 1 - core
            scores = partial[block, window, :] + mate[block, window, :]
            if crossed == 0:
                if relative == 0:
                    mine[...] = scores
                else:
                    across[:count] = scores
            named = names_block(listed, search, place - core + block)
            masked.append(jnp.where(named, scores, FLOOR))
        top = jnp.max(jnp.maximum(*masked), axis=1, keepdims=True)
        terms = [jnp.where(m > FLOOR, jnp.exp(m - top), 0.0) for m in masked]
        total = jnp.sum(terms[0] + terms[1], axis=1, keepdims=True)
        pair = jnp.where(lane == 0, top, jnp.where(lane == 1, total, 0.0)).T
        if relative == 0:
            own_stats[...] = pair[: own_stats.shape[0]]
        else:
            across[count:] = pair[: across.shape[0] - count]


def slot_kernel(search, slots_each, each, spot, mine, across, pair, facts, slots, chosen):
    group, place = spot[0], spot[3]
    count = mine.shape[0]
    same, other = mine[...], across[:count]
    first = group == 0
    scores = jnp.concatenate(
        [jnp.where(first, same, other), jnp.where(first, other, same)], axis=1
    )
    listed = facts[pl.ds(pl.multiple_of(group * count, count), count), :]
    named = names_block(listed, search, place)
    hit = jnp.where(named, 1.0, 0.0)
    row = lax.broadcasted_iota(jnp.int32, (count, LANES), 0)
    line = lax.broadcasted_iota(jnp.int32, (count, count), 0)
    column = lax.broadcasted_iota(jnp.int32, (count, count), 1)
    before = (column < line) & (column // each == line // each)
    rank = jnp.dot(
        jnp.where(before, 1.0, 0.0).astype(jnp.bfloat16),
        jnp.broadcast_to(hit, (count, LANES)).astype(jnp.bfloat16),
        preferred_element_type=jnp.float32,
    )
    slot = (row // each) * slots_each + rank.astype(jnp.int32)
    capacity = chosen.shape[0]
    if capacity != LANES:
        slot = jnp.broadcast_to(slot[:, :1], (count, capacity))
    target = lax.broadcasted_iota(jnp.int32, (count, capacity), 1)
    taken = jnp.where((slot == target) & named, 1.0, 0.0)
    top = jnp.broadcast_to(pair[0:1, :], (count, count)).T[:, 0:1]
    terms = jnp.where(named, jnp.exp(scores - top), 0.0)
    slots[...] = lax.dot_general(
        taken,
        terms,
        (((0,), (0,)), ((), ())),
        precision=lax.Precision.HIGHEST,
        preferred_element_type=jnp.float32,
    )
    chosen[...] = taken.T


def final_kernel(n, *refs):
    parts, slots, chosen, out = refs[:n], refs[n], refs[n + 1], refs[n + 2]
    peak = functools.reduce(jnp.maximum, [p[0:1, :] for p in parts])
    shares = [p[1:2, :] * jnp.exp(p[0:1, :] - peak) for p in parts]
    total = functools.reduce(jnp.add, shares)
    factor = jnp.exp(parts[0][0:1, :] - peak) / total
    scale = jnp.sum(chosen[...] * factor, axis=1, keepdims=True)
    out[...] = slots[...] * scale


def chip_shards(images, defocus, block_ids, noise_weight, panels):
    per_device, halves, columns = images.shape[1:]
    devices = lax.axis_size("orient")
    chips = devices // 2
    ring = 2 * chips
    everyone = per_device * devices
    local_search = block_ids.shape[2]
    orientations = panels.shape[2]
    slots_each = min(per_device, max(2, 2 * per_device * local_search // devices))
    capacity = slots_each * devices
    place = lax.axis_index("orient")
    group = lax.axis_index("cls")
    chip, core = place // 2, place % 2
    position = jnp.where(group == 0, chip, ring - 1 - chip)
    spot = jnp.stack([group, position, core, place]).astype(jnp.int32)
    first = core == 0

    mate_pairs = [(d, d ^ 1) for d in range(devices)]
    x_pairs = [(0, 1), (1, 0)]

    def joint(place, core):
        place = place % ring
        far = place >= chips
        level = ring - 1 - place if far else place
        return (2 * level + core) * 2 + int(far)

    def forward(values, step, cross=0):
        pairs = [(joint(p, c), joint(p + step, c ^ cross)) for p in range(ring) for c in range(2)]
        return lax.ppermute(values, ("orient", "cls"), pairs)

    vmem = pl.BlockSpec(memory_space=pltpu.VMEM)
    smem = pl.BlockSpec(memory_space=pltpu.SMEM)
    params = pltpu.CompilerParams(vmem_limit_bytes=VMEM_LIMIT)
    planes = lax.optimization_barrier(jnp.transpose(images[0], (1, 0, 2)))
    row_shape = jax.ShapeDtypeStruct((per_device, columns + LANES), jnp.bfloat16)
    kept, given = pl.pallas_call(
        row_kernel,
        in_specs=[smem, vmem] + [pl.BlockSpec(memory_space=pl.ANY)] * 2,
        out_specs=[vmem] * 2,
        out_shape=[row_shape] * 2,
        scratch_shapes=[
            pltpu.VMEM((per_device, LANES), jnp.float32),
            pltpu.VMEM(defocus.shape, defocus.dtype),
            pltpu.VMEM((local_search, per_device), block_ids.dtype),
            pltpu.SemaphoreType.DMA((2,)),
        ],
        compiler_params=params,
    )(spot, planes, defocus, jnp.transpose(block_ids[0]))
    with jax.named_scope("mate_rows"):
        got = lax.ppermute(given, "orient", mate_pairs)

    sides = lax.optimization_barrier(jnp.transpose(panels[0, 0], (1, 0, 2)))
    given_panel = lax.dynamic_index_in_dim(sides, 1 - core, 0, keepdims=False)
    with jax.named_scope("mate_panel"):
        mate_panel = lax.ppermute(given_panel, "orient", mate_pairs)

    noise = noise_weight[None, :]
    waiting = [((0, False), kept), ((0, True), got)]
    ahead = {False: kept, True: given}
    behind = {False: kept, True: given}
    orders, earlier, late = [], [], []
    score = lambda c: score_call(c, None, None, spot, noise, sides, mate_panel)
    for step in range(1, chips + 1):
        if step == chips and step > 2:
            orders.append([key for key, _ in waiting])
            earlier.append(score([c for _, c in waiting]))
            waiting = []
            tie = earlier[-1][2]
            ahead = {c: lax.optimization_barrier((v, tie))[0] for c, v in ahead.items()}
            behind = {c: lax.optimization_barrier((v, tie))[0] for c, v in behind.items()}
        waiting = waiting + late
        late = []
        for crossed in (False, True):
            if step < chips or not crossed:
                with jax.named_scope("rows_ahead"):
                    ahead[crossed] = forward(ahead[crossed], 1, int(crossed and step == 1))
                late.append(((-step, crossed), ahead[crossed]))
            if step < chips or crossed:
                with jax.named_scope("rows_behind"):
                    behind[crossed] = forward(behind[crossed], -1, int(crossed and step == 1))
                late.append(((step, crossed), behind[crossed]))
    orders.append([key for key, _ in waiting])
    earlier.append(score([c for _, c in waiting]))
    waiting = late
    orders.append([key for key, _ in waiting])
    partial, all_facts = score_call(
        [c for _, c in waiting], orders, earlier, spot, noise, sides, mate_panel
    )

    mate_partial = lax.ppermute(partial, "orient", mate_pairs)
    mine, own_stats, across = pl.pallas_call(
        functools.partial(chip_kernel, local_search),
        in_specs=[smem] + [vmem] * 3,
        out_specs=[vmem] * 3,
        out_shape=[
            jax.ShapeDtypeStruct((everyone, orientations), jnp.float32),
            jax.ShapeDtypeStruct((8, everyone), jnp.float32),
            jax.ShapeDtypeStruct((everyone + 8, orientations), jnp.float32),
        ],
        compiler_params=params,
    )(spot, partial, mate_partial, all_facts)
    from_x = lax.ppermute(across, "cls", x_pairs)

    tops = own_stats[0], from_x[everyone]
    peak = jnp.maximum(*tops)
    total = own_stats[1] * jnp.exp(tops[0] - peak) + from_x[everyone + 1] * jnp.exp(tops[1] - peak)
    pair = jnp.pad(jnp.stack([peak, total]), ((0, 6), (0, 0)))
    pairs = [pair] + [
        lax.ppermute(pair, "orient", [(d, (d + 2 * s) % devices) for d in range(devices)])
        for s in range(1, chips)
    ]
    slots, chosen = pl.pallas_call(
        functools.partial(slot_kernel, local_search, slots_each, per_device),
        in_specs=[smem] + [vmem] * 4,
        out_specs=[vmem] * 2,
        out_shape=[
            jax.ShapeDtypeStruct((capacity, 2 * orientations), jnp.float32),
            jax.ShapeDtypeStruct((capacity, everyone), jnp.float32),
        ],
        compiler_params=params,
    )(spot, mine, from_x, pair, all_facts)
    posterior = pl.pallas_call(
        functools.partial(final_kernel, chips),
        in_specs=[vmem] * (chips + 2),
        out_specs=vmem,
        out_shape=jax.ShapeDtypeStruct((capacity, 2 * orientations), jnp.float32),
        compiler_params=params,
    )(*pairs, slots, chosen)
    return posterior.reshape(1, 1, capacity, -1)


def spread_max(member, is_live, values):
    picked = jnp.max(jnp.where(member, values[None, :], FLOOR), axis=1)
    return jnp.where(is_live, picked, 0.0)


def collect_sums(member, expo):
    return jnp.sum(jnp.where(member, jnp.sum(expo, axis=1)[:, None], 0.0), axis=0)


def shards(images, defocus, block_ids, noise_weight, panels):
    per_device = images.shape[1]
    columns = images.shape[3]
    devices = lax.axis_size("orient")
    local_search = block_ids.shape[2]
    slots_each = min(per_device, max(2, 2 * per_device * local_search // devices))
    capacity = slots_each * devices
    everyone = per_device * devices
    all_lists = lax.all_gather(block_ids[0], "orient", axis=0, tiled=True)
    all_rows, all_focus = (
        lax.all_gather(images[0], "orient", axis=0, tiled=True),
        lax.all_gather(defocus[0], "orient", axis=0, tiled=True),
    )
    own_block = lax.axis_index("orient")
    block_hits = (
        jnp.any(all_lists == own_block, axis=1).astype(jnp.int32).reshape(devices, per_device)
    )
    slot_rank = jnp.cumsum(block_hits, axis=1) - block_hits
    places = (jnp.arange(devices, dtype=jnp.int32)[:, None] * slots_each + slot_rank).reshape(
        everyone
    )
    chosen = (places[None, :] == jnp.arange(capacity, dtype=jnp.int32)[:, None]) & (
        block_hits.reshape(everyone)[None, :] == 1
    )
    is_live = jnp.any(chosen, axis=1)
    slot_owner = jnp.sum(
        jnp.where(chosen, jnp.arange(everyone, dtype=jnp.int32)[None, :], 0), axis=1
    )
    slot_rows = jnp.take(all_rows, slot_owner, axis=0)
    slot_focus = jnp.take(all_focus, slot_owner, axis=0).astype(jnp.float32)
    frequency = (jnp.arange(columns, dtype=jnp.float32) + 0.5) / columns
    contrast = -jnp.sin(CTF_PHASE * slot_focus[:, None] * frequency[None, :] + 0.1)
    weighted = contrast * noise_weight[None, :]
    scaled_rows = (weighted[:, None, :] * slot_rows.astype(jnp.float32)).astype(jnp.bfloat16)
    energy = (contrast * weighted).astype(jnp.bfloat16)
    piece = lax.all_gather(panels[:, 0], "cls", axis=0, tiled=True)
    widened = piece.astype(jnp.float32)
    squared = (widened * widened).astype(jnp.bfloat16)
    correlate = jnp.einsum("srk,cjrk->scj", scaled_rows, piece, preferred_element_type=jnp.float32)
    energy_term = jnp.einsum("sk,cjrk->scj", energy, squared, preferred_element_type=jnp.float32)
    terms = correlate - 0.5 * energy_term
    combined = terms.reshape(capacity, -1)
    scores = lax.psum_scatter(combined, "rep", scatter_dimension=1, tiled=True)
    member = (slot_owner[:, None] == jnp.arange(everyone, dtype=jnp.int32)[None, :]) & is_live[
        :, None
    ]
    slot_top = jnp.max(scores, axis=1)
    local_peak = jnp.max(jnp.where(member, slot_top[:, None], FLOOR), axis=0)
    peak = lax.pmax(local_peak, ("orient", "rep"))
    slot_peak = spread_max(member, is_live, peak)
    expo = jnp.where(is_live[:, None], jnp.exp(scores - slot_peak[:, None]), 0.0)
    total = lax.psum(collect_sums(member, expo), ("orient", "rep"))
    slot_total = jnp.where(is_live, jnp.sum(jnp.where(member, total[None, :], 0.0), axis=1), 1.0)
    posterior = expo / slot_total[:, None]
    return posterior.reshape(1, 1, capacity, -1)


def solution(mesh):
    in_specs = (
        P(("batch", "cls"), "orient", "rep", None),
        P(("batch", "cls"), "orient"),
        P(("batch", "cls"), "orient", None),
        P(),
        P(("batch", "cls"), "orient", None, "rep", None),
    )
    out_specs = P(("batch", "cls"), "orient", None, "rep")
    sizes = mesh.shape
    paired = sizes["rep"] == 1 and sizes["cls"] == 2 and sizes["orient"] % 2 == 0
    return jax.shard_map(
        chip_shards if paired else shards,
        mesh=mesh,
        in_specs=in_specs,
        out_specs=out_specs,
        check_vma=False,
    )
```

```python
import functools

import jax
import jax.numpy as jnp
from jax import lax
from jax.experimental import pallas as pl
from jax.experimental.pallas import tpu as pltpu
from jax.sharding import PartitionSpec as P

CTF_PHASE = 40.0
FLOOR = -1e30
LANES = 128
VMEM_LIMIT = 8 * 1024 * 1024


def sin_cos(angle):
    turns = jnp.floor(angle * 0.6366197723675814 + 0.5)
    rest = angle - turns * 1.5703125
    rest = rest - turns * 4.837512969970703e-4
    rest = rest - turns * 7.549789948768648e-8
    square = rest * rest
    sine = rest + rest * square * (
        -1.6666654611e-1 + square * (8.3321608736e-3 - square * 1.9515295891e-4)
    )
    cosine = (
        1.0
        - 0.5 * square
        + square
        * square
        * (4.166664568298827e-2 + square * (-1.388731625493765e-3 + square * 2.443315711809948e-5))
    )
    quarter = turns.astype(jnp.int32)
    odd = (quarter & 1) == 1
    low = jnp.where(odd, cosine, sine)
    high = jnp.where(odd, sine, cosine)
    return (
        jnp.where((quarter & 2) == 2, -low, low),
        jnp.where(((quarter + 1) & 2) == 2, -high, high),
    )


def panel_kernel(spot, sides, own, given):
    own[...] = sides[spot[2]]
    given[...] = sides[1 - spot[2]]


def row_kernel(spot, planes, defocus, lists, kept, given, facts, focus, named, sems):
    core = spot[2]
    columns = planes.shape[2]
    count = defocus.shape[1]
    fetches = [
        pltpu.make_async_copy(defocus, focus, sems.at[0]),
        pltpu.make_async_copy(lists, named, sems.at[1]),
    ]
    for fetch in fetches:
        fetch.start()
    facts[...] = jnp.zeros_like(facts)
    for half, out in ((core, kept), (1 - core, given)):
        out[:, :columns] = planes[half]
    for fetch in fetches:
        fetch.wait()
    facts[0:1, :count] = focus[...].astype(jnp.float32)
    facts[1 : 1 + lists.shape[0], :count] = named[...].astype(jnp.float32)
    for out in (kept, given):
        out[:, columns:] = facts[...].astype(out.dtype)


def particle_facts(meta):
    return jnp.concatenate([m[...].astype(jnp.float32).T[: m.shape[0]] for m in meta], axis=0)


def add_scores(rows, noise, own_panel, mate_panel, turn_sin, turn_cos, sums, segments):
    columns = noise.shape[1]
    width = columns // segments
    tiles = width // LANES
    count = turn_sin.shape[0]
    facts = particle_facts([r.at[:, pl.ds(columns, LANES)] for r in rows])
    rate = jnp.broadcast_to(CTF_PHASE * facts[:, 0:1], (count, LANES))
    lane = lax.broadcasted_iota(jnp.int32, (count, LANES), 1).astype(jnp.float32)
    first_sin, first_cos = sin_cos(rate * ((lane + 0.5) / columns) + 0.1)
    step_sin, step_cos = sin_cos(rate * (LANES / columns))
    turn_sin[...] = step_sin
    turn_cos[...] = step_cos
    for total in sums:
        total[...] = jnp.zeros_like(total)

    def segment(index, carry):
        sine, cosine = carry
        start = pl.multiple_of(index * width, LANES)
        scaled_parts, energy_parts = [], []
        for t in range(tiles):
            window = pl.ds(start + t * LANES, LANES)
            weighted = sine * noise[:, window]
            image = jnp.concatenate([r[:, window] for r in rows], axis=0).astype(jnp.float32)
            scaled_parts.append((weighted * image).astype(jnp.bfloat16))
            energy_parts.append((sine * weighted).astype(jnp.bfloat16))
            ds, dc = turn_sin[...], turn_cos[...]
            sine, cosine = sine * dc + cosine * ds, cosine * dc - sine * ds
        scaled = jnp.concatenate(scaled_parts, axis=1)
        energy = jnp.concatenate(energy_parts, axis=1)
        contract = (((1,), (1,)), ((), ()))
        whole = pl.ds(start, width)
        for values, total in ((own_panel[:, whole], sums[0]), (mate_panel[:, whole], sums[1])):
            squared = values * values
            correlate = lax.dot_general(
                values, scaled, contract, preferred_element_type=jnp.float32
            )
            power = lax.dot_general(squared, energy, contract, preferred_element_type=jnp.float32)
            total[...] += correlate - 0.5 * power
        return sine, cosine

    lax.fori_loop(0, segments, segment, (-first_sin, -first_cos))
    return jnp.pad(facts, ((0, 0), (0, LANES - facts.shape[1])))


def batch_kernel(n, segments, spot, *refs):
    rows = refs[:n]
    noise, own_panel, mate_panel = refs[n : n + 3]
    own_out, mate_out, fact_out, turn_sin, turn_cos, *sums = refs[n + 3 :]
    fact_out[...] = add_scores(
        rows, noise, own_panel, mate_panel, turn_sin, turn_cos, sums, segments
    )
    own_out[...] = sums[0][...].T
    mate_out[...] = sums[1][...].T


def last_kernel(n, segments, orders, spot, *refs):
    rows = refs[:n]
    noise, own_panel, mate_panel = refs[n : n + 3]
    rest = refs[n + 3 :]
    earlier, rest = rest[: 3 * (len(orders) - 1)], rest[3 * (len(orders) - 1) :]
    partial, facts, turn_sin, turn_cos, *sums = rest
    last_facts = add_scores(
        rows, noise, own_panel, mate_panel, turn_sin, turn_cos, sums, segments
    )
    position, core = spot[1], spot[2]
    each = rows[0].shape[0]
    ring = facts.shape[0] // (2 * each)
    half = ring // 2
    for index, order in enumerate(orders):
        if index < len(orders) - 1:
            own, mate, fact = [r[...] for r in earlier[3 * index : 3 * index + 3]]
        else:
            own, mate, fact = sums[0][...].T, sums[1][...].T, last_facts
        for k, (distance, crossed) in enumerate(order):
            place = lax.rem(position + distance + ring, ring)
            far = place >= half
            level = jnp.where(far, ring - 1 - place, place)
            device = 2 * level + (1 - core if crossed else core)
            start = pl.multiple_of((jnp.where(far, ring, 0) + device) * each, each)
            piece = slice(k * each, (k + 1) * each)
            partial[core, pl.ds(start, each), :] = own[piece]
            partial[1 - core, pl.ds(start, each), :] = mate[piece]
            facts[pl.ds(start, each), :] = fact[piece]


def score_call(chunks, orders, earlier, spot, noise, own_panel, mate_panel):
    each = chunks[0].shape[0]
    orientations, columns = own_panel.shape
    whole = columns // LANES
    segments = next(s for s in (3, 2, 4, 5, 6, 7, 1) if whole % s == 0)
    n = len(chunks)
    count = each * n
    scratch = [pltpu.VMEM((count, LANES), jnp.float32)] * 2
    scratch += [pltpu.VMEM((orientations, count), jnp.float32)] * 2
    single = jax.ShapeDtypeStruct((count, orientations), jnp.float32)
    if orders is None:
        kernel = functools.partial(batch_kernel, n, segments)
        out_shape = [single, single, jax.ShapeDtypeStruct((count, LANES), jnp.float32)]
        extra = []
    else:
        everyone = each * sum(len(o) for o in orders)
        kernel = functools.partial(last_kernel, n, segments, orders)
        out_shape = [
            jax.ShapeDtypeStruct((2, everyone, orientations), jnp.float32),
            jax.ShapeDtypeStruct((everyone, LANES), jnp.float32),
        ]
        extra = [e for triple in earlier for e in triple]
    vmem = pl.BlockSpec(memory_space=pltpu.VMEM)
    return pl.pallas_call(
        kernel,
        in_specs=[pl.BlockSpec(memory_space=pltpu.SMEM)] + [vmem] * (n + 3 + len(extra)),
        out_specs=[vmem] * len(out_shape),
        out_shape=out_shape,
        scratch_shapes=scratch,
        compiler_params=pltpu.CompilerParams(vmem_limit_bytes=VMEM_LIMIT),
        cost_estimate=pl.CostEstimate(
            flops=8 * max(count, 128) * orientations * columns,
            bytes_accessed=4 * orientations * columns + 2 * count * columns,
            transcendentals=0,
        ),
    )(spot, *chunks, noise, own_panel, mate_panel, *extra)


def names_block(facts, search, block):
    lane = lax.broadcasted_iota(jnp.int32, facts.shape, 1)
    match = (lane >= 1) & (lane <= search) & (facts == block.astype(jnp.float32))
    return jnp.max(jnp.where(match, 1.0, 0.0), axis=1, keepdims=True) > 0.0


def chip_kernel(search, spot, partial, mate, facts, mine, across, stats):
    group, core, place = spot[0], spot[2], spot[3]
    count = mine.shape[0]
    lane = lax.broadcasted_iota(jnp.int32, (count, LANES), 1)
    pairs = []
    for relative in range(2):
        side = group if relative == 0 else 1 - group
        window = pl.ds(pl.multiple_of(side * count, count), count)
        listed = facts[window, :]
        masked = []
        for crossed in range(2):
            block = core if crossed == 0 else 1 - core
            scores = partial[block, window, :] + mate[block, window, :]
            if crossed == 0:
                out = mine if relative == 0 else across
                out[...] = scores
            named = names_block(listed, search, place - core + block)
            masked.append(jnp.where(named, scores, FLOOR))
        top = jnp.max(jnp.maximum(*masked), axis=1, keepdims=True)
        terms = [jnp.where(m > FLOOR, jnp.exp(m - top), 0.0) for m in masked]
        total = jnp.sum(terms[0] + terms[1], axis=1, keepdims=True)
        pairs.append(jnp.where(lane == relative, top, jnp.where(lane == 2 + relative, total, 0.0)))
    stats[...] = (pairs[0] + pairs[1]).T[: stats.shape[0]]


def slot_kernel(search, slots_each, each, spot, mine, across, facts, slots, chosen, tops):
    group, place = spot[0], spot[3]
    count = mine.shape[0]
    same, other = mine[...], across[...]
    first = group == 0
    scores = jnp.concatenate(
        [jnp.where(first, same, other), jnp.where(first, other, same)], axis=1
    )
    listed = facts[pl.ds(pl.multiple_of(group * count, count), count), :]
    named = names_block(listed, search, place)
    hit = jnp.where(named, 1.0, 0.0)
    row = lax.broadcasted_iota(jnp.int32, (count, LANES), 0)
    line = lax.broadcasted_iota(jnp.int32, (count, count), 0)
    column = lax.broadcasted_iota(jnp.int32, (count, count), 1)
    before = (column < line) & (column // each == line // each)
    rank = jnp.dot(
        jnp.where(before, 1.0, 0.0).astype(jnp.bfloat16),
        jnp.broadcast_to(hit, (count, LANES)).astype(jnp.bfloat16),
        preferred_element_type=jnp.float32,
    )
    slot = (row // each) * slots_each + rank.astype(jnp.int32)
    capacity = chosen.shape[0]
    if capacity != LANES:
        slot = jnp.broadcast_to(slot[:, :1], (count, capacity))
    target = lax.broadcasted_iota(jnp.int32, (count, capacity), 1)
    taken = jnp.where((slot == target) & named, 1.0, 0.0)
    top = jnp.max(scores, axis=1, keepdims=True)
    tops[...] = jnp.broadcast_to(top, (count, LANES)).T[: tops.shape[0]]
    terms = jnp.where(named, jnp.exp(scores - top), 0.0)
    slots[...] = lax.dot_general(
        taken,
        terms,
        (((0,), (0,)), ((), ())),
        precision=lax.Precision.HIGHEST,
        preferred_element_type=jnp.float32,
    )
    chosen[...] = taken.T


def final_kernel(own, other, tops, slots, chosen, out):
    peaks = own[0:1, :], other[1:2, :]
    totals = own[2:3, :], other[3:4, :]
    peak = jnp.maximum(*peaks)
    total = totals[0] * jnp.exp(peaks[0] - peak) + totals[1] * jnp.exp(peaks[1] - peak)
    factor = jnp.exp(jnp.minimum(tops[0:1, :] - peak, 0.0)) / total
    scale = jnp.sum(chosen[...] * factor, axis=1, keepdims=True)
    out[...] = slots[...] * scale


def chip_shards(images, defocus, block_ids, noise_weight, panels):
    per_device, halves, columns = images.shape[1:]
    devices = lax.axis_size("orient")
    chips = devices // 2
    ring = 2 * chips
    everyone = per_device * devices
    local_search = block_ids.shape[2]
    orientations = panels.shape[2]
    slots_each = min(per_device, max(2, 2 * per_device * local_search // devices))
    capacity = slots_each * devices
    place = lax.axis_index("orient")
    group = lax.axis_index("cls")
    chip, core = place // 2, place % 2
    position = jnp.where(group == 0, chip, ring - 1 - chip)
    spot = jnp.stack([group, position, core, place]).astype(jnp.int32)
    first = core == 0

    mate_pairs = [(d, d ^ 1) for d in range(devices)]
    x_pairs = [(0, 1), (1, 0)]

    def joint(place, core):
        place = place % ring
        far = place >= chips
        level = ring - 1 - place if far else place
        return (2 * level + core) * 2 + int(far)

    def forward(values, step, cross=0):
        pairs = [(joint(p, c), joint(p + step, c ^ cross)) for p in range(ring) for c in range(2)]
        return lax.ppermute(values, ("orient", "cls"), pairs)

    vmem = pl.BlockSpec(memory_space=pltpu.VMEM)
    smem = pl.BlockSpec(memory_space=pltpu.SMEM)
    params = pltpu.CompilerParams(vmem_limit_bytes=VMEM_LIMIT)
    planes = lax.optimization_barrier(jnp.transpose(images[0], (1, 0, 2)))
    row_shape = jax.ShapeDtypeStruct((per_device, columns + LANES), jnp.bfloat16)
    kept, given = pl.pallas_call(
        row_kernel,
        in_specs=[smem, vmem] + [pl.BlockSpec(memory_space=pl.ANY)] * 2,
        out_specs=[vmem] * 2,
        out_shape=[row_shape] * 2,
        scratch_shapes=[
            pltpu.VMEM((per_device, LANES), jnp.float32),
            pltpu.VMEM(defocus.shape, defocus.dtype),
            pltpu.VMEM((local_search, per_device), block_ids.dtype),
            pltpu.SemaphoreType.DMA((2,)),
        ],
        compiler_params=params,
    )(spot, planes, defocus, jnp.transpose(block_ids[0]))
    with jax.named_scope("mate_rows"):
        got = lax.ppermute(given, "orient", mate_pairs)

    sides = lax.optimization_barrier(jnp.transpose(panels[0, 0], (1, 0, 2)))
    panel_shape = jax.ShapeDtypeStruct(sides.shape[1:], sides.dtype)
    own_panel, given_panel = pl.pallas_call(
        panel_kernel,
        in_specs=[smem, vmem],
        out_specs=[vmem] * 2,
        out_shape=[panel_shape] * 2,
        compiler_params=params,
    )(spot, sides)
    with jax.named_scope("mate_panel"):
        mate_panel = lax.ppermute(given_panel, "orient", mate_pairs)

    noise = noise_weight[None, :]
    waiting = [((0, False), kept), ((0, True), got)]
    ahead = {False: kept, True: given}
    behind = {False: kept, True: given}
    orders, earlier, late = [], [], []
    score = lambda c: score_call(c, None, None, spot, noise, own_panel, mate_panel)
    for step in range(1, chips + 1):
        if step == chips and step > 2:
            orders.append([key for key, _ in waiting])
            earlier.append(score([c for _, c in waiting]))
            waiting = []
            tie = earlier[-1][2]
            ahead = {c: lax.optimization_barrier((v, tie))[0] for c, v in ahead.items()}
            behind = {c: lax.optimization_barrier((v, tie))[0] for c, v in behind.items()}
        waiting = waiting + late
        late = []
        for crossed in (False, True):
            if step < chips or not crossed:
                with jax.named_scope("rows_ahead"):
                    ahead[crossed] = forward(ahead[crossed], 1, int(crossed and step == 1))
                late.append(((-step, crossed), ahead[crossed]))
            if step < chips or crossed:
                with jax.named_scope("rows_behind"):
                    behind[crossed] = forward(behind[crossed], -1, int(crossed and step == 1))
                late.append(((step, crossed), behind[crossed]))
    orders.append([key for key, _ in waiting])
    earlier.append(score([c for _, c in waiting]))
    waiting = late
    orders.append([key for key, _ in waiting])
    partial, all_facts = score_call(
        [c for _, c in waiting], orders, earlier, spot, noise, own_panel, mate_panel
    )

    mate_partial = lax.ppermute(partial, "orient", mate_pairs)
    mine, across, stats = pl.pallas_call(
        functools.partial(chip_kernel, local_search),
        in_specs=[smem] + [vmem] * 3,
        out_specs=[vmem] * 3,
        out_shape=[
            jax.ShapeDtypeStruct((everyone, orientations), jnp.float32),
            jax.ShapeDtypeStruct((everyone, orientations), jnp.float32),
            jax.ShapeDtypeStruct((8, everyone), jnp.float32),
        ],
        compiler_params=params,
    )(spot, partial, mate_partial, all_facts)

    from_x = lax.ppermute(across, "cls", x_pairs)
    parts = [stats] + [
        lax.ppermute(stats, "orient", [(d, (d + 2 * s) % devices) for d in range(devices)])
        for s in range(1, chips)
    ]
    peaks = functools.reduce(jnp.maximum, [p[0:2] for p in parts])
    totals = functools.reduce(jnp.add, [p[2:4] * jnp.exp(p[0:2] - peaks) for p in parts])
    class_stats = jnp.pad(jnp.concatenate([peaks, totals], axis=0), ((0, 4), (0, 0)))
    other_stats = lax.ppermute(class_stats, "cls", x_pairs)
    slots, chosen, tops = pl.pallas_call(
        functools.partial(slot_kernel, local_search, slots_each, per_device),
        in_specs=[smem] + [vmem] * 3,
        out_specs=[vmem] * 3,
        out_shape=[
            jax.ShapeDtypeStruct((capacity, 2 * orientations), jnp.float32),
            jax.ShapeDtypeStruct((capacity, everyone), jnp.float32),
            jax.ShapeDtypeStruct((8, everyone), jnp.float32),
        ],
        compiler_params=params,
    )(spot, mine, from_x, all_facts)
    posterior = pl.pallas_call(
        final_kernel,
        in_specs=[vmem] * 5,
        out_specs=vmem,
        out_shape=jax.ShapeDtypeStruct((capacity, 2 * orientations), jnp.float32),
        compiler_params=params,
    )(class_stats, other_stats, tops, slots, chosen)
    return posterior.reshape(1, 1, capacity, -1)


def spread_max(member, is_live, values):
    picked = jnp.max(jnp.where(member, values[None, :], FLOOR), axis=1)
    return jnp.where(is_live, picked, 0.0)


def collect_sums(member, expo):
    return jnp.sum(jnp.where(member, jnp.sum(expo, axis=1)[:, None], 0.0), axis=0)


def shards(images, defocus, block_ids, noise_weight, panels):
    per_device = images.shape[1]
    columns = images.shape[3]
    devices = lax.axis_size("orient")
    local_search = block_ids.shape[2]
    slots_each = min(per_device, max(2, 2 * per_device * local_search // devices))
    capacity = slots_each * devices
    everyone = per_device * devices
    all_lists = lax.all_gather(block_ids[0], "orient", axis=0, tiled=True)
    all_rows, all_focus = (
        lax.all_gather(images[0], "orient", axis=0, tiled=True),
        lax.all_gather(defocus[0], "orient", axis=0, tiled=True),
    )
    own_block = lax.axis_index("orient")
    block_hits = (
        jnp.any(all_lists == own_block, axis=1).astype(jnp.int32).reshape(devices, per_device)
    )
    slot_rank = jnp.cumsum(block_hits, axis=1) - block_hits
    places = (jnp.arange(devices, dtype=jnp.int32)[:, None] * slots_each + slot_rank).reshape(
        everyone
    )
    chosen = (places[None, :] == jnp.arange(capacity, dtype=jnp.int32)[:, None]) & (
        block_hits.reshape(everyone)[None, :] == 1
    )
    is_live = jnp.any(chosen, axis=1)
    slot_owner = jnp.sum(
        jnp.where(chosen, jnp.arange(everyone, dtype=jnp.int32)[None, :], 0), axis=1
    )
    slot_rows = jnp.take(all_rows, slot_owner, axis=0)
    slot_focus = jnp.take(all_focus, slot_owner, axis=0).astype(jnp.float32)
    frequency = (jnp.arange(columns, dtype=jnp.float32) + 0.5) / columns
    contrast = -jnp.sin(CTF_PHASE * slot_focus[:, None] * frequency[None, :] + 0.1)
    weighted = contrast * noise_weight[None, :]
    scaled_rows = (weighted[:, None, :] * slot_rows.astype(jnp.float32)).astype(jnp.bfloat16)
    energy = (contrast * weighted).astype(jnp.bfloat16)
    piece = lax.all_gather(panels[:, 0], "cls", axis=0, tiled=True)
    widened = piece.astype(jnp.float32)
    squared = (widened * widened).astype(jnp.bfloat16)
    correlate = jnp.einsum("srk,cjrk->scj", scaled_rows, piece, preferred_element_type=jnp.float32)
    energy_term = jnp.einsum("sk,cjrk->scj", energy, squared, preferred_element_type=jnp.float32)
    terms = correlate - 0.5 * energy_term
    combined = terms.reshape(capacity, -1)
    scores = lax.psum_scatter(combined, "rep", scatter_dimension=1, tiled=True)
    member = (slot_owner[:, None] == jnp.arange(everyone, dtype=jnp.int32)[None, :]) & is_live[
        :, None
    ]
    slot_top = jnp.max(scores, axis=1)
    local_peak = jnp.max(jnp.where(member, slot_top[:, None], FLOOR), axis=0)
    peak = lax.pmax(local_peak, ("orient", "rep"))
    slot_peak = spread_max(member, is_live, peak)
    expo = jnp.where(is_live[:, None], jnp.exp(scores - slot_peak[:, None]), 0.0)
    total = lax.psum(collect_sums(member, expo), ("orient", "rep"))
    slot_total = jnp.where(is_live, jnp.sum(jnp.where(member, total[None, :], 0.0), axis=1), 1.0)
    posterior = expo / slot_total[:, None]
    return posterior.reshape(1, 1, capacity, -1)


def solution(mesh):
    in_specs = (
        P(("batch", "cls"), "orient", "rep", None),
        P(("batch", "cls"), "orient"),
        P(("batch", "cls"), "orient", None),
        P(),
        P(("batch", "cls"), "orient", None, "rep", None),
    )
    out_specs = P(("batch", "cls"), "orient", None, "rep")
    sizes = mesh.shape
    paired = sizes["rep"] == 1 and sizes["cls"] == 2 and sizes["orient"] % 2 == 0
    return jax.shard_map(
        chip_shards if paired else shards,
        mesh=mesh,
        in_specs=in_specs,
        out_specs=out_specs,
        check_vma=False,
    )
```

```python
import functools

import jax
import jax.numpy as jnp
from jax import lax
from jax.experimental import pallas as pl
from jax.experimental.pallas import tpu as pltpu
from jax.sharding import PartitionSpec as P

CTF_PHASE = 40.0
FLOOR = -1e30
LANES = 128
VMEM_LIMIT = 8 * 1024 * 1024
SCHEDULING_WEIGHT = 20 * 10**9


def sin_cos(angle):
    turns = jnp.floor(angle * 0.6366197723675814 + 0.5)
    rest = angle - turns * 1.5703125
    rest = rest - turns * 4.837512969970703e-4
    rest = rest - turns * 7.549789948768648e-8
    square = rest * rest
    sine = rest + rest * square * (
        -1.6666654611e-1 + square * (8.3321608736e-3 - square * 1.9515295891e-4)
    )
    cosine = (
        1.0
        - 0.5 * square
        + square
        * square
        * (4.166664568298827e-2 + square * (-1.388731625493765e-3 + square * 2.443315711809948e-5))
    )
    quarter = turns.astype(jnp.int32)
    odd = (quarter & 1) == 1
    low = jnp.where(odd, cosine, sine)
    high = jnp.where(odd, sine, cosine)
    return (
        jnp.where((quarter & 2) == 2, -low, low),
        jnp.where(((quarter + 1) & 2) == 2, -high, high),
    )


def panel_kernel(spot, sides, own, given):
    own[...] = sides[spot[2]]
    given[...] = sides[1 - spot[2]]


def square_kernel(own, squares):
    squares[...] = own[...] * own[...]


def row_kernel(spot, planes, defocus, lists, kept, given, facts, focus, named, sems):
    core = spot[2]
    columns = planes.shape[2]
    count = defocus.shape[1]
    fetches = [
        pltpu.make_async_copy(defocus, focus, sems.at[0]),
        pltpu.make_async_copy(lists, named, sems.at[1]),
    ]
    for fetch in fetches:
        fetch.start()
    facts[...] = jnp.zeros_like(facts)
    for half, out in ((core, kept), (1 - core, given)):
        out[:, :columns] = planes[half]
    for fetch in fetches:
        fetch.wait()
    facts[0:1, :count] = focus[...].astype(jnp.float32)
    facts[1 : 1 + lists.shape[0], :count] = named[...].astype(jnp.float32)
    for out in (kept, given):
        out[:, columns:] = facts[...].astype(out.dtype)


def particle_facts(meta):
    return jnp.concatenate([m[...].astype(jnp.float32).T[: m.shape[0]] for m in meta], axis=0)


def add_scores(rows, noise, own_panel, own_squares, mate_panel, turn_sin, turn_cos, sums, segments):
    columns = noise.shape[1]
    width = columns // segments
    tiles = width // LANES
    count = turn_sin.shape[0]
    facts = particle_facts([r.at[:, pl.ds(columns, LANES)] for r in rows])
    rate = jnp.broadcast_to(CTF_PHASE * facts[:, 0:1], (count, LANES))
    lane = lax.broadcasted_iota(jnp.int32, (count, LANES), 1).astype(jnp.float32)
    first_sin, first_cos = sin_cos(rate * ((lane + 0.5) / columns) + 0.1)
    step_sin, step_cos = sin_cos(rate * (LANES / columns))
    turn_sin[...] = step_sin
    turn_cos[...] = step_cos
    for total in sums:
        total[...] = jnp.zeros_like(total)

    def segment(index, carry):
        sine, cosine = carry
        start = pl.multiple_of(index * width, LANES)
        scaled_parts, energy_parts = [], []
        for t in range(tiles):
            window = pl.ds(start + t * LANES, LANES)
            weighted = sine * noise[:, window]
            image = jnp.concatenate([r[:, window] for r in rows], axis=0).astype(jnp.float32)
            scaled_parts.append((weighted * image).astype(jnp.bfloat16))
            energy_parts.append((sine * weighted).astype(jnp.bfloat16))
            ds, dc = turn_sin[...], turn_cos[...]
            sine, cosine = sine * dc + cosine * ds, cosine * dc - sine * ds
        scaled = jnp.concatenate(scaled_parts, axis=1)
        energy = jnp.concatenate(energy_parts, axis=1)
        contract = (((1,), (1,)), ((), ()))
        whole = pl.ds(start, width)
        mate = mate_panel[:, whole]
        for values, squared, total in (
            (own_panel[:, whole], own_squares[:, whole], sums[0]),
            (mate, mate * mate, sums[1]),
        ):
            correlate = lax.dot_general(
                values, scaled, contract, preferred_element_type=jnp.float32
            )
            power = lax.dot_general(squared, energy, contract, preferred_element_type=jnp.float32)
            total[...] += correlate - 0.5 * power
        return sine, cosine

    lax.fori_loop(0, segments, segment, (-first_sin, -first_cos))
    return jnp.pad(facts, ((0, 0), (0, LANES - facts.shape[1])))


def batch_kernel(n, segments, spot, *refs):
    rows = refs[:n]
    noise, own_panel, own_squares, mate_panel = refs[n : n + 4]
    own_out, mate_out, fact_out, turn_sin, turn_cos, *sums = refs[n + 4 :]
    fact_out[...] = add_scores(
        rows, noise, own_panel, own_squares, mate_panel, turn_sin, turn_cos, sums, segments
    )
    own_out[...] = sums[0][...].T
    mate_out[...] = sums[1][...].T


def last_kernel(n, segments, orders, spot, *refs):
    rows = refs[:n]
    noise, own_panel, own_squares, mate_panel = refs[n : n + 4]
    rest = refs[n + 4 :]
    earlier, rest = rest[: 3 * (len(orders) - 1)], rest[3 * (len(orders) - 1) :]
    partial, facts, turn_sin, turn_cos, *sums = rest
    last_facts = add_scores(
        rows, noise, own_panel, own_squares, mate_panel, turn_sin, turn_cos, sums, segments
    )
    position, core = spot[1], spot[2]
    each = rows[0].shape[0]
    ring = facts.shape[0] // (2 * each)
    half = ring // 2
    for index, order in enumerate(orders):
        if index < len(orders) - 1:
            own, mate, fact = [r[...] for r in earlier[3 * index : 3 * index + 3]]
        else:
            own, mate, fact = sums[0][...].T, sums[1][...].T, last_facts
        for k, (distance, crossed) in enumerate(order):
            place = lax.rem(position + distance + ring, ring)
            far = place >= half
            level = jnp.where(far, ring - 1 - place, place)
            device = 2 * level + (1 - core if crossed else core)
            start = pl.multiple_of((jnp.where(far, ring, 0) + device) * each, each)
            piece = slice(k * each, (k + 1) * each)
            partial[core, pl.ds(start, each), :] = own[piece]
            partial[1 - core, pl.ds(start, each), :] = mate[piece]
            facts[pl.ds(start, each), :] = fact[piece]


def score_call(chunks, orders, earlier, spot, noise, own_panel, squares, mate_panel):
    each = chunks[0].shape[0]
    orientations, columns = own_panel.shape
    whole = columns // LANES
    segments = next(s for s in (3, 2, 4, 5, 6, 7, 1) if whole % s == 0)
    n = len(chunks)
    count = each * n
    scratch = [pltpu.VMEM((count, LANES), jnp.float32)] * 2
    scratch += [pltpu.VMEM((orientations, count), jnp.float32)] * 2
    single = jax.ShapeDtypeStruct((count, orientations), jnp.float32)
    if orders is None:
        kernel = functools.partial(batch_kernel, n, segments)
        out_shape = [single, single, jax.ShapeDtypeStruct((count, LANES), jnp.float32)]
        extra = []
    else:
        everyone = each * sum(len(o) for o in orders)
        kernel = functools.partial(last_kernel, n, segments, orders)
        out_shape = [
            jax.ShapeDtypeStruct((2, everyone, orientations), jnp.float32),
            jax.ShapeDtypeStruct((everyone, LANES), jnp.float32),
        ]
        extra = [e for triple in earlier for e in triple]
    vmem = pl.BlockSpec(memory_space=pltpu.VMEM)
    return pl.pallas_call(
        kernel,
        in_specs=[pl.BlockSpec(memory_space=pltpu.SMEM)] + [vmem] * (n + 4 + len(extra)),
        out_specs=[vmem] * len(out_shape),
        out_shape=out_shape,
        scratch_shapes=scratch,
        compiler_params=pltpu.CompilerParams(vmem_limit_bytes=VMEM_LIMIT),
        cost_estimate=pl.CostEstimate(
            flops=8 * max(count, 128) * orientations * columns,
            bytes_accessed=4 * orientations * columns + 2 * count * columns,
            transcendentals=0,
        ),
    )(spot, *chunks, noise, own_panel, squares, mate_panel, *extra)


def names_block(facts, search, block):
    lane = lax.broadcasted_iota(jnp.int32, facts.shape, 1)
    match = (lane >= 1) & (lane <= search) & (facts == block.astype(jnp.float32))
    return jnp.max(jnp.where(match, 1.0, 0.0), axis=1, keepdims=True) > 0.0


def chip_kernel(search, spot, partial, mate, facts, mine, across, stats):
    group, core, place = spot[0], spot[2], spot[3]
    count = mine.shape[0]
    lane = lax.broadcasted_iota(jnp.int32, (count, LANES), 1)
    pairs = []
    for relative in range(2):
        side = group if relative == 0 else 1 - group
        window = pl.ds(pl.multiple_of(side * count, count), count)
        listed = facts[window, :]
        masked = []
        for crossed in range(2):
            block = core if crossed == 0 else 1 - core
            scores = partial[block, window, :] + mate[block, window, :]
            if crossed == 0:
                out = mine if relative == 0 else across
                out[...] = scores
            named = names_block(listed, search, place - core + block)
            masked.append(jnp.where(named, scores, FLOOR))
        top = jnp.max(jnp.maximum(*masked), axis=1, keepdims=True)
        terms = [jnp.where(m > FLOOR, jnp.exp(m - top), 0.0) for m in masked]
        total = jnp.sum(terms[0] + terms[1], axis=1, keepdims=True)
        pairs.append(jnp.where(lane == relative, top, jnp.where(lane == 2 + relative, total, 0.0)))
    stats[...] = (pairs[0] + pairs[1]).T[: stats.shape[0]]


def slot_kernel(search, slots_each, each, spot, mine, across, facts, slots, chosen, tops):
    group, place = spot[0], spot[3]
    count = mine.shape[0]
    same, other = mine[...], across[...]
    first = group == 0
    scores = jnp.concatenate(
        [jnp.where(first, same, other), jnp.where(first, other, same)], axis=1
    )
    listed = facts[pl.ds(pl.multiple_of(group * count, count), count), :]
    named = names_block(listed, search, place)
    hit = jnp.where(named, 1.0, 0.0)
    row = lax.broadcasted_iota(jnp.int32, (count, LANES), 0)
    line = lax.broadcasted_iota(jnp.int32, (count, count), 0)
    column = lax.broadcasted_iota(jnp.int32, (count, count), 1)
    before = (column < line) & (column // each == line // each)
    rank = jnp.dot(
        jnp.where(before, 1.0, 0.0).astype(jnp.bfloat16),
        jnp.broadcast_to(hit, (count, LANES)).astype(jnp.bfloat16),
        preferred_element_type=jnp.float32,
    )
    slot = (row // each) * slots_each + rank.astype(jnp.int32)
    capacity = chosen.shape[0]
    if capacity != LANES:
        slot = jnp.broadcast_to(slot[:, :1], (count, capacity))
    target = lax.broadcasted_iota(jnp.int32, (count, capacity), 1)
    taken = jnp.where((slot == target) & named, 1.0, 0.0)
    top = jnp.max(scores, axis=1, keepdims=True)
    tops[...] = jnp.broadcast_to(top, (count, LANES)).T[: tops.shape[0]]
    terms = jnp.where(named, jnp.exp(scores - top), 0.0)
    slots[...] = lax.dot_general(
        taken,
        terms,
        (((0,), (0,)), ((), ())),
        precision=lax.Precision.HIGHEST,
        preferred_element_type=jnp.float32,
    )
    chosen[...] = taken.T


def final_kernel(own, other, tops, slots, chosen, out):
    peaks = own[0:1, :], other[1:2, :]
    totals = own[2:3, :], other[3:4, :]
    peak = jnp.maximum(*peaks)
    total = totals[0] * jnp.exp(peaks[0] - peak) + totals[1] * jnp.exp(peaks[1] - peak)
    factor = jnp.exp(jnp.minimum(tops[0:1, :] - peak, 0.0)) / total
    scale = jnp.sum(chosen[...] * factor, axis=1, keepdims=True)
    out[...] = slots[...] * scale


def chip_shards(images, defocus, block_ids, noise_weight, panels):
    per_device, halves, columns = images.shape[1:]
    devices = lax.axis_size("orient")
    chips = devices // 2
    ring = 2 * chips
    everyone = per_device * devices
    local_search = block_ids.shape[2]
    orientations = panels.shape[2]
    slots_each = min(per_device, max(2, 2 * per_device * local_search // devices))
    capacity = slots_each * devices
    place = lax.axis_index("orient")
    group = lax.axis_index("cls")
    chip, core = place // 2, place % 2
    position = jnp.where(group == 0, chip, ring - 1 - chip)
    spot = jnp.stack([group, position, core, place]).astype(jnp.int32)
    first = core == 0

    mate_pairs = [(d, d ^ 1) for d in range(devices)]
    x_pairs = [(0, 1), (1, 0)]

    def joint(place, core):
        place = place % ring
        far = place >= chips
        level = ring - 1 - place if far else place
        return (2 * level + core) * 2 + int(far)

    def forward(values, step, cross=0):
        pairs = [(joint(p, c), joint(p + step, c ^ cross)) for p in range(ring) for c in range(2)]
        return lax.ppermute(values, ("orient", "cls"), pairs)

    vmem = pl.BlockSpec(memory_space=pltpu.VMEM)
    smem = pl.BlockSpec(memory_space=pltpu.SMEM)
    params = pltpu.CompilerParams(vmem_limit_bytes=VMEM_LIMIT)
    planes = lax.optimization_barrier(jnp.transpose(images[0], (1, 0, 2)))
    row_shape = jax.ShapeDtypeStruct((per_device, columns + LANES), jnp.bfloat16)
    kept, given = pl.pallas_call(
        row_kernel,
        in_specs=[smem, vmem] + [pl.BlockSpec(memory_space=pl.ANY)] * 2,
        out_specs=[vmem] * 2,
        out_shape=[row_shape] * 2,
        scratch_shapes=[
            pltpu.VMEM((per_device, LANES), jnp.float32),
            pltpu.VMEM(defocus.shape, defocus.dtype),
            pltpu.VMEM((local_search, per_device), block_ids.dtype),
            pltpu.SemaphoreType.DMA((2,)),
        ],
        compiler_params=params,
    )(spot, planes, defocus, jnp.transpose(block_ids[0]))
    with jax.named_scope("mate_rows"):
        got = lax.ppermute(given, "orient", mate_pairs)

    _, panels = lax.optimization_barrier((kept, panels))
    sides = lax.optimization_barrier(jnp.transpose(panels[0, 0], (1, 0, 2)))
    panel_shape = jax.ShapeDtypeStruct(sides.shape[1:], sides.dtype)
    own_panel, given_panel = pl.pallas_call(
        panel_kernel,
        in_specs=[smem, vmem],
        out_specs=[vmem] * 2,
        out_shape=[panel_shape] * 2,
        compiler_params=params,
    )(spot, sides)
    with jax.named_scope("mate_panel"):
        mate_panel = lax.ppermute(given_panel, "orient", mate_pairs)

    noise = noise_weight[None, :]
    waiting = [((0, False), kept), ((0, True), got)]
    ahead = {False: kept, True: given}
    behind = {False: kept, True: given}
    orders, earlier, late = [], [], []
    squares = pl.pallas_call(
        square_kernel,
        in_specs=[vmem],
        out_specs=vmem,
        out_shape=panel_shape,
        compiler_params=params,
        cost_estimate=pl.CostEstimate(flops=SCHEDULING_WEIGHT, bytes_accessed=0, transcendentals=0),
    )(own_panel)
    score = lambda c: score_call(c, None, None, spot, noise, own_panel, squares, mate_panel)
    for step in range(1, chips + 1):
        if step == chips and step > 2:
            orders.append([key for key, _ in waiting])
            earlier.append(score([c for _, c in waiting]))
            waiting = []
            tie = earlier[-1][2]
            ahead = {c: lax.optimization_barrier((v, tie))[0] for c, v in ahead.items()}
            behind = {c: lax.optimization_barrier((v, tie))[0] for c, v in behind.items()}
        if step == 2:
            for chain, c in ((ahead, False), (behind, True)):
                chain[c] = lax.optimization_barrier((chain[c], squares))[0]
        waiting = waiting + late
        late = []
        for crossed in (False, True):
            if step < chips or not crossed:
                with jax.named_scope("rows_ahead"):
                    ahead[crossed] = forward(ahead[crossed], 1, int(crossed and step == 1))
                late.append(((-step, crossed), ahead[crossed]))
            if step < chips or crossed:
                with jax.named_scope("rows_behind"):
                    behind[crossed] = forward(behind[crossed], -1, int(crossed and step == 1))
                late.append(((step, crossed), behind[crossed]))
    orders.append([key for key, _ in waiting])
    earlier.append(score([c for _, c in waiting]))
    waiting = late
    orders.append([key for key, _ in waiting])
    partial, all_facts = score_call(
        [c for _, c in waiting], orders, earlier, spot, noise, own_panel, squares, mate_panel
    )

    mate_partial = lax.ppermute(partial, "orient", mate_pairs)
    mine, across, stats = pl.pallas_call(
        functools.partial(chip_kernel, local_search),
        in_specs=[smem] + [vmem] * 3,
        out_specs=[vmem] * 3,
        out_shape=[
            jax.ShapeDtypeStruct((everyone, orientations), jnp.float32),
            jax.ShapeDtypeStruct((everyone, orientations), jnp.float32),
            jax.ShapeDtypeStruct((8, everyone), jnp.float32),
        ],
        compiler_params=params,
    )(spot, partial, mate_partial, all_facts)

    from_x = lax.ppermute(across, "cls", x_pairs)
    parts = [stats] + [
        lax.ppermute(stats, "orient", [(d, (d + 2 * s) % devices) for d in range(devices)])
        for s in range(1, chips)
    ]
    peaks = functools.reduce(jnp.maximum, [p[0:2] for p in parts])
    totals = functools.reduce(jnp.add, [p[2:4] * jnp.exp(p[0:2] - peaks) for p in parts])
    class_stats = jnp.pad(jnp.concatenate([peaks, totals], axis=0), ((0, 4), (0, 0)))
    other_stats = lax.ppermute(class_stats, "cls", x_pairs)
    slots, chosen, tops = pl.pallas_call(
        functools.partial(slot_kernel, local_search, slots_each, per_device),
        in_specs=[smem] + [vmem] * 3,
        out_specs=[vmem] * 3,
        out_shape=[
            jax.ShapeDtypeStruct((capacity, 2 * orientations), jnp.float32),
            jax.ShapeDtypeStruct((capacity, everyone), jnp.float32),
            jax.ShapeDtypeStruct((8, everyone), jnp.float32),
        ],
        compiler_params=params,
    )(spot, mine, from_x, all_facts)
    posterior = pl.pallas_call(
        final_kernel,
        in_specs=[vmem] * 5,
        out_specs=vmem,
        out_shape=jax.ShapeDtypeStruct((capacity, 2 * orientations), jnp.float32),
        compiler_params=params,
    )(class_stats, other_stats, tops, slots, chosen)
    return posterior.reshape(1, 1, capacity, -1)


def spread_max(member, is_live, values):
    picked = jnp.max(jnp.where(member, values[None, :], FLOOR), axis=1)
    return jnp.where(is_live, picked, 0.0)


def collect_sums(member, expo):
    return jnp.sum(jnp.where(member, jnp.sum(expo, axis=1)[:, None], 0.0), axis=0)


def shards(images, defocus, block_ids, noise_weight, panels):
    per_device = images.shape[1]
    columns = images.shape[3]
    devices = lax.axis_size("orient")
    local_search = block_ids.shape[2]
    slots_each = min(per_device, max(2, 2 * per_device * local_search // devices))
    capacity = slots_each * devices
    everyone = per_device * devices
    all_lists = lax.all_gather(block_ids[0], "orient", axis=0, tiled=True)
    all_rows, all_focus = (
        lax.all_gather(images[0], "orient", axis=0, tiled=True),
        lax.all_gather(defocus[0], "orient", axis=0, tiled=True),
    )
    own_block = lax.axis_index("orient")
    block_hits = (
        jnp.any(all_lists == own_block, axis=1).astype(jnp.int32).reshape(devices, per_device)
    )
    slot_rank = jnp.cumsum(block_hits, axis=1) - block_hits
    places = (jnp.arange(devices, dtype=jnp.int32)[:, None] * slots_each + slot_rank).reshape(
        everyone
    )
    chosen = (places[None, :] == jnp.arange(capacity, dtype=jnp.int32)[:, None]) & (
        block_hits.reshape(everyone)[None, :] == 1
    )
    is_live = jnp.any(chosen, axis=1)
    slot_owner = jnp.sum(
        jnp.where(chosen, jnp.arange(everyone, dtype=jnp.int32)[None, :], 0), axis=1
    )
    slot_rows = jnp.take(all_rows, slot_owner, axis=0)
    slot_focus = jnp.take(all_focus, slot_owner, axis=0).astype(jnp.float32)
    frequency = (jnp.arange(columns, dtype=jnp.float32) + 0.5) / columns
    contrast = -jnp.sin(CTF_PHASE * slot_focus[:, None] * frequency[None, :] + 0.1)
    weighted = contrast * noise_weight[None, :]
    scaled_rows = (weighted[:, None, :] * slot_rows.astype(jnp.float32)).astype(jnp.bfloat16)
    energy = (contrast * weighted).astype(jnp.bfloat16)
    piece = lax.all_gather(panels[:, 0], "cls", axis=0, tiled=True)
    widened = piece.astype(jnp.float32)
    squared = (widened * widened).astype(jnp.bfloat16)
    correlate = jnp.einsum("srk,cjrk->scj", scaled_rows, piece, preferred_element_type=jnp.float32)
    energy_term = jnp.einsum("sk,cjrk->scj", energy, squared, preferred_element_type=jnp.float32)
    terms = correlate - 0.5 * energy_term
    combined = terms.reshape(capacity, -1)
    scores = lax.psum_scatter(combined, "rep", scatter_dimension=1, tiled=True)
    member = (slot_owner[:, None] == jnp.arange(everyone, dtype=jnp.int32)[None, :]) & is_live[
        :, None
    ]
    slot_top = jnp.max(scores, axis=1)
    local_peak = jnp.max(jnp.where(member, slot_top[:, None], FLOOR), axis=0)
    peak = lax.pmax(local_peak, ("orient", "rep"))
    slot_peak = spread_max(member, is_live, peak)
    expo = jnp.where(is_live[:, None], jnp.exp(scores - slot_peak[:, None]), 0.0)
    total = lax.psum(collect_sums(member, expo), ("orient", "rep"))
    slot_total = jnp.where(is_live, jnp.sum(jnp.where(member, total[None, :], 0.0), axis=1), 1.0)
    posterior = expo / slot_total[:, None]
    return posterior.reshape(1, 1, capacity, -1)


def solution(mesh):
    in_specs = (
        P(("batch", "cls"), "orient", "rep", None),
        P(("batch", "cls"), "orient"),
        P(("batch", "cls"), "orient", None),
        P(),
        P(("batch", "cls"), "orient", None, "rep", None),
    )
    out_specs = P(("batch", "cls"), "orient", None, "rep")
    sizes = mesh.shape
    paired = sizes["rep"] == 1 and sizes["cls"] == 2 and sizes["orient"] % 2 == 0
    return jax.shard_map(
        chip_shards if paired else shards,
        mesh=mesh,
        in_specs=in_specs,
        out_specs=out_specs,
        check_vma=False,
    )
```

```python
import functools

import jax
import jax.numpy as jnp
from jax import lax
from jax.experimental import pallas as pl
from jax.experimental.pallas import tpu as pltpu
from jax.sharding import PartitionSpec as P

CTF_PHASE = 40.0
FLOOR = -1e30
LANES = 128
VMEM_LIMIT = 8 * 1024 * 1024
SCHEDULING_WEIGHT = 20 * 10**9


def sin_cos(angle):
    turns = jnp.floor(angle * 0.6366197723675814 + 0.5)
    rest = angle - turns * 1.5703125
    rest = rest - turns * 4.837512969970703e-4
    rest = rest - turns * 7.549789948768648e-8
    square = rest * rest
    sine = rest + rest * square * (
        -1.6666654611e-1 + square * (8.3321608736e-3 - square * 1.9515295891e-4)
    )
    cosine = (
        1.0
        - 0.5 * square
        + square
        * square
        * (4.166664568298827e-2 + square * (-1.388731625493765e-3 + square * 2.443315711809948e-5))
    )
    quarter = turns.astype(jnp.int32)
    odd = (quarter & 1) == 1
    low = jnp.where(odd, cosine, sine)
    high = jnp.where(odd, sine, cosine)
    return (
        jnp.where((quarter & 2) == 2, -low, low),
        jnp.where(((quarter + 1) & 2) == 2, -high, high),
    )


def panel_kernel(spot, sides, own, given):
    own[...] = sides[spot[2]]
    given[...] = sides[1 - spot[2]]


def square_kernel(own, squares):
    squares[...] = own[...] * own[...]


def row_kernel(spot, planes, defocus, lists, kept, given, facts, focus, named, sems):
    core = spot[2]
    columns = planes.shape[2]
    count = defocus.shape[1]
    fetches = [
        pltpu.make_async_copy(defocus, focus, sems.at[0]),
        pltpu.make_async_copy(lists, named, sems.at[1]),
    ]
    for fetch in fetches:
        fetch.start()
    facts[...] = jnp.zeros_like(facts)
    for half, out in ((core, kept), (1 - core, given)):
        out[:, :columns] = planes[half]
    for fetch in fetches:
        fetch.wait()
    facts[0:1, :count] = focus[...].astype(jnp.float32)
    facts[1 : 1 + lists.shape[0], :count] = named[...].astype(jnp.float32)
    for out in (kept, given):
        out[:, columns:] = facts[...].astype(out.dtype)


def particle_facts(meta):
    return jnp.concatenate([m[...].astype(jnp.float32).T[: m.shape[0]] for m in meta], axis=0)


def add_scores(rows, noise, own_panel, own_squares, mate_panel, turn_sin, turn_cos, sums, segments):
    columns = noise.shape[1]
    width = columns // segments
    tiles = width // LANES
    count = turn_sin.shape[0]
    facts = particle_facts([r.at[:, pl.ds(columns, LANES)] for r in rows])
    rate = jnp.broadcast_to(CTF_PHASE * facts[:, 0:1], (count, LANES))
    lane = lax.broadcasted_iota(jnp.int32, (count, LANES), 1).astype(jnp.float32)
    first_sin, first_cos = sin_cos(rate * ((lane + 0.5) / columns) + 0.1)
    step_sin, step_cos = sin_cos(rate * (LANES / columns))
    turn_sin[...] = step_sin
    turn_cos[...] = step_cos
    for total in sums:
        total[...] = jnp.zeros_like(total)

    def segment(index, carry):
        sine, cosine = carry
        start = pl.multiple_of(index * width, LANES)
        scaled_parts, energy_parts = [], []
        for t in range(tiles):
            window = pl.ds(start + t * LANES, LANES)
            weighted = sine * noise[:, window]
            image = jnp.concatenate([r[:, window] for r in rows], axis=0).astype(jnp.float32)
            scaled_parts.append((weighted * image).astype(jnp.bfloat16))
            energy_parts.append((sine * weighted).astype(jnp.bfloat16))
            ds, dc = turn_sin[...], turn_cos[...]
            sine, cosine = sine * dc + cosine * ds, cosine * dc - sine * ds
        scaled = jnp.concatenate(scaled_parts, axis=1)
        energy = jnp.concatenate(energy_parts, axis=1)
        contract = (((1,), (1,)), ((), ()))
        whole = pl.ds(start, width)
        mate = mate_panel[:, whole]
        for values, squared, total in (
            (own_panel[:, whole], own_squares[:, whole], sums[0]),
            (mate, mate * mate, sums[1]),
        ):
            correlate = lax.dot_general(
                values, scaled, contract, preferred_element_type=jnp.float32
            )
            power = lax.dot_general(squared, energy, contract, preferred_element_type=jnp.float32)
            total[...] += correlate - 0.5 * power
        return sine, cosine

    lax.fori_loop(0, segments, segment, (-first_sin, -first_cos))
    return jnp.pad(facts, ((0, 0), (0, LANES - facts.shape[1])))


def batch_kernel(n, segments, spot, *refs):
    rows = refs[:n]
    noise, own_panel, own_squares, mate_panel = refs[n : n + 4]
    own_out, mate_out, fact_out, turn_sin, turn_cos, *sums = refs[n + 4 :]
    fact_out[...] = add_scores(
        rows, noise, own_panel, own_squares, mate_panel, turn_sin, turn_cos, sums, segments
    )
    own_out[...] = sums[0][...].T
    mate_out[...] = sums[1][...].T


def last_kernel(n, segments, orders, spot, *refs):
    rows = refs[:n]
    noise, own_panel, own_squares, mate_panel = refs[n : n + 4]
    rest = refs[n + 4 :]
    earlier, rest = rest[: 3 * (len(orders) - 1)], rest[3 * (len(orders) - 1) :]
    partial, facts, turn_sin, turn_cos, *sums = rest
    last_facts = add_scores(
        rows, noise, own_panel, own_squares, mate_panel, turn_sin, turn_cos, sums, segments
    )
    position, core = spot[1], spot[2]
    each = rows[0].shape[0]
    ring = facts.shape[0] // (2 * each)
    half = ring // 2
    for index, order in enumerate(orders):
        if index < len(orders) - 1:
            own, mate, fact = [r[...] for r in earlier[3 * index : 3 * index + 3]]
        else:
            own, mate, fact = sums[0][...].T, sums[1][...].T, last_facts
        for k, (distance, crossed) in enumerate(order):
            place = lax.rem(position + distance + ring, ring)
            far = place >= half
            level = jnp.where(far, ring - 1 - place, place)
            device = 2 * level + (1 - core if crossed else core)
            start = pl.multiple_of((jnp.where(far, ring, 0) + device) * each, each)
            piece = slice(k * each, (k + 1) * each)
            partial[core, pl.ds(start, each), :] = own[piece]
            partial[1 - core, pl.ds(start, each), :] = mate[piece]
            facts[pl.ds(start, each), :] = fact[piece]


def score_call(chunks, orders, earlier, spot, noise, own_panel, squares, mate_panel):
    each = chunks[0].shape[0]
    orientations, columns = own_panel.shape
    whole = columns // LANES
    segments = next(s for s in (3, 2, 4, 5, 6, 7, 1) if whole % s == 0)
    n = len(chunks)
    count = each * n
    scratch = [pltpu.VMEM((count, LANES), jnp.float32)] * 2
    scratch += [pltpu.VMEM((orientations, count), jnp.float32)] * 2
    single = jax.ShapeDtypeStruct((count, orientations), jnp.float32)
    if orders is None:
        kernel = functools.partial(batch_kernel, n, segments)
        out_shape = [single, single, jax.ShapeDtypeStruct((count, LANES), jnp.float32)]
        extra = []
    else:
        everyone = each * sum(len(o) for o in orders)
        kernel = functools.partial(last_kernel, n, segments, orders)
        out_shape = [
            jax.ShapeDtypeStruct((2, everyone, orientations), jnp.float32),
            jax.ShapeDtypeStruct((everyone, LANES), jnp.float32),
        ]
        extra = [e for triple in earlier for e in triple]
    vmem = pl.BlockSpec(memory_space=pltpu.VMEM)
    return pl.pallas_call(
        kernel,
        in_specs=[pl.BlockSpec(memory_space=pltpu.SMEM)] + [vmem] * (n + 4 + len(extra)),
        out_specs=[vmem] * len(out_shape),
        out_shape=out_shape,
        scratch_shapes=scratch,
        compiler_params=pltpu.CompilerParams(vmem_limit_bytes=VMEM_LIMIT),
        cost_estimate=pl.CostEstimate(
            flops=8 * max(count, 128) * orientations * columns,
            bytes_accessed=4 * orientations * columns + 2 * count * columns,
            transcendentals=0,
        ),
    )(spot, *chunks, noise, own_panel, squares, mate_panel, *extra)


def names_block(facts, search, block):
    lane = lax.broadcasted_iota(jnp.int32, facts.shape, 1)
    match = (lane >= 1) & (lane <= search) & (facts == block.astype(jnp.float32))
    return jnp.max(jnp.where(match, 1.0, 0.0), axis=1, keepdims=True) > 0.0


def chip_kernel(search, spot, partial, mate, facts, mine, across, stats):
    group, core, place = spot[0], spot[2], spot[3]
    count = mine.shape[0]
    lane = lax.broadcasted_iota(jnp.int32, (count, LANES), 1)
    pairs = []
    for relative in range(2):
        side = group if relative == 0 else 1 - group
        window = pl.ds(pl.multiple_of(side * count, count), count)
        listed = facts[window, :]
        masked = []
        for crossed in range(2):
            block = core if crossed == 0 else 1 - core
            scores = partial[block, window, :] + mate[block, window, :]
            if crossed == 0:
                out = mine if relative == 0 else across
                out[...] = scores
            named = names_block(listed, search, place - core + block)
            masked.append(jnp.where(named, scores, FLOOR))
        top = jnp.max(jnp.maximum(*masked), axis=1, keepdims=True)
        terms = [jnp.where(m > FLOOR, jnp.exp(m - top), 0.0) for m in masked]
        total = jnp.sum(terms[0] + terms[1], axis=1, keepdims=True)
        pairs.append(jnp.where(lane == relative, top, jnp.where(lane == 2 + relative, total, 0.0)))
    stats[...] = (pairs[0] + pairs[1]).T[: stats.shape[0]]


def slot_kernel(search, slots_each, each, spot, mine, across, facts, slots, chosen, tops):
    group, place = spot[0], spot[3]
    count = mine.shape[0]
    same, other = mine[...], across[...]
    first = group == 0
    scores = jnp.concatenate(
        [jnp.where(first, same, other), jnp.where(first, other, same)], axis=1
    )
    listed = facts[pl.ds(pl.multiple_of(group * count, count), count), :]
    named = names_block(listed, search, place)
    hit = jnp.where(named, 1.0, 0.0)
    row = lax.broadcasted_iota(jnp.int32, (count, LANES), 0)
    line = lax.broadcasted_iota(jnp.int32, (count, count), 0)
    column = lax.broadcasted_iota(jnp.int32, (count, count), 1)
    before = (column < line) & (column // each == line // each)
    rank = jnp.dot(
        jnp.where(before, 1.0, 0.0).astype(jnp.bfloat16),
        jnp.broadcast_to(hit, (count, LANES)).astype(jnp.bfloat16),
        preferred_element_type=jnp.float32,
    )
    slot = (row // each) * slots_each + rank.astype(jnp.int32)
    capacity = chosen.shape[0]
    if capacity != LANES:
        slot = jnp.broadcast_to(slot[:, :1], (count, capacity))
    target = lax.broadcasted_iota(jnp.int32, (count, capacity), 1)
    taken = jnp.where((slot == target) & named, 1.0, 0.0)
    top = jnp.max(scores, axis=1, keepdims=True)
    tops[...] = jnp.broadcast_to(top, (count, LANES)).T[: tops.shape[0]]
    terms = jnp.where(named, jnp.exp(scores - top), 0.0)
    slots[...] = lax.dot_general(
        taken,
        terms,
        (((0,), (0,)), ((), ())),
        precision=lax.Precision.HIGHEST,
        preferred_element_type=jnp.float32,
    )
    chosen[...] = taken.T


def final_kernel(own, other, tops, slots, chosen, out):
    peaks = own[0:1, :], other[1:2, :]
    totals = own[2:3, :], other[3:4, :]
    peak = jnp.maximum(*peaks)
    total = totals[0] * jnp.exp(peaks[0] - peak) + totals[1] * jnp.exp(peaks[1] - peak)
    factor = jnp.exp(jnp.minimum(tops[0:1, :] - peak, 0.0)) / total
    scale = jnp.sum(chosen[...] * factor, axis=1, keepdims=True)
    out[...] = slots[...] * scale


def chip_shards(images, defocus, block_ids, noise_weight, panels):
    per_device, halves, columns = images.shape[1:]
    devices = lax.axis_size("orient")
    chips = devices // 2
    ring = 2 * chips
    everyone = per_device * devices
    local_search = block_ids.shape[2]
    orientations = panels.shape[2]
    slots_each = min(per_device, max(2, 2 * per_device * local_search // devices))
    capacity = slots_each * devices
    place = lax.axis_index("orient")
    group = lax.axis_index("cls")
    chip, core = place // 2, place % 2
    position = jnp.where(group == 0, chip, ring - 1 - chip)
    spot = jnp.stack([group, position, core, place]).astype(jnp.int32)
    first = core == 0

    mate_pairs = [(d, d ^ 1) for d in range(devices)]
    x_pairs = [(0, 1), (1, 0)]

    def joint(place, core):
        place = place % ring
        far = place >= chips
        level = ring - 1 - place if far else place
        return (2 * level + core) * 2 + int(far)

    def forward(values, step, cross=0):
        pairs = [(joint(p, c), joint(p + step, c ^ cross)) for p in range(ring) for c in range(2)]
        return lax.ppermute(values, ("orient", "cls"), pairs)

    vmem = pl.BlockSpec(memory_space=pltpu.VMEM)
    smem = pl.BlockSpec(memory_space=pltpu.SMEM)
    params = pltpu.CompilerParams(vmem_limit_bytes=VMEM_LIMIT)
    planes = lax.optimization_barrier(jnp.transpose(images[0], (1, 0, 2)))
    row_shape = jax.ShapeDtypeStruct((per_device, columns + LANES), jnp.bfloat16)
    kept, given = pl.pallas_call(
        row_kernel,
        in_specs=[smem, vmem] + [pl.BlockSpec(memory_space=pltpu.HBM)] * 2,
        out_specs=[vmem] * 2,
        out_shape=[row_shape] * 2,
        scratch_shapes=[
            pltpu.VMEM((per_device, LANES), jnp.float32),
            pltpu.VMEM(defocus.shape, defocus.dtype),
            pltpu.VMEM((local_search, per_device), block_ids.dtype),
            pltpu.SemaphoreType.DMA((2,)),
        ],
        compiler_params=params,
    )(spot, planes, defocus, jnp.transpose(block_ids[0]))
    with jax.named_scope("mate_rows"):
        got = lax.ppermute(given, "orient", mate_pairs)

    _, panels = lax.optimization_barrier((kept, panels))
    sides = lax.optimization_barrier(jnp.transpose(panels[0, 0], (1, 0, 2)))
    panel_shape = jax.ShapeDtypeStruct(sides.shape[1:], sides.dtype)
    own_panel, given_panel = pl.pallas_call(
        panel_kernel,
        in_specs=[smem, vmem],
        out_specs=[vmem] * 2,
        out_shape=[panel_shape] * 2,
        compiler_params=params,
    )(spot, sides)
    with jax.named_scope("mate_panel"):
        mate_panel = lax.ppermute(given_panel, "orient", mate_pairs)

    noise = noise_weight[None, :]
    waiting = [((0, False), kept), ((0, True), got)]
    ahead = {False: kept, True: given}
    behind = {False: kept, True: given}
    orders, earlier, late = [], [], []
    squares = pl.pallas_call(
        square_kernel,
        in_specs=[vmem],
        out_specs=vmem,
        out_shape=panel_shape,
        compiler_params=params,
        cost_estimate=pl.CostEstimate(flops=SCHEDULING_WEIGHT, bytes_accessed=0, transcendentals=0),
    )(own_panel)
    score = lambda c: score_call(c, None, None, spot, noise, own_panel, squares, mate_panel)
    for step in range(1, chips + 1):
        if step == 3:
            orders.append([key for key, _ in waiting])
            earlier.append(score([c for _, c in waiting]))
            waiting = []
            for chain, c in ((ahead, False), (behind, True)):
                chain[c] = lax.optimization_barrier((chain[c], earlier[-1][2]))[0]
        if step == 2:
            for chain, c in ((ahead, False), (behind, True)):
                chain[c] = lax.optimization_barrier((chain[c], squares))[0]
        waiting = waiting + late
        late = []
        for crossed in (False, True):
            if step < chips or not crossed:
                with jax.named_scope("rows_ahead"):
                    ahead[crossed] = forward(ahead[crossed], 1, int(crossed and step == 1))
                late.append(((-step, crossed), ahead[crossed]))
            if step < chips or crossed:
                with jax.named_scope("rows_behind"):
                    behind[crossed] = forward(behind[crossed], -1, int(crossed and step == 1))
                late.append(((step, crossed), behind[crossed]))
    orders.append([key for key, _ in waiting])
    earlier.append(score([c for _, c in waiting]))
    waiting = late
    orders.append([key for key, _ in waiting])
    partial, all_facts = score_call(
        [c for _, c in waiting], orders, earlier, spot, noise, own_panel, squares, mate_panel
    )

    mate_partial = lax.ppermute(partial, "orient", mate_pairs)
    mine, across, stats = pl.pallas_call(
        functools.partial(chip_kernel, local_search),
        in_specs=[smem] + [vmem] * 3,
        out_specs=[vmem] * 3,
        out_shape=[
            jax.ShapeDtypeStruct((everyone, orientations), jnp.float32),
            jax.ShapeDtypeStruct((everyone, orientations), jnp.float32),
            jax.ShapeDtypeStruct((8, everyone), jnp.float32),
        ],
        compiler_params=params,
    )(spot, partial, mate_partial, all_facts)

    from_x = lax.ppermute(across, "cls", x_pairs)
    class_stats = stats
    for bit in range(chips.bit_length() - 1):
        pairs = [(d, d ^ (2 << bit)) for d in range(devices)]
        both = class_stats, lax.ppermute(class_stats, "orient", pairs)
        peaks = jnp.maximum(both[0][0:2], both[1][0:2])
        totals = sum(v[2:4] * jnp.exp(v[0:2] - peaks) for v in both)
        class_stats = jnp.pad(jnp.concatenate([peaks, totals], axis=0), ((0, 4), (0, 0)))
    other_stats = lax.ppermute(class_stats, "cls", x_pairs)
    slots, chosen, tops = pl.pallas_call(
        functools.partial(slot_kernel, local_search, slots_each, per_device),
        in_specs=[smem] + [vmem] * 3,
        out_specs=[vmem] * 3,
        out_shape=[
            jax.ShapeDtypeStruct((capacity, 2 * orientations), jnp.float32),
            jax.ShapeDtypeStruct((capacity, everyone), jnp.float32),
            jax.ShapeDtypeStruct((8, everyone), jnp.float32),
        ],
        compiler_params=params,
    )(spot, mine, from_x, all_facts)
    posterior = pl.pallas_call(
        final_kernel,
        in_specs=[vmem] * 5,
        out_specs=vmem,
        out_shape=jax.ShapeDtypeStruct((capacity, 2 * orientations), jnp.float32),
        compiler_params=params,
    )(class_stats, other_stats, tops, slots, chosen)
    return posterior.reshape(1, 1, capacity, -1)


def spread_max(member, is_live, values):
    picked = jnp.max(jnp.where(member, values[None, :], FLOOR), axis=1)
    return jnp.where(is_live, picked, 0.0)


def collect_sums(member, expo):
    return jnp.sum(jnp.where(member, jnp.sum(expo, axis=1)[:, None], 0.0), axis=0)


def shards(images, defocus, block_ids, noise_weight, panels):
    per_device = images.shape[1]
    columns = images.shape[3]
    devices = lax.axis_size("orient")
    local_search = block_ids.shape[2]
    slots_each = min(per_device, max(2, 2 * per_device * local_search // devices))
    capacity = slots_each * devices
    everyone = per_device * devices
    all_lists = lax.all_gather(block_ids[0], "orient", axis=0, tiled=True)
    all_rows, all_focus = (
        lax.all_gather(images[0], "orient", axis=0, tiled=True),
        lax.all_gather(defocus[0], "orient", axis=0, tiled=True),
    )
    own_block = lax.axis_index("orient")
    block_hits = (
        jnp.any(all_lists == own_block, axis=1).astype(jnp.int32).reshape(devices, per_device)
    )
    slot_rank = jnp.cumsum(block_hits, axis=1) - block_hits
    places = (jnp.arange(devices, dtype=jnp.int32)[:, None] * slots_each + slot_rank).reshape(
        everyone
    )
    chosen = (places[None, :] == jnp.arange(capacity, dtype=jnp.int32)[:, None]) & (
        block_hits.reshape(everyone)[None, :] == 1
    )
    is_live = jnp.any(chosen, axis=1)
    slot_owner = jnp.sum(
        jnp.where(chosen, jnp.arange(everyone, dtype=jnp.int32)[None, :], 0), axis=1
    )
    slot_rows = jnp.take(all_rows, slot_owner, axis=0)
    slot_focus = jnp.take(all_focus, slot_owner, axis=0).astype(jnp.float32)
    frequency = (jnp.arange(columns, dtype=jnp.float32) + 0.5) / columns
    contrast = -jnp.sin(CTF_PHASE * slot_focus[:, None] * frequency[None, :] + 0.1)
    weighted = contrast * noise_weight[None, :]
    scaled_rows = (weighted[:, None, :] * slot_rows.astype(jnp.float32)).astype(jnp.bfloat16)
    energy = (contrast * weighted).astype(jnp.bfloat16)
    piece = lax.all_gather(panels[:, 0], "cls", axis=0, tiled=True)
    widened = piece.astype(jnp.float32)
    squared = (widened * widened).astype(jnp.bfloat16)
    correlate = jnp.einsum("srk,cjrk->scj", scaled_rows, piece, preferred_element_type=jnp.float32)
    energy_term = jnp.einsum("sk,cjrk->scj", energy, squared, preferred_element_type=jnp.float32)
    terms = correlate - 0.5 * energy_term
    combined = terms.reshape(capacity, -1)
    scores = lax.psum_scatter(combined, "rep", scatter_dimension=1, tiled=True)
    member = (slot_owner[:, None] == jnp.arange(everyone, dtype=jnp.int32)[None, :]) & is_live[
        :, None
    ]
    slot_top = jnp.max(scores, axis=1)
    local_peak = jnp.max(jnp.where(member, slot_top[:, None], FLOOR), axis=0)
    peak = lax.pmax(local_peak, ("orient", "rep"))
    slot_peak = spread_max(member, is_live, peak)
    expo = jnp.where(is_live[:, None], jnp.exp(scores - slot_peak[:, None]), 0.0)
    total = lax.psum(collect_sums(member, expo), ("orient", "rep"))
    slot_total = jnp.where(is_live, jnp.sum(jnp.where(member, total[None, :], 0.0), axis=1), 1.0)
    posterior = expo / slot_total[:, None]
    return posterior.reshape(1, 1, capacity, -1)


def solution(mesh):
    in_specs = (
        P(("batch", "cls"), "orient", "rep", None),
        P(("batch", "cls"), "orient"),
        P(("batch", "cls"), "orient", None),
        P(),
        P(("batch", "cls"), "orient", None, "rep", None),
    )
    out_specs = P(("batch", "cls"), "orient", None, "rep")
    sizes = mesh.shape
    paired = sizes["rep"] == 1 and sizes["cls"] == 2 and sizes["orient"] in (4, 8, 16, 32)
    return jax.shard_map(
        chip_shards if paired else shards,
        mesh=mesh,
        in_specs=in_specs,
        out_specs=out_specs,
        check_vma=False,
    )
```

```python
import functools

import jax
import jax.numpy as jnp
from jax import lax
from jax.experimental import pallas as pl
from jax.experimental.pallas import tpu as pltpu
from jax.sharding import PartitionSpec as P

CTF_PHASE = 40.0
FLOOR = -1e30
LANES = 128
VMEM_LIMIT = 8 * 1024 * 1024
SCHEDULING_WEIGHT = 20 * 10**9


def sin_cos(angle):
    turns = jnp.floor(angle * 0.6366197723675814 + 0.5)
    rest = angle - turns * 1.5703125
    rest = rest - turns * 4.837512969970703e-4
    rest = rest - turns * 7.549789948768648e-8
    square = rest * rest
    sine = rest + rest * square * (
        -1.6666654611e-1 + square * (8.3321608736e-3 - square * 1.9515295891e-4)
    )
    cosine = (
        1.0
        - 0.5 * square
        + square
        * square
        * (4.166664568298827e-2 + square * (-1.388731625493765e-3 + square * 2.443315711809948e-5))
    )
    quarter = turns.astype(jnp.int32)
    odd = (quarter & 1) == 1
    low = jnp.where(odd, cosine, sine)
    high = jnp.where(odd, sine, cosine)
    return (
        jnp.where((quarter & 2) == 2, -low, low),
        jnp.where(((quarter + 1) & 2) == 2, -high, high),
    )


def panel_kernel(spot, sides, own, given):
    own[...] = sides[spot[2]]
    given[...] = sides[1 - spot[2]]


def square_kernel(own, squares):
    squares[...] = own[...] * own[...]


def row_kernel(spot, planes, facts, kept, given, padded):
    core = spot[2]
    columns = planes.shape[2]
    padded[...] = jnp.zeros_like(padded)
    padded[: facts.shape[0], : facts.shape[1]] = facts[...]
    for half, out in ((core, kept), (1 - core, given)):
        out[:, :columns] = planes[half]
        out[:, columns:] = padded[...].astype(out.dtype)


def particle_facts(meta):
    return jnp.concatenate([m[...].astype(jnp.float32).T[: m.shape[0]] for m in meta], axis=0)


def add_scores(rows, noise, own_panel, own_squares, mate_panel, turn_sin, turn_cos, sums, segments):
    columns = noise.shape[1]
    width = columns // segments
    tiles = width // LANES
    count = turn_sin.shape[0]
    facts = particle_facts([r.at[:, pl.ds(columns, LANES)] for r in rows])
    rate = jnp.broadcast_to(CTF_PHASE * facts[:, 0:1], (count, LANES))
    lane = lax.broadcasted_iota(jnp.int32, (count, LANES), 1).astype(jnp.float32)
    first_sin, first_cos = sin_cos(rate * ((lane + 0.5) / columns) + 0.1)
    step_sin, step_cos = sin_cos(rate * (LANES / columns))
    turn_sin[...] = step_sin
    turn_cos[...] = step_cos
    for total in sums:
        total[...] = jnp.zeros_like(total)

    def segment(index, carry):
        sine, cosine = carry
        start = pl.multiple_of(index * width, LANES)
        scaled_parts, energy_parts = [], []
        for t in range(tiles):
            window = pl.ds(start + t * LANES, LANES)
            weighted = sine * noise[:, window]
            image = jnp.concatenate([r[:, window] for r in rows], axis=0).astype(jnp.float32)
            scaled_parts.append((weighted * image).astype(jnp.bfloat16))
            energy_parts.append((sine * weighted).astype(jnp.bfloat16))
            ds, dc = turn_sin[...], turn_cos[...]
            sine, cosine = sine * dc + cosine * ds, cosine * dc - sine * ds
        scaled = jnp.concatenate(scaled_parts, axis=1)
        energy = jnp.concatenate(energy_parts, axis=1)
        contract = (((1,), (1,)), ((), ()))
        whole = pl.ds(start, width)
        mate = mate_panel[:, whole]
        for values, squared, total in (
            (own_panel[:, whole], own_squares[:, whole], sums[0]),
            (mate, mate * mate, sums[1]),
        ):
            correlate = lax.dot_general(
                values, scaled, contract, preferred_element_type=jnp.float32
            )
            power = lax.dot_general(squared, energy, contract, preferred_element_type=jnp.float32)
            total[...] += correlate - 0.5 * power
        return sine, cosine

    lax.fori_loop(0, segments, segment, (-first_sin, -first_cos))
    return jnp.pad(facts, ((0, 0), (0, LANES - facts.shape[1])))


def batch_kernel(n, segments, spot, *refs):
    rows = refs[:n]
    noise, own_panel, own_squares, mate_panel = refs[n : n + 4]
    own_out, mate_out, fact_out, turn_sin, turn_cos, *sums = refs[n + 4 :]
    fact_out[...] = add_scores(
        rows, noise, own_panel, own_squares, mate_panel, turn_sin, turn_cos, sums, segments
    )
    own_out[...] = sums[0][...].T
    mate_out[...] = sums[1][...].T


def last_kernel(n, segments, orders, spot, *refs):
    rows = refs[:n]
    noise, own_panel, own_squares, mate_panel = refs[n : n + 4]
    rest = refs[n + 4 :]
    earlier, rest = rest[: 3 * (len(orders) - 1)], rest[3 * (len(orders) - 1) :]
    partial, facts, turn_sin, turn_cos, *sums = rest
    last_facts = add_scores(
        rows, noise, own_panel, own_squares, mate_panel, turn_sin, turn_cos, sums, segments
    )
    position, core = spot[1], spot[2]
    each = rows[0].shape[0]
    ring = facts.shape[0] // (2 * each)
    half = ring // 2
    for index, order in enumerate(orders):
        if index < len(orders) - 1:
            own, mate, fact = [r[...] for r in earlier[3 * index : 3 * index + 3]]
        else:
            own, mate, fact = sums[0][...].T, sums[1][...].T, last_facts
        for k, (distance, crossed) in enumerate(order):
            place = lax.rem(position + distance + ring, ring)
            far = place >= half
            level = jnp.where(far, ring - 1 - place, place)
            device = 2 * level + (1 - core if crossed else core)
            start = pl.multiple_of((jnp.where(far, ring, 0) + device) * each, each)
            piece = slice(k * each, (k + 1) * each)
            partial[core, pl.ds(start, each), :] = own[piece]
            partial[1 - core, pl.ds(start, each), :] = mate[piece]
            facts[pl.ds(start, each), :] = fact[piece]


def score_call(chunks, orders, earlier, spot, noise, own_panel, squares, mate_panel):
    each = chunks[0].shape[0]
    orientations, columns = own_panel.shape
    whole = columns // LANES
    segments = next(s for s in (3, 2, 4, 5, 6, 7, 1) if whole % s == 0)
    n = len(chunks)
    count = each * n
    scratch = [pltpu.VMEM((count, LANES), jnp.float32)] * 2
    scratch += [pltpu.VMEM((orientations, count), jnp.float32)] * 2
    single = jax.ShapeDtypeStruct((count, orientations), jnp.float32)
    if orders is None:
        kernel = functools.partial(batch_kernel, n, segments)
        out_shape = [single, single, jax.ShapeDtypeStruct((count, LANES), jnp.float32)]
        extra = []
    else:
        everyone = each * sum(len(o) for o in orders)
        kernel = functools.partial(last_kernel, n, segments, orders)
        out_shape = [
            jax.ShapeDtypeStruct((2, everyone, orientations), jnp.float32),
            jax.ShapeDtypeStruct((everyone, LANES), jnp.float32),
        ]
        extra = [e for triple in earlier for e in triple]
    vmem = pl.BlockSpec(memory_space=pltpu.VMEM)
    return pl.pallas_call(
        kernel,
        in_specs=[pl.BlockSpec(memory_space=pltpu.SMEM)] + [vmem] * (n + 4 + len(extra)),
        out_specs=[vmem] * len(out_shape),
        out_shape=out_shape,
        scratch_shapes=scratch,
        compiler_params=pltpu.CompilerParams(vmem_limit_bytes=VMEM_LIMIT),
        cost_estimate=pl.CostEstimate(
            flops=8 * max(count, 128) * orientations * columns,
            bytes_accessed=4 * orientations * columns + 2 * count * columns,
            transcendentals=0,
        ),
    )(spot, *chunks, noise, own_panel, squares, mate_panel, *extra)


def names_block(facts, search, block):
    lane = lax.broadcasted_iota(jnp.int32, facts.shape, 1)
    match = (lane >= 1) & (lane <= search) & (facts == block.astype(jnp.float32))
    return jnp.max(jnp.where(match, 1.0, 0.0), axis=1, keepdims=True) > 0.0


def chip_kernel(search, spot, partial, mate, facts, mine, across, stats):
    group, core, place = spot[0], spot[2], spot[3]
    count = mine.shape[0]
    lane = lax.broadcasted_iota(jnp.int32, (count, LANES), 1)
    pairs = []
    for relative in range(2):
        side = group if relative == 0 else 1 - group
        window = pl.ds(pl.multiple_of(side * count, count), count)
        listed = facts[window, :]
        masked = []
        for crossed in range(2):
            block = core if crossed == 0 else 1 - core
            scores = partial[block, window, :] + mate[block, window, :]
            if crossed == 0:
                out = mine if relative == 0 else across
                out[...] = scores
            named = names_block(listed, search, place - core + block)
            masked.append(jnp.where(named, scores, FLOOR))
        top = jnp.max(jnp.maximum(*masked), axis=1, keepdims=True)
        terms = [jnp.where(m > FLOOR, jnp.exp(m - top), 0.0) for m in masked]
        total = jnp.sum(terms[0] + terms[1], axis=1, keepdims=True)
        pairs.append(jnp.where(lane == relative, top, jnp.where(lane == 2 + relative, total, 0.0)))
    stats[...] = (pairs[0] + pairs[1]).T[: stats.shape[0]]


def slot_kernel(search, slots_each, each, spot, mine, across, facts, slots, chosen, tops):
    group, place = spot[0], spot[3]
    count = mine.shape[0]
    same, other = mine[...], across[...]
    first = group == 0
    scores = jnp.concatenate(
        [jnp.where(first, same, other), jnp.where(first, other, same)], axis=1
    )
    listed = facts[pl.ds(pl.multiple_of(group * count, count), count), :]
    named = names_block(listed, search, place)
    hit = jnp.where(named, 1.0, 0.0)
    row = lax.broadcasted_iota(jnp.int32, (count, LANES), 0)
    line = lax.broadcasted_iota(jnp.int32, (count, count), 0)
    column = lax.broadcasted_iota(jnp.int32, (count, count), 1)
    before = (column < line) & (column // each == line // each)
    rank = jnp.dot(
        jnp.where(before, 1.0, 0.0).astype(jnp.bfloat16),
        jnp.broadcast_to(hit, (count, LANES)).astype(jnp.bfloat16),
        preferred_element_type=jnp.float32,
    )
    slot = (row // each) * slots_each + rank.astype(jnp.int32)
    capacity = chosen.shape[0]
    if capacity != LANES:
        slot = jnp.broadcast_to(slot[:, :1], (count, capacity))
    target = lax.broadcasted_iota(jnp.int32, (count, capacity), 1)
    taken = jnp.where((slot == target) & named, 1.0, 0.0)
    top = jnp.max(scores, axis=1, keepdims=True)
    tops[...] = jnp.broadcast_to(top, (count, LANES)).T[: tops.shape[0]]
    terms = jnp.where(named, jnp.exp(scores - top), 0.0)
    slots[...] = lax.dot_general(
        taken,
        terms,
        (((0,), (0,)), ((), ())),
        precision=lax.Precision.HIGHEST,
        preferred_element_type=jnp.float32,
    )
    chosen[...] = taken.T


def final_kernel(n, *refs):
    parts, (tops, slots, chosen, out) = refs[:n], refs[n:]
    peak = functools.reduce(jnp.maximum, [p[0:1, :] for p in parts])
    shares = [p[1:2, :] * jnp.exp(p[0:1, :] - peak) for p in parts]
    total = functools.reduce(jnp.add, shares)
    factor = jnp.exp(jnp.minimum(tops[0:1, :] - peak, 0.0)) / total
    scale = jnp.sum(chosen[...] * factor, axis=1, keepdims=True)
    out[...] = slots[...] * scale


def chip_shards(images, defocus, block_ids, noise_weight, panels):
    per_device, halves, columns = images.shape[1:]
    devices = lax.axis_size("orient")
    chips = devices // 2
    ring = 2 * chips
    everyone = per_device * devices
    local_search = block_ids.shape[2]
    orientations = panels.shape[2]
    slots_each = min(per_device, max(2, 2 * per_device * local_search // devices))
    capacity = slots_each * devices
    place = lax.axis_index("orient")
    group = lax.axis_index("cls")
    chip, core = place // 2, place % 2
    position = jnp.where(group == 0, chip, ring - 1 - chip)
    spot = jnp.stack([group, position, core, place]).astype(jnp.int32)
    first = core == 0

    mate_pairs = [(d, d ^ 1) for d in range(devices)]
    x_pairs = [(0, 1), (1, 0)]

    def joint(place, core):
        place = place % ring
        far = place >= chips
        level = ring - 1 - place if far else place
        return (2 * level + core) * 2 + int(far)

    def forward(values, step, cross=0):
        pairs = [(joint(p, c), joint(p + step, c ^ cross)) for p in range(ring) for c in range(2)]
        return lax.ppermute(values, ("orient", "cls"), pairs)

    vmem = pl.BlockSpec(memory_space=pltpu.VMEM)
    smem = pl.BlockSpec(memory_space=pltpu.SMEM)
    params = pltpu.CompilerParams(vmem_limit_bytes=VMEM_LIMIT)
    planes = lax.optimization_barrier(jnp.transpose(images[0], (1, 0, 2)))
    row_shape = jax.ShapeDtypeStruct((per_device, columns + LANES), jnp.bfloat16)
    facts = jnp.concatenate([defocus, jnp.transpose(block_ids[0])], axis=0, dtype=jnp.float32)
    kept, given = pl.pallas_call(
        row_kernel,
        in_specs=[smem, vmem, vmem],
        out_specs=[vmem] * 2,
        out_shape=[row_shape] * 2,
        scratch_shapes=[pltpu.VMEM((per_device, LANES), jnp.float32)],
        compiler_params=params,
    )(spot, planes, facts)
    with jax.named_scope("mate_rows"):
        got = lax.ppermute(given, "orient", mate_pairs)

    _, panels = lax.optimization_barrier((kept, panels))
    sides = lax.optimization_barrier(jnp.transpose(panels[0, 0], (1, 0, 2)))
    panel_shape = jax.ShapeDtypeStruct(sides.shape[1:], sides.dtype)
    own_panel, given_panel = pl.pallas_call(
        panel_kernel,
        in_specs=[smem, vmem],
        out_specs=[vmem] * 2,
        out_shape=[panel_shape] * 2,
        compiler_params=params,
    )(spot, sides)
    with jax.named_scope("mate_panel"):
        mate_panel = lax.ppermute(given_panel, "orient", mate_pairs)

    noise = noise_weight[None, :]
    waiting = [((0, False), kept), ((0, True), got)]
    ahead = {False: kept, True: given}
    behind = {False: kept, True: given}
    orders, earlier, late = [], [], []
    squares = pl.pallas_call(
        square_kernel,
        in_specs=[vmem],
        out_specs=vmem,
        out_shape=panel_shape,
        compiler_params=params,
        cost_estimate=pl.CostEstimate(flops=SCHEDULING_WEIGHT, bytes_accessed=0, transcendentals=0),
    )(own_panel)
    score = lambda c: score_call(c, None, None, spot, noise, own_panel, squares, mate_panel)
    for step in range(1, chips + 1):
        if step == 3:
            orders.append([key for key, _ in waiting])
            earlier.append(score([c for _, c in waiting]))
            waiting = []
            for chain, c in ((ahead, False), (behind, True)):
                chain[c] = lax.optimization_barrier((chain[c], earlier[-1][2]))[0]
        if step == 2:
            for chain, c in ((ahead, False), (behind, True)):
                chain[c] = lax.optimization_barrier((chain[c], squares))[0]
        waiting = waiting + late
        late = []
        for crossed in (False, True):
            if step < chips or not crossed:
                with jax.named_scope("rows_ahead"):
                    ahead[crossed] = forward(ahead[crossed], 1, int(crossed and step == 1))
                late.append(((-step, crossed), ahead[crossed]))
            if step < chips or crossed:
                with jax.named_scope("rows_behind"):
                    behind[crossed] = forward(behind[crossed], -1, int(crossed and step == 1))
                late.append(((step, crossed), behind[crossed]))
    orders.append([key for key, _ in waiting])
    earlier.append(score([c for _, c in waiting]))
    waiting = late
    orders.append([key for key, _ in waiting])
    partial, all_facts = score_call(
        [c for _, c in waiting], orders, earlier, spot, noise, own_panel, squares, mate_panel
    )

    mate_partial = lax.ppermute(partial, "orient", mate_pairs)
    mine, across, stats = pl.pallas_call(
        functools.partial(chip_kernel, local_search),
        in_specs=[smem] + [vmem] * 3,
        out_specs=[vmem] * 3,
        out_shape=[
            jax.ShapeDtypeStruct((everyone, orientations), jnp.float32),
            jax.ShapeDtypeStruct((everyone, orientations), jnp.float32),
            jax.ShapeDtypeStruct((8, everyone), jnp.float32),
        ],
        compiler_params=params,
    )(spot, partial, mate_partial, all_facts)

    x_stats = lax.ppermute(stats, "cls", x_pairs)
    across, _ = lax.optimization_barrier((across, stats))
    from_x = lax.ppermute(across, "cls", x_pairs)
    peak = jnp.maximum(stats[0], x_stats[1])
    total = stats[2] * jnp.exp(stats[0] - peak) + x_stats[3] * jnp.exp(x_stats[1] - peak)
    pair = jnp.pad(jnp.stack([peak, total]), ((0, 6), (0, 0)))
    parts = [pair] + [
        lax.ppermute(pair, "orient", [(d, (d + 2 * s) % devices) for d in range(devices)])
        for s in range(1, chips)
    ]
    slots, chosen, tops = pl.pallas_call(
        functools.partial(slot_kernel, local_search, slots_each, per_device),
        in_specs=[smem] + [vmem] * 3,
        out_specs=[vmem] * 3,
        out_shape=[
            jax.ShapeDtypeStruct((capacity, 2 * orientations), jnp.float32),
            jax.ShapeDtypeStruct((capacity, everyone), jnp.float32),
            jax.ShapeDtypeStruct((8, everyone), jnp.float32),
        ],
        compiler_params=params,
    )(spot, mine, from_x, all_facts)
    posterior = pl.pallas_call(
        functools.partial(final_kernel, chips),
        in_specs=[vmem] * (chips + 3),
        out_specs=vmem,
        out_shape=jax.ShapeDtypeStruct((capacity, 2 * orientations), jnp.float32),
        compiler_params=params,
    )(*parts, tops, slots, chosen)
    return posterior.reshape(1, 1, capacity, -1)


def spread_max(member, is_live, values):
    picked = jnp.max(jnp.where(member, values[None, :], FLOOR), axis=1)
    return jnp.where(is_live, picked, 0.0)


def collect_sums(member, expo):
    return jnp.sum(jnp.where(member, jnp.sum(expo, axis=1)[:, None], 0.0), axis=0)


def shards(images, defocus, block_ids, noise_weight, panels):
    per_device = images.shape[1]
    columns = images.shape[3]
    devices = lax.axis_size("orient")
    local_search = block_ids.shape[2]
    slots_each = min(per_device, max(2, 2 * per_device * local_search // devices))
    capacity = slots_each * devices
    everyone = per_device * devices
    all_lists = lax.all_gather(block_ids[0], "orient", axis=0, tiled=True)
    all_rows, all_focus = (
        lax.all_gather(images[0], "orient", axis=0, tiled=True),
        lax.all_gather(defocus[0], "orient", axis=0, tiled=True),
    )
    own_block = lax.axis_index("orient")
    block_hits = (
        jnp.any(all_lists == own_block, axis=1).astype(jnp.int32).reshape(devices, per_device)
    )
    slot_rank = jnp.cumsum(block_hits, axis=1) - block_hits
    places = (jnp.arange(devices, dtype=jnp.int32)[:, None] * slots_each + slot_rank).reshape(
        everyone
    )
    chosen = (places[None, :] == jnp.arange(capacity, dtype=jnp.int32)[:, None]) & (
        block_hits.reshape(everyone)[None, :] == 1
    )
    is_live = jnp.any(chosen, axis=1)
    slot_owner = jnp.sum(
        jnp.where(chosen, jnp.arange(everyone, dtype=jnp.int32)[None, :], 0), axis=1
    )
    slot_rows = jnp.take(all_rows, slot_owner, axis=0)
    slot_focus = jnp.take(all_focus, slot_owner, axis=0).astype(jnp.float32)
    frequency = (jnp.arange(columns, dtype=jnp.float32) + 0.5) / columns
    contrast = -jnp.sin(CTF_PHASE * slot_focus[:, None] * frequency[None, :] + 0.1)
    weighted = contrast * noise_weight[None, :]
    scaled_rows = (weighted[:, None, :] * slot_rows.astype(jnp.float32)).astype(jnp.bfloat16)
    energy = (contrast * weighted).astype(jnp.bfloat16)
    piece = lax.all_gather(panels[:, 0], "cls", axis=0, tiled=True)
    widened = piece.astype(jnp.float32)
    squared = (widened * widened).astype(jnp.bfloat16)
    correlate = jnp.einsum("srk,cjrk->scj", scaled_rows, piece, preferred_element_type=jnp.float32)
    energy_term = jnp.einsum("sk,cjrk->scj", energy, squared, preferred_element_type=jnp.float32)
    terms = correlate - 0.5 * energy_term
    combined = terms.reshape(capacity, -1)
    scores = lax.psum_scatter(combined, "rep", scatter_dimension=1, tiled=True)
    member = (slot_owner[:, None] == jnp.arange(everyone, dtype=jnp.int32)[None, :]) & is_live[
        :, None
    ]
    slot_top = jnp.max(scores, axis=1)
    local_peak = jnp.max(jnp.where(member, slot_top[:, None], FLOOR), axis=0)
    peak = lax.pmax(local_peak, ("orient", "rep"))
    slot_peak = spread_max(member, is_live, peak)
    expo = jnp.where(is_live[:, None], jnp.exp(scores - slot_peak[:, None]), 0.0)
    total = lax.psum(collect_sums(member, expo), ("orient", "rep"))
    slot_total = jnp.where(is_live, jnp.sum(jnp.where(member, total[None, :], 0.0), axis=1), 1.0)
    posterior = expo / slot_total[:, None]
    return posterior.reshape(1, 1, capacity, -1)


def solution(mesh):
    in_specs = (
        P(("batch", "cls"), "orient", "rep", None),
        P(("batch", "cls"), "orient"),
        P(("batch", "cls"), "orient", None),
        P(),
        P(("batch", "cls"), "orient", None, "rep", None),
    )
    out_specs = P(("batch", "cls"), "orient", None, "rep")
    sizes = mesh.shape
    paired = sizes["rep"] == 1 and sizes["cls"] == 2 and sizes["orient"] in (4, 8, 16, 32)
    return jax.shard_map(
        chip_shards if paired else shards,
        mesh=mesh,
        in_specs=in_specs,
        out_specs=out_specs,
        check_vma=False,
    )
```

```python
import functools

import jax
import jax.numpy as jnp
from jax import lax
from jax.experimental import pallas as pl
from jax.experimental.pallas import tpu as pltpu
from jax.sharding import PartitionSpec as P

CTF_PHASE = 40.0
FLOOR = -1e30
LANES = 128
VMEM_LIMIT = 8 * 1024 * 1024
SCHEDULING_WEIGHT = 20 * 10**9


def sin_cos(angle):
    turns = jnp.floor(angle * 0.6366197723675814 + 0.5)
    rest = angle - turns * 1.5703125
    rest = rest - turns * 4.837512969970703e-4
    rest = rest - turns * 7.549789948768648e-8
    square = rest * rest
    sine = rest + rest * square * (
        -1.6666654611e-1 + square * (8.3321608736e-3 - square * 1.9515295891e-4)
    )
    cosine = (
        1.0
        - 0.5 * square
        + square
        * square
        * (4.166664568298827e-2 + square * (-1.388731625493765e-3 + square * 2.443315711809948e-5))
    )
    quarter = turns.astype(jnp.int32)
    odd = (quarter & 1) == 1
    low = jnp.where(odd, cosine, sine)
    high = jnp.where(odd, sine, cosine)
    return (
        jnp.where((quarter & 2) == 2, -low, low),
        jnp.where(((quarter + 1) & 2) == 2, -high, high),
    )


def panel_kernel(spot, sides, own, given):
    own[...] = sides[spot[2]]
    given[...] = sides[1 - spot[2]]


def square_kernel(own, squares):
    squares[...] = own[...] * own[...]


def row_kernel(spot, planes, facts, kept, given, padded):
    core = spot[2]
    columns = planes.shape[2]
    padded[...] = jnp.zeros_like(padded)
    padded[: facts.shape[0], : facts.shape[1]] = facts[...]
    for half, out in ((core, kept), (1 - core, given)):
        out[:, :columns] = planes[half]
        out[:, columns:] = padded[...].astype(out.dtype)


def particle_facts(meta):
    return jnp.concatenate([m[...].astype(jnp.float32).T[: m.shape[0]] for m in meta], axis=0)


def add_scores(rows, noise, own_panel, own_squares, mate_panel, turn_sin, turn_cos, sums, segments):
    columns = noise.shape[1]
    width = columns // segments
    tiles = width // LANES
    count = turn_sin.shape[0]
    facts = particle_facts([r.at[:, pl.ds(columns, LANES)] for r in rows])
    rate = jnp.broadcast_to(CTF_PHASE * facts[:, 0:1], (count, LANES))
    lane = lax.broadcasted_iota(jnp.int32, (count, LANES), 1).astype(jnp.float32)
    first_sin, first_cos = sin_cos(rate * ((lane + 0.5) / columns) + 0.1)
    step_sin, step_cos = sin_cos(rate * (LANES / columns))
    turn_sin[...] = step_sin
    turn_cos[...] = step_cos
    for total in sums:
        total[...] = jnp.zeros_like(total)

    def segment(index, carry):
        sine, cosine = carry
        start = pl.multiple_of(index * width, LANES)
        scaled_parts, energy_parts = [], []
        for t in range(tiles):
            window = pl.ds(start + t * LANES, LANES)
            weighted = sine * noise[:, window]
            image = jnp.concatenate([r[:, window] for r in rows], axis=0).astype(jnp.float32)
            scaled_parts.append((weighted * image).astype(jnp.bfloat16))
            energy_parts.append((sine * weighted).astype(jnp.bfloat16))
            ds, dc = turn_sin[...], turn_cos[...]
            sine, cosine = sine * dc + cosine * ds, cosine * dc - sine * ds
        scaled = jnp.concatenate(scaled_parts, axis=1)
        energy = jnp.concatenate(energy_parts, axis=1)
        contract = (((1,), (1,)), ((), ()))
        whole = pl.ds(start, width)
        mate = mate_panel[:, whole]
        for values, squared, total in (
            (own_panel[:, whole], own_squares[:, whole], sums[0]),
            (mate, mate * mate, sums[1]),
        ):
            correlate = lax.dot_general(
                values, scaled, contract, preferred_element_type=jnp.float32
            )
            power = lax.dot_general(squared, energy, contract, preferred_element_type=jnp.float32)
            total[...] += correlate - 0.5 * power
        return sine, cosine

    lax.fori_loop(0, segments, segment, (-first_sin, -first_cos))
    return jnp.pad(facts, ((0, 0), (0, LANES - facts.shape[1])))


def batch_kernel(n, segments, spot, *refs):
    rows = refs[:n]
    noise, own_panel, own_squares, mate_panel = refs[n : n + 4]
    own_out, mate_out, fact_out, turn_sin, turn_cos, *sums = refs[n + 4 :]
    fact_out[...] = add_scores(
        rows, noise, own_panel, own_squares, mate_panel, turn_sin, turn_cos, sums, segments
    )
    own_out[...] = sums[0][...].T
    mate_out[...] = sums[1][...].T


def last_kernel(n, segments, orders, spot, *refs):
    rows = refs[:n]
    noise, own_panel, own_squares, mate_panel = refs[n : n + 4]
    rest = refs[n + 4 :]
    earlier, rest = rest[: 3 * (len(orders) - 1)], rest[3 * (len(orders) - 1) :]
    partial, facts, turn_sin, turn_cos, *sums = rest
    last_facts = add_scores(
        rows, noise, own_panel, own_squares, mate_panel, turn_sin, turn_cos, sums, segments
    )
    position, core = spot[1], spot[2]
    each = rows[0].shape[0]
    ring = facts.shape[0] // (2 * each)
    half = ring // 2
    for index, order in enumerate(orders):
        if index < len(orders) - 1:
            own, mate, fact = [r[...] for r in earlier[3 * index : 3 * index + 3]]
        else:
            own, mate, fact = sums[0][...].T, sums[1][...].T, last_facts
        for k, (distance, crossed) in enumerate(order):
            place = lax.rem(position + distance + ring, ring)
            far = place >= half
            level = jnp.where(far, ring - 1 - place, place)
            device = 2 * level + (1 - core if crossed else core)
            start = pl.multiple_of((jnp.where(far, ring, 0) + device) * each, each)
            piece = slice(k * each, (k + 1) * each)
            partial[core, pl.ds(start, each), :] = own[piece]
            partial[1 - core, pl.ds(start, each), :] = mate[piece]
            facts[pl.ds(start, each), :] = fact[piece]


def score_call(chunks, orders, earlier, spot, noise, own_panel, squares, mate_panel):
    each = chunks[0].shape[0]
    orientations, columns = own_panel.shape
    whole = columns // LANES
    segments = next(s for s in (3, 2, 4, 5, 6, 7, 1) if whole % s == 0)
    n = len(chunks)
    count = each * n
    scratch = [pltpu.VMEM((count, LANES), jnp.float32)] * 2
    scratch += [pltpu.VMEM((orientations, count), jnp.float32)] * 2
    single = jax.ShapeDtypeStruct((count, orientations), jnp.float32)
    if orders is None:
        kernel = functools.partial(batch_kernel, n, segments)
        out_shape = [single, single, jax.ShapeDtypeStruct((count, LANES), jnp.float32)]
        extra = []
    else:
        everyone = each * sum(len(o) for o in orders)
        kernel = functools.partial(last_kernel, n, segments, orders)
        out_shape = [
            jax.ShapeDtypeStruct((2, everyone, orientations), jnp.float32),
            jax.ShapeDtypeStruct((everyone, LANES), jnp.float32),
        ]
        extra = [e for triple in earlier for e in triple]
    vmem = pl.BlockSpec(memory_space=pltpu.VMEM)
    return pl.pallas_call(
        kernel,
        in_specs=[pl.BlockSpec(memory_space=pltpu.SMEM)] + [vmem] * (n + 4 + len(extra)),
        out_specs=[vmem] * len(out_shape),
        out_shape=out_shape,
        scratch_shapes=scratch,
        compiler_params=pltpu.CompilerParams(vmem_limit_bytes=VMEM_LIMIT),
        cost_estimate=pl.CostEstimate(
            flops=8 * max(count, 128) * orientations * columns,
            bytes_accessed=4 * orientations * columns + 2 * count * columns,
            transcendentals=0,
        ),
    )(spot, *chunks, noise, own_panel, squares, mate_panel, *extra)


def names_block(facts, search, block):
    lane = lax.broadcasted_iota(jnp.int32, facts.shape, 1)
    match = (lane >= 1) & (lane <= search) & (facts == block.astype(jnp.float32))
    return jnp.max(jnp.where(match, 1.0, 0.0), axis=1, keepdims=True) > 0.0


def chip_kernel(search, spot, partial, mate, facts, mine, across, stats):
    group, core, place = spot[0], spot[2], spot[3]
    count = mine.shape[0]
    lane = lax.broadcasted_iota(jnp.int32, (count, LANES), 1)
    pairs = []
    for relative in range(2):
        side = group if relative == 0 else 1 - group
        window = pl.ds(pl.multiple_of(side * count, count), count)
        listed = facts[window, :]
        masked = []
        for crossed in range(2):
            block = core if crossed == 0 else 1 - core
            scores = partial[block, window, :] + mate[block, window, :]
            if crossed == 0:
                out = mine if relative == 0 else across
                out[...] = scores
            named = names_block(listed, search, place - core + block)
            masked.append(jnp.where(named, scores, FLOOR))
        top = jnp.max(jnp.maximum(*masked), axis=1, keepdims=True)
        terms = [jnp.where(m > FLOOR, jnp.exp(m - top), 0.0) for m in masked]
        total = jnp.sum(terms[0] + terms[1], axis=1, keepdims=True)
        pairs.append(jnp.where(lane == relative, top, jnp.where(lane == 2 + relative, total, 0.0)))
    stats[...] = (pairs[0] + pairs[1]).T[: stats.shape[0]]


def slot_kernel(search, slots_each, each, spot, mine, across, facts, slots, chosen, tops):
    group, place = spot[0], spot[3]
    count = mine.shape[0]
    same, other = mine[...], across[...]
    first = group == 0
    scores = jnp.concatenate(
        [jnp.where(first, same, other), jnp.where(first, other, same)], axis=1
    )
    listed = facts[pl.ds(pl.multiple_of(group * count, count), count), :]
    named = names_block(listed, search, place)
    hit = jnp.where(named, 1.0, 0.0)
    row = lax.broadcasted_iota(jnp.int32, (count, LANES), 0)
    line = lax.broadcasted_iota(jnp.int32, (count, count), 0)
    column = lax.broadcasted_iota(jnp.int32, (count, count), 1)
    before = (column < line) & (column // each == line // each)
    rank = jnp.dot(
        jnp.where(before, 1.0, 0.0).astype(jnp.bfloat16),
        jnp.broadcast_to(hit, (count, LANES)).astype(jnp.bfloat16),
        preferred_element_type=jnp.float32,
    )
    slot = (row // each) * slots_each + rank.astype(jnp.int32)
    capacity = chosen.shape[0]
    if capacity != LANES:
        slot = jnp.broadcast_to(slot[:, :1], (count, capacity))
    target = lax.broadcasted_iota(jnp.int32, (count, capacity), 1)
    taken = jnp.where((slot == target) & named, 1.0, 0.0)
    top = jnp.max(scores, axis=1, keepdims=True)
    tops[...] = jnp.broadcast_to(top, (count, LANES)).T[: tops.shape[0]]
    terms = jnp.where(named, jnp.exp(scores - top), 0.0)
    slots[...] = lax.dot_general(
        taken,
        terms,
        (((0,), (0,)), ((), ())),
        precision=lax.Precision.HIGHEST,
        preferred_element_type=jnp.float32,
    )
    chosen[...] = taken.T


def final_kernel(n, *refs):
    parts, (tops, slots, chosen, out) = refs[:n], refs[n:]
    peak = functools.reduce(jnp.maximum, [p[0:1, :] for p in parts])
    shares = [p[1:2, :] * jnp.exp(p[0:1, :] - peak) for p in parts]
    total = functools.reduce(jnp.add, shares)
    factor = jnp.exp(jnp.minimum(tops[0:1, :] - peak, 0.0)) / total
    scale = jnp.sum(chosen[...] * factor, axis=1, keepdims=True)
    out[...] = slots[...] * scale


def chip_shards(images, defocus, block_ids, noise_weight, panels):
    per_device, halves, columns = images.shape[1:]
    devices = lax.axis_size("orient")
    chips = devices // 2
    ring = 2 * chips
    everyone = per_device * devices
    local_search = block_ids.shape[2]
    orientations = panels.shape[2]
    slots_each = min(per_device, max(2, 2 * per_device * local_search // devices))
    capacity = slots_each * devices
    place = lax.axis_index("orient")
    group = lax.axis_index("cls")
    chip, core = place // 2, place % 2
    position = jnp.where(group == 0, chip, ring - 1 - chip)
    spot = jnp.stack([group, position, core, place]).astype(jnp.int32)
    first = core == 0

    mate_pairs = [(d, d ^ 1) for d in range(devices)]
    x_pairs = [(0, 1), (1, 0)]

    def joint(place, core):
        place = place % ring
        far = place >= chips
        level = ring - 1 - place if far else place
        return (2 * level + core) * 2 + int(far)

    def forward(values, step, cross=0):
        pairs = [(joint(p, c), joint(p + step, c ^ cross)) for p in range(ring) for c in range(2)]
        return lax.ppermute(values, ("orient", "cls"), pairs)

    vmem = pl.BlockSpec(memory_space=pltpu.VMEM)
    smem = pl.BlockSpec(memory_space=pltpu.SMEM)
    params = pltpu.CompilerParams(vmem_limit_bytes=VMEM_LIMIT)
    planes = lax.optimization_barrier(jnp.transpose(images[0], (1, 0, 2)))
    row_shape = jax.ShapeDtypeStruct((per_device, columns + LANES), jnp.bfloat16)
    facts = jnp.concatenate([defocus, jnp.transpose(block_ids[0])], axis=0, dtype=jnp.float32)
    kept, given = pl.pallas_call(
        row_kernel,
        in_specs=[smem, vmem, vmem],
        out_specs=[vmem] * 2,
        out_shape=[row_shape] * 2,
        scratch_shapes=[pltpu.VMEM((per_device, LANES), jnp.float32)],
        compiler_params=params,
    )(spot, planes, facts)
    with jax.named_scope("mate_rows"):
        got = lax.ppermute(given, "orient", mate_pairs)

    _, panels = lax.optimization_barrier((kept, panels))
    sides = lax.optimization_barrier(jnp.transpose(panels[0, 0], (1, 0, 2)))
    panel_shape = jax.ShapeDtypeStruct(sides.shape[1:], sides.dtype)
    own_panel, given_panel = pl.pallas_call(
        panel_kernel,
        in_specs=[smem, vmem],
        out_specs=[vmem] * 2,
        out_shape=[panel_shape] * 2,
        compiler_params=params,
    )(spot, sides)
    with jax.named_scope("mate_panel"):
        mate_panel = lax.ppermute(given_panel, "orient", mate_pairs)

    noise = noise_weight[None, :]
    waiting = [((0, False), kept), ((0, True), got)]
    ahead = {False: kept, True: given}
    behind = {False: kept, True: given}
    orders, earlier, late = [], [], []
    squares = pl.pallas_call(
        square_kernel,
        in_specs=[vmem],
        out_specs=vmem,
        out_shape=panel_shape,
        compiler_params=params,
        cost_estimate=pl.CostEstimate(flops=SCHEDULING_WEIGHT, bytes_accessed=0, transcendentals=0),
    )(own_panel)
    score = lambda c: score_call(c, None, None, spot, noise, own_panel, squares, mate_panel)
    for step in range(1, chips + 1):
        if step == 3:
            orders.append([key for key, _ in waiting])
            earlier.append(score([c for _, c in waiting]))
            waiting = []
            for chain, c in ((ahead, False), (behind, True)):
                chain[c] = lax.optimization_barrier((chain[c], earlier[-1][2]))[0]
        if step == 2:
            for chain, c in ((ahead, False), (behind, True)):
                chain[c] = lax.optimization_barrier((chain[c], squares))[0]
        waiting = waiting + late
        late = []
        for crossed in (False, True):
            if step < chips or not crossed:
                with jax.named_scope("rows_ahead"):
                    ahead[crossed] = forward(ahead[crossed], 1, int(crossed and step == 1))
                late.append(((-step, crossed), ahead[crossed]))
            if step < chips or crossed:
                with jax.named_scope("rows_behind"):
                    behind[crossed] = forward(behind[crossed], -1, int(crossed and step == 1))
                late.append(((step, crossed), behind[crossed]))
    orders.append([key for key, _ in waiting])
    earlier.append(score([c for _, c in waiting]))
    waiting = late
    orders.append([key for key, _ in waiting])
    partial, all_facts = score_call(
        [c for _, c in waiting], orders, earlier, spot, noise, own_panel, squares, mate_panel
    )

    mate_partial = lax.ppermute(partial, "orient", mate_pairs)
    mine, across, stats = pl.pallas_call(
        functools.partial(chip_kernel, local_search),
        in_specs=[smem] + [vmem] * 3,
        out_specs=[vmem] * 3,
        out_shape=[
            jax.ShapeDtypeStruct((everyone, orientations), jnp.float32),
            jax.ShapeDtypeStruct((everyone, orientations), jnp.float32),
            jax.ShapeDtypeStruct((8, everyone), jnp.float32),
        ],
        compiler_params=params,
    )(spot, partial, mate_partial, all_facts)

    x_stats = lax.ppermute(stats, "cls", x_pairs)
    across, _ = lax.optimization_barrier((across, stats))
    from_x = lax.ppermute(across, "cls", x_pairs)
    peak = jnp.maximum(stats[0], x_stats[1])
    total = stats[2] * jnp.exp(stats[0] - peak) + x_stats[3] * jnp.exp(x_stats[1] - peak)
    pair = jnp.pad(jnp.stack([peak, total]), ((0, 6), (0, 0)))
    if chips == 4:
        near = lax.ppermute(pair, "orient", [(d, d ^ (2 << d % 2)) for d in range(devices)])
        far = lax.ppermute(pair, "orient", [(d, d ^ 6) for d in range(devices)])
        parts = [pair, near, lax.ppermute(near, "orient", mate_pairs), far]
    else:
        parts = [pair] + [
            lax.ppermute(pair, "orient", [(d, (d + 2 * s) % devices) for d in range(devices)])
            for s in range(1, chips)
        ]
    slots, chosen, tops = pl.pallas_call(
        functools.partial(slot_kernel, local_search, slots_each, per_device),
        in_specs=[smem] + [vmem] * 3,
        out_specs=[vmem] * 3,
        out_shape=[
            jax.ShapeDtypeStruct((capacity, 2 * orientations), jnp.float32),
            jax.ShapeDtypeStruct((capacity, everyone), jnp.float32),
            jax.ShapeDtypeStruct((8, everyone), jnp.float32),
        ],
        compiler_params=params,
    )(spot, mine, from_x, all_facts)
    posterior = pl.pallas_call(
        functools.partial(final_kernel, chips),
        in_specs=[vmem] * (chips + 3),
        out_specs=vmem,
        out_shape=jax.ShapeDtypeStruct((capacity, 2 * orientations), jnp.float32),
        compiler_params=params,
    )(*parts, tops, slots, chosen)
    return posterior.reshape(1, 1, capacity, -1)


def spread_max(member, is_live, values):
    picked = jnp.max(jnp.where(member, values[None, :], FLOOR), axis=1)
    return jnp.where(is_live, picked, 0.0)


def collect_sums(member, expo):
    return jnp.sum(jnp.where(member, jnp.sum(expo, axis=1)[:, None], 0.0), axis=0)


def shards(images, defocus, block_ids, noise_weight, panels):
    per_device = images.shape[1]
    columns = images.shape[3]
    devices = lax.axis_size("orient")
    local_search = block_ids.shape[2]
    slots_each = min(per_device, max(2, 2 * per_device * local_search // devices))
    capacity = slots_each * devices
    everyone = per_device * devices
    all_lists = lax.all_gather(block_ids[0], "orient", axis=0, tiled=True)
    all_rows, all_focus = (
        lax.all_gather(images[0], "orient", axis=0, tiled=True),
        lax.all_gather(defocus[0], "orient", axis=0, tiled=True),
    )
    own_block = lax.axis_index("orient")
    block_hits = (
        jnp.any(all_lists == own_block, axis=1).astype(jnp.int32).reshape(devices, per_device)
    )
    slot_rank = jnp.cumsum(block_hits, axis=1) - block_hits
    places = (jnp.arange(devices, dtype=jnp.int32)[:, None] * slots_each + slot_rank).reshape(
        everyone
    )
    chosen = (places[None, :] == jnp.arange(capacity, dtype=jnp.int32)[:, None]) & (
        block_hits.reshape(everyone)[None, :] == 1
    )
    is_live = jnp.any(chosen, axis=1)
    slot_owner = jnp.sum(
        jnp.where(chosen, jnp.arange(everyone, dtype=jnp.int32)[None, :], 0), axis=1
    )
    slot_rows = jnp.take(all_rows, slot_owner, axis=0)
    slot_focus = jnp.take(all_focus, slot_owner, axis=0).astype(jnp.float32)
    frequency = (jnp.arange(columns, dtype=jnp.float32) + 0.5) / columns
    contrast = -jnp.sin(CTF_PHASE * slot_focus[:, None] * frequency[None, :] + 0.1)
    weighted = contrast * noise_weight[None, :]
    scaled_rows = (weighted[:, None, :] * slot_rows.astype(jnp.float32)).astype(jnp.bfloat16)
    energy = (contrast * weighted).astype(jnp.bfloat16)
    piece = lax.all_gather(panels[:, 0], "cls", axis=0, tiled=True)
    widened = piece.astype(jnp.float32)
    squared = (widened * widened).astype(jnp.bfloat16)
    correlate = jnp.einsum("srk,cjrk->scj", scaled_rows, piece, preferred_element_type=jnp.float32)
    energy_term = jnp.einsum("sk,cjrk->scj", energy, squared, preferred_element_type=jnp.float32)
    terms = correlate - 0.5 * energy_term
    combined = terms.reshape(capacity, -1)
    scores = lax.psum_scatter(combined, "rep", scatter_dimension=1, tiled=True)
    member = (slot_owner[:, None] == jnp.arange(everyone, dtype=jnp.int32)[None, :]) & is_live[
        :, None
    ]
    slot_top = jnp.max(scores, axis=1)
    local_peak = jnp.max(jnp.where(member, slot_top[:, None], FLOOR), axis=0)
    peak = lax.pmax(local_peak, ("orient", "rep"))
    slot_peak = spread_max(member, is_live, peak)
    expo = jnp.where(is_live[:, None], jnp.exp(scores - slot_peak[:, None]), 0.0)
    total = lax.psum(collect_sums(member, expo), ("orient", "rep"))
    slot_total = jnp.where(is_live, jnp.sum(jnp.where(member, total[None, :], 0.0), axis=1), 1.0)
    posterior = expo / slot_total[:, None]
    return posterior.reshape(1, 1, capacity, -1)


def solution(mesh):
    in_specs = (
        P(("batch", "cls"), "orient", "rep", None),
        P(("batch", "cls"), "orient"),
        P(("batch", "cls"), "orient", None),
        P(),
        P(("batch", "cls"), "orient", None, "rep", None),
    )
    out_specs = P(("batch", "cls"), "orient", None, "rep")
    sizes = mesh.shape
    paired = sizes["rep"] == 1 and sizes["cls"] == 2 and sizes["orient"] in (4, 8, 16, 32)
    return jax.shard_map(
        chip_shards if paired else shards,
        mesh=mesh,
        in_specs=in_specs,
        out_specs=out_specs,
        check_vma=False,
    )
```

```python
import functools

import jax
import jax.numpy as jnp
from jax import lax
from jax.experimental import pallas as pl
from jax.experimental.pallas import tpu as pltpu
from jax.sharding import PartitionSpec as P

CTF_PHASE = 40.0
FLOOR = -1e30
LANES = 128
VMEM_LIMIT = 8 * 1024 * 1024
SCHEDULING_WEIGHT = 20 * 10**9


def sin_cos(angle):
    turns = jnp.floor(angle * 0.6366197723675814 + 0.5)
    rest = angle - turns * 1.5703125
    rest = rest - turns * 4.837512969970703e-4
    rest = rest - turns * 7.549789948768648e-8
    square = rest * rest
    sine = rest + rest * square * (
        -1.6666654611e-1 + square * (8.3321608736e-3 - square * 1.9515295891e-4)
    )
    cosine = (
        1.0
        - 0.5 * square
        + square
        * square
        * (4.166664568298827e-2 + square * (-1.388731625493765e-3 + square * 2.443315711809948e-5))
    )
    quarter = turns.astype(jnp.int32)
    odd = (quarter & 1) == 1
    low = jnp.where(odd, cosine, sine)
    high = jnp.where(odd, sine, cosine)
    return (
        jnp.where((quarter & 2) == 2, -low, low),
        jnp.where(((quarter + 1) & 2) == 2, -high, high),
    )


def panel_kernel(spot, sides, own, given):
    own[...] = sides[spot[2]]
    given[...] = sides[1 - spot[2]]


def square_kernel(own, squares):
    squares[...] = own[...] * own[...]


def particle_facts(meta):
    return jnp.concatenate([m[...].astype(jnp.float32).T[: m.shape[0]] for m in meta], axis=0)


def add_scores(rows, noise, own_panel, own_squares, mate_panel, turn_sin, turn_cos, sums, segments):
    columns = noise.shape[1]
    width = columns // segments
    tiles = width // LANES
    count = turn_sin.shape[0]
    facts = particle_facts([r.at[:, pl.ds(columns, LANES)] for r in rows])
    rate = jnp.broadcast_to(CTF_PHASE * facts[:, 0:1], (count, LANES))
    lane = lax.broadcasted_iota(jnp.int32, (count, LANES), 1).astype(jnp.float32)
    first_sin, first_cos = sin_cos(rate * ((lane + 0.5) / columns) + 0.1)
    step_sin, step_cos = sin_cos(rate * (LANES / columns))
    turn_sin[...] = step_sin
    turn_cos[...] = step_cos
    for total in sums:
        total[...] = jnp.zeros_like(total)

    def segment(index, carry):
        sine, cosine = carry
        start = pl.multiple_of(index * width, LANES)
        scaled_parts, energy_parts = [], []
        for t in range(tiles):
            window = pl.ds(start + t * LANES, LANES)
            weighted = sine * noise[:, window]
            image = jnp.concatenate([r[:, window] for r in rows], axis=0).astype(jnp.float32)
            scaled_parts.append((weighted * image).astype(jnp.bfloat16))
            energy_parts.append((sine * weighted).astype(jnp.bfloat16))
            ds, dc = turn_sin[...], turn_cos[...]
            sine, cosine = sine * dc + cosine * ds, cosine * dc - sine * ds
        scaled = jnp.concatenate(scaled_parts, axis=1)
        energy = jnp.concatenate(energy_parts, axis=1)
        contract = (((1,), (1,)), ((), ()))
        whole = pl.ds(start, width)
        mate = mate_panel[:, whole]
        for values, squared, total in (
            (own_panel[:, whole], own_squares[:, whole], sums[0]),
            (mate, mate * mate, sums[1]),
        ):
            correlate = lax.dot_general(
                values, scaled, contract, preferred_element_type=jnp.float32
            )
            power = lax.dot_general(squared, energy, contract, preferred_element_type=jnp.float32)
            total[...] += correlate - 0.5 * power
        return sine, cosine

    lax.fori_loop(0, segments, segment, (-first_sin, -first_cos))
    return jnp.pad(facts, ((0, 0), (0, LANES - facts.shape[1])))


def batch_kernel(n, segments, spot, *refs):
    rows = refs[:n]
    noise, own_panel, own_squares, mate_panel = refs[n : n + 4]
    own_out, mate_out, fact_out, turn_sin, turn_cos, *sums = refs[n + 4 :]
    fact_out[...] = add_scores(
        rows, noise, own_panel, own_squares, mate_panel, turn_sin, turn_cos, sums, segments
    )
    own_out[...] = sums[0][...].T
    mate_out[...] = sums[1][...].T


def last_kernel(n, segments, orders, spot, *refs):
    rows = refs[:n]
    noise, own_panel, own_squares, mate_panel = refs[n : n + 4]
    rest = refs[n + 4 :]
    earlier, rest = rest[: 3 * (len(orders) - 1)], rest[3 * (len(orders) - 1) :]
    partial, facts, turn_sin, turn_cos, *sums = rest
    last_facts = add_scores(
        rows, noise, own_panel, own_squares, mate_panel, turn_sin, turn_cos, sums, segments
    )
    position, core = spot[1], spot[2]
    each = rows[0].shape[0]
    ring = facts.shape[0] // (2 * each)
    half = ring // 2
    for index, order in enumerate(orders):
        if index < len(orders) - 1:
            own, mate, fact = [r[...] for r in earlier[3 * index : 3 * index + 3]]
        else:
            own, mate, fact = sums[0][...].T, sums[1][...].T, last_facts
        for k, (distance, crossed) in enumerate(order):
            place = lax.rem(position + distance + ring, ring)
            far = place >= half
            level = jnp.where(far, ring - 1 - place, place)
            device = 2 * level + (1 - core if crossed else core)
            start = pl.multiple_of((jnp.where(far, ring, 0) + device) * each, each)
            piece = slice(k * each, (k + 1) * each)
            partial[core, pl.ds(start, each), :] = own[piece]
            partial[1 - core, pl.ds(start, each), :] = mate[piece]
            facts[pl.ds(start, each), :] = fact[piece]


def score_call(chunks, orders, earlier, spot, noise, own_panel, squares, mate_panel):
    each = chunks[0].shape[0]
    orientations, columns = own_panel.shape
    whole = columns // LANES
    segments = 1
    n = len(chunks)
    count = each * n
    scratch = [pltpu.VMEM((count, LANES), jnp.float32)] * 2
    scratch += [pltpu.VMEM((orientations, count), jnp.float32)] * 2
    single = jax.ShapeDtypeStruct((count, orientations), jnp.float32)
    if orders is None:
        kernel = functools.partial(batch_kernel, n, segments)
        out_shape = [single, single, jax.ShapeDtypeStruct((count, LANES), jnp.float32)]
        extra = []
    else:
        everyone = each * sum(len(o) for o in orders)
        kernel = functools.partial(last_kernel, n, segments, orders)
        out_shape = [
            jax.ShapeDtypeStruct((2, everyone, orientations), jnp.float32),
            jax.ShapeDtypeStruct((everyone, LANES), jnp.float32),
        ]
        extra = [e for triple in earlier for e in triple]
    vmem = pl.BlockSpec(memory_space=pltpu.VMEM)
    return pl.pallas_call(
        kernel,
        in_specs=[pl.BlockSpec(memory_space=pltpu.SMEM)] + [vmem] * (n + 4 + len(extra)),
        out_specs=[vmem] * len(out_shape),
        out_shape=out_shape,
        scratch_shapes=scratch,
        compiler_params=pltpu.CompilerParams(vmem_limit_bytes=VMEM_LIMIT),
        cost_estimate=pl.CostEstimate(
            flops=8 * max(count, 128) * orientations * columns,
            bytes_accessed=4 * orientations * columns + 2 * count * columns,
            transcendentals=0,
        ),
    )(spot, *chunks, noise, own_panel, squares, mate_panel, *extra)


def names_block(facts, search, block):
    lane = lax.broadcasted_iota(jnp.int32, facts.shape, 1)
    match = (lane >= 1) & (lane <= search) & (facts == block.astype(jnp.float32))
    return jnp.max(jnp.where(match, 1.0, 0.0), axis=1, keepdims=True) > 0.0


def chip_kernel(search, spot, partial, mate, facts, mine, across, stats):
    group, core, place = spot[0], spot[2], spot[3]
    count = mine.shape[0]
    lane = lax.broadcasted_iota(jnp.int32, (count, LANES), 1)
    pairs = []
    for relative in range(2):
        side = group if relative == 0 else 1 - group
        window = pl.ds(pl.multiple_of(side * count, count), count)
        listed = facts[window, :]
        masked = []
        for crossed in range(2):
            block = core if crossed == 0 else 1 - core
            scores = partial[block, window, :] + mate[block, window, :]
            if crossed == 0:
                out = mine if relative == 0 else across
                out[...] = scores
            named = names_block(listed, search, place - core + block)
            masked.append(jnp.where(named, scores, FLOOR))
        top = jnp.max(jnp.maximum(*masked), axis=1, keepdims=True)
        terms = [jnp.where(m > FLOOR, jnp.exp(m - top), 0.0) for m in masked]
        total = jnp.sum(terms[0] + terms[1], axis=1, keepdims=True)
        pairs.append(jnp.where(lane == relative, top, jnp.where(lane == 2 + relative, total, 0.0)))
    stats[...] = (pairs[0] + pairs[1]).T[: stats.shape[0]]


def slot_kernel(search, slots_each, each, spot, mine, across, facts, slots, chosen, tops):
    group, place = spot[0], spot[3]
    count = mine.shape[0]
    same, other = mine[...], across[...]
    first = group == 0
    scores = jnp.concatenate(
        [jnp.where(first, same, other), jnp.where(first, other, same)], axis=1
    )
    listed = facts[pl.ds(pl.multiple_of(group * count, count), count), :]
    named = names_block(listed, search, place)
    hit = jnp.where(named, 1.0, 0.0)
    row = lax.broadcasted_iota(jnp.int32, (count, LANES), 0)
    line = lax.broadcasted_iota(jnp.int32, (count, count), 0)
    column = lax.broadcasted_iota(jnp.int32, (count, count), 1)
    before = (column < line) & (column // each == line // each)
    rank = jnp.dot(
        jnp.where(before, 1.0, 0.0).astype(jnp.bfloat16),
        jnp.broadcast_to(hit, (count, LANES)).astype(jnp.bfloat16),
        preferred_element_type=jnp.float32,
    )
    slot = (row // each) * slots_each + rank.astype(jnp.int32)
    capacity = chosen.shape[0]
    if capacity != LANES:
        slot = jnp.broadcast_to(slot[:, :1], (count, capacity))
    target = lax.broadcasted_iota(jnp.int32, (count, capacity), 1)
    taken = jnp.where((slot == target) & named, 1.0, 0.0)
    top = jnp.max(scores, axis=1, keepdims=True)
    tops[...] = jnp.broadcast_to(top, (count, LANES)).T[: tops.shape[0]]
    terms = jnp.where(named, jnp.exp(scores - top), 0.0)
    slots[...] = lax.dot_general(
        taken,
        terms,
        (((0,), (0,)), ((), ())),
        precision=lax.Precision.HIGHEST,
        preferred_element_type=jnp.float32,
    )
    chosen[...] = taken.T


def final_kernel(n, *refs):
    parts, (tops, slots, chosen, out) = refs[:n], refs[n:]
    peak = functools.reduce(jnp.maximum, [p[0:1, :] for p in parts])
    shares = [p[1:2, :] * jnp.exp(p[0:1, :] - peak) for p in parts]
    total = functools.reduce(jnp.add, shares)
    factor = jnp.exp(jnp.minimum(tops[0:1, :] - peak, 0.0)) / total
    scale = jnp.sum(chosen[...] * factor, axis=1, keepdims=True)
    out[...] = slots[...] * scale


def chip_shards(images, defocus, block_ids, noise_weight, panels):
    per_device, halves, columns = images.shape[1:]
    devices = lax.axis_size("orient")
    chips = devices // 2
    ring = 2 * chips
    everyone = per_device * devices
    local_search = block_ids.shape[2]
    orientations = panels.shape[2]
    slots_each = min(per_device, max(2, 2 * per_device * local_search // devices))
    capacity = slots_each * devices
    place = lax.axis_index("orient")
    group = lax.axis_index("cls")
    chip, core = place // 2, place % 2
    position = jnp.where(group == 0, chip, ring - 1 - chip)
    spot = jnp.stack([group, position, core, place]).astype(jnp.int32)

    mate_pairs = [(d, d ^ 1) for d in range(devices)]
    x_pairs = [(0, 1), (1, 0)]

    def joint(place, core):
        place = place % ring
        far = place >= chips
        level = ring - 1 - place if far else place
        return (2 * level + core) * 2 + int(far)

    def forward(values, step, cross=0):
        pairs = [(joint(p, c), joint(p + step, c ^ cross)) for p in range(ring) for c in range(2)]
        return lax.ppermute(values, ("orient", "cls"), pairs)

    vmem = pl.BlockSpec(memory_space=pltpu.VMEM)
    smem = pl.BlockSpec(memory_space=pltpu.SMEM)
    params = pltpu.CompilerParams(vmem_limit_bytes=VMEM_LIMIT)
    first = core == 0
    planes = lax.optimization_barrier(jnp.transpose(images[0], (1, 0, 2)))
    facts = jnp.concatenate([defocus, jnp.transpose(block_ids[0]).astype(jnp.bfloat16)], axis=0)
    facts = jnp.pad(facts, ((0, per_device - facts.shape[0]), (0, LANES - per_device)))
    kept = jnp.concatenate([jnp.where(first, planes[0], planes[1]), facts], axis=1)
    given = jnp.concatenate([jnp.where(first, planes[1], planes[0]), facts], axis=1)
    _, panels = lax.optimization_barrier((kept, panels))
    sides = lax.optimization_barrier(jnp.transpose(panels[0, 0], (1, 0, 2)))
    panel_shape = jax.ShapeDtypeStruct(sides.shape[1:], sides.dtype)
    own_panel, given_panel = pl.pallas_call(
        panel_kernel,
        in_specs=[smem, vmem],
        out_specs=[vmem] * 2,
        out_shape=[panel_shape] * 2,
        compiler_params=params,
    )(spot, sides)
    with jax.named_scope("mate_panel"):
        mate_panel = lax.ppermute(given_panel, "orient", mate_pairs)

    noise = noise_weight[None, :]
    waiting = []
    ahead = {False: kept, True: given}
    behind = {False: kept, True: given}
    orders, earlier, late = [], [], []
    squares = pl.pallas_call(
        square_kernel,
        in_specs=[vmem],
        out_specs=vmem,
        out_shape=panel_shape,
        compiler_params=params,
        cost_estimate=pl.CostEstimate(flops=SCHEDULING_WEIGHT, bytes_accessed=0, transcendentals=0),
    )(own_panel)
    score = lambda c: score_call(c, None, None, spot, noise, own_panel, squares, mate_panel)
    for step in range(1, chips + 1):
        if step == 3:
            orders.append([key for key, _ in waiting])
            earlier.append(score([c for _, c in waiting]))
            waiting = []
            for chain, c in ((ahead, False), (behind, True)):
                chain[c] = lax.optimization_barrier((chain[c], earlier[-1][2]))[0]
        if step == 2:
            for chain, c in ((ahead, False), (behind, True)):
                chain[c] = lax.optimization_barrier((chain[c], squares))[0]
        waiting = waiting + late
        late = []
        for crossed in (False, True):
            if step < chips or not crossed:
                with jax.named_scope("rows_ahead"):
                    ahead[crossed] = forward(ahead[crossed], 1, int(crossed and step == 1))
                late.append(((-step, crossed), ahead[crossed]))
            if step < chips or crossed:
                with jax.named_scope("rows_behind"):
                    behind[crossed] = forward(behind[crossed], -1, int(crossed and step == 1))
                late.append(((step, crossed), behind[crossed]))
        if step == 1:
            late_given, _ = lax.optimization_barrier((given, kept))
            with jax.named_scope("mate_rows"):
                got = lax.ppermute(late_given, "orient", mate_pairs)
            late = [((0, False), kept), ((0, True), got)] + late
    orders.append([key for key, _ in waiting])
    earlier.append(score([c for _, c in waiting]))
    waiting = late
    orders.append([key for key, _ in waiting])
    partial, all_facts = score_call(
        [c for _, c in waiting], orders, earlier, spot, noise, own_panel, squares, mate_panel
    )

    mate_partial = lax.ppermute(partial, "orient", mate_pairs)
    mine, across, stats = pl.pallas_call(
        functools.partial(chip_kernel, local_search),
        in_specs=[smem] + [vmem] * 3,
        out_specs=[vmem] * 3,
        out_shape=[
            jax.ShapeDtypeStruct((everyone, orientations), jnp.float32),
            jax.ShapeDtypeStruct((everyone, orientations), jnp.float32),
            jax.ShapeDtypeStruct((8, everyone), jnp.float32),
        ],
        compiler_params=params,
    )(spot, partial, mate_partial, all_facts)

    x_stats = lax.ppermute(stats, "cls", x_pairs)
    across, _ = lax.optimization_barrier((across, stats))
    from_x = lax.ppermute(across, "cls", x_pairs)
    peak = jnp.maximum(stats[0], x_stats[1])
    total = stats[2] * jnp.exp(stats[0] - peak) + x_stats[3] * jnp.exp(x_stats[1] - peak)
    pair = jnp.pad(jnp.stack([peak, total]), ((0, 6), (0, 0)))
    if chips == 4:
        near = lax.ppermute(pair, "orient", [(d, d ^ (2 << d % 2)) for d in range(devices)])
        far = lax.ppermute(pair, "orient", [(d, d ^ 6) for d in range(devices)])
        parts = [pair, near, lax.ppermute(near, "orient", mate_pairs), far]
    else:
        parts = [pair] + [
            lax.ppermute(pair, "orient", [(d, (d + 2 * s) % devices) for d in range(devices)])
            for s in range(1, chips)
        ]
    slots, chosen, tops = pl.pallas_call(
        functools.partial(slot_kernel, local_search, slots_each, per_device),
        in_specs=[smem] + [vmem] * 3,
        out_specs=[vmem] * 3,
        out_shape=[
            jax.ShapeDtypeStruct((capacity, 2 * orientations), jnp.float32),
            jax.ShapeDtypeStruct((capacity, everyone), jnp.float32),
            jax.ShapeDtypeStruct((8, everyone), jnp.float32),
        ],
        compiler_params=params,
    )(spot, mine, from_x, all_facts)
    posterior = pl.pallas_call(
        functools.partial(final_kernel, chips),
        in_specs=[vmem] * (chips + 3),
        out_specs=vmem,
        out_shape=jax.ShapeDtypeStruct((capacity, 2 * orientations), jnp.float32),
        compiler_params=params,
    )(*parts, tops, slots, chosen)
    return posterior.reshape(1, 1, capacity, -1)


def spread_max(member, is_live, values):
    picked = jnp.max(jnp.where(member, values[None, :], FLOOR), axis=1)
    return jnp.where(is_live, picked, 0.0)


def collect_sums(member, expo):
    return jnp.sum(jnp.where(member, jnp.sum(expo, axis=1)[:, None], 0.0), axis=0)


def shards(images, defocus, block_ids, noise_weight, panels):
    per_device = images.shape[1]
    columns = images.shape[3]
    devices = lax.axis_size("orient")
    local_search = block_ids.shape[2]
    slots_each = min(per_device, max(2, 2 * per_device * local_search // devices))
    capacity = slots_each * devices
    everyone = per_device * devices
    all_lists = lax.all_gather(block_ids[0], "orient", axis=0, tiled=True)
    all_rows, all_focus = (
        lax.all_gather(images[0], "orient", axis=0, tiled=True),
        lax.all_gather(defocus[0], "orient", axis=0, tiled=True),
    )
    own_block = lax.axis_index("orient")
    block_hits = (
        jnp.any(all_lists == own_block, axis=1).astype(jnp.int32).reshape(devices, per_device)
    )
    slot_rank = jnp.cumsum(block_hits, axis=1) - block_hits
    places = (jnp.arange(devices, dtype=jnp.int32)[:, None] * slots_each + slot_rank).reshape(
        everyone
    )
    chosen = (places[None, :] == jnp.arange(capacity, dtype=jnp.int32)[:, None]) & (
        block_hits.reshape(everyone)[None, :] == 1
    )
    is_live = jnp.any(chosen, axis=1)
    slot_owner = jnp.sum(
        jnp.where(chosen, jnp.arange(everyone, dtype=jnp.int32)[None, :], 0), axis=1
    )
    slot_rows = jnp.take(all_rows, slot_owner, axis=0)
    slot_focus = jnp.take(all_focus, slot_owner, axis=0).astype(jnp.float32)
    frequency = (jnp.arange(columns, dtype=jnp.float32) + 0.5) / columns
    contrast = -jnp.sin(CTF_PHASE * slot_focus[:, None] * frequency[None, :] + 0.1)
    weighted = contrast * noise_weight[None, :]
    scaled_rows = (weighted[:, None, :] * slot_rows.astype(jnp.float32)).astype(jnp.bfloat16)
    energy = (contrast * weighted).astype(jnp.bfloat16)
    piece = lax.all_gather(panels[:, 0], "cls", axis=0, tiled=True)
    widened = piece.astype(jnp.float32)
    squared = (widened * widened).astype(jnp.bfloat16)
    correlate = jnp.einsum("srk,cjrk->scj", scaled_rows, piece, preferred_element_type=jnp.float32)
    energy_term = jnp.einsum("sk,cjrk->scj", energy, squared, preferred_element_type=jnp.float32)
    terms = correlate - 0.5 * energy_term
    combined = terms.reshape(capacity, -1)
    scores = lax.psum_scatter(combined, "rep", scatter_dimension=1, tiled=True)
    member = (slot_owner[:, None] == jnp.arange(everyone, dtype=jnp.int32)[None, :]) & is_live[
        :, None
    ]
    slot_top = jnp.max(scores, axis=1)
    local_peak = jnp.max(jnp.where(member, slot_top[:, None], FLOOR), axis=0)
    peak = lax.pmax(local_peak, ("orient", "rep"))
    slot_peak = spread_max(member, is_live, peak)
    expo = jnp.where(is_live[:, None], jnp.exp(scores - slot_peak[:, None]), 0.0)
    total = lax.psum(collect_sums(member, expo), ("orient", "rep"))
    slot_total = jnp.where(is_live, jnp.sum(jnp.where(member, total[None, :], 0.0), axis=1), 1.0)
    posterior = expo / slot_total[:, None]
    return posterior.reshape(1, 1, capacity, -1)


def solution(mesh):
    in_specs = (
        P(("batch", "cls"), "orient", "rep", None),
        P(("batch", "cls"), "orient"),
        P(("batch", "cls"), "orient", None),
        P(),
        P(("batch", "cls"), "orient", None, "rep", None),
    )
    out_specs = P(("batch", "cls"), "orient", None, "rep")
    sizes = mesh.shape
    paired = sizes["rep"] == 1 and sizes["cls"] == 2 and sizes["orient"] in (4, 8, 16, 32)
    return jax.shard_map(
        chip_shards if paired else shards,
        mesh=mesh,
        in_specs=in_specs,
        out_specs=out_specs,
        check_vma=False,
    )
```

```python
import functools

import jax
import jax.numpy as jnp
from jax import lax
from jax.experimental import pallas as pl
from jax.experimental.pallas import tpu as pltpu
from jax.sharding import PartitionSpec as P

CTF_PHASE = 40.0
FLOOR = -1e30
LANES = 128
VMEM_LIMIT = 8 * 1024 * 1024
SCHEDULING_WEIGHT = 20 * 10**9


def sin_cos(angle):
    turns = jnp.floor(angle * 0.6366197723675814 + 0.5)
    rest = angle - turns * 1.5703125
    rest = rest - turns * 4.837512969970703e-4
    rest = rest - turns * 7.549789948768648e-8
    square = rest * rest
    sine = rest + rest * square * (
        -1.6666654611e-1 + square * (8.3321608736e-3 - square * 1.9515295891e-4)
    )
    cosine = (
        1.0
        - 0.5 * square
        + square
        * square
        * (4.166664568298827e-2 + square * (-1.388731625493765e-3 + square * 2.443315711809948e-5))
    )
    quarter = turns.astype(jnp.int32)
    odd = (quarter & 1) == 1
    low = jnp.where(odd, cosine, sine)
    high = jnp.where(odd, sine, cosine)
    return (
        jnp.where((quarter & 2) == 2, -low, low),
        jnp.where(((quarter + 1) & 2) == 2, -high, high),
    )


def panel_kernel(spot, sides, own, given):
    own[...] = sides[spot[2]]
    given[...] = sides[1 - spot[2]]


def square_kernel(own, squares):
    squares[...] = own[...] * own[...]


def row_kernel(spot, planes, facts, kept, given):
    core = spot[2]
    columns = planes.shape[2]
    for half, out in ((core, kept), (1 - core, given)):
        out[:, :columns] = planes[half]
        out[:, columns:] = facts[...]


def particle_facts(meta):
    return jnp.concatenate([m[...].astype(jnp.float32).T[: m.shape[0]] for m in meta], axis=0)


def add_scores(rows, noise, own_panel, own_squares, mate_panel, turn_sin, turn_cos, sums, segments):
    columns = noise.shape[1]
    width = columns // segments
    tiles = width // LANES
    count = turn_sin.shape[0]
    facts = particle_facts([r.at[:, pl.ds(columns, LANES)] for r in rows])
    rate = jnp.broadcast_to(CTF_PHASE * facts[:, 0:1], (count, LANES))
    lane = lax.broadcasted_iota(jnp.int32, (count, LANES), 1).astype(jnp.float32)
    first_sin, first_cos = sin_cos(rate * ((lane + 0.5) / columns) + 0.1)
    step_sin, step_cos = sin_cos(rate * (LANES / columns))
    turn_sin[...] = step_sin
    turn_cos[...] = step_cos
    for total in sums:
        total[...] = jnp.zeros_like(total)

    def segment(index, carry):
        sine, cosine = carry
        start = pl.multiple_of(index * width, LANES)
        scaled_parts, energy_parts = [], []
        for t in range(tiles):
            window = pl.ds(start + t * LANES, LANES)
            weighted = sine * noise[:, window]
            image = jnp.concatenate([r[:, window] for r in rows], axis=0).astype(jnp.float32)
            scaled_parts.append((weighted * image).astype(jnp.bfloat16))
            energy_parts.append((sine * weighted).astype(jnp.bfloat16))
            ds, dc = turn_sin[...], turn_cos[...]
            sine, cosine = sine * dc + cosine * ds, cosine * dc - sine * ds
        scaled = jnp.concatenate(scaled_parts, axis=1)
        energy = jnp.concatenate(energy_parts, axis=1)
        contract = (((1,), (1,)), ((), ()))
        whole = pl.ds(start, width)
        mate = mate_panel[:, whole]
        for values, squared, total in (
            (own_panel[:, whole], own_squares[:, whole], sums[0]),
            (mate, mate * mate, sums[1]),
        ):
            correlate = lax.dot_general(
                values, scaled, contract, preferred_element_type=jnp.float32
            )
            power = lax.dot_general(squared, energy, contract, preferred_element_type=jnp.float32)
            total[...] += correlate - 0.5 * power
        return sine, cosine

    lax.fori_loop(0, segments, segment, (-first_sin, -first_cos))
    return jnp.pad(facts, ((0, 0), (0, LANES - facts.shape[1])))


def batch_kernel(n, segments, spot, *refs):
    rows = refs[:n]
    noise, own_panel, own_squares, mate_panel = refs[n : n + 4]
    own_out, mate_out, fact_out, turn_sin, turn_cos, *sums = refs[n + 4 :]
    fact_out[...] = add_scores(
        rows, noise, own_panel, own_squares, mate_panel, turn_sin, turn_cos, sums, segments
    )
    own_out[...] = sums[0][...].T
    mate_out[...] = sums[1][...].T


def last_kernel(n, segments, orders, spot, *refs):
    rows = refs[:n]
    noise, own_panel, own_squares, mate_panel = refs[n : n + 4]
    rest = refs[n + 4 :]
    earlier, rest = rest[: 3 * (len(orders) - 1)], rest[3 * (len(orders) - 1) :]
    partial, facts, turn_sin, turn_cos, *sums = rest
    last_facts = add_scores(
        rows, noise, own_panel, own_squares, mate_panel, turn_sin, turn_cos, sums, segments
    )
    position, core = spot[1], spot[2]
    each = rows[0].shape[0]
    ring = facts.shape[0] // (2 * each)
    half = ring // 2
    for index, order in enumerate(orders):
        if index < len(orders) - 1:
            own, mate, fact = [r[...] for r in earlier[3 * index : 3 * index + 3]]
        else:
            own, mate, fact = sums[0][...].T, sums[1][...].T, last_facts
        for k, (distance, crossed) in enumerate(order):
            place = lax.rem(position + distance + ring, ring)
            far = place >= half
            level = jnp.where(far, ring - 1 - place, place)
            device = 2 * level + (1 - core if crossed else core)
            start = pl.multiple_of((jnp.where(far, ring, 0) + device) * each, each)
            piece = slice(k * each, (k + 1) * each)
            partial[core, pl.ds(start, each), :] = own[piece]
            partial[1 - core, pl.ds(start, each), :] = mate[piece]
            facts[pl.ds(start, each), :] = fact[piece]


def score_call(chunks, orders, earlier, spot, noise, own_panel, squares, mate_panel):
    each = chunks[0].shape[0]
    orientations, columns = own_panel.shape
    whole = columns // LANES
    segments = 1
    n = len(chunks)
    count = each * n
    scratch = [pltpu.VMEM((count, LANES), jnp.float32)] * 2
    scratch += [pltpu.VMEM((orientations, count), jnp.float32)] * 2
    single = jax.ShapeDtypeStruct((count, orientations), jnp.float32)
    if orders is None:
        kernel = functools.partial(batch_kernel, n, segments)
        out_shape = [single, single, jax.ShapeDtypeStruct((count, LANES), jnp.float32)]
        extra = []
    else:
        everyone = each * sum(len(o) for o in orders)
        kernel = functools.partial(last_kernel, n, segments, orders)
        out_shape = [
            jax.ShapeDtypeStruct((2, everyone, orientations), jnp.float32),
            jax.ShapeDtypeStruct((everyone, LANES), jnp.float32),
        ]
        extra = [e for triple in earlier for e in triple]
    vmem = pl.BlockSpec(memory_space=pltpu.VMEM)
    return pl.pallas_call(
        kernel,
        in_specs=[pl.BlockSpec(memory_space=pltpu.SMEM)] + [vmem] * (n + 4 + len(extra)),
        out_specs=[vmem] * len(out_shape),
        out_shape=out_shape,
        scratch_shapes=scratch,
        compiler_params=pltpu.CompilerParams(vmem_limit_bytes=VMEM_LIMIT),
        cost_estimate=pl.CostEstimate(
            flops=8 * max(count, 128) * orientations * columns,
            bytes_accessed=4 * orientations * columns + 2 * count * columns,
            transcendentals=0,
        ),
    )(spot, *chunks, noise, own_panel, squares, mate_panel, *extra)


def names_block(facts, search, block):
    lane = lax.broadcasted_iota(jnp.int32, facts.shape, 1)
    match = (lane >= 1) & (lane <= search) & (facts == block.astype(jnp.float32))
    return jnp.max(jnp.where(match, 1.0, 0.0), axis=1, keepdims=True) > 0.0


def chip_kernel(search, spot, partial, mate, facts, mine, across, stats):
    group, core, place = spot[0], spot[2], spot[3]
    count = mine.shape[0]
    lane = lax.broadcasted_iota(jnp.int32, (count, LANES), 1)
    pairs = []
    for relative in range(2):
        side = group if relative == 0 else 1 - group
        window = pl.ds(pl.multiple_of(side * count, count), count)
        listed = facts[window, :]
        masked = []
        for crossed in range(2):
            block = core if crossed == 0 else 1 - core
            scores = partial[block, window, :] + mate[block, window, :]
            if crossed == 0:
                out = mine if relative == 0 else across
                out[...] = scores
            named = names_block(listed, search, place - core + block)
            masked.append(jnp.where(named, scores, FLOOR))
        top = jnp.max(jnp.maximum(*masked), axis=1, keepdims=True)
        terms = [jnp.where(m > FLOOR, jnp.exp(m - top), 0.0) for m in masked]
        total = jnp.sum(terms[0] + terms[1], axis=1, keepdims=True)
        pairs.append(jnp.where(lane == relative, top, jnp.where(lane == 2 + relative, total, 0.0)))
    stats[...] = (pairs[0] + pairs[1]).T[: stats.shape[0]]


def slot_kernel(search, slots_each, each, spot, mine, across, facts, slots, chosen, tops):
    group, place = spot[0], spot[3]
    count = mine.shape[0]
    same, other = mine[...], across[...]
    first = group == 0
    scores = jnp.concatenate(
        [jnp.where(first, same, other), jnp.where(first, other, same)], axis=1
    )
    listed = facts[pl.ds(pl.multiple_of(group * count, count), count), :]
    named = names_block(listed, search, place)
    hit = jnp.where(named, 1.0, 0.0)
    row = lax.broadcasted_iota(jnp.int32, (count, LANES), 0)
    line = lax.broadcasted_iota(jnp.int32, (count, count), 0)
    column = lax.broadcasted_iota(jnp.int32, (count, count), 1)
    before = (column < line) & (column // each == line // each)
    rank = jnp.dot(
        jnp.where(before, 1.0, 0.0).astype(jnp.bfloat16),
        jnp.broadcast_to(hit, (count, LANES)).astype(jnp.bfloat16),
        preferred_element_type=jnp.float32,
    )
    slot = (row // each) * slots_each + rank.astype(jnp.int32)
    capacity = chosen.shape[0]
    if capacity != LANES:
        slot = jnp.broadcast_to(slot[:, :1], (count, capacity))
    target = lax.broadcasted_iota(jnp.int32, (count, capacity), 1)
    taken = jnp.where((slot == target) & named, 1.0, 0.0)
    top = jnp.max(scores, axis=1, keepdims=True)
    tops[...] = jnp.broadcast_to(top, (count, LANES)).T[: tops.shape[0]]
    terms = jnp.where(named, jnp.exp(scores - top), 0.0)
    slots[...] = lax.dot_general(
        taken,
        terms,
        (((0,), (0,)), ((), ())),
        precision=lax.Precision.HIGHEST,
        preferred_element_type=jnp.float32,
    )
    chosen[...] = taken.T


def final_kernel(n, *refs):
    parts, (tops, slots, chosen, out) = refs[:n], refs[n:]
    peak = functools.reduce(jnp.maximum, [p[0:1, :] for p in parts])
    shares = [p[1:2, :] * jnp.exp(p[0:1, :] - peak) for p in parts]
    total = functools.reduce(jnp.add, shares)
    factor = jnp.exp(jnp.minimum(tops[0:1, :] - peak, 0.0)) / total
    scale = jnp.sum(chosen[...] * factor, axis=1, keepdims=True)
    out[...] = slots[...] * scale


def chip_shards(images, defocus, block_ids, noise_weight, panels):
    per_device, halves, columns = images.shape[1:]
    devices = lax.axis_size("orient")
    chips = devices // 2
    ring = 2 * chips
    everyone = per_device * devices
    local_search = block_ids.shape[2]
    orientations = panels.shape[2]
    slots_each = min(per_device, max(2, 2 * per_device * local_search // devices))
    capacity = slots_each * devices
    place = lax.axis_index("orient")
    group = lax.axis_index("cls")
    chip, core = place // 2, place % 2
    position = jnp.where(group == 0, chip, ring - 1 - chip)
    spot = jnp.stack([group, position, core, place]).astype(jnp.int32)

    mate_pairs = [(d, d ^ 1) for d in range(devices)]
    x_pairs = [(0, 1), (1, 0)]

    def joint(place, core):
        place = place % ring
        far = place >= chips
        level = ring - 1 - place if far else place
        return (2 * level + core) * 2 + int(far)

    def forward(values, step, cross=0):
        pairs = [(joint(p, c), joint(p + step, c ^ cross)) for p in range(ring) for c in range(2)]
        return lax.ppermute(values, ("orient", "cls"), pairs)

    vmem = pl.BlockSpec(memory_space=pltpu.VMEM)
    smem = pl.BlockSpec(memory_space=pltpu.SMEM)
    params = pltpu.CompilerParams(vmem_limit_bytes=VMEM_LIMIT)
    planes = lax.optimization_barrier(jnp.transpose(images[0], (1, 0, 2)))
    facts = jnp.concatenate([defocus, jnp.transpose(block_ids[0]).astype(jnp.bfloat16)], axis=0)
    facts = jnp.pad(facts, ((0, per_device - facts.shape[0]), (0, LANES - per_device)))
    row_shape = jax.ShapeDtypeStruct((per_device, columns + LANES), jnp.bfloat16)
    kept, given = pl.pallas_call(
        row_kernel,
        in_specs=[smem, vmem, vmem],
        out_specs=[vmem] * 2,
        out_shape=[row_shape] * 2,
        compiler_params=params,
    )(spot, planes, facts)

    _, panels = lax.optimization_barrier((kept, panels))
    sides = lax.optimization_barrier(jnp.transpose(panels[0, 0], (1, 0, 2)))
    panel_shape = jax.ShapeDtypeStruct(sides.shape[1:], sides.dtype)
    own_panel, given_panel = pl.pallas_call(
        panel_kernel,
        in_specs=[smem, vmem],
        out_specs=[vmem] * 2,
        out_shape=[panel_shape] * 2,
        compiler_params=params,
    )(spot, sides)
    with jax.named_scope("mate_panel"):
        mate_panel = lax.ppermute(given_panel, "orient", mate_pairs)

    noise = noise_weight[None, :]
    waiting = []
    ahead = {False: kept, True: given}
    behind = {False: kept, True: given}
    orders, earlier, late = [], [], []
    squares = pl.pallas_call(
        square_kernel,
        in_specs=[vmem],
        out_specs=vmem,
        out_shape=panel_shape,
        compiler_params=params,
        cost_estimate=pl.CostEstimate(flops=SCHEDULING_WEIGHT, bytes_accessed=0, transcendentals=0),
    )(own_panel)
    score = lambda c: score_call(c, None, None, spot, noise, own_panel, squares, mate_panel)
    for step in range(1, chips + 1):
        if step == 3:
            orders.append([key for key, _ in waiting])
            earlier.append(score([c for _, c in waiting]))
            waiting = []
            for chain, c in ((ahead, False), (behind, True)):
                chain[c] = lax.optimization_barrier((chain[c], earlier[-1][2]))[0]
        if step == 2:
            for chain, c in ((ahead, False), (behind, True)):
                chain[c] = lax.optimization_barrier((chain[c], squares))[0]
        waiting = waiting + late
        late = []
        for crossed in (False, True):
            if step < chips or not crossed:
                with jax.named_scope("rows_ahead"):
                    ahead[crossed] = forward(ahead[crossed], 1, int(crossed and step == 1))
                late.append(((-step, crossed), ahead[crossed]))
            if step < chips or crossed:
                with jax.named_scope("rows_behind"):
                    behind[crossed] = forward(behind[crossed], -1, int(crossed and step == 1))
                late.append(((step, crossed), behind[crossed]))
        if step == 1:
            late_given, _ = lax.optimization_barrier((given, kept))
            with jax.named_scope("mate_rows"):
                got = lax.ppermute(late_given, "orient", mate_pairs)
            late = [((0, False), kept), ((0, True), got)] + late
    orders.append([key for key, _ in waiting])
    earlier.append(score([c for _, c in waiting]))
    waiting = late
    orders.append([key for key, _ in waiting])
    partial, all_facts = score_call(
        [c for _, c in waiting], orders, earlier, spot, noise, own_panel, squares, mate_panel
    )

    mate_partial = lax.ppermute(partial, "orient", mate_pairs)
    mine, across, stats = pl.pallas_call(
        functools.partial(chip_kernel, local_search),
        in_specs=[smem] + [vmem] * 3,
        out_specs=[vmem] * 3,
        out_shape=[
            jax.ShapeDtypeStruct((everyone, orientations), jnp.float32),
            jax.ShapeDtypeStruct((everyone, orientations), jnp.float32),
            jax.ShapeDtypeStruct((8, everyone), jnp.float32),
        ],
        compiler_params=params,
    )(spot, partial, mate_partial, all_facts)

    x_stats = lax.ppermute(stats, "cls", x_pairs)
    across, _ = lax.optimization_barrier((across, stats))
    from_x = lax.ppermute(across, "cls", x_pairs)
    peak = jnp.maximum(stats[0], x_stats[1])
    total = stats[2] * jnp.exp(stats[0] - peak) + x_stats[3] * jnp.exp(x_stats[1] - peak)
    pair = jnp.pad(jnp.stack([peak, total]), ((0, 6), (0, 0)))
    if chips == 4:
        near = lax.ppermute(pair, "orient", [(d, d ^ (2 << d % 2)) for d in range(devices)])
        far = lax.ppermute(pair, "orient", [(d, d ^ 6) for d in range(devices)])
        parts = [pair, near, lax.ppermute(near, "orient", mate_pairs), far]
    else:
        parts = [pair] + [
            lax.ppermute(pair, "orient", [(d, (d + 2 * s) % devices) for d in range(devices)])
            for s in range(1, chips)
        ]
    slots, chosen, tops = pl.pallas_call(
        functools.partial(slot_kernel, local_search, slots_each, per_device),
        in_specs=[smem] + [vmem] * 3,
        out_specs=[vmem] * 3,
        out_shape=[
            jax.ShapeDtypeStruct((capacity, 2 * orientations), jnp.float32),
            jax.ShapeDtypeStruct((capacity, everyone), jnp.float32),
            jax.ShapeDtypeStruct((8, everyone), jnp.float32),
        ],
        compiler_params=params,
    )(spot, mine, from_x, all_facts)
    posterior = pl.pallas_call(
        functools.partial(final_kernel, chips),
        in_specs=[vmem] * (chips + 3),
        out_specs=vmem,
        out_shape=jax.ShapeDtypeStruct((capacity, 2 * orientations), jnp.float32),
        compiler_params=params,
    )(*parts, tops, slots, chosen)
    return posterior.reshape(1, 1, capacity, -1)


def spread_max(member, is_live, values):
    picked = jnp.max(jnp.where(member, values[None, :], FLOOR), axis=1)
    return jnp.where(is_live, picked, 0.0)


def collect_sums(member, expo):
    return jnp.sum(jnp.where(member, jnp.sum(expo, axis=1)[:, None], 0.0), axis=0)


def shards(images, defocus, block_ids, noise_weight, panels):
    per_device = images.shape[1]
    columns = images.shape[3]
    devices = lax.axis_size("orient")
    local_search = block_ids.shape[2]
    slots_each = min(per_device, max(2, 2 * per_device * local_search // devices))
    capacity = slots_each * devices
    everyone = per_device * devices
    all_lists = lax.all_gather(block_ids[0], "orient", axis=0, tiled=True)
    all_rows, all_focus = (
        lax.all_gather(images[0], "orient", axis=0, tiled=True),
        lax.all_gather(defocus[0], "orient", axis=0, tiled=True),
    )
    own_block = lax.axis_index("orient")
    block_hits = (
        jnp.any(all_lists == own_block, axis=1).astype(jnp.int32).reshape(devices, per_device)
    )
    slot_rank = jnp.cumsum(block_hits, axis=1) - block_hits
    places = (jnp.arange(devices, dtype=jnp.int32)[:, None] * slots_each + slot_rank).reshape(
        everyone
    )
    chosen = (places[None, :] == jnp.arange(capacity, dtype=jnp.int32)[:, None]) & (
        block_hits.reshape(everyone)[None, :] == 1
    )
    is_live = jnp.any(chosen, axis=1)
    slot_owner = jnp.sum(
        jnp.where(chosen, jnp.arange(everyone, dtype=jnp.int32)[None, :], 0), axis=1
    )
    slot_rows = jnp.take(all_rows, slot_owner, axis=0)
    slot_focus = jnp.take(all_focus, slot_owner, axis=0).astype(jnp.float32)
    frequency = (jnp.arange(columns, dtype=jnp.float32) + 0.5) / columns
    contrast = -jnp.sin(CTF_PHASE * slot_focus[:, None] * frequency[None, :] + 0.1)
    weighted = contrast * noise_weight[None, :]
    scaled_rows = (weighted[:, None, :] * slot_rows.astype(jnp.float32)).astype(jnp.bfloat16)
    energy = (contrast * weighted).astype(jnp.bfloat16)
    piece = lax.all_gather(panels[:, 0], "cls", axis=0, tiled=True)
    widened = piece.astype(jnp.float32)
    squared = (widened * widened).astype(jnp.bfloat16)
    correlate = jnp.einsum("srk,cjrk->scj", scaled_rows, piece, preferred_element_type=jnp.float32)
    energy_term = jnp.einsum("sk,cjrk->scj", energy, squared, preferred_element_type=jnp.float32)
    terms = correlate - 0.5 * energy_term
    combined = terms.reshape(capacity, -1)
    scores = lax.psum_scatter(combined, "rep", scatter_dimension=1, tiled=True)
    member = (slot_owner[:, None] == jnp.arange(everyone, dtype=jnp.int32)[None, :]) & is_live[
        :, None
    ]
    slot_top = jnp.max(scores, axis=1)
    local_peak = jnp.max(jnp.where(member, slot_top[:, None], FLOOR), axis=0)
    peak = lax.pmax(local_peak, ("orient", "rep"))
    slot_peak = spread_max(member, is_live, peak)
    expo = jnp.where(is_live[:, None], jnp.exp(scores - slot_peak[:, None]), 0.0)
    total = lax.psum(collect_sums(member, expo), ("orient", "rep"))
    slot_total = jnp.where(is_live, jnp.sum(jnp.where(member, total[None, :], 0.0), axis=1), 1.0)
    posterior = expo / slot_total[:, None]
    return posterior.reshape(1, 1, capacity, -1)


def solution(mesh):
    in_specs = (
        P(("batch", "cls"), "orient", "rep", None),
        P(("batch", "cls"), "orient"),
        P(("batch", "cls"), "orient", None),
        P(),
        P(("batch", "cls"), "orient", None, "rep", None),
    )
    out_specs = P(("batch", "cls"), "orient", None, "rep")
    sizes = mesh.shape
    paired = sizes["rep"] == 1 and sizes["cls"] == 2 and sizes["orient"] in (4, 8, 16, 32)
    return jax.shard_map(
        chip_shards if paired else shards,
        mesh=mesh,
        in_specs=in_specs,
        out_specs=out_specs,
        check_vma=False,
    )
```

```python
import functools

import jax
import jax.numpy as jnp
from jax import lax
from jax.experimental import pallas as pl
from jax.experimental.pallas import tpu as pltpu
from jax.sharding import PartitionSpec as P

CTF_PHASE = 40.0
FLOOR = -1e30
LANES = 128
VMEM_LIMIT = 8 * 1024 * 1024
SCHEDULING_WEIGHT = 20 * 10**9


def sin_cos(angle):
    turns = jnp.floor(angle * 0.6366197723675814 + 0.5)
    rest = angle - turns * 1.5703125
    rest = rest - turns * 4.837512969970703e-4
    rest = rest - turns * 7.549789948768648e-8
    square = rest * rest
    sine = rest + rest * square * (
        -1.6666654611e-1 + square * (8.3321608736e-3 - square * 1.9515295891e-4)
    )
    cosine = (
        1.0
        - 0.5 * square
        + square
        * square
        * (4.166664568298827e-2 + square * (-1.388731625493765e-3 + square * 2.443315711809948e-5))
    )
    quarter = turns.astype(jnp.int32)
    odd = (quarter & 1) == 1
    low = jnp.where(odd, cosine, sine)
    high = jnp.where(odd, sine, cosine)
    return (
        jnp.where((quarter & 2) == 2, -low, low),
        jnp.where(((quarter + 1) & 2) == 2, -high, high),
    )


def panel_kernel(spot, sides, own, given):
    own[...] = sides[spot[2]]
    given[...] = sides[1 - spot[2]]


def square_kernel(own, squares):
    squares[...] = own[...] * own[...]


def row_kernel(spot, planes, facts, kept, given):
    core = spot[2]
    columns = planes.shape[2]
    for half, out in ((core, kept), (1 - core, given)):
        out[:, :columns] = planes[half]
        out[:, columns:] = facts[...]


def particle_facts(meta):
    return jnp.concatenate([m[...].astype(jnp.float32).T[: m.shape[0]] for m in meta], axis=0)


def add_scores(rows, noise, own_panel, own_squares, mate_panel, turn_sin, turn_cos, sums, segments):
    columns = noise.shape[1]
    width = columns // segments
    tiles = width // LANES
    count = turn_sin.shape[0]
    facts = particle_facts([r.at[:, pl.ds(columns, LANES)] for r in rows])
    rate = jnp.broadcast_to(CTF_PHASE * facts[:, 0:1], (count, LANES))
    lane = lax.broadcasted_iota(jnp.int32, (count, LANES), 1).astype(jnp.float32)
    first_sin, first_cos = sin_cos(rate * ((lane + 0.5) / columns) + 0.1)
    step_sin, step_cos = sin_cos(rate * (LANES / columns))
    turn_sin[...] = step_sin
    turn_cos[...] = step_cos
    for total in sums:
        total[...] = jnp.zeros_like(total)

    def segment(index, carry):
        sine, cosine = carry
        start = pl.multiple_of(index * width, LANES)
        scaled_parts, energy_parts = [], []
        for t in range(tiles):
            window = pl.ds(start + t * LANES, LANES)
            weighted = sine * noise[:, window]
            image = jnp.concatenate([r[:, window] for r in rows], axis=0).astype(jnp.float32)
            scaled_parts.append((weighted * image).astype(jnp.bfloat16))
            energy_parts.append((sine * weighted).astype(jnp.bfloat16))
            ds, dc = turn_sin[...], turn_cos[...]
            sine, cosine = sine * dc + cosine * ds, cosine * dc - sine * ds
        scaled = jnp.concatenate(scaled_parts, axis=1)
        energy = jnp.concatenate(energy_parts, axis=1)
        contract = (((1,), (1,)), ((), ()))
        whole = pl.ds(start, width)
        mate = mate_panel[:, whole]
        for values, squared, total in (
            (own_panel[:, whole], own_squares[:, whole], sums[0]),
            (mate, mate * mate, sums[1]),
        ):
            correlate = lax.dot_general(
                values, scaled, contract, preferred_element_type=jnp.float32
            )
            power = lax.dot_general(squared, energy, contract, preferred_element_type=jnp.float32)
            total[...] += correlate - 0.5 * power
        return sine, cosine

    lax.fori_loop(0, segments, segment, (-first_sin, -first_cos))
    return jnp.pad(facts, ((0, 0), (0, LANES - facts.shape[1])))


def batch_kernel(n, segments, spot, *refs):
    rows = refs[:n]
    noise, own_panel, own_squares, mate_panel = refs[n : n + 4]
    own_out, mate_out, fact_out, turn_sin, turn_cos, *sums = refs[n + 4 :]
    fact_out[...] = add_scores(
        rows, noise, own_panel, own_squares, mate_panel, turn_sin, turn_cos, sums, segments
    )
    own_out[...] = sums[0][...].T
    mate_out[...] = sums[1][...].T


def last_kernel(n, segments, orders, spot, *refs):
    rows = refs[:n]
    noise, own_panel, own_squares, mate_panel = refs[n : n + 4]
    rest = refs[n + 4 :]
    earlier, rest = rest[: 3 * (len(orders) - 1)], rest[3 * (len(orders) - 1) :]
    partial, facts, turn_sin, turn_cos, *sums = rest
    last_facts = add_scores(
        rows, noise, own_panel, own_squares, mate_panel, turn_sin, turn_cos, sums, segments
    )
    position, core = spot[1], spot[2]
    each = rows[0].shape[0]
    ring = facts.shape[0] // (2 * each)
    half = ring // 2
    for index, order in enumerate(orders):
        if index < len(orders) - 1:
            own, mate, fact = [r[...] for r in earlier[3 * index : 3 * index + 3]]
        else:
            own, mate, fact = sums[0][...].T, sums[1][...].T, last_facts
        for k, (distance, crossed) in enumerate(order):
            place = lax.rem(position + distance + ring, ring)
            far = place >= half
            level = jnp.where(far, ring - 1 - place, place)
            device = 2 * level + (1 - core if crossed else core)
            start = pl.multiple_of((jnp.where(far, ring, 0) + device) * each, each)
            piece = slice(k * each, (k + 1) * each)
            partial[core, pl.ds(start, each), :] = own[piece]
            partial[1 - core, pl.ds(start, each), :] = mate[piece]
            facts[pl.ds(start, each), :] = fact[piece]


def score_call(chunks, orders, earlier, spot, noise, own_panel, squares, mate_panel):
    each = chunks[0].shape[0]
    orientations, columns = own_panel.shape
    whole = columns // LANES
    segments = 1
    n = len(chunks)
    count = each * n
    scratch = [pltpu.VMEM((count, LANES), jnp.float32)] * 2
    scratch += [pltpu.VMEM((orientations, count), jnp.float32)] * 2
    single = jax.ShapeDtypeStruct((count, orientations), jnp.float32)
    if orders is None:
        kernel = functools.partial(batch_kernel, n, segments)
        out_shape = [single, single, jax.ShapeDtypeStruct((count, LANES), jnp.float32)]
        extra = []
    else:
        everyone = each * sum(len(o) for o in orders)
        kernel = functools.partial(last_kernel, n, segments, orders)
        out_shape = [
            jax.ShapeDtypeStruct((2, everyone, orientations), jnp.float32),
            jax.ShapeDtypeStruct((everyone, LANES), jnp.float32),
        ]
        extra = [e for triple in earlier for e in triple]
    vmem = pl.BlockSpec(memory_space=pltpu.VMEM)
    return pl.pallas_call(
        kernel,
        in_specs=[pl.BlockSpec(memory_space=pltpu.SMEM)] + [vmem] * (n + 4 + len(extra)),
        out_specs=[vmem] * len(out_shape),
        out_shape=out_shape,
        scratch_shapes=scratch,
        compiler_params=pltpu.CompilerParams(vmem_limit_bytes=VMEM_LIMIT),
        cost_estimate=pl.CostEstimate(
            flops=8 * max(count, 128) * orientations * columns,
            bytes_accessed=4 * orientations * columns + 2 * count * columns,
            transcendentals=0,
        ),
    )(spot, *chunks, noise, own_panel, squares, mate_panel, *extra)


def names_block(facts, search, block):
    lane = lax.broadcasted_iota(jnp.int32, facts.shape, 1)
    match = (lane >= 1) & (lane <= search) & (facts == block.astype(jnp.float32))
    return jnp.max(jnp.where(match, 1.0, 0.0), axis=1, keepdims=True) > 0.0


def chip_kernel(search, spot, partial, mate, facts, mine, across, stats):
    group, core, place = spot[0], spot[2], spot[3]
    count = mine.shape[0]
    lane = lax.broadcasted_iota(jnp.int32, (count, LANES), 1)
    pairs = []
    for relative in range(2):
        side = group if relative == 0 else 1 - group
        window = pl.ds(pl.multiple_of(side * count, count), count)
        listed = facts[window, :]
        masked = []
        for crossed in range(2):
            block = core if crossed == 0 else 1 - core
            scores = partial[block, window, :] + mate[block, window, :]
            if crossed == 0:
                out = mine if relative == 0 else across
                out[...] = scores
            named = names_block(listed, search, place - core + block)
            masked.append(jnp.where(named, scores, FLOOR))
        top = jnp.max(jnp.maximum(*masked), axis=1, keepdims=True)
        terms = [jnp.where(m > FLOOR, jnp.exp(m - top), 0.0) for m in masked]
        total = jnp.sum(terms[0] + terms[1], axis=1, keepdims=True)
        pairs.append(jnp.where(lane == relative, top, jnp.where(lane == 2 + relative, total, 0.0)))
    stats[...] = (pairs[0] + pairs[1]).T[: stats.shape[0]]


def slot_kernel(search, slots_each, each, spot, mine, across, facts, slots, chosen, tops):
    group, place = spot[0], spot[3]
    count = mine.shape[0]
    same, other = mine[...], across[...]
    first = group == 0
    scores = jnp.concatenate(
        [jnp.where(first, same, other), jnp.where(first, other, same)], axis=1
    )
    listed = facts[pl.ds(pl.multiple_of(group * count, count), count), :]
    named = names_block(listed, search, place)
    hit = jnp.where(named, 1.0, 0.0)
    row = lax.broadcasted_iota(jnp.int32, (count, LANES), 0)
    line = lax.broadcasted_iota(jnp.int32, (count, count), 0)
    column = lax.broadcasted_iota(jnp.int32, (count, count), 1)
    before = (column < line) & (column // each == line // each)
    rank = jnp.dot(
        jnp.where(before, 1.0, 0.0).astype(jnp.bfloat16),
        jnp.broadcast_to(hit, (count, LANES)).astype(jnp.bfloat16),
        preferred_element_type=jnp.float32,
    )
    slot = (row // each) * slots_each + rank.astype(jnp.int32)
    capacity = chosen.shape[0]
    if capacity != LANES:
        slot = jnp.broadcast_to(slot[:, :1], (count, capacity))
    target = lax.broadcasted_iota(jnp.int32, (count, capacity), 1)
    taken = jnp.where((slot == target) & named, 1.0, 0.0)
    top = jnp.max(scores, axis=1, keepdims=True)
    tops[...] = jnp.broadcast_to(top, (count, LANES)).T[: tops.shape[0]]
    terms = jnp.where(named, jnp.exp(scores - top), 0.0)
    slots[...] = lax.dot_general(
        taken,
        terms,
        (((0,), (0,)), ((), ())),
        precision=lax.Precision.HIGHEST,
        preferred_element_type=jnp.float32,
    )
    chosen[...] = taken.T


def final_kernel(n, *refs):
    parts, (tops, slots, chosen, out) = refs[:n], refs[n:]
    peak = functools.reduce(jnp.maximum, [p[0:1, :] for p in parts])
    shares = [p[1:2, :] * jnp.exp(p[0:1, :] - peak) for p in parts]
    total = functools.reduce(jnp.add, shares)
    factor = jnp.exp(jnp.minimum(tops[0:1, :] - peak, 0.0)) / total
    scale = jnp.sum(chosen[...] * factor, axis=1, keepdims=True)
    out[...] = slots[...] * scale


def chip_shards(images, defocus, block_ids, noise_weight, panels):
    per_device, halves, columns = images.shape[1:]
    devices = lax.axis_size("orient")
    chips = devices // 2
    ring = 2 * chips
    everyone = per_device * devices
    local_search = block_ids.shape[2]
    orientations = panels.shape[2]
    slots_each = min(per_device, max(2, 2 * per_device * local_search // devices))
    capacity = slots_each * devices
    place = lax.axis_index("orient")
    group = lax.axis_index("cls")
    chip, core = place // 2, place % 2
    position = jnp.where(group == 0, chip, ring - 1 - chip)
    spot = jnp.stack([group, position, core, place]).astype(jnp.int32)

    mate_pairs = [(d, d ^ 1) for d in range(devices)]
    x_pairs = [(0, 1), (1, 0)]

    def joint(place, core):
        place = place % ring
        far = place >= chips
        level = ring - 1 - place if far else place
        return (2 * level + core) * 2 + int(far)

    def forward(values, step, cross=0):
        pairs = [(joint(p, c), joint(p + step, c ^ cross)) for p in range(ring) for c in range(2)]
        return lax.ppermute(values, ("orient", "cls"), pairs)

    vmem = pl.BlockSpec(memory_space=pltpu.VMEM)
    smem = pl.BlockSpec(memory_space=pltpu.SMEM)
    params = pltpu.CompilerParams(vmem_limit_bytes=VMEM_LIMIT)
    planes = lax.optimization_barrier(jnp.transpose(images[0], (1, 0, 2)))
    facts = jnp.concatenate([defocus, jnp.transpose(block_ids[0]).astype(jnp.bfloat16)], axis=0)
    facts = jnp.pad(facts, ((0, per_device - facts.shape[0]), (0, LANES - per_device)))
    row_shape = jax.ShapeDtypeStruct((per_device, columns + LANES), jnp.bfloat16)
    kept, given = pl.pallas_call(
        row_kernel,
        in_specs=[smem, vmem, vmem],
        out_specs=[vmem] * 2,
        out_shape=[row_shape] * 2,
        compiler_params=params,
    )(spot, planes, facts)

    _, panels = lax.optimization_barrier((kept, panels))
    sides = lax.optimization_barrier(jnp.transpose(panels[0, 0], (1, 0, 2)))
    panel_shape = jax.ShapeDtypeStruct(sides.shape[1:], sides.dtype)
    own_panel, given_panel = pl.pallas_call(
        panel_kernel,
        in_specs=[smem, vmem],
        out_specs=[vmem] * 2,
        out_shape=[panel_shape] * 2,
        compiler_params=params,
    )(spot, sides)
    with jax.named_scope("mate_panel"):
        mate_panel = lax.ppermute(given_panel, "orient", mate_pairs)

    noise = noise_weight[None, :]
    waiting = []
    ahead = {False: kept, True: given}
    behind = {False: kept, True: given}
    orders, earlier, late = [], [], []
    squares = pl.pallas_call(
        square_kernel,
        in_specs=[vmem],
        out_specs=vmem,
        out_shape=panel_shape,
        compiler_params=params,
        cost_estimate=pl.CostEstimate(flops=SCHEDULING_WEIGHT, bytes_accessed=0, transcendentals=0),
    )(own_panel)
    score = lambda c: score_call(c, None, None, spot, noise, own_panel, squares, mate_panel)
    for step in range(1, chips + 1):
        if step == 3:
            orders.append([key for key, _ in waiting])
            earlier.append(score([c for _, c in waiting]))
            waiting = []
            for chain, c in ((ahead, False), (behind, True)):
                chain[c] = lax.optimization_barrier((chain[c], earlier[-1][2]))[0]
        if step == 2:
            for chain, c in ((ahead, False), (behind, True)):
                chain[c] = lax.optimization_barrier((chain[c], squares))[0]
        waiting = waiting + late
        late = []
        for crossed in (False, True):
            if step < chips or not crossed:
                with jax.named_scope("rows_ahead"):
                    ahead[crossed] = forward(ahead[crossed], 1, int(crossed and step == 1))
                late.append(((-step, crossed), ahead[crossed]))
            if step < chips or crossed:
                with jax.named_scope("rows_behind"):
                    behind[crossed] = forward(behind[crossed], -1, int(crossed and step == 1))
                late.append(((step, crossed), behind[crossed]))
        if step == 1:
            late_given, _ = lax.optimization_barrier((given, kept))
            with jax.named_scope("mate_rows"):
                got = lax.ppermute(late_given, "orient", mate_pairs)
            late = [((0, False), kept), ((0, True), got)] + late
    orders.append([key for key, _ in waiting])
    earlier.append(score([c for _, c in waiting]))
    waiting = late
    orders.append([key for key, _ in waiting])
    partial, all_facts = score_call(
        [c for _, c in waiting], orders, earlier, spot, noise, own_panel, squares, mate_panel
    )

    mate_partial = lax.ppermute(partial, "orient", mate_pairs)
    mine, across, stats = pl.pallas_call(
        functools.partial(chip_kernel, local_search),
        in_specs=[smem] + [vmem] * 3,
        out_specs=[vmem] * 3,
        out_shape=[
            jax.ShapeDtypeStruct((everyone, orientations), jnp.float32),
            jax.ShapeDtypeStruct((everyone, orientations), jnp.float32),
            jax.ShapeDtypeStruct((8, everyone), jnp.float32),
        ],
        compiler_params=params,
    )(spot, partial, mate_partial, all_facts)

    x_stats = lax.ppermute(stats, "cls", x_pairs)
    across, _ = lax.optimization_barrier((across, stats))
    from_x = lax.ppermute(across, "cls", x_pairs)
    peak = jnp.maximum(stats[0], x_stats[1])
    total = stats[2] * jnp.exp(stats[0] - peak) + x_stats[3] * jnp.exp(x_stats[1] - peak)
    pair = jnp.pad(jnp.stack([peak, total]), ((0, 6), (0, 0)))
    slots, chosen, tops = pl.pallas_call(
        functools.partial(slot_kernel, local_search, slots_each, per_device),
        in_specs=[smem] + [vmem] * 3,
        out_specs=[vmem] * 3,
        out_shape=[
            jax.ShapeDtypeStruct((capacity, 2 * orientations), jnp.float32),
            jax.ShapeDtypeStruct((capacity, everyone), jnp.float32),
            jax.ShapeDtypeStruct((8, everyone), jnp.float32),
        ],
        compiler_params=params,
    )(spot, mine, from_x, all_facts)
    if chips == 4:
        near = lax.ppermute(pair, "orient", [(d, d ^ (2 << d % 2)) for d in range(devices)])
        far = lax.ppermute(pair, "orient", [(d, d ^ 6) for d in range(devices)])
        near, tops = lax.optimization_barrier((near, tops))
        parts = [pair, near, lax.ppermute(near, "orient", mate_pairs), far]
    else:
        parts = [pair] + [
            lax.ppermute(pair, "orient", [(d, (d + 2 * s) % devices) for d in range(devices)])
            for s in range(1, chips)
        ]
    posterior = pl.pallas_call(
        functools.partial(final_kernel, chips),
        in_specs=[vmem] * (chips + 3),
        out_specs=vmem,
        out_shape=jax.ShapeDtypeStruct((capacity, 2 * orientations), jnp.float32),
        compiler_params=params,
    )(*parts, tops, slots, chosen)
    return posterior.reshape(1, 1, capacity, -1)


def spread_max(member, is_live, values):
    picked = jnp.max(jnp.where(member, values[None, :], FLOOR), axis=1)
    return jnp.where(is_live, picked, 0.0)


def collect_sums(member, expo):
    return jnp.sum(jnp.where(member, jnp.sum(expo, axis=1)[:, None], 0.0), axis=0)


def shards(images, defocus, block_ids, noise_weight, panels):
    per_device = images.shape[1]
    columns = images.shape[3]
    devices = lax.axis_size("orient")
    local_search = block_ids.shape[2]
    slots_each = min(per_device, max(2, 2 * per_device * local_search // devices))
    capacity = slots_each * devices
    everyone = per_device * devices
    all_lists = lax.all_gather(block_ids[0], "orient", axis=0, tiled=True)
    all_rows, all_focus = (
        lax.all_gather(images[0], "orient", axis=0, tiled=True),
        lax.all_gather(defocus[0], "orient", axis=0, tiled=True),
    )
    own_block = lax.axis_index("orient")
    block_hits = (
        jnp.any(all_lists == own_block, axis=1).astype(jnp.int32).reshape(devices, per_device)
    )
    slot_rank = jnp.cumsum(block_hits, axis=1) - block_hits
    places = (jnp.arange(devices, dtype=jnp.int32)[:, None] * slots_each + slot_rank).reshape(
        everyone
    )
    chosen = (places[None, :] == jnp.arange(capacity, dtype=jnp.int32)[:, None]) & (
        block_hits.reshape(everyone)[None, :] == 1
    )
    is_live = jnp.any(chosen, axis=1)
    slot_owner = jnp.sum(
        jnp.where(chosen, jnp.arange(everyone, dtype=jnp.int32)[None, :], 0), axis=1
    )
    slot_rows = jnp.take(all_rows, slot_owner, axis=0)
    slot_focus = jnp.take(all_focus, slot_owner, axis=0).astype(jnp.float32)
    frequency = (jnp.arange(columns, dtype=jnp.float32) + 0.5) / columns
    contrast = -jnp.sin(CTF_PHASE * slot_focus[:, None] * frequency[None, :] + 0.1)
    weighted = contrast * noise_weight[None, :]
    scaled_rows = (weighted[:, None, :] * slot_rows.astype(jnp.float32)).astype(jnp.bfloat16)
    energy = (contrast * weighted).astype(jnp.bfloat16)
    piece = lax.all_gather(panels[:, 0], "cls", axis=0, tiled=True)
    widened = piece.astype(jnp.float32)
    squared = (widened * widened).astype(jnp.bfloat16)
    correlate = jnp.einsum("srk,cjrk->scj", scaled_rows, piece, preferred_element_type=jnp.float32)
    energy_term = jnp.einsum("sk,cjrk->scj", energy, squared, preferred_element_type=jnp.float32)
    terms = correlate - 0.5 * energy_term
    combined = terms.reshape(capacity, -1)
    scores = lax.psum_scatter(combined, "rep", scatter_dimension=1, tiled=True)
    member = (slot_owner[:, None] == jnp.arange(everyone, dtype=jnp.int32)[None, :]) & is_live[
        :, None
    ]
    slot_top = jnp.max(scores, axis=1)
    local_peak = jnp.max(jnp.where(member, slot_top[:, None], FLOOR), axis=0)
    peak = lax.pmax(local_peak, ("orient", "rep"))
    slot_peak = spread_max(member, is_live, peak)
    expo = jnp.where(is_live[:, None], jnp.exp(scores - slot_peak[:, None]), 0.0)
    total = lax.psum(collect_sums(member, expo), ("orient", "rep"))
    slot_total = jnp.where(is_live, jnp.sum(jnp.where(member, total[None, :], 0.0), axis=1), 1.0)
    posterior = expo / slot_total[:, None]
    return posterior.reshape(1, 1, capacity, -1)


def solution(mesh):
    in_specs = (
        P(("batch", "cls"), "orient", "rep", None),
        P(("batch", "cls"), "orient"),
        P(("batch", "cls"), "orient", None),
        P(),
        P(("batch", "cls"), "orient", None, "rep", None),
    )
    out_specs = P(("batch", "cls"), "orient", None, "rep")
    sizes = mesh.shape
    paired = sizes["rep"] == 1 and sizes["cls"] == 2 and sizes["orient"] in (4, 8, 16, 32)
    return jax.shard_map(
        chip_shards if paired else shards,
        mesh=mesh,
        in_specs=in_specs,
        out_specs=out_specs,
        check_vma=False,
    )
```

```python
import functools

import jax
import jax.numpy as jnp
from jax import lax
from jax.experimental import pallas as pl
from jax.experimental.pallas import tpu as pltpu
from jax.sharding import PartitionSpec as P

CTF_PHASE = 40.0
FLOOR = -1e30
LANES = 128
VMEM_LIMIT = 8 * 1024 * 1024
SCHEDULING_WEIGHT = 20 * 10**9


def sin_cos(angle):
    turns = jnp.floor(angle * 0.6366197723675814 + 0.5)
    rest = angle - turns * 1.5703125
    rest = rest - turns * 4.837512969970703e-4
    rest = rest - turns * 7.549789948768648e-8
    square = rest * rest
    sine = rest + rest * square * (
        -1.6666654611e-1 + square * (8.3321608736e-3 - square * 1.9515295891e-4)
    )
    cosine = (
        1.0
        - 0.5 * square
        + square
        * square
        * (4.166664568298827e-2 + square * (-1.388731625493765e-3 + square * 2.443315711809948e-5))
    )
    quarter = turns.astype(jnp.int32)
    odd = (quarter & 1) == 1
    low = jnp.where(odd, cosine, sine)
    high = jnp.where(odd, sine, cosine)
    return (
        jnp.where((quarter & 2) == 2, -low, low),
        jnp.where(((quarter + 1) & 2) == 2, -high, high),
    )


def panel_kernel(spot, sides, own, given):
    own[...] = sides[spot[2]]
    given[...] = sides[1 - spot[2]]


def square_kernel(own, squares):
    squares[...] = own[...] * own[...]


def row_kernel(spot, planes, facts, kept, given):
    core = spot[2]
    columns = planes.shape[2]
    for half, out in ((core, kept), (1 - core, given)):
        out[:, :columns] = planes[half]
        out[:, columns:] = facts[...]


def particle_facts(meta):
    return jnp.concatenate([m[...].astype(jnp.float32).T[: m.shape[0]] for m in meta], axis=0)


def add_scores(rows, noise, own_panel, own_squares, mate_panel, turn_sin, turn_cos, sums, segments):
    columns = noise.shape[1]
    width = columns // segments
    tiles = width // LANES
    count = turn_sin.shape[0]
    facts = particle_facts([r.at[:, pl.ds(columns, LANES)] for r in rows])
    rate = jnp.broadcast_to(CTF_PHASE * facts[:, 0:1], (count, LANES))
    lane = lax.broadcasted_iota(jnp.int32, (count, LANES), 1).astype(jnp.float32)
    first_sin, first_cos = sin_cos(rate * ((lane + 0.5) / columns) + 0.1)
    step_sin, step_cos = sin_cos(rate * (LANES / columns))
    turn_sin[...] = step_sin
    turn_cos[...] = step_cos
    for total in sums:
        total[...] = jnp.zeros_like(total)

    def segment(index, carry):
        sine, cosine = carry
        start = pl.multiple_of(index * width, LANES)
        scaled_parts, energy_parts = [], []
        for t in range(tiles):
            window = pl.ds(start + t * LANES, LANES)
            weighted = sine * noise[:, window]
            image = jnp.concatenate([r[:, window] for r in rows], axis=0).astype(jnp.float32)
            scaled_parts.append((weighted * image).astype(jnp.bfloat16))
            energy_parts.append((sine * weighted).astype(jnp.bfloat16))
            ds, dc = turn_sin[...], turn_cos[...]
            sine, cosine = sine * dc + cosine * ds, cosine * dc - sine * ds
        scaled = jnp.concatenate(scaled_parts, axis=1)
        energy = jnp.concatenate(energy_parts, axis=1)
        contract = (((1,), (1,)), ((), ()))
        whole = pl.ds(start, width)
        mate = mate_panel[:, whole]
        for values, squared, total in (
            (own_panel[:, whole], own_squares[:, whole], sums[0]),
            (mate, mate * mate, sums[1]),
        ):
            correlate = lax.dot_general(
                values, scaled, contract, preferred_element_type=jnp.float32
            )
            power = lax.dot_general(squared, energy, contract, preferred_element_type=jnp.float32)
            total[...] += correlate - 0.5 * power
        return sine, cosine

    lax.fori_loop(0, segments, segment, (-first_sin, -first_cos))
    return jnp.pad(facts, ((0, 0), (0, LANES - facts.shape[1])))


def batch_kernel(n, segments, spot, *refs):
    rows = refs[:n]
    noise, own_panel, own_squares, mate_panel = refs[n : n + 4]
    own_out, mate_out, fact_out, turn_sin, turn_cos, *sums = refs[n + 4 :]
    fact_out[...] = add_scores(
        rows, noise, own_panel, own_squares, mate_panel, turn_sin, turn_cos, sums, segments
    )
    own_out[...] = sums[0][...].T
    mate_out[...] = sums[1][...].T


def last_kernel(n, segments, orders, spot, *refs):
    rows = refs[:n]
    noise, own_panel, own_squares, mate_panel = refs[n : n + 4]
    rest = refs[n + 4 :]
    earlier, rest = rest[: 3 * (len(orders) - 1)], rest[3 * (len(orders) - 1) :]
    partial, facts, turn_sin, turn_cos, *sums = rest
    last_facts = add_scores(
        rows, noise, own_panel, own_squares, mate_panel, turn_sin, turn_cos, sums, segments
    )
    position, core = spot[1], spot[2]
    each = rows[0].shape[0]
    ring = facts.shape[0] // (2 * each)
    half = ring // 2
    for index, order in enumerate(orders):
        if index < len(orders) - 1:
            own, mate, fact = [r[...] for r in earlier[3 * index : 3 * index + 3]]
        else:
            own, mate, fact = sums[0][...].T, sums[1][...].T, last_facts
        for k, (distance, crossed) in enumerate(order):
            place = lax.rem(position + distance + ring, ring)
            far = place >= half
            level = jnp.where(far, ring - 1 - place, place)
            device = 2 * level + (1 - core if crossed else core)
            start = pl.multiple_of((jnp.where(far, ring, 0) + device) * each, each)
            piece = slice(k * each, (k + 1) * each)
            partial[core, pl.ds(start, each), :] = own[piece]
            partial[1 - core, pl.ds(start, each), :] = mate[piece]
            facts[pl.ds(start, each), :] = fact[piece]


def score_call(chunks, orders, earlier, spot, noise, own_panel, squares, mate_panel):
    each = chunks[0].shape[0]
    orientations, columns = own_panel.shape
    whole = columns // LANES
    segments = 1
    n = len(chunks)
    count = each * n
    scratch = [pltpu.VMEM((count, LANES), jnp.float32)] * 2
    scratch += [pltpu.VMEM((orientations, count), jnp.float32)] * 2
    single = jax.ShapeDtypeStruct((count, orientations), jnp.float32)
    if orders is None:
        kernel = functools.partial(batch_kernel, n, segments)
        out_shape = [single, single, jax.ShapeDtypeStruct((count, LANES), jnp.float32)]
        extra = []
    else:
        everyone = each * sum(len(o) for o in orders)
        kernel = functools.partial(last_kernel, n, segments, orders)
        out_shape = [
            jax.ShapeDtypeStruct((2, everyone, orientations), jnp.float32),
            jax.ShapeDtypeStruct((everyone, LANES), jnp.float32),
        ]
        extra = [e for triple in earlier for e in triple]
    vmem = pl.BlockSpec(memory_space=pltpu.VMEM)
    return pl.pallas_call(
        kernel,
        in_specs=[pl.BlockSpec(memory_space=pltpu.SMEM)] + [vmem] * (n + 4 + len(extra)),
        out_specs=[vmem] * len(out_shape),
        out_shape=out_shape,
        scratch_shapes=scratch,
        compiler_params=pltpu.CompilerParams(vmem_limit_bytes=VMEM_LIMIT),
        cost_estimate=pl.CostEstimate(
            flops=8 * max(count, 128) * orientations * columns,
            bytes_accessed=4 * orientations * columns + 2 * count * columns,
            transcendentals=0,
        ),
    )(spot, *chunks, noise, own_panel, squares, mate_panel, *extra)


def names_block(facts, search, block):
    lane = lax.broadcasted_iota(jnp.int32, facts.shape, 1)
    match = (lane >= 1) & (lane <= search) & (facts == block.astype(jnp.float32))
    return jnp.max(jnp.where(match, 1.0, 0.0), axis=1, keepdims=True) > 0.0


def chip_kernel(search, spot, partial, mate, facts, mine, across, stats):
    group, core, place = spot[0], spot[2], spot[3]
    count = mine.shape[0]
    lane = lax.broadcasted_iota(jnp.int32, (count, LANES), 1)
    pairs = []
    for relative in range(2):
        side = group if relative == 0 else 1 - group
        window = pl.ds(pl.multiple_of(side * count, count), count)
        listed = facts[window, :]
        masked = []
        for crossed in range(2):
            block = core if crossed == 0 else 1 - core
            scores = partial[block, window, :] + mate[block, window, :]
            if crossed == 0:
                out = mine if relative == 0 else across
                out[...] = scores
            named = names_block(listed, search, place - core + block)
            masked.append(jnp.where(named, scores, FLOOR))
        top = jnp.max(jnp.maximum(*masked), axis=1, keepdims=True)
        terms = [jnp.where(m > FLOOR, jnp.exp(m - top), 0.0) for m in masked]
        total = jnp.sum(terms[0] + terms[1], axis=1, keepdims=True)
        pairs.append(jnp.where(lane == relative, top, jnp.where(lane == 2 + relative, total, 0.0)))
    stats[...] = (pairs[0] + pairs[1]).T[: stats.shape[0]]


def slot_kernel(search, slots_each, each, spot, mine, across, facts, slots, chosen, tops):
    group, place = spot[0], spot[3]
    count = mine.shape[0]
    same, other = mine[...], across[...]
    first = group == 0
    scores = jnp.concatenate(
        [jnp.where(first, same, other), jnp.where(first, other, same)], axis=1
    )
    listed = facts[pl.ds(pl.multiple_of(group * count, count), count), :]
    named = names_block(listed, search, place)
    hit = jnp.where(named, 1.0, 0.0)
    row = lax.broadcasted_iota(jnp.int32, (count, LANES), 0)
    line = lax.broadcasted_iota(jnp.int32, (count, count), 0)
    column = lax.broadcasted_iota(jnp.int32, (count, count), 1)
    before = (column < line) & (column // each == line // each)
    rank = jnp.dot(
        jnp.where(before, 1.0, 0.0).astype(jnp.bfloat16),
        jnp.broadcast_to(hit, (count, LANES)).astype(jnp.bfloat16),
        preferred_element_type=jnp.float32,
    )
    slot = (row // each) * slots_each + rank.astype(jnp.int32)
    capacity = chosen.shape[0]
    if capacity != LANES:
        slot = jnp.broadcast_to(slot[:, :1], (count, capacity))
    target = lax.broadcasted_iota(jnp.int32, (count, capacity), 1)
    taken = jnp.where((slot == target) & named, 1.0, 0.0)
    top = jnp.max(scores, axis=1, keepdims=True)
    tops[...] = jnp.broadcast_to(top, (count, LANES)).T[: tops.shape[0]]
    terms = jnp.where(named, jnp.exp(scores - top), 0.0)
    slots[...] = lax.dot_general(
        taken,
        terms,
        (((0,), (0,)), ((), ())),
        precision=lax.Precision.HIGHEST,
        preferred_element_type=jnp.float32,
    )
    chosen[...] = taken.T


def final_kernel(n, *refs):
    parts, (tops, slots, chosen, out) = refs[:n], refs[n:]
    peak = functools.reduce(jnp.maximum, [p[0:1, :] for p in parts])
    shares = [p[1:2, :] * jnp.exp(p[0:1, :] - peak) for p in parts]
    total = functools.reduce(jnp.add, shares)
    factor = jnp.exp(jnp.minimum(tops[0:1, :] - peak, 0.0)) / total
    scale = jnp.sum(chosen[...] * factor, axis=1, keepdims=True)
    out[...] = slots[...] * scale


def chip_shards(images, defocus, block_ids, noise_weight, panels):
    per_device, halves, columns = images.shape[1:]
    devices = lax.axis_size("orient")
    chips = devices // 2
    ring = 2 * chips
    everyone = per_device * devices
    local_search = block_ids.shape[2]
    orientations = panels.shape[2]
    slots_each = min(per_device, max(2, 2 * per_device * local_search // devices))
    capacity = slots_each * devices
    place = lax.axis_index("orient")
    group = lax.axis_index("cls")
    chip, core = place // 2, place % 2
    position = jnp.where(group == 0, chip, ring - 1 - chip)
    spot = jnp.stack([group, position, core, place]).astype(jnp.int32)

    mate_pairs = [(d, d ^ 1) for d in range(devices)]
    x_pairs = [(0, 1), (1, 0)]

    def joint(place, core):
        place = place % ring
        far = place >= chips
        level = ring - 1 - place if far else place
        return (2 * level + core) * 2 + int(far)

    def forward(values, step, cross=0):
        pairs = [(joint(p, c), joint(p + step, c ^ cross)) for p in range(ring) for c in range(2)]
        return lax.ppermute(values, ("orient", "cls"), pairs)

    vmem = pl.BlockSpec(memory_space=pltpu.VMEM)
    smem = pl.BlockSpec(memory_space=pltpu.SMEM)
    params = pltpu.CompilerParams(vmem_limit_bytes=VMEM_LIMIT)
    planes = lax.optimization_barrier(jnp.transpose(images[0], (1, 0, 2)))
    facts = jnp.concatenate([defocus, jnp.transpose(block_ids[0]).astype(jnp.bfloat16)], axis=0)
    facts = jnp.pad(facts, ((0, per_device - facts.shape[0]), (0, LANES - per_device)))
    row_shape = jax.ShapeDtypeStruct((per_device, columns + LANES), jnp.bfloat16)
    kept, given = pl.pallas_call(
        row_kernel,
        in_specs=[smem, vmem, vmem],
        out_specs=[vmem] * 2,
        out_shape=[row_shape] * 2,
        compiler_params=params,
    )(spot, planes, facts)

    _, panels = lax.optimization_barrier((kept, panels))
    sides = lax.optimization_barrier(jnp.transpose(panels[0, 0], (1, 0, 2)))
    panel_shape = jax.ShapeDtypeStruct(sides.shape[1:], sides.dtype)
    own_panel, given_panel = pl.pallas_call(
        panel_kernel,
        in_specs=[smem, vmem],
        out_specs=[vmem] * 2,
        out_shape=[panel_shape] * 2,
        compiler_params=params,
    )(spot, sides)
    with jax.named_scope("mate_panel"):
        mate_panel = lax.ppermute(given_panel, "orient", mate_pairs)

    noise = noise_weight[None, :]
    waiting = []
    ahead = {False: kept, True: given}
    behind = {False: kept, True: given}
    orders, earlier, late = [], [], []
    squares = pl.pallas_call(
        square_kernel,
        in_specs=[vmem],
        out_specs=vmem,
        out_shape=panel_shape,
        compiler_params=params,
        cost_estimate=pl.CostEstimate(flops=SCHEDULING_WEIGHT, bytes_accessed=0, transcendentals=0),
    )(own_panel)
    score = lambda c: score_call(c, None, None, spot, noise, own_panel, squares, mate_panel)
    for step in range(1, chips + 1):
        if step == 3:
            orders.append([key for key, _ in waiting])
            earlier.append(score([c for _, c in waiting]))
            waiting = []
            for chain, c in ((ahead, False), (behind, True)):
                chain[c] = lax.optimization_barrier((chain[c], earlier[-1][2]))[0]
        if step == 2:
            for chain, c in ((ahead, False), (behind, True)):
                chain[c] = lax.optimization_barrier((chain[c], squares))[0]
        waiting = waiting + late
        late = []
        for crossed in (False, True):
            if step < chips or not crossed:
                with jax.named_scope("rows_ahead"):
                    ahead[crossed] = forward(ahead[crossed], 1, int(crossed and step == 1))
                late.append(((-step, crossed), ahead[crossed]))
            if step < chips or crossed:
                with jax.named_scope("rows_behind"):
                    behind[crossed] = forward(behind[crossed], -1, int(crossed and step == 1))
                late.append(((step, crossed), behind[crossed]))
        if step == 1:
            late_given, _ = lax.optimization_barrier((given, kept))
            with jax.named_scope("mate_rows"):
                got = lax.ppermute(late_given, "orient", mate_pairs)
            late = [((0, False), kept), ((0, True), got)] + late
    orders.append([key for key, _ in waiting])
    earlier.append(score([c for _, c in waiting]))
    waiting = late
    orders.append([key for key, _ in waiting])
    partial, all_facts = score_call(
        [c for _, c in waiting], orders, earlier, spot, noise, own_panel, squares, mate_panel
    )

    mate_partial = lax.ppermute(partial, "orient", mate_pairs)
    mine, across, stats = pl.pallas_call(
        functools.partial(chip_kernel, local_search),
        in_specs=[smem] + [vmem] * 3,
        out_specs=[vmem] * 3,
        out_shape=[
            jax.ShapeDtypeStruct((everyone, orientations), jnp.float32),
            jax.ShapeDtypeStruct((everyone, orientations), jnp.float32),
            jax.ShapeDtypeStruct((8, everyone), jnp.float32),
        ],
        compiler_params=params,
    )(spot, partial, mate_partial, all_facts)

    x_stats = lax.ppermute(stats, "cls", x_pairs)
    across, _ = lax.optimization_barrier((across, stats))
    from_x = lax.ppermute(across, "cls", x_pairs)
    peak = jnp.maximum(stats[0], x_stats[1])
    total = stats[2] * jnp.exp(stats[0] - peak) + x_stats[3] * jnp.exp(x_stats[1] - peak)
    pair = jnp.pad(jnp.stack([peak, total]), ((0, 6), (0, 0)))
    slots, chosen, tops = pl.pallas_call(
        functools.partial(slot_kernel, local_search, slots_each, per_device),
        in_specs=[smem] + [vmem] * 3,
        out_specs=[vmem] * 3,
        out_shape=[
            jax.ShapeDtypeStruct((capacity, 2 * orientations), jnp.float32),
            jax.ShapeDtypeStruct((capacity, everyone), jnp.float32),
            jax.ShapeDtypeStruct((8, everyone), jnp.float32),
        ],
        compiler_params=params,
    )(spot, mine, from_x, all_facts)
    parts = [pair] + [
        lax.ppermute(pair, "orient", [(d, d ^ (2 * s)) for d in range(devices)])
        for s in reversed(range(1, chips))
    ]
    posterior = pl.pallas_call(
        functools.partial(final_kernel, chips),
        in_specs=[vmem] * (chips + 3),
        out_specs=vmem,
        out_shape=jax.ShapeDtypeStruct((capacity, 2 * orientations), jnp.float32),
        compiler_params=params,
    )(*parts, tops, slots, chosen)
    return posterior.reshape(1, 1, capacity, -1)


def spread_max(member, is_live, values):
    picked = jnp.max(jnp.where(member, values[None, :], FLOOR), axis=1)
    return jnp.where(is_live, picked, 0.0)


def collect_sums(member, expo):
    return jnp.sum(jnp.where(member, jnp.sum(expo, axis=1)[:, None], 0.0), axis=0)


def shards(images, defocus, block_ids, noise_weight, panels):
    per_device = images.shape[1]
    columns = images.shape[3]
    devices = lax.axis_size("orient")
    local_search = block_ids.shape[2]
    slots_each = min(per_device, max(2, 2 * per_device * local_search // devices))
    capacity = slots_each * devices
    everyone = per_device * devices
    all_lists = lax.all_gather(block_ids[0], "orient", axis=0, tiled=True)
    all_rows, all_focus = (
        lax.all_gather(images[0], "orient", axis=0, tiled=True),
        lax.all_gather(defocus[0], "orient", axis=0, tiled=True),
    )
    own_block = lax.axis_index("orient")
    block_hits = (
        jnp.any(all_lists == own_block, axis=1).astype(jnp.int32).reshape(devices, per_device)
    )
    slot_rank = jnp.cumsum(block_hits, axis=1) - block_hits
    places = (jnp.arange(devices, dtype=jnp.int32)[:, None] * slots_each + slot_rank).reshape(
        everyone
    )
    chosen = (places[None, :] == jnp.arange(capacity, dtype=jnp.int32)[:, None]) & (
        block_hits.reshape(everyone)[None, :] == 1
    )
    is_live = jnp.any(chosen, axis=1)
    slot_owner = jnp.sum(
        jnp.where(chosen, jnp.arange(everyone, dtype=jnp.int32)[None, :], 0), axis=1
    )
    slot_rows = jnp.take(all_rows, slot_owner, axis=0)
    slot_focus = jnp.take(all_focus, slot_owner, axis=0).astype(jnp.float32)
    frequency = (jnp.arange(columns, dtype=jnp.float32) + 0.5) / columns
    contrast = -jnp.sin(CTF_PHASE * slot_focus[:, None] * frequency[None, :] + 0.1)
    weighted = contrast * noise_weight[None, :]
    scaled_rows = (weighted[:, None, :] * slot_rows.astype(jnp.float32)).astype(jnp.bfloat16)
    energy = (contrast * weighted).astype(jnp.bfloat16)
    piece = lax.all_gather(panels[:, 0], "cls", axis=0, tiled=True)
    widened = piece.astype(jnp.float32)
    squared = (widened * widened).astype(jnp.bfloat16)
    correlate = jnp.einsum("srk,cjrk->scj", scaled_rows, piece, preferred_element_type=jnp.float32)
    energy_term = jnp.einsum("sk,cjrk->scj", energy, squared, preferred_element_type=jnp.float32)
    terms = correlate - 0.5 * energy_term
    combined = terms.reshape(capacity, -1)
    scores = lax.psum_scatter(combined, "rep", scatter_dimension=1, tiled=True)
    member = (slot_owner[:, None] == jnp.arange(everyone, dtype=jnp.int32)[None, :]) & is_live[
        :, None
    ]
    slot_top = jnp.max(scores, axis=1)
    local_peak = jnp.max(jnp.where(member, slot_top[:, None], FLOOR), axis=0)
    peak = lax.pmax(local_peak, ("orient", "rep"))
    slot_peak = spread_max(member, is_live, peak)
    expo = jnp.where(is_live[:, None], jnp.exp(scores - slot_peak[:, None]), 0.0)
    total = lax.psum(collect_sums(member, expo), ("orient", "rep"))
    slot_total = jnp.where(is_live, jnp.sum(jnp.where(member, total[None, :], 0.0), axis=1), 1.0)
    posterior = expo / slot_total[:, None]
    return posterior.reshape(1, 1, capacity, -1)


def solution(mesh):
    in_specs = (
        P(("batch", "cls"), "orient", "rep", None),
        P(("batch", "cls"), "orient"),
        P(("batch", "cls"), "orient", None),
        P(),
        P(("batch", "cls"), "orient", None, "rep", None),
    )
    out_specs = P(("batch", "cls"), "orient", None, "rep")
    sizes = mesh.shape
    paired = sizes["rep"] == 1 and sizes["cls"] == 2 and sizes["orient"] in (4, 8, 16, 32)
    return jax.shard_map(
        chip_shards if paired else shards,
        mesh=mesh,
        in_specs=in_specs,
        out_specs=out_specs,
        check_vma=False,
    )
```

```python
import functools

import jax
import jax.numpy as jnp
from jax import lax
from jax.experimental import pallas as pl
from jax.experimental.pallas import tpu as pltpu
from jax.sharding import PartitionSpec as P

CTF_PHASE = 40.0
FLOOR = -1e30
LANES = 128
VMEM_LIMIT = 5 * 1024 * 1024
SCHEDULING_WEIGHT = 20 * 10**9


def sin_cos(angle):
    turns = jnp.floor(angle * 0.6366197723675814 + 0.5)
    rest = angle - turns * 1.5703125
    rest = rest - turns * 4.837512969970703e-4
    rest = rest - turns * 7.549789948768648e-8
    square = rest * rest
    sine = rest + rest * square * (
        -1.6666654611e-1 + square * (8.3321608736e-3 - square * 1.9515295891e-4)
    )
    cosine = (
        1.0
        - 0.5 * square
        + square
        * square
        * (4.166664568298827e-2 + square * (-1.388731625493765e-3 + square * 2.443315711809948e-5))
    )
    quarter = turns.astype(jnp.int32)
    odd = (quarter & 1) == 1
    low = jnp.where(odd, cosine, sine)
    high = jnp.where(odd, sine, cosine)
    return (
        jnp.where((quarter & 2) == 2, -low, low),
        jnp.where(((quarter + 1) & 2) == 2, -high, high),
    )


def panel_kernel(spot, sides, own, given):
    own[...] = sides[spot[2]]
    given[...] = sides[1 - spot[2]]


def square_kernel(own, squares):
    squares[...] = own[...] * own[...]


def particle_facts(meta):
    return jnp.concatenate([m[...].astype(jnp.float32).T[: m.shape[0]] for m in meta], axis=0)


def add_scores(rows, noise, own_panel, own_squares, mate_panel, turn_sin, turn_cos, sums, segments):
    columns = noise.shape[1]
    width = columns // segments
    tiles = width // LANES
    count = turn_sin.shape[0]
    facts = particle_facts([r.at[:, pl.ds(columns, LANES)] for r in rows])
    rate = jnp.broadcast_to(CTF_PHASE * facts[:, 0:1], (count, LANES))
    lane = lax.broadcasted_iota(jnp.int32, (count, LANES), 1).astype(jnp.float32)
    first_sin, first_cos = sin_cos(rate * ((lane + 0.5) / columns) + 0.1)
    step_sin, step_cos = sin_cos(rate * (LANES / columns))
    turn_sin[...] = step_sin
    turn_cos[...] = step_cos
    for total in sums:
        total[...] = jnp.zeros_like(total)

    def segment(index, carry):
        sine, cosine = carry
        start = pl.multiple_of(index * width, LANES)
        scaled_parts, energy_parts = [], []
        for t in range(tiles):
            window = pl.ds(start + t * LANES, LANES)
            weighted = sine * noise[:, window]
            image = jnp.concatenate([r[:, window] for r in rows], axis=0).astype(jnp.float32)
            scaled_parts.append((weighted * image).astype(jnp.bfloat16))
            energy_parts.append((sine * weighted).astype(jnp.bfloat16))
            ds, dc = turn_sin[...], turn_cos[...]
            sine, cosine = sine * dc + cosine * ds, cosine * dc - sine * ds
        scaled = jnp.concatenate(scaled_parts, axis=1)
        energy = jnp.concatenate(energy_parts, axis=1)
        contract = (((1,), (1,)), ((), ()))
        whole = pl.ds(start, width)
        mate = mate_panel[:, whole]
        for values, squared, total in (
            (own_panel[:, whole], own_squares[:, whole], sums[0]),
            (mate, mate * mate, sums[1]),
        ):
            correlate = lax.dot_general(
                values, scaled, contract, preferred_element_type=jnp.float32
            )
            power = lax.dot_general(squared, energy, contract, preferred_element_type=jnp.float32)
            total[...] += correlate - 0.5 * power
        return sine, cosine

    lax.fori_loop(0, segments, segment, (-first_sin, -first_cos))
    return jnp.pad(facts, ((0, 0), (0, LANES - facts.shape[1])))


def batch_kernel(n, segments, spot, *refs):
    rows = refs[:n]
    noise, own_panel, own_squares, mate_panel = refs[n : n + 4]
    own_out, mate_out, fact_out, turn_sin, turn_cos, *sums = refs[n + 4 :]
    fact_out[...] = add_scores(
        rows, noise, own_panel, own_squares, mate_panel, turn_sin, turn_cos, sums, segments
    )
    own_out[...] = sums[0][...].T
    mate_out[...] = sums[1][...].T


def last_kernel(n, segments, orders, spot, *refs):
    rows = refs[:n]
    noise, own_panel, own_squares, mate_panel = refs[n : n + 4]
    rest = refs[n + 4 :]
    earlier, rest = rest[: 3 * (len(orders) - 1)], rest[3 * (len(orders) - 1) :]
    partial, facts, turn_sin, turn_cos, *sums = rest
    last_facts = add_scores(
        rows, noise, own_panel, own_squares, mate_panel, turn_sin, turn_cos, sums, segments
    )
    position, core = spot[1], spot[2]
    each = rows[0].shape[0]
    ring = facts.shape[0] // (2 * each)
    half = ring // 2
    for index, order in enumerate(orders):
        if index < len(orders) - 1:
            own, mate, fact = [r[...] for r in earlier[3 * index : 3 * index + 3]]
        else:
            own, mate, fact = sums[0][...].T, sums[1][...].T, last_facts
        for k, (distance, crossed) in enumerate(order):
            place = lax.rem(position + distance + ring, ring)
            far = place >= half
            level = jnp.where(far, ring - 1 - place, place)
            device = 2 * level + (1 - core if crossed else core)
            start = pl.multiple_of((jnp.where(far, ring, 0) + device) * each, each)
            piece = slice(k * each, (k + 1) * each)
            partial[core, pl.ds(start, each), :] = own[piece]
            partial[1 - core, pl.ds(start, each), :] = mate[piece]
            facts[pl.ds(start, each), :] = fact[piece]


def score_call(chunks, orders, earlier, spot, noise, own_panel, squares, mate_panel):
    each = chunks[0].shape[0]
    orientations, columns = own_panel.shape
    whole = columns // LANES
    segments = 1
    n = len(chunks)
    count = each * n
    scratch = [pltpu.VMEM((count, LANES), jnp.float32)] * 2
    scratch += [pltpu.VMEM((orientations, count), jnp.float32)] * 2
    single = jax.ShapeDtypeStruct((count, orientations), jnp.float32)
    if orders is None:
        kernel = functools.partial(batch_kernel, n, segments)
        out_shape = [single, single, jax.ShapeDtypeStruct((count, LANES), jnp.float32)]
        extra = []
    else:
        everyone = each * sum(len(o) for o in orders)
        kernel = functools.partial(last_kernel, n, segments, orders)
        out_shape = [
            jax.ShapeDtypeStruct((2, everyone, orientations), jnp.float32),
            jax.ShapeDtypeStruct((everyone, LANES), jnp.float32),
        ]
        extra = [e for triple in earlier for e in triple]
    vmem = pl.BlockSpec(memory_space=pltpu.VMEM)
    return pl.pallas_call(
        kernel,
        in_specs=[pl.BlockSpec(memory_space=pltpu.SMEM)] + [vmem] * (n + 4 + len(extra)),
        out_specs=[vmem] * len(out_shape),
        out_shape=out_shape,
        scratch_shapes=scratch,
        compiler_params=pltpu.CompilerParams(vmem_limit_bytes=VMEM_LIMIT),
        cost_estimate=pl.CostEstimate(
            flops=8 * max(count, 128) * orientations * columns,
            bytes_accessed=4 * orientations * columns + 2 * count * columns,
            transcendentals=0,
        ),
    )(spot, *chunks, noise, own_panel, squares, mate_panel, *extra)


def names_block(facts, search, block):
    lane = lax.broadcasted_iota(jnp.int32, facts.shape, 1)
    match = (lane >= 1) & (lane <= search) & (facts == block.astype(jnp.float32))
    return jnp.max(jnp.where(match, 1.0, 0.0), axis=1, keepdims=True) > 0.0


def chip_kernel(search, spot, partial, mate, facts, mine, across, stats):
    group, core, place = spot[0], spot[2], spot[3]
    count = mine.shape[0]
    lane = lax.broadcasted_iota(jnp.int32, (count, LANES), 1)
    pairs = []
    for relative in range(2):
        side = group if relative == 0 else 1 - group
        window = pl.ds(pl.multiple_of(side * count, count), count)
        listed = facts[window, :]
        masked = []
        for crossed in range(2):
            block = core if crossed == 0 else 1 - core
            scores = partial[block, window, :] + mate[block, window, :]
            if crossed == 0:
                out = mine if relative == 0 else across
                out[...] = scores
            named = names_block(listed, search, place - core + block)
            masked.append(jnp.where(named, scores, FLOOR))
        top = jnp.max(jnp.maximum(*masked), axis=1, keepdims=True)
        terms = [jnp.where(m > FLOOR, jnp.exp(m - top), 0.0) for m in masked]
        total = jnp.sum(terms[0] + terms[1], axis=1, keepdims=True)
        pairs.append(jnp.where(lane == relative, top, jnp.where(lane == 2 + relative, total, 0.0)))
    stats[...] = (pairs[0] + pairs[1]).T[: stats.shape[0]]


def slot_kernel(search, slots_each, each, spot, mine, across, facts, slots, chosen, tops):
    group, place = spot[0], spot[3]
    count = mine.shape[0]
    same, other = mine[...], across[...]
    first = group == 0
    scores = jnp.concatenate(
        [jnp.where(first, same, other), jnp.where(first, other, same)], axis=1
    )
    listed = facts[pl.ds(pl.multiple_of(group * count, count), count), :]
    named = names_block(listed, search, place)
    hit = jnp.where(named, 1.0, 0.0)
    row = lax.broadcasted_iota(jnp.int32, (count, LANES), 0)
    line = lax.broadcasted_iota(jnp.int32, (count, count), 0)
    column = lax.broadcasted_iota(jnp.int32, (count, count), 1)
    before = (column < line) & (column // each == line // each)
    rank = jnp.dot(
        jnp.where(before, 1.0, 0.0).astype(jnp.bfloat16),
        jnp.broadcast_to(hit, (count, LANES)).astype(jnp.bfloat16),
        preferred_element_type=jnp.float32,
    )
    slot = (row // each) * slots_each + rank.astype(jnp.int32)
    capacity = chosen.shape[0]
    if capacity != LANES:
        slot = jnp.broadcast_to(slot[:, :1], (count, capacity))
    target = lax.broadcasted_iota(jnp.int32, (count, capacity), 1)
    taken = jnp.where((slot == target) & named, 1.0, 0.0)
    top = jnp.max(scores, axis=1, keepdims=True)
    tops[...] = jnp.broadcast_to(top, (count, LANES)).T[: tops.shape[0]]
    terms = jnp.where(named, jnp.exp(scores - top), 0.0)
    slots[...] = lax.dot_general(
        taken,
        terms,
        (((0,), (0,)), ((), ())),
        precision=lax.Precision.HIGHEST,
        preferred_element_type=jnp.float32,
    )
    chosen[...] = taken.T


def final_kernel(n, *refs):
    parts, (tops, slots, chosen, out) = refs[:n], refs[n:]
    peak = functools.reduce(jnp.maximum, [p[0:1, :] for p in parts])
    shares = [p[1:2, :] * jnp.exp(p[0:1, :] - peak) for p in parts]
    total = functools.reduce(jnp.add, shares)
    factor = jnp.exp(jnp.minimum(tops[0:1, :] - peak, 0.0)) / total
    scale = jnp.sum(chosen[...] * factor, axis=1, keepdims=True)
    out[...] = slots[...] * scale


def chip_shards(images, defocus, block_ids, noise_weight, panels):
    per_device, halves, columns = images.shape[1:]
    devices = lax.axis_size("orient")
    chips = devices // 2
    ring = 2 * chips
    everyone = per_device * devices
    local_search = block_ids.shape[2]
    orientations = panels.shape[2]
    slots_each = min(per_device, max(2, 2 * per_device * local_search // devices))
    capacity = slots_each * devices
    place = lax.axis_index("orient")
    group = lax.axis_index("cls")
    chip, core = place // 2, place % 2
    position = jnp.where(group == 0, chip, ring - 1 - chip)
    spot = jnp.stack([group, position, core, place]).astype(jnp.int32)

    mate_pairs = [(d, d ^ 1) for d in range(devices)]
    x_pairs = [(0, 1), (1, 0)]

    def joint(place, core):
        place = place % ring
        far = place >= chips
        level = ring - 1 - place if far else place
        return (2 * level + core) * 2 + int(far)

    def forward(values, step, cross=0):
        pairs = [(joint(p, c), joint(p + step, c ^ cross)) for p in range(ring) for c in range(2)]
        return lax.ppermute(values, ("orient", "cls"), pairs)

    vmem = pl.BlockSpec(memory_space=pltpu.VMEM)
    smem = pl.BlockSpec(memory_space=pltpu.SMEM)
    params = pltpu.CompilerParams(vmem_limit_bytes=VMEM_LIMIT)
    first = core == 0
    planes = lax.optimization_barrier(jnp.transpose(images[0], (1, 0, 2)))
    facts = jnp.concatenate([defocus, jnp.transpose(block_ids[0]).astype(jnp.bfloat16)], axis=0)
    facts = jnp.pad(facts, ((0, per_device - facts.shape[0]), (0, LANES - per_device)))
    kept = jnp.concatenate([jnp.where(first, planes[0], planes[1]), facts], axis=1)
    given = jnp.concatenate([jnp.where(first, planes[1], planes[0]), facts], axis=1)
    _, panels = lax.optimization_barrier((kept, panels))
    sides = lax.optimization_barrier(jnp.transpose(panels[0, 0], (1, 0, 2)))
    panel_shape = jax.ShapeDtypeStruct(sides.shape[1:], sides.dtype)
    own_panel, given_panel = pl.pallas_call(
        panel_kernel,
        in_specs=[smem, vmem],
        out_specs=[vmem] * 2,
        out_shape=[panel_shape] * 2,
        compiler_params=params,
    )(spot, sides)
    with jax.named_scope("mate_panel"):
        mate_panel = lax.ppermute(given_panel, "orient", mate_pairs)

    noise = noise_weight[None, :]
    waiting = []
    ahead = {False: kept, True: given}
    behind = {False: kept, True: given}
    orders, earlier, late = [], [], []
    squares = pl.pallas_call(
        square_kernel,
        in_specs=[vmem],
        out_specs=vmem,
        out_shape=panel_shape,
        compiler_params=params,
        cost_estimate=pl.CostEstimate(flops=SCHEDULING_WEIGHT, bytes_accessed=0, transcendentals=0),
    )(own_panel)
    score = lambda c: score_call(c, None, None, spot, noise, own_panel, squares, mate_panel)
    for step in range(1, chips + 1):
        if step == 3:
            orders.append([key for key, _ in waiting])
            earlier.append(score([c for _, c in waiting]))
            waiting = []
            for chain, c in ((ahead, False), (behind, True)):
                chain[c] = lax.optimization_barrier((chain[c], earlier[-1][2]))[0]
        if step == 2:
            for chain, c in ((ahead, False), (behind, True)):
                chain[c] = lax.optimization_barrier((chain[c], squares))[0]
        waiting = waiting + late
        late = []
        for crossed in (False, True):
            if step < chips or not crossed:
                with jax.named_scope("rows_ahead"):
                    ahead[crossed] = forward(ahead[crossed], 1, int(crossed and step == 1))
                late.append(((-step, crossed), ahead[crossed]))
            if step < chips or crossed:
                with jax.named_scope("rows_behind"):
                    behind[crossed] = forward(behind[crossed], -1, int(crossed and step == 1))
                late.append(((step, crossed), behind[crossed]))
        if step == 1:
            late_given, _ = lax.optimization_barrier((given, kept))
            with jax.named_scope("mate_rows"):
                got = lax.ppermute(late_given, "orient", mate_pairs)
            late = [((0, False), kept), ((0, True), got)] + late
    orders.append([key for key, _ in waiting])
    earlier.append(score([c for _, c in waiting]))
    waiting = late
    orders.append([key for key, _ in waiting])
    partial, all_facts = score_call(
        [c for _, c in waiting], orders, earlier, spot, noise, own_panel, squares, mate_panel
    )

    mate_partial = lax.ppermute(partial, "orient", mate_pairs)
    mine, across, stats = pl.pallas_call(
        functools.partial(chip_kernel, local_search),
        in_specs=[smem] + [vmem] * 3,
        out_specs=[vmem] * 3,
        out_shape=[
            jax.ShapeDtypeStruct((everyone, orientations), jnp.float32),
            jax.ShapeDtypeStruct((everyone, orientations), jnp.float32),
            jax.ShapeDtypeStruct((8, everyone), jnp.float32),
        ],
        compiler_params=params,
    )(spot, partial, mate_partial, all_facts)

    x_stats = lax.ppermute(stats, "cls", x_pairs)
    across, _ = lax.optimization_barrier((across, stats))
    from_x = lax.ppermute(across, "cls", x_pairs)
    peak = jnp.maximum(stats[0], x_stats[1])
    total = stats[2] * jnp.exp(stats[0] - peak) + x_stats[3] * jnp.exp(x_stats[1] - peak)
    pair = jnp.pad(jnp.stack([peak, total]), ((0, 6), (0, 0)))
    slots, chosen, tops = pl.pallas_call(
        functools.partial(slot_kernel, local_search, slots_each, per_device),
        in_specs=[smem] + [vmem] * 3,
        out_specs=[vmem] * 3,
        out_shape=[
            jax.ShapeDtypeStruct((capacity, 2 * orientations), jnp.float32),
            jax.ShapeDtypeStruct((capacity, everyone), jnp.float32),
            jax.ShapeDtypeStruct((8, everyone), jnp.float32),
        ],
        compiler_params=params,
    )(spot, mine, from_x, all_facts)
    if chips == 4:
        near = lax.ppermute(pair, "orient", [(d, d ^ (2 << d % 2)) for d in range(devices)])
        far = lax.ppermute(pair, "orient", [(d, d ^ 6) for d in range(devices)])
        near, tops = lax.optimization_barrier((near, tops))
        parts = [pair, near, lax.ppermute(near, "orient", mate_pairs), far]
    else:
        parts = [pair] + [
            lax.ppermute(pair, "orient", [(d, (d + 2 * s) % devices) for d in range(devices)])
            for s in range(1, chips)
        ]
    posterior = pl.pallas_call(
        functools.partial(final_kernel, chips),
        in_specs=[vmem] * (chips + 3),
        out_specs=vmem,
        out_shape=jax.ShapeDtypeStruct((capacity, 2 * orientations), jnp.float32),
        compiler_params=params,
    )(*parts, tops, slots, chosen)
    return posterior.reshape(1, 1, capacity, -1)


def spread_max(member, is_live, values):
    picked = jnp.max(jnp.where(member, values[None, :], FLOOR), axis=1)
    return jnp.where(is_live, picked, 0.0)


def collect_sums(member, expo):
    return jnp.sum(jnp.where(member, jnp.sum(expo, axis=1)[:, None], 0.0), axis=0)


def shards(images, defocus, block_ids, noise_weight, panels):
    per_device = images.shape[1]
    columns = images.shape[3]
    devices = lax.axis_size("orient")
    local_search = block_ids.shape[2]
    slots_each = min(per_device, max(2, 2 * per_device * local_search // devices))
    capacity = slots_each * devices
    everyone = per_device * devices
    all_lists = lax.all_gather(block_ids[0], "orient", axis=0, tiled=True)
    all_rows, all_focus = (
        lax.all_gather(images[0], "orient", axis=0, tiled=True),
        lax.all_gather(defocus[0], "orient", axis=0, tiled=True),
    )
    own_block = lax.axis_index("orient")
    block_hits = (
        jnp.any(all_lists == own_block, axis=1).astype(jnp.int32).reshape(devices, per_device)
    )
    slot_rank = jnp.cumsum(block_hits, axis=1) - block_hits
    places = (jnp.arange(devices, dtype=jnp.int32)[:, None] * slots_each + slot_rank).reshape(
        everyone
    )
    chosen = (places[None, :] == jnp.arange(capacity, dtype=jnp.int32)[:, None]) & (
        block_hits.reshape(everyone)[None, :] == 1
    )
    is_live = jnp.any(chosen, axis=1)
    slot_owner = jnp.sum(
        jnp.where(chosen, jnp.arange(everyone, dtype=jnp.int32)[None, :], 0), axis=1
    )
    slot_rows = jnp.take(all_rows, slot_owner, axis=0)
    slot_focus = jnp.take(all_focus, slot_owner, axis=0).astype(jnp.float32)
    frequency = (jnp.arange(columns, dtype=jnp.float32) + 0.5) / columns
    contrast = -jnp.sin(CTF_PHASE * slot_focus[:, None] * frequency[None, :] + 0.1)
    weighted = contrast * noise_weight[None, :]
    scaled_rows = (weighted[:, None, :] * slot_rows.astype(jnp.float32)).astype(jnp.bfloat16)
    energy = (contrast * weighted).astype(jnp.bfloat16)
    piece = lax.all_gather(panels[:, 0], "cls", axis=0, tiled=True)
    widened = piece.astype(jnp.float32)
    squared = (widened * widened).astype(jnp.bfloat16)
    correlate = jnp.einsum("srk,cjrk->scj", scaled_rows, piece, preferred_element_type=jnp.float32)
    energy_term = jnp.einsum("sk,cjrk->scj", energy, squared, preferred_element_type=jnp.float32)
    terms = correlate - 0.5 * energy_term
    combined = terms.reshape(capacity, -1)
    scores = lax.psum_scatter(combined, "rep", scatter_dimension=1, tiled=True)
    member = (slot_owner[:, None] == jnp.arange(everyone, dtype=jnp.int32)[None, :]) & is_live[
        :, None
    ]
    slot_top = jnp.max(scores, axis=1)
    local_peak = jnp.max(jnp.where(member, slot_top[:, None], FLOOR), axis=0)
    peak = lax.pmax(local_peak, ("orient", "rep"))
    slot_peak = spread_max(member, is_live, peak)
    expo = jnp.where(is_live[:, None], jnp.exp(scores - slot_peak[:, None]), 0.0)
    total = lax.psum(collect_sums(member, expo), ("orient", "rep"))
    slot_total = jnp.where(is_live, jnp.sum(jnp.where(member, total[None, :], 0.0), axis=1), 1.0)
    posterior = expo / slot_total[:, None]
    return posterior.reshape(1, 1, capacity, -1)


def solution(mesh):
    in_specs = (
        P(("batch", "cls"), "orient", "rep", None),
        P(("batch", "cls"), "orient"),
        P(("batch", "cls"), "orient", None),
        P(),
        P(("batch", "cls"), "orient", None, "rep", None),
    )
    out_specs = P(("batch", "cls"), "orient", None, "rep")
    sizes = mesh.shape
    paired = sizes["rep"] == 1 and sizes["cls"] == 2 and sizes["orient"] in (4, 8, 16, 32)
    return jax.shard_map(
        chip_shards if paired else shards,
        mesh=mesh,
        in_specs=in_specs,
        out_specs=out_specs,
        check_vma=False,
    )
```

```python
import functools

import jax
import jax.numpy as jnp
from jax import lax
from jax.experimental import pallas as pl
from jax.experimental.pallas import tpu as pltpu
from jax.sharding import PartitionSpec as P

CTF_PHASE = 40.0
FLOOR = -1e30
LANES = 128
VMEM_LIMIT = 8 * 1024 * 1024
SCHEDULING_WEIGHT = 20 * 10**9


def sin_cos(angle):
    turns = jnp.floor(angle * 0.6366197723675814 + 0.5)
    rest = angle - turns * 1.5703125
    rest = rest - turns * 4.837512969970703e-4
    rest = rest - turns * 7.549789948768648e-8
    square = rest * rest
    sine = rest + rest * square * (
        -1.6666654611e-1 + square * (8.3321608736e-3 - square * 1.9515295891e-4)
    )
    cosine = (
        1.0
        - 0.5 * square
        + square
        * square
        * (4.166664568298827e-2 + square * (-1.388731625493765e-3 + square * 2.443315711809948e-5))
    )
    quarter = turns.astype(jnp.int32)
    odd = (quarter & 1) == 1
    low = jnp.where(odd, cosine, sine)
    high = jnp.where(odd, sine, cosine)
    return (
        jnp.where((quarter & 2) == 2, -low, low),
        jnp.where(((quarter + 1) & 2) == 2, -high, high),
    )


def panel_kernel(spot, sides, own, given):
    own[...] = sides[spot[2]]
    given[...] = sides[1 - spot[2]]


def square_kernel(own, squares):
    squares[...] = own[...] * own[...]


def row_kernel(spot, planes, facts, kept, given):
    core = spot[2]
    columns = planes.shape[2]
    for half, out in ((core, kept), (1 - core, given)):
        out[:, :columns] = planes[half]
        out[:, columns:] = facts[...]


def particle_facts(meta):
    return jnp.concatenate([m[...].astype(jnp.float32).T[: m.shape[0]] for m in meta], axis=0)


def add_scores(rows, noise, own_panel, own_squares, mate_panel, turn_sin, turn_cos, sums, segments):
    columns = noise.shape[1]
    width = columns // segments
    tiles = width // LANES
    count = turn_sin.shape[0]
    facts = particle_facts([r.at[:, pl.ds(columns, LANES)] for r in rows])
    rate = jnp.broadcast_to(CTF_PHASE * facts[:, 0:1], (count, LANES))
    lane = lax.broadcasted_iota(jnp.int32, (count, LANES), 1).astype(jnp.float32)
    first_sin, first_cos = sin_cos(rate * ((lane + 0.5) / columns) + 0.1)
    step_sin, step_cos = sin_cos(rate * (LANES / columns))
    turn_sin[...] = step_sin
    turn_cos[...] = step_cos
    for total in sums:
        total[...] = jnp.zeros_like(total)

    def segment(index, carry):
        sine, cosine = carry
        start = pl.multiple_of(index * width, LANES)
        scaled_parts, energy_parts = [], []
        for t in range(tiles):
            window = pl.ds(start + t * LANES, LANES)
            weighted = sine * noise[:, window]
            image = jnp.concatenate([r[:, window] for r in rows], axis=0).astype(jnp.float32)
            scaled_parts.append((weighted * image).astype(jnp.bfloat16))
            energy_parts.append((sine * weighted).astype(jnp.bfloat16))
            ds, dc = turn_sin[...], turn_cos[...]
            sine, cosine = sine * dc + cosine * ds, cosine * dc - sine * ds
        scaled = jnp.concatenate(scaled_parts, axis=1)
        energy = jnp.concatenate(energy_parts, axis=1)
        contract = (((1,), (1,)), ((), ()))
        whole = pl.ds(start, width)
        mate = mate_panel[:, whole]
        for values, squared, total in (
            (own_panel[:, whole], own_squares[:, whole], sums[0]),
            (mate, mate * mate, sums[1]),
        ):
            correlate = lax.dot_general(
                values, scaled, contract, preferred_element_type=jnp.float32
            )
            power = lax.dot_general(squared, energy, contract, preferred_element_type=jnp.float32)
            total[...] += correlate - 0.5 * power
        return sine, cosine

    lax.fori_loop(0, segments, segment, (-first_sin, -first_cos))
    return jnp.pad(facts, ((0, 0), (0, LANES - facts.shape[1])))


def batch_kernel(n, segments, spot, *refs):
    rows = refs[:n]
    noise, own_panel, own_squares, mate_panel = refs[n : n + 4]
    own_out, mate_out, fact_out, turn_sin, turn_cos, *sums = refs[n + 4 :]
    fact_out[...] = add_scores(
        rows, noise, own_panel, own_squares, mate_panel, turn_sin, turn_cos, sums, segments
    )
    own_out[...] = sums[0][...].T
    mate_out[...] = sums[1][...].T


def last_kernel(n, segments, orders, spot, *refs):
    rows = refs[:n]
    noise, own_panel, own_squares, mate_panel = refs[n : n + 4]
    rest = refs[n + 4 :]
    earlier, rest = rest[: 3 * (len(orders) - 1)], rest[3 * (len(orders) - 1) :]
    partial, facts, turn_sin, turn_cos, *sums = rest
    last_facts = add_scores(
        rows, noise, own_panel, own_squares, mate_panel, turn_sin, turn_cos, sums, segments
    )
    position, core = spot[1], spot[2]
    each = rows[0].shape[0]
    ring = facts.shape[0] // (2 * each)
    half = ring // 2
    for index, order in enumerate(orders):
        if index < len(orders) - 1:
            own, mate, fact = [r[...] for r in earlier[3 * index : 3 * index + 3]]
        else:
            own, mate, fact = sums[0][...].T, sums[1][...].T, last_facts
        for k, (distance, crossed) in enumerate(order):
            place = lax.rem(position + distance + ring, ring)
            far = place >= half
            level = jnp.where(far, ring - 1 - place, place)
            device = 2 * level + (1 - core if crossed else core)
            start = pl.multiple_of((jnp.where(far, ring, 0) + device) * each, each)
            piece = slice(k * each, (k + 1) * each)
            partial[core, pl.ds(start, each), :] = own[piece]
            partial[1 - core, pl.ds(start, each), :] = mate[piece]
            facts[pl.ds(start, each), :] = fact[piece]


def score_call(chunks, orders, earlier, spot, noise, own_panel, squares, mate_panel):
    each = chunks[0].shape[0]
    orientations, columns = own_panel.shape
    whole = columns // LANES
    segments = 1
    n = len(chunks)
    count = each * n
    scratch = [pltpu.VMEM((count, LANES), jnp.float32)] * 2
    scratch += [pltpu.VMEM((orientations, count), jnp.float32)] * 2
    single = jax.ShapeDtypeStruct((count, orientations), jnp.float32)
    if orders is None:
        kernel = functools.partial(batch_kernel, n, segments)
        out_shape = [single, single, jax.ShapeDtypeStruct((count, LANES), jnp.float32)]
        extra = []
    else:
        everyone = each * sum(len(o) for o in orders)
        kernel = functools.partial(last_kernel, n, segments, orders)
        out_shape = [
            jax.ShapeDtypeStruct((2, everyone, orientations), jnp.float32),
            jax.ShapeDtypeStruct((everyone, LANES), jnp.float32),
        ]
        extra = [e for triple in earlier for e in triple]
    vmem = pl.BlockSpec(memory_space=pltpu.VMEM)
    return pl.pallas_call(
        kernel,
        in_specs=[pl.BlockSpec(memory_space=pltpu.SMEM)] + [vmem] * (n + 4 + len(extra)),
        out_specs=[vmem] * len(out_shape),
        out_shape=out_shape,
        scratch_shapes=scratch,
        compiler_params=pltpu.CompilerParams(vmem_limit_bytes=VMEM_LIMIT),
        cost_estimate=pl.CostEstimate(
            flops=8 * max(count, 128) * orientations * columns,
            bytes_accessed=4 * orientations * columns + 2 * count * columns,
            transcendentals=0,
        ),
    )(spot, *chunks, noise, own_panel, squares, mate_panel, *extra)


def names_block(facts, search, block):
    lane = lax.broadcasted_iota(jnp.int32, facts.shape, 1)
    match = (lane >= 1) & (lane <= search) & (facts == block.astype(jnp.float32))
    return jnp.max(jnp.where(match, 1.0, 0.0), axis=1, keepdims=True) > 0.0


def chip_kernel(search, spot, partial, mate, facts, mine, across, stats):
    group, core, place = spot[0], spot[2], spot[3]
    count = mine.shape[0]
    lane = lax.broadcasted_iota(jnp.int32, (count, LANES), 1)
    pairs = []
    for relative in range(2):
        side = group if relative == 0 else 1 - group
        window = pl.ds(pl.multiple_of(side * count, count), count)
        listed = facts[window, :]
        masked = []
        for crossed in range(2):
            block = core if crossed == 0 else 1 - core
            scores = partial[block, window, :] + mate[block, window, :]
            if crossed == 0:
                out = mine if relative == 0 else across
                out[...] = scores
            named = names_block(listed, search, place - core + block)
            masked.append(jnp.where(named, scores, FLOOR))
        top = jnp.max(jnp.maximum(*masked), axis=1, keepdims=True)
        terms = [jnp.where(m > FLOOR, jnp.exp(m - top), 0.0) for m in masked]
        total = jnp.sum(terms[0] + terms[1], axis=1, keepdims=True)
        pairs.append(jnp.where(lane == relative, top, jnp.where(lane == 2 + relative, total, 0.0)))
    stats[...] = (pairs[0] + pairs[1]).T[: stats.shape[0]]


def slot_kernel(search, slots_each, each, spot, mine, across, facts, slots, chosen, tops):
    group, place = spot[0], spot[3]
    count = mine.shape[0]
    same, other = mine[...], across[...]
    first = group == 0
    scores = jnp.concatenate(
        [jnp.where(first, same, other), jnp.where(first, other, same)], axis=1
    )
    listed = facts[pl.ds(pl.multiple_of(group * count, count), count), :]
    named = names_block(listed, search, place)
    hit = jnp.where(named, 1.0, 0.0)
    row = lax.broadcasted_iota(jnp.int32, (count, LANES), 0)
    line = lax.broadcasted_iota(jnp.int32, (count, count), 0)
    column = lax.broadcasted_iota(jnp.int32, (count, count), 1)
    before = (column < line) & (column // each == line // each)
    rank = jnp.dot(
        jnp.where(before, 1.0, 0.0).astype(jnp.bfloat16),
        jnp.broadcast_to(hit, (count, LANES)).astype(jnp.bfloat16),
        preferred_element_type=jnp.float32,
    )
    slot = (row // each) * slots_each + rank.astype(jnp.int32)
    capacity = chosen.shape[0]
    if capacity != LANES:
        slot = jnp.broadcast_to(slot[:, :1], (count, capacity))
    target = lax.broadcasted_iota(jnp.int32, (count, capacity), 1)
    taken = jnp.where((slot == target) & named, 1.0, 0.0)
    top = jnp.max(scores, axis=1, keepdims=True)
    tops[...] = jnp.broadcast_to(top, (count, LANES)).T[: tops.shape[0]]
    terms = jnp.where(named, jnp.exp(scores - top), 0.0)
    slots[...] = lax.dot_general(
        taken,
        terms,
        (((0,), (0,)), ((), ())),
        precision=lax.Precision.HIGHEST,
        preferred_element_type=jnp.float32,
    )
    chosen[...] = taken.T


def final_kernel(n, *refs):
    parts, (tops, slots, chosen, out) = refs[:n], refs[n:]
    peak = functools.reduce(jnp.maximum, [p[0:1, :] for p in parts])
    shares = [p[1:2, :] * jnp.exp(p[0:1, :] - peak) for p in parts]
    total = functools.reduce(jnp.add, shares)
    factor = jnp.exp(jnp.minimum(tops[0:1, :] - peak, 0.0)) / total
    scale = jnp.sum(chosen[...] * factor, axis=1, keepdims=True)
    out[...] = slots[...] * scale


def chip_shards(images, defocus, block_ids, noise_weight, panels):
    per_device, halves, columns = images.shape[1:]
    devices = lax.axis_size("orient")
    chips = devices // 2
    ring = 2 * chips
    everyone = per_device * devices
    local_search = block_ids.shape[2]
    orientations = panels.shape[2]
    slots_each = min(per_device, max(2, 2 * per_device * local_search // devices))
    capacity = slots_each * devices
    place = lax.axis_index("orient")
    group = lax.axis_index("cls")
    chip, core = place // 2, place % 2
    position = jnp.where(group == 0, chip, ring - 1 - chip)
    spot = jnp.stack([group, position, core, place]).astype(jnp.int32)

    mate_pairs = [(d, d ^ 1) for d in range(devices)]
    x_pairs = [(0, 1), (1, 0)]

    def joint(place, core):
        place = place % ring
        far = place >= chips
        level = ring - 1 - place if far else place
        return (2 * level + core) * 2 + int(far)

    def forward(values, step, cross=0):
        pairs = [(joint(p, c), joint(p + step, c ^ cross)) for p in range(ring) for c in range(2)]
        return lax.ppermute(values, ("orient", "cls"), pairs)

    vmem = pl.BlockSpec(memory_space=pltpu.VMEM)
    smem = pl.BlockSpec(memory_space=pltpu.SMEM)
    params = pltpu.CompilerParams(vmem_limit_bytes=VMEM_LIMIT)
    planes = lax.optimization_barrier(jnp.transpose(images[0], (1, 0, 2)))
    facts = jnp.concatenate([defocus, jnp.transpose(block_ids[0]).astype(jnp.bfloat16)], axis=0)
    facts = jnp.pad(facts, ((0, per_device - facts.shape[0]), (0, LANES - per_device)))
    row_shape = jax.ShapeDtypeStruct((per_device, columns + LANES), jnp.bfloat16)
    kept, given = pl.pallas_call(
        row_kernel,
        in_specs=[smem, vmem, vmem],
        out_specs=[vmem] * 2,
        out_shape=[row_shape] * 2,
        compiler_params=params,
    )(spot, planes, facts)

    with jax.named_scope("mate_rows"):
        got = lax.ppermute(given, "orient", mate_pairs)

    _, panels = lax.optimization_barrier((got, panels))
    sides = lax.optimization_barrier(jnp.transpose(panels[0, 0], (1, 0, 2)))
    panel_shape = jax.ShapeDtypeStruct(sides.shape[1:], sides.dtype)
    own_panel, given_panel = pl.pallas_call(
        panel_kernel,
        in_specs=[smem, vmem],
        out_specs=[vmem] * 2,
        out_shape=[panel_shape] * 2,
        compiler_params=params,
    )(spot, sides)
    with jax.named_scope("mate_panel"):
        mate_panel = lax.ppermute(given_panel, "orient", mate_pairs)

    noise = noise_weight[None, :]
    waiting = [((0, False), kept), ((0, True), got)]
    ahead = {False: kept, True: given}
    behind = {False: kept, True: given}
    orders, earlier, late = [], [], []
    squares = pl.pallas_call(
        square_kernel,
        in_specs=[vmem],
        out_specs=vmem,
        out_shape=panel_shape,
        compiler_params=params,
        cost_estimate=pl.CostEstimate(flops=SCHEDULING_WEIGHT, bytes_accessed=0, transcendentals=0),
    )(own_panel)
    score = lambda c: score_call(c, None, None, spot, noise, own_panel, squares, mate_panel)
    for step in range(1, chips + 1):
        if step == 3:
            orders.append([key for key, _ in waiting])
            earlier.append(score([c for _, c in waiting]))
            waiting = []
            for chain, c in ((ahead, False), (behind, True)):
                chain[c] = lax.optimization_barrier((chain[c], earlier[-1][2]))[0]
        if step == 2:
            for chain, c in ((ahead, False), (behind, False)):
                chain[c] = lax.optimization_barrier((chain[c], squares))[0]
        waiting = waiting + late
        late = []
        for crossed in (False, True):
            if step < chips or not crossed:
                with jax.named_scope("rows_ahead"):
                    ahead[crossed] = forward(ahead[crossed], 1, int(crossed and step == 1))
                late.append(((-step, crossed), ahead[crossed]))
            if step < chips or crossed:
                with jax.named_scope("rows_behind"):
                    behind[crossed] = forward(behind[crossed], -1, int(crossed and step == 1))
                late.append(((step, crossed), behind[crossed]))
    orders.append([key for key, _ in waiting])
    earlier.append(score([c for _, c in waiting]))
    waiting = late
    orders.append([key for key, _ in waiting])
    partial, all_facts = score_call(
        [c for _, c in waiting], orders, earlier, spot, noise, own_panel, squares, mate_panel
    )

    mate_partial = lax.ppermute(partial, "orient", mate_pairs)
    mine, across, stats = pl.pallas_call(
        functools.partial(chip_kernel, local_search),
        in_specs=[smem] + [vmem] * 3,
        out_specs=[vmem] * 3,
        out_shape=[
            jax.ShapeDtypeStruct((everyone, orientations), jnp.float32),
            jax.ShapeDtypeStruct((everyone, orientations), jnp.float32),
            jax.ShapeDtypeStruct((8, everyone), jnp.float32),
        ],
        compiler_params=params,
    )(spot, partial, mate_partial, all_facts)

    x_stats = lax.ppermute(stats, "cls", x_pairs)
    across, _ = lax.optimization_barrier((across, stats))
    from_x = lax.ppermute(across, "cls", x_pairs)
    peak = jnp.maximum(stats[0], x_stats[1])
    total = stats[2] * jnp.exp(stats[0] - peak) + x_stats[3] * jnp.exp(x_stats[1] - peak)
    pair = jnp.pad(jnp.stack([peak, total]), ((0, 6), (0, 0)))
    slots, chosen, tops = pl.pallas_call(
        functools.partial(slot_kernel, local_search, slots_each, per_device),
        in_specs=[smem] + [vmem] * 3,
        out_specs=[vmem] * 3,
        out_shape=[
            jax.ShapeDtypeStruct((capacity, 2 * orientations), jnp.float32),
            jax.ShapeDtypeStruct((capacity, everyone), jnp.float32),
            jax.ShapeDtypeStruct((8, everyone), jnp.float32),
        ],
        compiler_params=params,
    )(spot, mine, from_x, all_facts)
    if chips == 4:
        near = lax.ppermute(pair, "orient", [(d, d ^ (2 << d % 2)) for d in range(devices)])
        far = lax.ppermute(pair, "orient", [(d, d ^ 6) for d in range(devices)])
        near, tops = lax.optimization_barrier((near, tops))
        parts = [pair, near, lax.ppermute(near, "orient", mate_pairs), far]
    else:
        parts = [pair] + [
            lax.ppermute(pair, "orient", [(d, (d + 2 * s) % devices) for d in range(devices)])
            for s in range(1, chips)
        ]
    posterior = pl.pallas_call(
        functools.partial(final_kernel, chips),
        in_specs=[vmem] * (chips + 3),
        out_specs=vmem,
        out_shape=jax.ShapeDtypeStruct((capacity, 2 * orientations), jnp.float32),
        compiler_params=params,
    )(*parts, tops, slots, chosen)
    return posterior.reshape(1, 1, capacity, -1)


def spread_max(member, is_live, values):
    picked = jnp.max(jnp.where(member, values[None, :], FLOOR), axis=1)
    return jnp.where(is_live, picked, 0.0)


def collect_sums(member, expo):
    return jnp.sum(jnp.where(member, jnp.sum(expo, axis=1)[:, None], 0.0), axis=0)


def shards(images, defocus, block_ids, noise_weight, panels):
    per_device = images.shape[1]
    columns = images.shape[3]
    devices = lax.axis_size("orient")
    local_search = block_ids.shape[2]
    slots_each = min(per_device, max(2, 2 * per_device * local_search // devices))
    capacity = slots_each * devices
    everyone = per_device * devices
    all_lists = lax.all_gather(block_ids[0], "orient", axis=0, tiled=True)
    all_rows, all_focus = (
        lax.all_gather(images[0], "orient", axis=0, tiled=True),
        lax.all_gather(defocus[0], "orient", axis=0, tiled=True),
    )
    own_block = lax.axis_index("orient")
    block_hits = (
        jnp.any(all_lists == own_block, axis=1).astype(jnp.int32).reshape(devices, per_device)
    )
    slot_rank = jnp.cumsum(block_hits, axis=1) - block_hits
    places = (jnp.arange(devices, dtype=jnp.int32)[:, None] * slots_each + slot_rank).reshape(
        everyone
    )
    chosen = (places[None, :] == jnp.arange(capacity, dtype=jnp.int32)[:, None]) & (
        block_hits.reshape(everyone)[None, :] == 1
    )
    is_live = jnp.any(chosen, axis=1)
    slot_owner = jnp.sum(
        jnp.where(chosen, jnp.arange(everyone, dtype=jnp.int32)[None, :], 0), axis=1
    )
    slot_rows = jnp.take(all_rows, slot_owner, axis=0)
    slot_focus = jnp.take(all_focus, slot_owner, axis=0).astype(jnp.float32)
    frequency = (jnp.arange(columns, dtype=jnp.float32) + 0.5) / columns
    contrast = -jnp.sin(CTF_PHASE * slot_focus[:, None] * frequency[None, :] + 0.1)
    weighted = contrast * noise_weight[None, :]
    scaled_rows = (weighted[:, None, :] * slot_rows.astype(jnp.float32)).astype(jnp.bfloat16)
    energy = (contrast * weighted).astype(jnp.bfloat16)
    piece = lax.all_gather(panels[:, 0], "cls", axis=0, tiled=True)
    widened = piece.astype(jnp.float32)
    squared = (widened * widened).astype(jnp.bfloat16)
    correlate = jnp.einsum("srk,cjrk->scj", scaled_rows, piece, preferred_element_type=jnp.float32)
    energy_term = jnp.einsum("sk,cjrk->scj", energy, squared, preferred_element_type=jnp.float32)
    terms = correlate - 0.5 * energy_term
    combined = terms.reshape(capacity, -1)
    scores = lax.psum_scatter(combined, "rep", scatter_dimension=1, tiled=True)
    member = (slot_owner[:, None] == jnp.arange(everyone, dtype=jnp.int32)[None, :]) & is_live[
        :, None
    ]
    slot_top = jnp.max(scores, axis=1)
    local_peak = jnp.max(jnp.where(member, slot_top[:, None], FLOOR), axis=0)
    peak = lax.pmax(local_peak, ("orient", "rep"))
    slot_peak = spread_max(member, is_live, peak)
    expo = jnp.where(is_live[:, None], jnp.exp(scores - slot_peak[:, None]), 0.0)
    total = lax.psum(collect_sums(member, expo), ("orient", "rep"))
    slot_total = jnp.where(is_live, jnp.sum(jnp.where(member, total[None, :], 0.0), axis=1), 1.0)
    posterior = expo / slot_total[:, None]
    return posterior.reshape(1, 1, capacity, -1)


def solution(mesh):
    in_specs = (
        P(("batch", "cls"), "orient", "rep", None),
        P(("batch", "cls"), "orient"),
        P(("batch", "cls"), "orient", None),
        P(),
        P(("batch", "cls"), "orient", None, "rep", None),
    )
    out_specs = P(("batch", "cls"), "orient", None, "rep")
    sizes = mesh.shape
    paired = sizes["rep"] == 1 and sizes["cls"] == 2 and sizes["orient"] in (4, 8, 16, 32)
    return jax.shard_map(
        chip_shards if paired else shards,
        mesh=mesh,
        in_specs=in_specs,
        out_specs=out_specs,
        check_vma=False,
    )
```

```python
import functools

import jax
import jax.numpy as jnp
from jax import lax
from jax.experimental import pallas as pl
from jax.experimental.pallas import tpu as pltpu
from jax.sharding import PartitionSpec as P

CTF_PHASE = 40.0
FLOOR = -1e30
LANES = 128
VMEM_LIMIT = 8 * 1024 * 1024
SCHEDULING_WEIGHT = 20 * 10**9


def sin_cos(angle):
    turns = jnp.floor(angle * 0.6366197723675814 + 0.5)
    rest = angle - turns * 1.5703125
    rest = rest - turns * 4.837512969970703e-4
    rest = rest - turns * 7.549789948768648e-8
    square = rest * rest
    sine = rest + rest * square * (
        -1.6666654611e-1 + square * (8.3321608736e-3 - square * 1.9515295891e-4)
    )
    cosine = (
        1.0
        - 0.5 * square
        + square
        * square
        * (4.166664568298827e-2 + square * (-1.388731625493765e-3 + square * 2.443315711809948e-5))
    )
    quarter = turns.astype(jnp.int32)
    odd = (quarter & 1) == 1
    low = jnp.where(odd, cosine, sine)
    high = jnp.where(odd, sine, cosine)
    return (
        jnp.where((quarter & 2) == 2, -low, low),
        jnp.where(((quarter + 1) & 2) == 2, -high, high),
    )


def panel_kernel(spot, sides, own, given):
    own[...] = sides[spot[2]]
    given[...] = sides[1 - spot[2]]


def square_kernel(own, squares):
    squares[...] = own[...] * own[...]


def row_kernel(spot, planes, facts, kept, given):
    core = spot[2]
    columns = planes.shape[2]
    for half, out in ((core, kept), (1 - core, given)):
        out[:, :columns] = planes[half]
        out[:, columns:] = facts[...]


def particle_facts(meta):
    return jnp.concatenate([m[...].astype(jnp.float32).T[: m.shape[0]] for m in meta], axis=0)


def add_scores(rows, noise, own_panel, own_squares, mate_panel, turn_sin, turn_cos, sums, segments):
    columns = noise.shape[1]
    width = columns // segments
    tiles = width // LANES
    count = turn_sin.shape[0]
    facts = particle_facts([r.at[:, pl.ds(columns, LANES)] for r in rows])
    rate = jnp.broadcast_to(CTF_PHASE * facts[:, 0:1], (count, LANES))
    lane = lax.broadcasted_iota(jnp.int32, (count, LANES), 1).astype(jnp.float32)
    first_sin, first_cos = sin_cos(rate * ((lane + 0.5) / columns) + 0.1)
    step_sin, step_cos = sin_cos(rate * (LANES / columns))
    turn_sin[...] = step_sin
    turn_cos[...] = step_cos
    for total in sums:
        total[...] = jnp.zeros_like(total)

    def segment(index, carry):
        sine, cosine = carry
        start = pl.multiple_of(index * width, LANES)
        scaled_parts, energy_parts = [], []
        for t in range(tiles):
            window = pl.ds(start + t * LANES, LANES)
            weighted = sine * noise[:, window]
            image = jnp.concatenate([r[:, window] for r in rows], axis=0).astype(jnp.float32)
            scaled_parts.append((weighted * image).astype(jnp.bfloat16))
            energy_parts.append((sine * weighted).astype(jnp.bfloat16))
            ds, dc = turn_sin[...], turn_cos[...]
            sine, cosine = sine * dc + cosine * ds, cosine * dc - sine * ds
        scaled = jnp.concatenate(scaled_parts, axis=1)
        energy = jnp.concatenate(energy_parts, axis=1)
        contract = (((1,), (1,)), ((), ()))
        whole = pl.ds(start, width)
        mate = mate_panel[:, whole]
        for values, squared, total in (
            (own_panel[:, whole], own_squares[:, whole], sums[0]),
            (mate, mate * mate, sums[1]),
        ):
            correlate = lax.dot_general(
                values, scaled, contract, preferred_element_type=jnp.float32
            )
            power = lax.dot_general(squared, energy, contract, preferred_element_type=jnp.float32)
            total[...] += correlate - 0.5 * power
        return sine, cosine

    lax.fori_loop(0, segments, segment, (-first_sin, -first_cos))
    return jnp.pad(facts, ((0, 0), (0, LANES - facts.shape[1])))


def batch_kernel(n, segments, spot, *refs):
    rows = refs[:n]
    noise, own_panel, own_squares, mate_panel = refs[n : n + 4]
    own_out, mate_out, fact_out, turn_sin, turn_cos, *sums = refs[n + 4 :]
    fact_out[...] = add_scores(
        rows, noise, own_panel, own_squares, mate_panel, turn_sin, turn_cos, sums, segments
    )
    own_out[...] = sums[0][...].T
    mate_out[...] = sums[1][...].T


def last_kernel(n, segments, orders, spot, *refs):
    rows = refs[:n]
    noise, own_panel, own_squares, mate_panel = refs[n : n + 4]
    rest = refs[n + 4 :]
    earlier, rest = rest[: 3 * (len(orders) - 1)], rest[3 * (len(orders) - 1) :]
    partial, facts, turn_sin, turn_cos, *sums = rest
    last_facts = add_scores(
        rows, noise, own_panel, own_squares, mate_panel, turn_sin, turn_cos, sums, segments
    )
    position, core = spot[1], spot[2]
    each = rows[0].shape[0]
    ring = facts.shape[0] // (2 * each)
    half = ring // 2
    for index, order in enumerate(orders):
        if index < len(orders) - 1:
            own, mate, fact = [r[...] for r in earlier[3 * index : 3 * index + 3]]
        else:
            own, mate, fact = sums[0][...].T, sums[1][...].T, last_facts
        for k, (distance, crossed) in enumerate(order):
            place = lax.rem(position + distance + ring, ring)
            far = place >= half
            level = jnp.where(far, ring - 1 - place, place)
            device = 2 * level + (1 - core if crossed else core)
            start = pl.multiple_of((jnp.where(far, ring, 0) + device) * each, each)
            piece = slice(k * each, (k + 1) * each)
            partial[core, pl.ds(start, each), :] = own[piece]
            partial[1 - core, pl.ds(start, each), :] = mate[piece]
            facts[pl.ds(start, each), :] = fact[piece]


def score_call(chunks, orders, earlier, spot, noise, own_panel, squares, mate_panel):
    each = chunks[0].shape[0]
    orientations, columns = own_panel.shape
    whole = columns // LANES
    segments = 1
    n = len(chunks)
    count = each * n
    scratch = [pltpu.VMEM((count, LANES), jnp.float32)] * 2
    scratch += [pltpu.VMEM((orientations, count), jnp.float32)] * 2
    single = jax.ShapeDtypeStruct((count, orientations), jnp.float32)
    if orders is None:
        kernel = functools.partial(batch_kernel, n, segments)
        out_shape = [single, single, jax.ShapeDtypeStruct((count, LANES), jnp.float32)]
        extra = []
    else:
        everyone = each * sum(len(o) for o in orders)
        kernel = functools.partial(last_kernel, n, segments, orders)
        out_shape = [
            jax.ShapeDtypeStruct((2, everyone, orientations), jnp.float32),
            jax.ShapeDtypeStruct((everyone, LANES), jnp.float32),
        ]
        extra = [e for triple in earlier for e in triple]
    vmem = pl.BlockSpec(memory_space=pltpu.VMEM)
    return pl.pallas_call(
        kernel,
        in_specs=[pl.BlockSpec(memory_space=pltpu.SMEM)] + [vmem] * (n + 4 + len(extra)),
        out_specs=[vmem] * len(out_shape),
        out_shape=out_shape,
        scratch_shapes=scratch,
        compiler_params=pltpu.CompilerParams(vmem_limit_bytes=VMEM_LIMIT),
        cost_estimate=pl.CostEstimate(
            flops=8 * max(count, 128) * orientations * columns,
            bytes_accessed=4 * orientations * columns + 2 * count * columns,
            transcendentals=0,
        ),
    )(spot, *chunks, noise, own_panel, squares, mate_panel, *extra)


def names_block(facts, search, block):
    lane = lax.broadcasted_iota(jnp.int32, facts.shape, 1)
    match = (lane >= 1) & (lane <= search) & (facts == block.astype(jnp.float32))
    return jnp.max(jnp.where(match, 1.0, 0.0), axis=1, keepdims=True) > 0.0


def mask_kernel(search, spot, facts, masks):
    core, place = spot[2], spot[3]
    for block in range(2):
        named = names_block(facts[...], search, place - core + block)
        masks[block] = jnp.broadcast_to(jnp.where(named, 1.0, 0.0), masks.shape[1:])


def chip_kernel(spot, partial, mate, masks, mine, across, stats):
    group, core = spot[0], spot[2]
    count = mine.shape[0]
    lane = lax.broadcasted_iota(jnp.int32, (count, LANES), 1)
    pairs = []
    for relative in range(2):
        side = group if relative == 0 else 1 - group
        window = pl.ds(pl.multiple_of(side * count, count), count)
        masked = []
        for crossed in range(2):
            block = core if crossed == 0 else 1 - core
            scores = partial[block, window, :] + mate[block, window, :]
            if crossed == 0:
                out = mine if relative == 0 else across
                out[...] = scores
            masked.append(jnp.where(masks[block, window, :] > 0.0, scores, FLOOR))
        top = jnp.max(jnp.maximum(*masked), axis=1, keepdims=True)
        terms = [jnp.where(m > FLOOR, jnp.exp(m - top), 0.0) for m in masked]
        total = jnp.sum(terms[0] + terms[1], axis=1, keepdims=True)
        pairs.append(jnp.where(lane == relative, top, jnp.where(lane == 2 + relative, total, 0.0)))
    stats[...] = (pairs[0] + pairs[1]).T[: stats.shape[0]]


def slot_kernel(search, slots_each, each, spot, mine, across, facts, slots, chosen, tops):
    group, place = spot[0], spot[3]
    count = mine.shape[0]
    same, other = mine[...], across[...]
    first = group == 0
    scores = jnp.concatenate(
        [jnp.where(first, same, other), jnp.where(first, other, same)], axis=1
    )
    listed = facts[pl.ds(pl.multiple_of(group * count, count), count), :]
    named = names_block(listed, search, place)
    hit = jnp.where(named, 1.0, 0.0)
    row = lax.broadcasted_iota(jnp.int32, (count, LANES), 0)
    line = lax.broadcasted_iota(jnp.int32, (count, count), 0)
    column = lax.broadcasted_iota(jnp.int32, (count, count), 1)
    before = (column < line) & (column // each == line // each)
    rank = jnp.dot(
        jnp.where(before, 1.0, 0.0).astype(jnp.bfloat16),
        jnp.broadcast_to(hit, (count, LANES)).astype(jnp.bfloat16),
        preferred_element_type=jnp.float32,
    )
    slot = (row // each) * slots_each + rank.astype(jnp.int32)
    capacity = chosen.shape[0]
    if capacity != LANES:
        slot = jnp.broadcast_to(slot[:, :1], (count, capacity))
    target = lax.broadcasted_iota(jnp.int32, (count, capacity), 1)
    taken = jnp.where((slot == target) & named, 1.0, 0.0)
    top = jnp.max(scores, axis=1, keepdims=True)
    tops[...] = jnp.broadcast_to(top, (count, LANES)).T[: tops.shape[0]]
    terms = jnp.where(named, jnp.exp(scores - top), 0.0)
    slots[...] = lax.dot_general(
        taken,
        terms,
        (((0,), (0,)), ((), ())),
        precision=lax.Precision.HIGHEST,
        preferred_element_type=jnp.float32,
    )
    chosen[...] = taken.T


def final_kernel(n, *refs):
    parts, (tops, slots, chosen, out) = refs[:n], refs[n:]
    peak = functools.reduce(jnp.maximum, [p[0:1, :] for p in parts])
    shares = [p[1:2, :] * jnp.exp(p[0:1, :] - peak) for p in parts]
    total = functools.reduce(jnp.add, shares)
    factor = jnp.exp(jnp.minimum(tops[0:1, :] - peak, 0.0)) / total
    scale = jnp.sum(chosen[...] * factor, axis=1, keepdims=True)
    out[...] = slots[...] * scale


def chip_shards(images, defocus, block_ids, noise_weight, panels):
    per_device, halves, columns = images.shape[1:]
    devices = lax.axis_size("orient")
    chips = devices // 2
    ring = 2 * chips
    everyone = per_device * devices
    local_search = block_ids.shape[2]
    orientations = panels.shape[2]
    slots_each = min(per_device, max(2, 2 * per_device * local_search // devices))
    capacity = slots_each * devices
    place = lax.axis_index("orient")
    group = lax.axis_index("cls")
    chip, core = place // 2, place % 2
    position = jnp.where(group == 0, chip, ring - 1 - chip)
    spot = jnp.stack([group, position, core, place]).astype(jnp.int32)

    mate_pairs = [(d, d ^ 1) for d in range(devices)]
    x_pairs = [(0, 1), (1, 0)]

    def joint(place, core):
        place = place % ring
        far = place >= chips
        level = ring - 1 - place if far else place
        return (2 * level + core) * 2 + int(far)

    def forward(values, step, cross=0):
        pairs = [(joint(p, c), joint(p + step, c ^ cross)) for p in range(ring) for c in range(2)]
        return lax.ppermute(values, ("orient", "cls"), pairs)

    vmem = pl.BlockSpec(memory_space=pltpu.VMEM)
    smem = pl.BlockSpec(memory_space=pltpu.SMEM)
    params = pltpu.CompilerParams(vmem_limit_bytes=VMEM_LIMIT)
    planes = lax.optimization_barrier(jnp.transpose(images[0], (1, 0, 2)))
    facts = jnp.concatenate([defocus, jnp.transpose(block_ids[0]).astype(jnp.bfloat16)], axis=0)
    facts = jnp.pad(facts, ((0, per_device - facts.shape[0]), (0, LANES - per_device)))
    row_shape = jax.ShapeDtypeStruct((per_device, columns + LANES), jnp.bfloat16)
    kept, given = pl.pallas_call(
        row_kernel,
        in_specs=[smem, vmem, vmem],
        out_specs=[vmem] * 2,
        out_shape=[row_shape] * 2,
        compiler_params=params,
    )(spot, planes, facts)

    _, panels = lax.optimization_barrier((kept, panels))
    sides = lax.optimization_barrier(jnp.transpose(panels[0, 0], (1, 0, 2)))
    panel_shape = jax.ShapeDtypeStruct(sides.shape[1:], sides.dtype)
    own_panel, given_panel = pl.pallas_call(
        panel_kernel,
        in_specs=[smem, vmem],
        out_specs=[vmem] * 2,
        out_shape=[panel_shape] * 2,
        compiler_params=params,
    )(spot, sides)
    with jax.named_scope("mate_panel"):
        mate_panel = lax.ppermute(given_panel, "orient", mate_pairs)

    noise = noise_weight[None, :]
    waiting = []
    ahead = {False: kept, True: given}
    behind = {False: kept, True: given}
    orders, earlier, late = [], [], []
    squares = pl.pallas_call(
        square_kernel,
        in_specs=[vmem],
        out_specs=vmem,
        out_shape=panel_shape,
        compiler_params=params,
        cost_estimate=pl.CostEstimate(flops=SCHEDULING_WEIGHT, bytes_accessed=0, transcendentals=0),
    )(own_panel)
    score = lambda c: score_call(c, None, None, spot, noise, own_panel, squares, mate_panel)
    for step in range(1, chips + 1):
        if step == 3:
            orders.append([key for key, _ in waiting])
            earlier.append(score([c for _, c in waiting]))
            waiting = []
            for chain, c in ((ahead, False), (behind, True)):
                chain[c] = lax.optimization_barrier((chain[c], earlier[-1][2]))[0]
        if step == 2:
            for chain, c in ((ahead, False), (behind, True)):
                chain[c] = lax.optimization_barrier((chain[c], squares))[0]
        waiting = waiting + late
        late = []
        for crossed in (False, True):
            if step < chips or not crossed:
                with jax.named_scope("rows_ahead"):
                    ahead[crossed] = forward(ahead[crossed], 1, int(crossed and step == 1))
                late.append(((-step, crossed), ahead[crossed]))
            if step < chips or crossed:
                with jax.named_scope("rows_behind"):
                    behind[crossed] = forward(behind[crossed], -1, int(crossed and step == 1))
                late.append(((step, crossed), behind[crossed]))
        if step == 1:
            late_given, _ = lax.optimization_barrier((given, kept))
            with jax.named_scope("mate_rows"):
                got = lax.ppermute(late_given, "orient", mate_pairs)
            late = [((0, False), kept), ((0, True), got)] + late
    orders.append([key for key, _ in waiting])
    earlier.append(score([c for _, c in waiting]))
    waiting = late
    orders.append([key for key, _ in waiting])
    partial, all_facts = score_call(
        [c for _, c in waiting], orders, earlier, spot, noise, own_panel, squares, mate_panel
    )

    mate_partial = lax.ppermute(partial, "orient", mate_pairs)
    masks = pl.pallas_call(
        functools.partial(mask_kernel, local_search),
        in_specs=[smem, vmem],
        out_specs=vmem,
        out_shape=jax.ShapeDtypeStruct((2, 2 * everyone, orientations), jnp.float32),
        compiler_params=params,
    )(spot, all_facts)
    mine, across, stats = pl.pallas_call(
        chip_kernel,
        in_specs=[smem] + [vmem] * 3,
        out_specs=[vmem] * 3,
        out_shape=[
            jax.ShapeDtypeStruct((everyone, orientations), jnp.float32),
            jax.ShapeDtypeStruct((everyone, orientations), jnp.float32),
            jax.ShapeDtypeStruct((8, everyone), jnp.float32),
        ],
        compiler_params=params,
    )(spot, partial, mate_partial, masks)

    x_stats = lax.ppermute(stats, "cls", x_pairs)
    across, _ = lax.optimization_barrier((across, stats))
    from_x = lax.ppermute(across, "cls", x_pairs)
    peak = jnp.maximum(stats[0], x_stats[1])
    total = stats[2] * jnp.exp(stats[0] - peak) + x_stats[3] * jnp.exp(x_stats[1] - peak)
    pair = jnp.pad(jnp.stack([peak, total]), ((0, 6), (0, 0)))
    slots, chosen, tops = pl.pallas_call(
        functools.partial(slot_kernel, local_search, slots_each, per_device),
        in_specs=[smem] + [vmem] * 3,
        out_specs=[vmem] * 3,
        out_shape=[
            jax.ShapeDtypeStruct((capacity, 2 * orientations), jnp.float32),
            jax.ShapeDtypeStruct((capacity, everyone), jnp.float32),
            jax.ShapeDtypeStruct((8, everyone), jnp.float32),
        ],
        compiler_params=params,
    )(spot, mine, from_x, all_facts)
    if chips == 4:
        near = lax.ppermute(pair, "orient", [(d, d ^ (2 << d % 2)) for d in range(devices)])
        far = lax.ppermute(pair, "orient", [(d, d ^ 6) for d in range(devices)])
        near, tops = lax.optimization_barrier((near, tops))
        parts = [pair, near, lax.ppermute(near, "orient", mate_pairs), far]
    else:
        parts = [pair] + [
            lax.ppermute(pair, "orient", [(d, (d + 2 * s) % devices) for d in range(devices)])
            for s in range(1, chips)
        ]
    posterior = pl.pallas_call(
        functools.partial(final_kernel, chips),
        in_specs=[vmem] * (chips + 3),
        out_specs=vmem,
        out_shape=jax.ShapeDtypeStruct((capacity, 2 * orientations), jnp.float32),
        compiler_params=params,
    )(*parts, tops, slots, chosen)
    return posterior.reshape(1, 1, capacity, -1)


def spread_max(member, is_live, values):
    picked = jnp.max(jnp.where(member, values[None, :], FLOOR), axis=1)
    return jnp.where(is_live, picked, 0.0)


def collect_sums(member, expo):
    return jnp.sum(jnp.where(member, jnp.sum(expo, axis=1)[:, None], 0.0), axis=0)


def shards(images, defocus, block_ids, noise_weight, panels):
    per_device = images.shape[1]
    columns = images.shape[3]
    devices = lax.axis_size("orient")
    local_search = block_ids.shape[2]
    slots_each = min(per_device, max(2, 2 * per_device * local_search // devices))
    capacity = slots_each * devices
    everyone = per_device * devices
    all_lists = lax.all_gather(block_ids[0], "orient", axis=0, tiled=True)
    all_rows, all_focus = (
        lax.all_gather(images[0], "orient", axis=0, tiled=True),
        lax.all_gather(defocus[0], "orient", axis=0, tiled=True),
    )
    own_block = lax.axis_index("orient")
    block_hits = (
        jnp.any(all_lists == own_block, axis=1).astype(jnp.int32).reshape(devices, per_device)
    )
    slot_rank = jnp.cumsum(block_hits, axis=1) - block_hits
    places = (jnp.arange(devices, dtype=jnp.int32)[:, None] * slots_each + slot_rank).reshape(
        everyone
    )
    chosen = (places[None, :] == jnp.arange(capacity, dtype=jnp.int32)[:, None]) & (
        block_hits.reshape(everyone)[None, :] == 1
    )
    is_live = jnp.any(chosen, axis=1)
    slot_owner = jnp.sum(
        jnp.where(chosen, jnp.arange(everyone, dtype=jnp.int32)[None, :], 0), axis=1
    )
    slot_rows = jnp.take(all_rows, slot_owner, axis=0)
    slot_focus = jnp.take(all_focus, slot_owner, axis=0).astype(jnp.float32)
    frequency = (jnp.arange(columns, dtype=jnp.float32) + 0.5) / columns
    contrast = -jnp.sin(CTF_PHASE * slot_focus[:, None] * frequency[None, :] + 0.1)
    weighted = contrast * noise_weight[None, :]
    scaled_rows = (weighted[:, None, :] * slot_rows.astype(jnp.float32)).astype(jnp.bfloat16)
    energy = (contrast * weighted).astype(jnp.bfloat16)
    piece = lax.all_gather(panels[:, 0], "cls", axis=0, tiled=True)
    widened = piece.astype(jnp.float32)
    squared = (widened * widened).astype(jnp.bfloat16)
    correlate = jnp.einsum("srk,cjrk->scj", scaled_rows, piece, preferred_element_type=jnp.float32)
    energy_term = jnp.einsum("sk,cjrk->scj", energy, squared, preferred_element_type=jnp.float32)
    terms = correlate - 0.5 * energy_term
    combined = terms.reshape(capacity, -1)
    scores = lax.psum_scatter(combined, "rep", scatter_dimension=1, tiled=True)
    member = (slot_owner[:, None] == jnp.arange(everyone, dtype=jnp.int32)[None, :]) & is_live[
        :, None
    ]
    slot_top = jnp.max(scores, axis=1)
    local_peak = jnp.max(jnp.where(member, slot_top[:, None], FLOOR), axis=0)
    peak = lax.pmax(local_peak, ("orient", "rep"))
    slot_peak = spread_max(member, is_live, peak)
    expo = jnp.where(is_live[:, None], jnp.exp(scores - slot_peak[:, None]), 0.0)
    total = lax.psum(collect_sums(member, expo), ("orient", "rep"))
    slot_total = jnp.where(is_live, jnp.sum(jnp.where(member, total[None, :], 0.0), axis=1), 1.0)
    posterior = expo / slot_total[:, None]
    return posterior.reshape(1, 1, capacity, -1)


def solution(mesh):
    in_specs = (
        P(("batch", "cls"), "orient", "rep", None),
        P(("batch", "cls"), "orient"),
        P(("batch", "cls"), "orient", None),
        P(),
        P(("batch", "cls"), "orient", None, "rep", None),
    )
    out_specs = P(("batch", "cls"), "orient", None, "rep")
    sizes = mesh.shape
    paired = sizes["rep"] == 1 and sizes["cls"] == 2 and sizes["orient"] in (4, 8, 16, 32)
    return jax.shard_map(
        chip_shards if paired else shards,
        mesh=mesh,
        in_specs=in_specs,
        out_specs=out_specs,
        check_vma=False,
    )
```

```python
import functools

import jax
import jax.numpy as jnp
from jax import lax
from jax.experimental import pallas as pl
from jax.experimental.pallas import tpu as pltpu
from jax.sharding import PartitionSpec as P

CTF_PHASE = 40.0
FLOOR = -1e30
LANES = 128
VMEM_LIMIT = 8 * 1024 * 1024
SCHEDULING_WEIGHT = 20 * 10**9


def sin_cos(angle):
    turns = jnp.floor(angle * 0.6366197723675814 + 0.5)
    rest = angle - turns * 1.5703125
    rest = rest - turns * 4.837512969970703e-4
    rest = rest - turns * 7.549789948768648e-8
    square = rest * rest
    sine = rest + rest * square * (
        -1.6666654611e-1 + square * (8.3321608736e-3 - square * 1.9515295891e-4)
    )
    cosine = (
        1.0
        - 0.5 * square
        + square
        * square
        * (4.166664568298827e-2 + square * (-1.388731625493765e-3 + square * 2.443315711809948e-5))
    )
    quarter = turns.astype(jnp.int32)
    odd = (quarter & 1) == 1
    low = jnp.where(odd, cosine, sine)
    high = jnp.where(odd, sine, cosine)
    return (
        jnp.where((quarter & 2) == 2, -low, low),
        jnp.where(((quarter + 1) & 2) == 2, -high, high),
    )


def panel_kernel(spot, sides, own, given):
    own[...] = sides[spot[2]]
    given[...] = sides[1 - spot[2]]


def square_kernel(own, squares):
    squares[...] = own[...] * own[...]


def row_kernel(spot, planes, facts, kept, given):
    core = spot[2]
    columns = planes.shape[2]
    for half, out in ((core, kept), (1 - core, given)):
        out[:, :columns] = planes[half]
        out[:, columns:] = facts[...]


def particle_facts(meta):
    return jnp.concatenate([m[...].astype(jnp.float32).T[: m.shape[0]] for m in meta], axis=0)


def add_scores(rows, noise, own_panel, own_squares, mate_panel, turn_sin, turn_cos, sums, segments):
    columns = noise.shape[1]
    width = columns // segments
    tiles = width // LANES
    count = turn_sin.shape[0]
    facts = particle_facts([r.at[:, pl.ds(columns, LANES)] for r in rows])
    rate = jnp.broadcast_to(CTF_PHASE * facts[:, 0:1], (count, LANES))
    lane = lax.broadcasted_iota(jnp.int32, (count, LANES), 1).astype(jnp.float32)
    first_sin, first_cos = sin_cos(rate * ((lane + 0.5) / columns) + 0.1)
    step_sin, step_cos = sin_cos(rate * (LANES / columns))
    turn_sin[...] = step_sin
    turn_cos[...] = step_cos
    for total in sums:
        total[...] = jnp.zeros_like(total)

    def segment(index, carry):
        sine, cosine = carry
        start = pl.multiple_of(index * width, LANES)
        scaled_parts, energy_parts = [], []
        for t in range(tiles):
            window = pl.ds(start + t * LANES, LANES)
            weighted = sine * noise[:, window]
            image = jnp.concatenate([r[:, window] for r in rows], axis=0).astype(jnp.float32)
            scaled_parts.append((weighted * image).astype(jnp.bfloat16))
            energy_parts.append((sine * weighted).astype(jnp.bfloat16))
            ds, dc = turn_sin[...], turn_cos[...]
            sine, cosine = sine * dc + cosine * ds, cosine * dc - sine * ds
        scaled = jnp.concatenate(scaled_parts, axis=1)
        energy = jnp.concatenate(energy_parts, axis=1)
        contract = (((1,), (1,)), ((), ()))
        whole = pl.ds(start, width)
        mate = mate_panel[:, whole]
        for values, squared, total in (
            (own_panel[:, whole], own_squares[:, whole], sums[0]),
            (mate, mate * mate, sums[1]),
        ):
            correlate = lax.dot_general(
                values, scaled, contract, preferred_element_type=jnp.float32
            )
            power = lax.dot_general(squared, energy, contract, preferred_element_type=jnp.float32)
            total[...] += correlate - 0.5 * power
        return sine, cosine

    lax.fori_loop(0, segments, segment, (-first_sin, -first_cos))
    return jnp.pad(facts, ((0, 0), (0, LANES - facts.shape[1])))


def batch_kernel(n, segments, spot, *refs):
    rows = refs[:n]
    noise, own_panel, own_squares, mate_panel = refs[n : n + 4]
    own_out, mate_out, fact_out, turn_sin, turn_cos, *sums = refs[n + 4 :]
    fact_out[...] = add_scores(
        rows, noise, own_panel, own_squares, mate_panel, turn_sin, turn_cos, sums, segments
    )
    own_out[...] = sums[0][...].T
    mate_out[...] = sums[1][...].T


def last_kernel(n, segments, orders, spot, *refs):
    rows = refs[:n]
    noise, own_panel, own_squares, mate_panel = refs[n : n + 4]
    rest = refs[n + 4 :]
    earlier, rest = rest[: 3 * (len(orders) - 1)], rest[3 * (len(orders) - 1) :]
    partial, facts, turn_sin, turn_cos, *sums = rest
    last_facts = add_scores(
        rows, noise, own_panel, own_squares, mate_panel, turn_sin, turn_cos, sums, segments
    )
    position, core = spot[1], spot[2]
    each = rows[0].shape[0]
    ring = facts.shape[0] // (2 * each)
    half = ring // 2
    for index, order in enumerate(orders):
        if index < len(orders) - 1:
            own, mate, fact = [r[...] for r in earlier[3 * index : 3 * index + 3]]
        else:
            own, mate, fact = sums[0][...].T, sums[1][...].T, last_facts
        for k, (distance, crossed) in enumerate(order):
            place = lax.rem(position + distance + ring, ring)
            far = place >= half
            level = jnp.where(far, ring - 1 - place, place)
            device = 2 * level + (1 - core if crossed else core)
            start = pl.multiple_of((jnp.where(far, ring, 0) + device) * each, each)
            piece = slice(k * each, (k + 1) * each)
            partial[core, pl.ds(start, each), :] = own[piece]
            partial[1 - core, pl.ds(start, each), :] = mate[piece]
            facts[pl.ds(start, each), :] = fact[piece]


def score_call(chunks, orders, earlier, spot, noise, own_panel, squares, mate_panel):
    each = chunks[0].shape[0]
    orientations, columns = own_panel.shape
    whole = columns // LANES
    segments = 1
    n = len(chunks)
    count = each * n
    scratch = [pltpu.VMEM((count, LANES), jnp.float32)] * 2
    scratch += [pltpu.VMEM((orientations, count), jnp.float32)] * 2
    single = jax.ShapeDtypeStruct((count, orientations), jnp.float32)
    if orders is None:
        kernel = functools.partial(batch_kernel, n, segments)
        out_shape = [single, single, jax.ShapeDtypeStruct((count, LANES), jnp.float32)]
        extra = []
    else:
        everyone = each * sum(len(o) for o in orders)
        kernel = functools.partial(last_kernel, n, segments, orders)
        out_shape = [
            jax.ShapeDtypeStruct((2, everyone, orientations), jnp.float32),
            jax.ShapeDtypeStruct((everyone, LANES), jnp.float32),
        ]
        extra = [e for triple in earlier for e in triple]
    vmem = pl.BlockSpec(memory_space=pltpu.VMEM)
    return pl.pallas_call(
        kernel,
        in_specs=[pl.BlockSpec(memory_space=pltpu.SMEM)] + [vmem] * (n + 4 + len(extra)),
        out_specs=[vmem] * len(out_shape),
        out_shape=out_shape,
        scratch_shapes=scratch,
        compiler_params=pltpu.CompilerParams(vmem_limit_bytes=VMEM_LIMIT),
        cost_estimate=pl.CostEstimate(
            flops=8 * max(count, 128) * orientations * columns,
            bytes_accessed=4 * orientations * columns + 2 * count * columns,
            transcendentals=0,
        ),
    )(spot, *chunks, noise, own_panel, squares, mate_panel, *extra)


def names_block(facts, search, block):
    lane = lax.broadcasted_iota(jnp.int32, facts.shape, 1)
    match = (lane >= 1) & (lane <= search) & (facts == block.astype(jnp.float32))
    return jnp.max(jnp.where(match, 1.0, 0.0), axis=1, keepdims=True) > 0.0


def mask_kernel(search, spot, facts, masks):
    core, place = spot[2], spot[3]
    for block in range(2):
        named = names_block(facts[...], search, place - core + block)
        masks[block] = jnp.broadcast_to(jnp.where(named, 1.0, 0.0), masks.shape[1:])


def chip_kernel(spot, partial, mate, masks, mine, across, stats):
    group, core = spot[0], spot[2]
    count = mine.shape[0]
    lane = lax.broadcasted_iota(jnp.int32, (count, LANES), 1)
    pairs = []
    for relative in range(2):
        side = group if relative == 0 else 1 - group
        window = pl.ds(pl.multiple_of(side * count, count), count)
        masked = []
        for crossed in range(2):
            block = core if crossed == 0 else 1 - core
            scores = partial[block, window, :] + mate[block, window, :]
            if crossed == 0:
                out = mine if relative == 0 else across
                out[...] = scores
            masked.append(jnp.where(masks[block, window, :] > 0.0, scores, FLOOR))
        top = jnp.max(jnp.maximum(*masked), axis=1, keepdims=True)
        terms = [jnp.where(m > FLOOR, jnp.exp(m - top), 0.0) for m in masked]
        total = jnp.sum(terms[0] + terms[1], axis=1, keepdims=True)
        pairs.append(jnp.where(lane == relative, top, jnp.where(lane == 2 + relative, total, 0.0)))
    stats[...] = (pairs[0] + pairs[1]).T[: stats.shape[0]]


def slot_kernel(search, slots_each, each, spot, mine, across, facts, slots, chosen, tops):
    group, place = spot[0], spot[3]
    count = mine.shape[0]
    same, other = mine[...], across[...]
    first = group == 0
    scores = jnp.concatenate(
        [jnp.where(first, same, other), jnp.where(first, other, same)], axis=1
    )
    listed = facts[pl.ds(pl.multiple_of(group * count, count), count), :]
    named = names_block(listed, search, place)
    hit = jnp.where(named, 1.0, 0.0)
    row = lax.broadcasted_iota(jnp.int32, (count, LANES), 0)
    line = lax.broadcasted_iota(jnp.int32, (count, count), 0)
    column = lax.broadcasted_iota(jnp.int32, (count, count), 1)
    before = (column < line) & (column // each == line // each)
    rank = jnp.dot(
        jnp.where(before, 1.0, 0.0).astype(jnp.bfloat16),
        jnp.broadcast_to(hit, (count, LANES)).astype(jnp.bfloat16),
        preferred_element_type=jnp.float32,
    )
    slot = (row // each) * slots_each + rank.astype(jnp.int32)
    capacity = chosen.shape[0]
    if capacity != LANES:
        slot = jnp.broadcast_to(slot[:, :1], (count, capacity))
    target = lax.broadcasted_iota(jnp.int32, (count, capacity), 1)
    taken = jnp.where((slot == target) & named, 1.0, 0.0)
    top = jnp.max(scores, axis=1, keepdims=True)
    tops[...] = jnp.broadcast_to(top, (count, LANES)).T[: tops.shape[0]]
    terms = jnp.where(named, jnp.exp(scores - top), 0.0)
    slots[...] = lax.dot_general(
        taken,
        terms,
        (((0,), (0,)), ((), ())),
        precision=lax.Precision.HIGHEST,
        preferred_element_type=jnp.float32,
    )
    chosen[...] = taken.T


def final_kernel(n, *refs):
    parts, (tops, slots, chosen, out) = refs[:n], refs[n:]
    peak = functools.reduce(jnp.maximum, [p[0:1, :] for p in parts])
    shares = [p[1:2, :] * jnp.exp(p[0:1, :] - peak) for p in parts]
    total = functools.reduce(jnp.add, shares)
    factor = jnp.exp(jnp.minimum(tops[0:1, :] - peak, 0.0)) / total
    scale = jnp.sum(chosen[...] * factor, axis=1, keepdims=True)
    out[...] = slots[...] * scale


def chip_shards(images, defocus, block_ids, noise_weight, panels):
    per_device, halves, columns = images.shape[1:]
    devices = lax.axis_size("orient")
    chips = devices // 2
    ring = 2 * chips
    everyone = per_device * devices
    local_search = block_ids.shape[2]
    orientations = panels.shape[2]
    slots_each = min(per_device, max(2, 2 * per_device * local_search // devices))
    capacity = slots_each * devices
    place = lax.axis_index("orient")
    group = lax.axis_index("cls")
    chip, core = place // 2, place % 2
    position = jnp.where(group == 0, chip, ring - 1 - chip)
    spot = jnp.stack([group, position, core, place]).astype(jnp.int32)

    mate_pairs = [(d, d ^ 1) for d in range(devices)]
    x_pairs = [(0, 1), (1, 0)]

    def joint(place, core):
        place = place % ring
        far = place >= chips
        level = ring - 1 - place if far else place
        return (2 * level + core) * 2 + int(far)

    def forward(values, step, cross=0):
        pairs = [(joint(p, c), joint(p + step, c ^ cross)) for p in range(ring) for c in range(2)]
        return lax.ppermute(values, ("orient", "cls"), pairs)

    vmem = pl.BlockSpec(memory_space=pltpu.VMEM)
    smem = pl.BlockSpec(memory_space=pltpu.SMEM)
    params = pltpu.CompilerParams(vmem_limit_bytes=VMEM_LIMIT)
    planes = lax.optimization_barrier(jnp.transpose(images[0], (1, 0, 2)))
    facts = jnp.concatenate([defocus, jnp.transpose(block_ids[0]).astype(jnp.bfloat16)], axis=0)
    facts = jnp.pad(facts, ((0, per_device - facts.shape[0]), (0, LANES - per_device)))
    row_shape = jax.ShapeDtypeStruct((per_device, columns + LANES), jnp.bfloat16)
    kept, given = pl.pallas_call(
        row_kernel,
        in_specs=[smem, vmem, vmem],
        out_specs=[vmem] * 2,
        out_shape=[row_shape] * 2,
        compiler_params=params,
    )(spot, planes, facts)

    with jax.named_scope("mate_rows"):
        got = lax.ppermute(given, "orient", mate_pairs)

    _, panels = lax.optimization_barrier((got, panels))
    sides = lax.optimization_barrier(jnp.transpose(panels[0, 0], (1, 0, 2)))
    panel_shape = jax.ShapeDtypeStruct(sides.shape[1:], sides.dtype)
    own_panel, given_panel = pl.pallas_call(
        panel_kernel,
        in_specs=[smem, vmem],
        out_specs=[vmem] * 2,
        out_shape=[panel_shape] * 2,
        compiler_params=params,
    )(spot, sides)
    with jax.named_scope("mate_panel"):
        mate_panel = lax.ppermute(given_panel, "orient", mate_pairs)

    noise = noise_weight[None, :]
    waiting = [((0, False), kept), ((0, True), got)]
    ahead = {False: kept, True: given}
    behind = {False: kept, True: given}
    orders, earlier, late = [], [], []
    squares = pl.pallas_call(
        square_kernel,
        in_specs=[vmem],
        out_specs=vmem,
        out_shape=panel_shape,
        compiler_params=params,
        cost_estimate=pl.CostEstimate(flops=SCHEDULING_WEIGHT, bytes_accessed=0, transcendentals=0),
    )(own_panel)
    score = lambda c: score_call(c, None, None, spot, noise, own_panel, squares, mate_panel)
    for step in range(1, chips + 1):
        if step == 3:
            orders.append([key for key, _ in waiting])
            earlier.append(score([c for _, c in waiting]))
            waiting = []
            for chain, c in ((ahead, False), (behind, True)):
                chain[c] = lax.optimization_barrier((chain[c], earlier[-1][2]))[0]
        if step == 2:
            for chain, c in ((ahead, False), (behind, False)):
                chain[c] = lax.optimization_barrier((chain[c], squares))[0]
        waiting = waiting + late
        late = []
        for crossed in (False, True):
            if step < chips or not crossed:
                with jax.named_scope("rows_ahead"):
                    ahead[crossed] = forward(ahead[crossed], 1, int(crossed and step == 1))
                late.append(((-step, crossed), ahead[crossed]))
            if step < chips or crossed:
                with jax.named_scope("rows_behind"):
                    behind[crossed] = forward(behind[crossed], -1, int(crossed and step == 1))
                late.append(((step, crossed), behind[crossed]))
    orders.append([key for key, _ in waiting])
    earlier.append(score([c for _, c in waiting]))
    waiting = late
    orders.append([key for key, _ in waiting])
    partial, all_facts = score_call(
        [c for _, c in waiting], orders, earlier, spot, noise, own_panel, squares, mate_panel
    )

    mate_partial = lax.ppermute(partial, "orient", mate_pairs)
    masks = pl.pallas_call(
        functools.partial(mask_kernel, local_search),
        in_specs=[smem, vmem],
        out_specs=vmem,
        out_shape=jax.ShapeDtypeStruct((2, 2 * everyone, orientations), jnp.float32),
        compiler_params=params,
    )(spot, all_facts)
    mine, across, stats = pl.pallas_call(
        chip_kernel,
        in_specs=[smem] + [vmem] * 3,
        out_specs=[vmem] * 3,
        out_shape=[
            jax.ShapeDtypeStruct((everyone, orientations), jnp.float32),
            jax.ShapeDtypeStruct((everyone, orientations), jnp.float32),
            jax.ShapeDtypeStruct((8, everyone), jnp.float32),
        ],
        compiler_params=params,
    )(spot, partial, mate_partial, masks)

    x_stats = lax.ppermute(stats, "cls", x_pairs)
    across, _ = lax.optimization_barrier((across, stats))
    from_x = lax.ppermute(across, "cls", x_pairs)
    peak = jnp.maximum(stats[0], x_stats[1])
    total = stats[2] * jnp.exp(stats[0] - peak) + x_stats[3] * jnp.exp(x_stats[1] - peak)
    pair = jnp.pad(jnp.stack([peak, total]), ((0, 6), (0, 0)))
    slots, chosen, tops = pl.pallas_call(
        functools.partial(slot_kernel, local_search, slots_each, per_device),
        in_specs=[smem] + [vmem] * 3,
        out_specs=[vmem] * 3,
        out_shape=[
            jax.ShapeDtypeStruct((capacity, 2 * orientations), jnp.float32),
            jax.ShapeDtypeStruct((capacity, everyone), jnp.float32),
            jax.ShapeDtypeStruct((8, everyone), jnp.float32),
        ],
        compiler_params=params,
    )(spot, mine, from_x, all_facts)
    if chips == 4:
        near = lax.ppermute(pair, "orient", [(d, d ^ (2 << d % 2)) for d in range(devices)])
        far = lax.ppermute(pair, "orient", [(d, d ^ 6) for d in range(devices)])
        near, tops = lax.optimization_barrier((near, tops))
        parts = [pair, near, lax.ppermute(near, "orient", mate_pairs), far]
    else:
        parts = [pair] + [
            lax.ppermute(pair, "orient", [(d, (d + 2 * s) % devices) for d in range(devices)])
            for s in range(1, chips)
        ]
    posterior = pl.pallas_call(
        functools.partial(final_kernel, chips),
        in_specs=[vmem] * (chips + 3),
        out_specs=vmem,
        out_shape=jax.ShapeDtypeStruct((capacity, 2 * orientations), jnp.float32),
        compiler_params=params,
    )(*parts, tops, slots, chosen)
    return posterior.reshape(1, 1, capacity, -1)


def spread_max(member, is_live, values):
    picked = jnp.max(jnp.where(member, values[None, :], FLOOR), axis=1)
    return jnp.where(is_live, picked, 0.0)


def collect_sums(member, expo):
    return jnp.sum(jnp.where(member, jnp.sum(expo, axis=1)[:, None], 0.0), axis=0)


def shards(images, defocus, block_ids, noise_weight, panels):
    per_device = images.shape[1]
    columns = images.shape[3]
    devices = lax.axis_size("orient")
    local_search = block_ids.shape[2]
    slots_each = min(per_device, max(2, 2 * per_device * local_search // devices))
    capacity = slots_each * devices
    everyone = per_device * devices
    all_lists = lax.all_gather(block_ids[0], "orient", axis=0, tiled=True)
    all_rows, all_focus = (
        lax.all_gather(images[0], "orient", axis=0, tiled=True),
        lax.all_gather(defocus[0], "orient", axis=0, tiled=True),
    )
    own_block = lax.axis_index("orient")
    block_hits = (
        jnp.any(all_lists == own_block, axis=1).astype(jnp.int32).reshape(devices, per_device)
    )
    slot_rank = jnp.cumsum(block_hits, axis=1) - block_hits
    places = (jnp.arange(devices, dtype=jnp.int32)[:, None] * slots_each + slot_rank).reshape(
        everyone
    )
    chosen = (places[None, :] == jnp.arange(capacity, dtype=jnp.int32)[:, None]) & (
        block_hits.reshape(everyone)[None, :] == 1
    )
    is_live = jnp.any(chosen, axis=1)
    slot_owner = jnp.sum(
        jnp.where(chosen, jnp.arange(everyone, dtype=jnp.int32)[None, :], 0), axis=1
    )
    slot_rows = jnp.take(all_rows, slot_owner, axis=0)
    slot_focus = jnp.take(all_focus, slot_owner, axis=0).astype(jnp.float32)
    frequency = (jnp.arange(columns, dtype=jnp.float32) + 0.5) / columns
    contrast = -jnp.sin(CTF_PHASE * slot_focus[:, None] * frequency[None, :] + 0.1)
    weighted = contrast * noise_weight[None, :]
    scaled_rows = (weighted[:, None, :] * slot_rows.astype(jnp.float32)).astype(jnp.bfloat16)
    energy = (contrast * weighted).astype(jnp.bfloat16)
    piece = lax.all_gather(panels[:, 0], "cls", axis=0, tiled=True)
    widened = piece.astype(jnp.float32)
    squared = (widened * widened).astype(jnp.bfloat16)
    correlate = jnp.einsum("srk,cjrk->scj", scaled_rows, piece, preferred_element_type=jnp.float32)
    energy_term = jnp.einsum("sk,cjrk->scj", energy, squared, preferred_element_type=jnp.float32)
    terms = correlate - 0.5 * energy_term
    combined = terms.reshape(capacity, -1)
    scores = lax.psum_scatter(combined, "rep", scatter_dimension=1, tiled=True)
    member = (slot_owner[:, None] == jnp.arange(everyone, dtype=jnp.int32)[None, :]) & is_live[
        :, None
    ]
    slot_top = jnp.max(scores, axis=1)
    local_peak = jnp.max(jnp.where(member, slot_top[:, None], FLOOR), axis=0)
    peak = lax.pmax(local_peak, ("orient", "rep"))
    slot_peak = spread_max(member, is_live, peak)
    expo = jnp.where(is_live[:, None], jnp.exp(scores - slot_peak[:, None]), 0.0)
    total = lax.psum(collect_sums(member, expo), ("orient", "rep"))
    slot_total = jnp.where(is_live, jnp.sum(jnp.where(member, total[None, :], 0.0), axis=1), 1.0)
    posterior = expo / slot_total[:, None]
    return posterior.reshape(1, 1, capacity, -1)


def solution(mesh):
    in_specs = (
        P(("batch", "cls"), "orient", "rep", None),
        P(("batch", "cls"), "orient"),
        P(("batch", "cls"), "orient", None),
        P(),
        P(("batch", "cls"), "orient", None, "rep", None),
    )
    out_specs = P(("batch", "cls"), "orient", None, "rep")
    sizes = mesh.shape
    paired = sizes["rep"] == 1 and sizes["cls"] == 2 and sizes["orient"] in (4, 8, 16, 32)
    return jax.shard_map(
        chip_shards if paired else shards,
        mesh=mesh,
        in_specs=in_specs,
        out_specs=out_specs,
        check_vma=False,
    )
```
